32 devices in a mesh: ctx: 8 (over z, y), exp: 4 (over x, core).
Axes of the slice: x: 2, y: 2, z: 4, core: 2. Of those that a mesh axis runs over, the one named last changes fastest.
Arguments:
- tokens: bfloat16 [4, 1024, 1536], P('exp', 'ctx'), may hold values from -6 to 6
- cotangent: bfloat16 [4, 1024, 1536], P('exp', 'ctx'), may hold values from -6 to 6
- lengths: int32 [4, 2], P('exp'), may hold values from 512 to 512, as said below
- span_perm: int32 [4, 16], P('exp'), may hold values from 0 to 15, as said below
- routes: int32 [4, 1024, 8], P('exp', 'ctx'), may hold values from 0 to 39, all different within a row; in each aligned block of 128 rows (0 to 127, 128 to 255, ..., all dimensions but the last counted through in order) at most 38 rows name the same one
- norm_attn: float32 [1536], P(('ctx', 'exp')), may hold values from 0.25 to 1.75
- attn_q: float32 [1536, 1536], P(('ctx', 'exp')), may hold values from -0.15625 to 0.15625
- attn_k: float32 [1536, 512], P(('ctx', 'exp')), may hold values from -0.15625 to 0.15625
- attn_v: float32 [1536, 512], P(('ctx', 'exp')), may hold values from -0.15625 to 0.15625
- attn_o: float32 [1536, 1536], P(('ctx', 'exp')), may hold values from -2.5 to 2.5
- router: float32 [1536, 40], P(('ctx', 'exp')), may hold values from -0.078125 to 0.078125
- norm_moe: float32 [1536], P(('ctx', 'exp')), may hold values from 0.25 to 1.75
- expert_in: float32 [1536, 40, 1024], P('ctx', 'exp'), may hold values from -0.15625 to 0.15625
- expert_out: float32 [1536, 40, 512], P('ctx', 'exp'), may hold values from -1 to 1
Outputs:
- output: bfloat16 [4, 1024, 1536], P('exp', 'ctx')
- grad_tokens: float32 [4, 1024, 1536], P('exp', 'ctx')
- grad_norm_attn: float32 [1536], P(('ctx', 'exp'))
- grad_attn_q: float32 [1536, 1536], P(('ctx', 'exp'))
- grad_attn_k: float32 [1536, 512], P(('ctx', 'exp'))
- grad_attn_v: float32 [1536, 512], P(('ctx', 'exp'))
- grad_attn_o: float32 [1536, 1536], P(('ctx', 'exp'))
- grad_router: float32 [1536, 40], P(('ctx', 'exp'))
- grad_norm_moe: float32 [1536], P(('ctx', 'exp'))
- grad_expert_in: float32 [1536, 40, 1024], P('ctx', 'exp')
- grad_expert_out: float32 [1536, 40, 512], P('ctx', 'exp')
The draws below stay inside these ranges and needn't reach their ends.
Inputs may be any that keep to these rules, and one draw needn't show every extreme that they name: Each group has 2 sequences whose lengths sum to 1024; the longer one has 512 rows or more; in group 0 it has 512. `span_perm`: each row is a permutation; slots 2 d and 2 d + 1 hold spans j and 15 - j for some j. `routes`: each row names 8 different experts; in the 128 rows of one device no expert is named more than 38 times.
All inputs are finite; a program needn't handle non-finite values.
Results may differ from the reference program's by a relative error of at most 0.03.
Values may be sent and summed in bfloat16 or wider, within the bound.
A program may use at most 448 MiB of HBM per device.

```python
import math
import jax
import jax.numpy as jnp
import numpy as np
from jax import lax

D = 1536
HEADS = 24
KV_HEADS = 8
HEAD = 64
HID = 512
TOP = 8
TOK_DEV = 128
MINLEN = 512
EXPERTS = 40
SPAN = 64
GROUP_TOK = 1024
GROUPS = 4
SLOTS = 16
CAP = 38
N_CTX = 8
N_EXP = 4


def draw_lengths(key, part):
    key = jax.random.fold_in(key, 11)
    keys = jax.random.split(key, 2)
    longer = jax.random.randint(keys[0], (GROUPS,), GROUP_TOK // 2, GROUP_TOK - MINLEN + 1)
    longer = longer.at[0].set(GROUP_TOK - MINLEN)
    flipped = jax.random.randint(keys[1], (GROUPS,), 0, 2)
    first = jnp.where(flipped == 1, longer, GROUP_TOK - longer)
    return jnp.stack([first, GROUP_TOK - first], axis=1).astype(jnp.int32)


def draw_span_perm(key, part):
    key = jax.random.fold_in(key, 23)
    pairs = SLOTS // 2

    def deal_group(subkey):
        first_key, second_key = jax.random.split(subkey)
        owners = jax.random.permutation(first_key, pairs).astype(jnp.int32)
        flipped = jax.random.randint(second_key, (pairs,), 0, 2)
        lower = jnp.arange(pairs, dtype=jnp.int32)
        table = jnp.zeros((SLOTS,), jnp.int32)
        table = table.at[2 * owners + flipped].set(lower)
        table = table.at[2 * owners + 1 - flipped].set(SLOTS - 1 - lower)
        return table
    return jax.vmap(deal_group)(jax.random.split(key, GROUPS))


def level_of(key, extent, cuts, least, top_value):
    loudness, own = 1.0, jax.random.fold_in(key, 6)
    for dim, parts in cuts:
        steps = jnp.exp(jax.random.uniform(jax.random.fold_in(own, dim), (parts,), jnp.float32, least / len(cuts), top_value / len(cuts)))
        loudness = loudness * jnp.repeat(steps, extent[dim] // parts).reshape([-1 if axis == dim else 1 for axis in range(len(extent))])
    return loudness


def shared_out(own_key, own, number, rows, number_of, top, most, skew):
    sequence = jax.random.permutation(own_key, number_of)
    packed, ordinary = portions_of(number_of, rows * top, most, skew, True), portions_of(number_of, rows * top, most, skew, False)
    places = jnp.arange(number_of)

    def named(sizes, offset_by):
        used = int((sizes > 0).sum())
        fixed = max(1, used // 4)
        shifted = fixed + (places - fixed + offset_by * (used - fixed)) % max(1, number_of - fixed)
        return jnp.zeros((number_of,), jnp.int32).at[sequence[jnp.where(places < fixed, places, shifted)]].set(jnp.asarray(sizes, jnp.int32))

    sizes = jnp.where(number % 4 == 0, named(packed, number // 4), named(ordinary, number - number // 4 - 1))
    mixed = jax.random.permutation(jax.random.fold_in(own, 3), number_of)
    source_of, sink = mixed[0:number_of // 2 * 2:2], mixed[1:number_of // 2 * 2:2]
    room = jnp.minimum(sizes[source_of] - 1, most - sizes[sink]) // 2
    room = jnp.where((source_of == sequence[0]) | (sink == sequence[0]) | (sizes[sink] == 0), 0, jnp.maximum(room, 0))
    shifted = jax.random.randint(jax.random.fold_in(own, 4), (number_of // 2,), 0, 1 << 20) % (room + 1)
    sizes = sizes.at[source_of].add(-shifted).at[sink].add(shifted)
    labels = jnp.searchsorted(jnp.cumsum(sizes), jnp.arange(rows * top), side="right").astype(jnp.int32)
    grid = labels.reshape(top, rows).T
    grid = grid[jax.random.permutation(jax.random.fold_in(own, 1), rows)]
    offset_by = jax.random.randint(jax.random.fold_in(own, 2), (rows, 1), 0, top)
    return jnp.take_along_axis(grid, (jnp.arange(top)[None, :] + offset_by) % top, axis=1)


def portions_of(number_of, total, most, skew, full):
    loads = [(1 << 20) // math.isqrt(rank ** skew) + 1 for rank in range(1, number_of + 1)]
    largest = most if full else min(most, max(-(-total // number_of), total * loads[0] // sum(loads)))
    least = 1 if total - largest >= number_of - 1 else 0
    given, rest = [largest] + [least] * (number_of - 1), total - largest - least * (number_of - 1)
    while rest > 0:
        candidates = [i for i in range(1, number_of) if given[i] < largest] or [i for i in range(1, number_of) if given[i] < most]
        mass, remaining = sum([loads[i] for i in candidates]), rest
        for i in candidates:
            addition = min(most - given[i], max(1, remaining * loads[i] // mass), rest)
            given[i] = given[i] + addition
            rest = rest - addition
    return np.array(given)


def gaussian(key, dims, spread, limit, shards=(), held_as=jnp.bfloat16):
    array = spread * jax.random.normal(key, dims, jnp.float32)
    if shards:
        array = array * level_of(key, dims, shards, -0.22, 0.18)
    return jnp.clip(array, -limit, limit).astype(held_as)


def setup_inputs(seed: int = 0) -> dict:
    key_of = jax.random.split(jax.random.key(seed), 15)
    tokens = gaussian(key_of[0], (GROUPS, GROUP_TOK, D), 1.0, 6.0, ((0, 4), (1, 8)))
    cotangent = gaussian(key_of[1], (GROUPS, GROUP_TOK, D), 1.0, 6.0, ((0, 4), (1, 8)))
    lengths = draw_lengths(jax.random.fold_in(key_of[14], 71), 0)
    span_perm = draw_span_perm(jax.random.fold_in(key_of[14], 71), 0)
    routes_keys = jax.random.split(jax.random.fold_in(key_of[4], 1), GROUPS * GROUP_TOK // TOK_DEV)
    routes_turns = jax.random.permutation(jax.random.fold_in(key_of[4], 3), GROUPS * GROUP_TOK // TOK_DEV)
    routes = jax.vmap(lambda own, number: shared_out(jax.random.fold_in(key_of[4], 2), own, number, TOK_DEV, EXPERTS, TOP, CAP, 1))(routes_keys, routes_turns).reshape((GROUPS, GROUP_TOK, TOP))
    norm_attn = jnp.clip(1.0 + 0.15 * jax.random.normal(key_of[5], (D,), jnp.float32), 0.25, 1.75)
    attn_q = gaussian(key_of[6], (D, D), D ** -0.5, 0.15625, ((0, 32),), jnp.float32)
    attn_k = gaussian(key_of[7], (D, KV_HEADS * HEAD), D ** -0.5, 0.15625, ((0, 32),), jnp.float32)
    attn_v = gaussian(key_of[8], (D, KV_HEADS * HEAD), D ** -0.5, 0.15625, ((0, 32),), jnp.float32)
    attn_o = gaussian(key_of[9], (D, D), (max(1, 4 * D // GROUP_TOK)) ** -0.5, 2.5, ((0, 32),), jnp.float32)
    router = gaussian(key_of[10], (D, EXPERTS), (4 * D) ** -0.5, 0.078125, ((0, 32),), jnp.float32)
    norm_moe = jnp.clip(1.0 + 0.15 * jax.random.normal(key_of[11], (D,), jnp.float32), 0.25, 1.75)
    expert_in = gaussian(key_of[12], (D, EXPERTS, 2 * HID), D ** -0.5, 0.15625, ((0, 8), (1, 4)), jnp.float32)
    expert_out = gaussian(key_of[13], (D, EXPERTS, HID), (HID // 16) ** -0.5, 1.0, ((0, 8), (1, 4)), jnp.float32)
    return dict(tokens=tokens, cotangent=cotangent, lengths=lengths, span_perm=span_perm, routes=routes, norm_attn=norm_attn, attn_q=attn_q, attn_k=attn_k, attn_v=attn_v, attn_o=attn_o, router=router, norm_moe=norm_moe, expert_in=expert_in, expert_out=expert_out)


@jax.custom_vjp
def low(v):
    return lax.optimization_barrier(v.astype(jnp.bfloat16)).astype(jnp.float32)

@jax.custom_vjp
def low_back(v):
    return v

def low_keep(v):
    return (low(v), None)

def low_pass(kept, grad):
    return (grad,)

def back_keep(v):
    return (v, None)

def back_low(kept, grad):
    return (low(grad),)
low.defvjp(low_keep, low_pass)
low_back.defvjp(back_keep, back_low)
EPSILON = 1e-06
NEGATIVE = -1e+30
HIGHEST = lax.Precision.HIGHEST

def rotary(tensor, position, sign):
    half = HEAD // 2
    freqs = jnp.exp(jnp.arange(half, dtype=jnp.float32) * (-2.0 * math.log(10000.0) / HEAD))
    angle = position.astype(jnp.float32)[:, None] * freqs[None, :]
    cosine = jnp.cos(angle)[:, None, :]
    sine = sign * jnp.sin(angle)[:, None, :]
    first, second = (tensor[..., :half], tensor[..., half:])
    return jnp.concatenate([first * cosine - second * sine, second * cosine + first * sine], axis=-1)

def normalize(values):
    return values * lax.rsqrt(lax.optimization_barrier(jnp.mean(values * values, axis=-1, keepdims=True)) + EPSILON)

def sequence_rows(perm_row):
    rows = jnp.arange(GROUP_TOK, dtype=jnp.int32)
    return (perm_row[rows // SPAN] * SPAN + rows % SPAN).astype(jnp.int32)

def attend_group(queries, keys, values, seq_rows, first_len):
    block = math.gcd(GROUP_TOK, 512)
    query_blocks = queries.reshape(GROUP_TOK // block, block, KV_HEADS, HEADS // KV_HEADS, HEAD)
    row_blocks = seq_rows.reshape(GROUP_TOK // block, block)
    softmax_scale = HEAD ** (-0.5)

    def one_block(inputs):
        query_block, query_rows = inputs
        scores = jnp.einsum('qgrd,kgd->grqk', query_block, keys, precision=HIGHEST) * softmax_scale
        scores = low_back(scores)
        later = seq_rows[None, :] <= query_rows[:, None]
        same_seq = (seq_rows[None, :] >= first_len) == (query_rows[:, None] >= first_len)
        scores = jnp.where((later & same_seq)[None, None], scores, NEGATIVE)
        weights = low(jax.nn.softmax(scores, axis=-1))
        return jnp.einsum('grqk,kgd->qgrd', weights, values, precision=HIGHEST)
    attended = lax.map(jax.checkpoint(one_block), (query_blocks, row_blocks))
    return attended.reshape(GROUP_TOK, HEADS * HEAD)

def block_forward(tokens, norm_attn, attn_q, attn_k, attn_v, attn_o, router, norm_moe, expert_in, expert_out, seq_rows, first_lens, routes):
    gain_one = low(norm_attn)
    weight_q = low(attn_q)
    weight_k = low(attn_k)
    weight_v = low(attn_v)
    weight_o = low(attn_o)
    weight_r = low(router)
    gain_two = low(norm_moe)
    weight_in = low(expert_in)
    weight_out = low(expert_out)
    middles = []
    for group in range(GROUPS):
        resid = tokens[group]
        rows = seq_rows[group]
        first_len = first_lens[group]
        position = rows - jnp.where(rows >= first_len, first_len, 0)
        hidden = low(normalize(resid) * gain_one)
        queries = jnp.dot(hidden, weight_q, precision=HIGHEST).reshape(GROUP_TOK, HEADS, HEAD)
        queries = low(rotary(low_back(queries), position, 1.0)).reshape(GROUP_TOK, KV_HEADS, HEADS // KV_HEADS, HEAD)
        keys = jnp.dot(hidden, weight_k, precision=HIGHEST).reshape(GROUP_TOK, KV_HEADS, HEAD)
        keys = low(rotary(low_back(keys), position, 1.0))
        values = low(low_back(jnp.dot(hidden, weight_v, precision=HIGHEST).reshape(GROUP_TOK, KV_HEADS, HEAD)))
        attended = low(low_back(attend_group(queries, keys, values, rows, first_len)))
        branch = low_back(jnp.dot(attended, weight_o, precision=HIGHEST))
        middles.append(resid + branch)
    middle = jnp.concatenate(middles, axis=0)
    hidden_two = low(normalize(middle) * gain_two)
    logits = low_back(jnp.dot(hidden_two, weight_r, precision=HIGHEST))
    chosen = routes.reshape(-1, TOP)
    selected = jnp.take_along_axis(logits, chosen, axis=1)
    gates = low(jax.nn.softmax(selected, axis=-1)).reshape(-1)
    flat_routes = chosen.reshape(-1)
    most_rows = CAP * N_CTX * N_EXP

    def route_table(index):
        hit = flat_routes == index
        route_ids = jnp.nonzero(hit, size=most_rows, fill_value=0)[0].astype(jnp.int32)
        valid = jnp.arange(most_rows) < jnp.sum(hit.astype(jnp.int32))
        return (route_ids, valid)
    expert_ids = jnp.arange(EXPERTS, dtype=jnp.int32)
    all_routes, all_valid = lax.map(route_table, expert_ids)

    def one_expert(inputs):
        index, route_ids, valid = inputs
        token_ids = route_ids // TOP
        rows_in = low_back(hidden_two[token_ids])
        expert_up = lax.dynamic_index_in_dim(weight_in, index, 1, keepdims=False)
        expert_down = lax.dynamic_index_in_dim(weight_out, index, 1, keepdims=False)
        gate_up = low_back(jnp.dot(rows_in, expert_up, precision=HIGHEST))
        active = low(low_back(jax.nn.silu(gate_up[:, :HID]) * gate_up[:, HID:]))
        produced = low(low_back(jnp.dot(active, expert_down.T, precision=HIGHEST)))
        return jnp.where(valid, gates[route_ids], 0.0)[:, None] * produced
    contributions = lax.map(jax.checkpoint(one_expert), (expert_ids, all_routes, all_valid))
    token_all = (all_routes // TOP).reshape(-1)
    mixture = jnp.zeros((GROUPS * GROUP_TOK, D), jnp.float32).at[token_all].add(contributions.reshape(-1, D))
    mixture = low_back(mixture)
    return (middle + mixture).reshape(GROUPS, GROUP_TOK, D)

def reference(tokens, cotangent, lengths, span_perm, routes, norm_attn, attn_q, attn_k, attn_v, attn_o, router, norm_moe, expert_in, expert_out):
    seq_rows = jax.vmap(sequence_rows)(span_perm)
    first_lens = lengths[:, 0]

    def forward(tokens_f, gain_a, query_w, key_w, value_w, out_w, router_w, gain_m, up_w, down_w):
        return block_forward(tokens_f, gain_a, query_w, key_w, value_w, out_w, router_w, gain_m, up_w, down_w, seq_rows, first_lens, routes)
    result, pull = jax.vjp(forward, tokens.astype(jnp.float32), norm_attn, attn_q, attn_k, attn_v, attn_o, router, norm_moe, expert_in, expert_out)
    grads = pull(cotangent.astype(jnp.float32))
    return (result.astype(jnp.bfloat16), grads[0], grads[1], grads[2], grads[3], grads[4], grads[5], grads[6], grads[7], grads[8], grads[9])
```

```python
import math

import jax
import jax.numpy as jnp
from jax import lax
from jax.experimental import pallas as pl
from jax.experimental.pallas import tpu as pltpu
from jax.sharding import PartitionSpec as P

D = 1536
HEADS = 24
KV_HEADS = 8
HEAD = 64
HID = 512
TOP = 8
EXP_DEV = 10
SPAN = 64


EPSILON = 1e-06
NEGATIVE = -1e30


def global_rows(perm_row, rows):
    slots = rows // SPAN
    match = slots[:, None] == jnp.arange(perm_row.shape[0], dtype=jnp.int32)[None, :]
    spans = jnp.sum(jnp.where(match, perm_row[None, :], 0), axis=1)
    return spans * SPAN + rows % SPAN


def rotary(tensor, position, sign):
    half = HEAD // 2
    freqs = jnp.exp(jnp.arange(half, dtype=jnp.float32) * (-2.0 * math.log(10000.0) / HEAD))
    angle = position.astype(jnp.float32)[:, None] * freqs[None, :]
    cosine = jnp.cos(angle)[:, None, :]
    sine = sign * jnp.sin(angle)[:, None, :]
    first, second = (tensor[..., :half], tensor[..., half:])
    return jnp.concatenate(
        [first * cosine - second * sine, second * cosine + first * sine], axis=-1
    )


def allowed(query_rows, key_rows, first_len):
    later = key_rows[None, :] <= query_rows[:, None]
    same_seq = (key_rows[None, :] >= first_len) == (query_rows[:, None] >= first_len)
    return later & same_seq


def contract_rows(left, right):
    return lax.dot_general(
        left, right, (((0,), (0,)), ((), ())), preferred_element_type=jnp.float32
    )


def contract_cols(left, right):
    return lax.dot_general(
        left, right, (((1,), (1,)), ((), ())), preferred_element_type=jnp.float32
    )


def block_grads(
    query_block,
    grad_block,
    lse_block,
    drift_block,
    query_rows,
    key_block,
    value_block,
    key_rows,
    first_len,
):
    softmax_scale = HEAD ** (-0.5)
    scores = (
        jnp.einsum("qgrd,kgd->grqk", query_block, key_block, preferred_element_type=jnp.float32)
        * softmax_scale
    )
    mask = allowed(query_rows, key_rows, first_len)[None, None]
    weights = jnp.where(mask, jnp.exp(scores - lse_block.transpose(1, 2, 0)[..., None]), 0.0)
    prob_grad = jnp.einsum(
        "qgrd,kgd->grqk", grad_block, value_block, preferred_element_type=jnp.float32
    )
    score_grad = (weights * (prob_grad - drift_block.transpose(1, 2, 0)[..., None])).astype(
        jnp.bfloat16
    )
    query_grad = None
    key_grad = None
    value_grad = None
    query_grad = (
        jnp.einsum("grqk,kgd->qgrd", score_grad, key_block, preferred_element_type=jnp.float32)
        * softmax_scale
    )
    value_grad = jnp.einsum(
        "grqk,qgrd->kgd",
        weights.astype(jnp.bfloat16),
        grad_block,
        preferred_element_type=jnp.float32,
    )
    key_grad = (
        jnp.einsum("grqk,qgrd->kgd", score_grad, query_block, preferred_element_type=jnp.float32)
        * softmax_scale
    )
    return (query_grad, key_grad, value_grad)


def body_general(
    tokens,
    cotangent,
    lengths,
    span_perm,
    routes,
    norm_attn,
    attn_q,
    attn_k,
    attn_v,
    attn_o,
    router,
    norm_moe,
    expert_in,
    expert_out,
):
    count = tokens.shape[1]
    repeat = HEADS // KV_HEADS
    experts = EXP_DEV * lax.axis_size("exp")
    capacity = count * TOP * 3 // (2 * experts)
    softmax_scale = HEAD ** (-0.5)
    perm_row = span_perm[0]
    first_len = lengths[0, 0]
    query_rows = global_rows(
        perm_row, lax.axis_index("ctx") * count + jnp.arange(count, dtype=jnp.int32)
    )
    position = query_rows - jnp.where(query_rows >= first_len, first_len, 0)
    gathered = (
        lax.all_gather(norm_attn.astype(jnp.bfloat16), ("ctx", "exp"), axis=0, tiled=True),
        lax.all_gather(attn_q.astype(jnp.bfloat16), ("ctx", "exp"), axis=0, tiled=True),
        lax.all_gather(attn_k.astype(jnp.bfloat16), ("ctx", "exp"), axis=0, tiled=True),
        lax.all_gather(attn_v.astype(jnp.bfloat16), ("ctx", "exp"), axis=0, tiled=True),
        lax.all_gather(attn_o.astype(jnp.bfloat16), ("ctx", "exp"), axis=0, tiled=True),
        lax.all_gather(router.astype(jnp.bfloat16), ("ctx", "exp"), axis=0, tiled=True),
        lax.all_gather(norm_moe.astype(jnp.bfloat16), ("ctx", "exp"), axis=0, tiled=True),
    )
    gain_one, weight_q, weight_k, weight_v, weight_o, weight_r, gain_two = gathered
    weight_in, weight_out = (
        lax.all_gather(expert_in.astype(jnp.bfloat16), "ctx", axis=0, tiled=True),
        lax.all_gather(expert_out.astype(jnp.bfloat16), "ctx", axis=0, tiled=True),
    )
    gain_one_f = gain_one.astype(jnp.float32)
    gain_two_f = gain_two.astype(jnp.float32)
    resid = tokens[0].astype(jnp.float32)
    scale_one = lax.rsqrt(jnp.mean(resid * resid, axis=-1, keepdims=True) + EPSILON)
    normed_one = resid * scale_one
    hidden_one = (normed_one * gain_one_f).astype(jnp.bfloat16)
    query_pre = jnp.dot(hidden_one, weight_q, preferred_element_type=jnp.float32).reshape(
        count, HEADS, HEAD
    )
    queries = (
        rotary(query_pre, position, 1.0).astype(jnp.bfloat16).reshape(count, KV_HEADS, repeat, HEAD)
    )
    key_pre = jnp.dot(hidden_one, weight_k, preferred_element_type=jnp.float32).reshape(
        count, KV_HEADS, HEAD
    )
    keys = rotary(key_pre, position, 1.0).astype(jnp.bfloat16)
    values = (
        jnp.dot(hidden_one, weight_v, preferred_element_type=jnp.float32)
        .astype(jnp.bfloat16)
        .reshape(count, KV_HEADS, HEAD)
    )
    start_state = (
        jnp.full((KV_HEADS, repeat, count), NEGATIVE, jnp.float32),
        jnp.zeros((KV_HEADS, repeat, count), jnp.float32),
        jnp.zeros((KV_HEADS, repeat, count, HEAD), jnp.float32),
    )
    carry = start_state
    key_piece = lax.all_gather(keys, "ctx", axis=0, tiled=True)
    value_piece = lax.all_gather(values, "ctx", axis=0, tiled=True)
    size = key_piece.shape[0]
    block = math.gcd(size, 512)
    number = size // block
    key_blocks = key_piece.reshape(number, block, KV_HEADS, HEAD)
    value_blocks = value_piece.reshape(number, block, KV_HEADS, HEAD)
    offsets = jnp.arange(size, dtype=jnp.int32).reshape(number, block)

    def forward_step(state, inputs):
        highest, total, accum = state
        key_block, value_block, offset = inputs
        key_rows = global_rows(perm_row, offset)
        scores = (
            jnp.einsum("qgrd,kgd->grqk", queries, key_block, preferred_element_type=jnp.float32)
            * softmax_scale
        )
        mask = allowed(query_rows, key_rows, first_len)[None, None]
        scores = jnp.where(mask, scores, NEGATIVE)
        newmax = jnp.maximum(highest, jnp.max(scores, axis=-1))
        weights = jnp.where(mask, jnp.exp(scores - newmax[..., None]), 0.0)
        factor = jnp.exp(highest - newmax)
        total = total * factor + jnp.sum(weights, axis=-1)
        accum = accum * factor[..., None] + jnp.einsum(
            "grqk,kgd->grqd",
            weights.astype(jnp.bfloat16),
            value_block,
            preferred_element_type=jnp.float32,
        )
        return ((newmax, total, accum), None)

    carry, _ = lax.scan(forward_step, carry, (key_blocks, value_blocks, offsets))
    highest, total, accum = carry
    log_total = (highest + jnp.log(total)).transpose(2, 0, 1)
    attended = (accum / total[..., None]).transpose(2, 0, 1, 3)
    attended_b = attended.reshape(count, HEADS * HEAD).astype(jnp.bfloat16)
    middle = resid + jnp.dot(attended_b, weight_o, preferred_element_type=jnp.float32)
    scale_two = lax.rsqrt(jnp.mean(middle * middle, axis=-1, keepdims=True) + EPSILON)
    normed_two = middle * scale_two
    hidden_two = (normed_two * gain_two_f).astype(jnp.bfloat16)
    logits = jnp.dot(hidden_two, weight_r, preferred_element_type=jnp.float32)
    chosen = routes[0]
    picks = chosen[:, :, None] == jnp.arange(experts, dtype=jnp.int32)[None, None, :]
    selected = jnp.sum(jnp.where(picks, logits[:, None, :], 0.0), axis=-1)
    gates = jax.nn.softmax(selected, axis=-1)
    gates_b = gates.astype(jnp.bfloat16)
    flat_picks = picks.reshape(count * TOP, experts).astype(jnp.int32)
    placed = jnp.sum((jnp.cumsum(flat_picks, axis=0) - 1) * flat_picks, axis=-1)
    column = chosen.reshape(-1) * capacity + placed
    hits = (
        column.reshape(count, TOP)[:, :, None]
        == jnp.arange(experts * capacity, dtype=jnp.int32)[None, None, :]
    )
    spread = jnp.any(hits, axis=1).astype(jnp.bfloat16)
    weighted = jnp.sum(
        jnp.where(hits, gates_b.astype(jnp.float32)[:, :, None], 0.0), axis=1
    ).astype(jnp.bfloat16)
    outgoing = contract_rows(spread, hidden_two).astype(jnp.bfloat16).reshape(experts, capacity, D)
    incoming = lax.all_to_all(outgoing, "exp", split_axis=0, concat_axis=1, tiled=True)
    gate_up = jnp.einsum("erd,dec->erc", incoming, weight_in, preferred_element_type=jnp.float32)
    gate_part = gate_up[..., :HID]
    up_part = gate_up[..., HID:]
    sigmoid_gate = jax.nn.sigmoid(gate_part)
    silu_gate = gate_part * sigmoid_gate
    activated = (silu_gate * up_part).astype(jnp.bfloat16)
    produced = jnp.einsum(
        "erh,deh->erd", activated, weight_out, preferred_element_type=jnp.float32
    ).astype(jnp.bfloat16)
    returned = lax.all_to_all(produced, "exp", split_axis=1, concat_axis=0, tiled=True).reshape(
        experts * capacity, D
    )
    mixture = jnp.dot(weighted, returned, preferred_element_type=jnp.float32)
    output = (middle + mixture).astype(jnp.bfloat16)
    upstream = cotangent[0].astype(jnp.float32)
    upstream_b = upstream.astype(jnp.bfloat16)
    sent_grad = (
        contract_rows(weighted, upstream_b).astype(jnp.bfloat16).reshape(experts, capacity, D)
    )
    grad_in = lax.all_to_all(sent_grad, "exp", split_axis=0, concat_axis=1, tiled=True)
    picked = jnp.take(returned, column, axis=0).reshape(count, TOP, D)
    gate_grad = jnp.einsum("tkd,td->tk", picked, upstream_b, preferred_element_type=jnp.float32)
    grad_act = (
        jnp.einsum("erd,deh->erh", grad_in, weight_out, preferred_element_type=jnp.float32)
        .astype(jnp.bfloat16)
        .astype(jnp.float32)
    )
    grad_gate = grad_act * up_part * (sigmoid_gate * (1.0 + gate_part * (1.0 - sigmoid_gate)))
    grad_up = grad_act * silu_gate
    grad_gu = jnp.concatenate([grad_gate, grad_up], axis=-1).astype(jnp.bfloat16)
    grad_weight_out = jnp.einsum(
        "erd,erh->deh", grad_in, activated, preferred_element_type=jnp.float32
    )
    grad_weight_in = jnp.einsum(
        "erd,erc->dec", incoming, grad_gu, preferred_element_type=jnp.float32
    )
    grad_rows = jnp.einsum(
        "erc,dec->erd", grad_gu, weight_in, preferred_element_type=jnp.float32
    ).astype(jnp.bfloat16)
    back_rows = lax.all_to_all(grad_rows, "exp", split_axis=1, concat_axis=0, tiled=True).reshape(
        experts * capacity, D
    )
    expert_sums = (
        lax.psum_scatter(
            grad_weight_in.astype(jnp.bfloat16), "ctx", scatter_dimension=0, tiled=True
        ).astype(jnp.float32),
        lax.psum_scatter(
            grad_weight_out.astype(jnp.bfloat16), "ctx", scatter_dimension=0, tiled=True
        ).astype(jnp.float32),
    )
    centered = gate_grad - jnp.sum(gates * gate_grad, axis=-1, keepdims=True)
    select_grad = gates * centered
    logit_grad = jnp.sum(jnp.where(picks, select_grad[:, :, None], 0.0), axis=1).astype(
        jnp.bfloat16
    )
    grad_router = contract_rows(hidden_two, logit_grad)
    grad_norm_two = jnp.dot(spread, back_rows, preferred_element_type=jnp.float32) + contract_cols(
        logit_grad, weight_r
    )
    grad_gain_two = jnp.sum(grad_norm_two * normed_two, axis=0)
    scaled_two = grad_norm_two * gain_two_f
    grad_middle = upstream + scale_two * (
        scaled_two - normed_two * jnp.mean(scaled_two * normed_two, axis=-1, keepdims=True)
    )
    branch_grad = grad_middle.astype(jnp.bfloat16)
    grad_weight_o = contract_rows(attended_b, branch_grad)
    grad_heads = (
        contract_cols(branch_grad, weight_o)
        .astype(jnp.bfloat16)
        .reshape(count, KV_HEADS, repeat, HEAD)
    )
    drift = jnp.sum(grad_heads.astype(jnp.float32) * attended, axis=-1)
    query_acc = jnp.zeros((count, KV_HEADS, repeat, HEAD), jnp.float32)
    key_piece = lax.all_gather(keys, "ctx", axis=0, tiled=True)
    value_piece = lax.all_gather(values, "ctx", axis=0, tiled=True)
    size = key_piece.shape[0]
    block = math.gcd(size, 512)
    number = size // block
    key_blocks = key_piece.reshape(number, block, KV_HEADS, HEAD)
    value_blocks = value_piece.reshape(number, block, KV_HEADS, HEAD)
    offsets = jnp.arange(size, dtype=jnp.int32).reshape(number, block)

    def backward_step(acc, inputs):
        key_block, value_block, offset = inputs
        part_q, part_k, part_v = block_grads(
            queries,
            grad_heads,
            log_total,
            drift,
            query_rows,
            key_block,
            value_block,
            global_rows(perm_row, offset),
            first_len,
        )
        joined = jnp.concatenate(
            [part_k.reshape(block, KV_HEADS * HEAD), part_v.reshape(block, KV_HEADS * HEAD)],
            axis=-1,
        )
        return (acc + part_q, joined)

    query_acc, joined_parts = lax.scan(
        backward_step, query_acc, (key_blocks, value_blocks, offsets)
    )
    pair_acc = joined_parts.reshape(size, 2 * KV_HEADS * HEAD)
    query_grad, pair_acc = (query_acc, pair_acc)
    pair_own = lax.psum_scatter(
        pair_acc.astype(jnp.bfloat16), "ctx", scatter_dimension=0, tiled=True
    ).astype(jnp.float32)
    key_grad = pair_own[:, : KV_HEADS * HEAD].reshape(count, KV_HEADS, HEAD)
    value_grad = pair_own[:, KV_HEADS * HEAD :].reshape(count, KV_HEADS, HEAD)
    query_grad_b = (
        rotary(query_grad.reshape(count, HEADS, HEAD), position, -1.0)
        .astype(jnp.bfloat16)
        .reshape(count, HEADS * HEAD)
    )
    key_grad_b = (
        rotary(key_grad, position, -1.0).astype(jnp.bfloat16).reshape(count, KV_HEADS * HEAD)
    )
    value_grad_b = value_grad.astype(jnp.bfloat16).reshape(count, KV_HEADS * HEAD)
    grad_weight_q = contract_rows(hidden_one, query_grad_b)
    grad_weight_k = contract_rows(hidden_one, key_grad_b)
    grad_weight_v = contract_rows(hidden_one, value_grad_b)
    grad_hidden_one = (
        contract_cols(query_grad_b, weight_q)
        + contract_cols(key_grad_b, weight_k)
        + contract_cols(value_grad_b, weight_v)
    )
    grad_gain_one = jnp.sum(grad_hidden_one * normed_one, axis=0)
    scaled_one = grad_hidden_one * gain_one_f
    grad_tokens = grad_middle + scale_one * (
        scaled_one - normed_one * jnp.mean(scaled_one * normed_one, axis=-1, keepdims=True)
    )
    attn_sums = (
        lax.psum_scatter(grad_gain_one, ("ctx", "exp"), scatter_dimension=0, tiled=True),
        lax.psum_scatter(grad_weight_q, ("ctx", "exp"), scatter_dimension=0, tiled=True),
        lax.psum_scatter(grad_weight_k, ("ctx", "exp"), scatter_dimension=0, tiled=True),
        lax.psum_scatter(grad_weight_v, ("ctx", "exp"), scatter_dimension=0, tiled=True),
        lax.psum_scatter(grad_weight_o, ("ctx", "exp"), scatter_dimension=0, tiled=True),
        lax.psum_scatter(grad_router, ("ctx", "exp"), scatter_dimension=0, tiled=True),
        lax.psum_scatter(grad_gain_two, ("ctx", "exp"), scatter_dimension=0, tiled=True),
    )
    return (
        output[None],
        grad_tokens[None],
        attn_sums[0],
        attn_sums[1],
        attn_sums[2],
        attn_sums[3],
        attn_sums[4],
        attn_sums[5],
        attn_sums[6],
        expert_sums[0],
        expert_sums[1],
    )


def rotate(tensor, cosine, sine):
    half = HEAD // 2
    first, second = (tensor[..., :half], tensor[..., half:])
    return jnp.concatenate(
        [first * cosine - second * sine, second * cosine + first * sine], axis=-1
    )


def unit_kernel(first_ref, gate_ref, up_ref, down_ref, unit_ref):
    half = gate_ref.shape[-1]
    unit_ref[0, :, :half] = gate_ref[0].astype(unit_ref.dtype)
    unit_ref[0, :, half : 2 * half] = up_ref[0].astype(unit_ref.dtype)
    unit_ref[0, :, 2 * half :] = down_ref[0].astype(unit_ref.dtype)


def take_units(first, number, win, wout):
    depth, half = win.shape[1], HID // 2
    return pl.pallas_call(
        unit_kernel,
        grid_spec=pltpu.PrefetchScalarGridSpec(
            num_scalar_prefetch=1,
            grid=(number,),
            in_specs=[
                pl.BlockSpec(
                    (1, depth, half), lambda j, f: ((f[0] + j) // 2, 0, lax.rem(f[0] + j, 2))
                ),
                pl.BlockSpec(
                    (1, depth, half), lambda j, f: ((f[0] + j) // 2, 0, 2 + lax.rem(f[0] + j, 2))
                ),
                pl.BlockSpec(
                    (1, depth, half), lambda j, f: ((f[0] + j) // 2, 0, lax.rem(f[0] + j, 2))
                ),
            ],
            out_specs=pl.BlockSpec((1, depth, 3 * half), lambda j, f: (j, 0, 0)),
        ),
        out_shape=jax.ShapeDtypeStruct((number, depth, 3 * half), jnp.bfloat16),
        name="take_units",
    )(first.reshape(1), win, win, wout)


def expert_kernel(depth, meta, x_ref, g_ref, gate_ref, *refs):
    parts, (y_ref, d_ref), outs = refs[:8], refs[8:10], refs[10:18]
    weight, du_ref, act_ref = refs[18:]
    bf16, f32 = jnp.bfloat16, jnp.float32
    j = pl.program_id(0)
    shift, z, y, base = meta[0], meta[1], meta[2], meta[3]
    half = HID // 2
    offsets = [
        pl.multiple_of(((z ^ (i % 4)) * 2 + (y ^ (i // 4))) * depth, 64) for i in range(8)
    ]
    for part, offset in zip(parts, offsets):
        weight[pl.ds(offset, depth), :] = part[0]
    expert = base + (j + shift) // 2
    first = jnp.logical_or(j == 0, lax.rem(j + shift, 2) == 0)
    keep = jnp.where(first, 0.0, 1.0)
    pairs, _, rows, _ = x_ref.shape
    step = 2

    def forward(i, carry):
        at = pl.ds(i * step, step)
        flat = pl.ds(pl.multiple_of(i * step * rows, 32), step * rows)
        x = x_ref[at, 0].reshape(step * rows, D)
        g = g_ref[at, 0].reshape(step * rows, D)
        gate = gate_ref[0, flat, :]
        u = jnp.dot(x, weight[:, : 2 * half], preferred_element_type=f32)
        raw = jnp.dot(g, weight[:, 2 * half :], preferred_element_type=f32)
        u1, u2 = u[:, :half], u[:, half:]
        sig = jax.nn.sigmoid(u1)
        silu = u1 * sig
        act = (silu * u2).astype(bf16).astype(f32)
        dgate = jnp.sum(raw * act, axis=-1, keepdims=True)
        dact = raw * gate
        du1 = dact * u2 * (sig * (1.0 + u1 * (1.0 - sig)))
        du = jnp.concatenate([du1, dact * silu], axis=-1).astype(bf16)
        act_gated = (act * gate).astype(bf16)
        du_ref[flat, :] = du
        act_ref[flat, :] = act_gated
        made = contract_cols(act_gated, weight[:, 2 * half :])
        back = contract_cols(du, weight[:, : 2 * half])
        lane = lax.broadcasted_iota(jnp.int32, (step * rows, 128), 1)
        tail = jnp.where(lane == expert, dgate, 0.0)

        @pl.when(first)
        def _():
            y_ref[at, 0] = made.astype(bf16).reshape(step, rows, D)
            d_ref[at, 0, :, :D] = back.astype(bf16).reshape(step, rows, D)
            d_ref[at, 0, :, D:] = tail.astype(bf16).reshape(step, rows, 128)

        @pl.when(jnp.logical_not(first))
        def _():
            old_y = y_ref[at, 0].reshape(step * rows, D).astype(f32)
            y_ref[at, 0] = (made + old_y).astype(bf16).reshape(step, rows, D)
            old_d = d_ref[at, 0].reshape(step * rows, D + 128).astype(f32)
            d_ref[at, 0, :, :D] = (back + old_d[:, :D]).astype(bf16).reshape(step, rows, D)
            d_ref[at, 0, :, D:] = (tail + old_d[:, D:]).astype(bf16).reshape(step, rows, 128)

        return carry

    lax.fori_loop(0, pairs // step, forward, 0)

    def gradient(i, carry):
        at = pl.ds(pl.multiple_of(i * 256, 256), 256)
        x = x_ref[:, 0, :, at].reshape(pairs * rows, 256)
        g = g_ref[:, 0, :, at].reshape(pairs * rows, 256)
        weight[at, : 2 * half] = contract_rows(x, du_ref[...]).astype(bf16)
        weight[at, 2 * half :] = contract_rows(g, act_ref[...]).astype(bf16)
        return carry

    lax.fori_loop(0, D // 256, gradient, 0)
    for out, offset in zip(outs, offsets):
        out[0] = weight[pl.ds(offset, depth), :]


def run_experts(meta, row_in, row_up, slot_gate, parts):
    pairs, held, rows, _ = row_in.shape
    units, depth, columns = parts[0].shape
    held_block = lambda width: pl.BlockSpec(
        (pairs, 1, rows, width), lambda j, m: (0, (j + m[0]) // 2, 0, 0)
    )
    unit_block = pl.BlockSpec((1, depth, columns), lambda j, m: (j, 0, 0))
    bf16 = jnp.bfloat16
    total = units * pairs * rows * D * columns * 6
    return pl.pallas_call(
        lambda *refs: expert_kernel(depth, *refs),
        grid_spec=pltpu.PrefetchScalarGridSpec(
            num_scalar_prefetch=1,
            grid=(units,),
            in_specs=[
                held_block(D),
                held_block(D),
                pl.BlockSpec((1, pairs * rows, 1), lambda j, m: ((j + m[0]) // 2, 0, 0)),
            ]
            + [unit_block] * 8,
            out_specs=[held_block(D), held_block(D + 128)] + [unit_block] * 8,
            scratch_shapes=[
                pltpu.VMEM((D, columns), bf16),
                pltpu.VMEM((pairs * rows, HID), bf16),
                pltpu.VMEM((pairs * rows, HID // 2), bf16),
            ],
        ),
        out_shape=[
            jax.ShapeDtypeStruct((pairs, held, rows, D), bf16),
            jax.ShapeDtypeStruct((pairs, held, rows, D + 128), bf16),
        ]
        + [jax.ShapeDtypeStruct((units, depth, columns), bf16)] * 8,
        compiler_params=pltpu.CompilerParams(vmem_limit_bytes=56 * 2**20),
        cost_estimate=pl.CostEstimate(
            flops=total, bytes_accessed=60 * 2**20, transcendentals=units * pairs * rows * HID
        ),
        name="experts",
    )(meta, row_in, row_up, slot_gate, *parts)


def spread_kernel(z_ref, low_ref, high_ref, in_ref, out_ref):
    half = low_ref.shape[-1] // 3
    for h, ref in enumerate((low_ref, high_ref)):
        for p in range(2):
            at = p * 2 * half + h * half
            in_ref[0, :, at : at + half] = ref[0, :, p * half : (p + 1) * half].astype(in_ref.dtype)
        out_ref[0, :, h * half : (h + 1) * half] = ref[0, :, 2 * half :].astype(out_ref.dtype)


def place_units(z_index, units, number):
    depth, columns = units.shape[1:]

    def pick(h):
        def index(i, z):
            unit = 2 * i + h
            return ((unit // number) ^ z[0]) * number + lax.rem(unit, number), 0, 0

        return pl.BlockSpec((1, depth, columns), index)

    return pl.pallas_call(
        spread_kernel,
        grid_spec=pltpu.PrefetchScalarGridSpec(
            num_scalar_prefetch=1,
            grid=(EXP_DEV,),
            in_specs=[pick(0), pick(1)],
            out_specs=[
                pl.BlockSpec((1, depth, 2 * HID), lambda i, z: (i, 0, 0)),
                pl.BlockSpec((1, depth, HID), lambda i, z: (i, 0, 0)),
            ],
        ),
        out_shape=[
            jax.ShapeDtypeStruct((EXP_DEV, depth, 2 * HID), jnp.float32),
            jax.ShapeDtypeStruct((EXP_DEV, depth, HID), jnp.float32),
        ],
        name="place_units",
    )(z_index.reshape(1), units, units)


def body_heads(
    tokens,
    cotangent,
    lengths,
    span_perm,
    routes,
    norm_attn,
    attn_q,
    attn_k,
    attn_v,
    attn_o,
    router,
    norm_moe,
    expert_in,
    expert_out,
):
    bf16, f32 = jnp.bfloat16, jnp.float32
    ctx_axes, tok_axes, all_axes = ("z", "y"), ("z", "exp"), ("z", "y", "exp")
    n_z, n_y, n_exp = (lax.axis_size(a) for a in all_axes)
    n_ctx = n_z * n_y
    count = tokens.shape[1]
    group = count * n_ctx
    repeat = HEADS // KV_HEADS
    width = repeat * HEAD
    experts = EXP_DEV * n_exp
    capacity = count * TOP * 3 // (2 * experts)
    slots = -(-capacity // 8) * 8
    own = attn_q.shape[0]
    softmax_scale = HEAD ** (-0.5)
    z_index = lax.axis_index("z")

    units = 2 * EXP_DEV // n_z
    y_index = lax.axis_index("y")
    win = expert_in.transpose(1, 0, 2)
    wout = expert_out.transpose(1, 0, 2)
    swap_z = [[(i, i ^ s) for i in range(n_z)] for s in range(n_z)]
    swap_y = [(i, i ^ 1) for i in range(n_y)]
    near = [None] * 4
    for s in (3, 2, 1, 0):
        near[s] = take_units(units * (z_index ^ s), units, win, wout)
        if s:
            near[s] = lax.ppermute(near[s], "z", swap_z[s])
    parts = near + [lax.ppermute(a, "y", swap_y) for a in near]

    wq, wk, wv = (a.astype(bf16) for a in (attn_q, attn_k, attn_v))
    wqkv = jnp.concatenate(
        [
            wq.reshape(own, n_ctx, width),
            wk.reshape(own, n_ctx, HEAD),
            wv.reshape(own, n_ctx, HEAD),
        ],
        axis=-1,
    )
    own_qkv = wqkv
    wqkv = lax.all_to_all(
        wqkv.transpose(1, 0, 2), ctx_axes, split_axis=0, concat_axis=0, tiled=True
    )
    wqkv = lax.all_gather(wqkv, "exp", axis=1).reshape(D, width + 2 * HEAD)
    wo = lax.all_gather(attn_o.astype(bf16), "exp", axis=0, tiled=True)
    small = jnp.concatenate(
        [
            router.astype(bf16),
            norm_attn.astype(bf16)[:, None],
            norm_moe.astype(bf16)[:, None],
            jnp.zeros((own, 128 - experts - 2), bf16),
        ],
        axis=1,
    )
    small = lax.all_gather(small, all_axes, axis=0, tiled=True)
    weight_r = small[:, :experts]
    gain_one_f = small[:, experts].astype(f32)
    gain_two_f = small[:, experts + 1].astype(f32)

    token_all = lax.all_gather(tokens[0], ctx_axes, axis=0, tiled=True)
    upstream_blocks = lax.all_gather(cotangent[0], tok_axes, axis=0)
    route_blocks = lax.all_gather(routes[0], tok_axes, axis=0)
    perm_row = span_perm[0]
    first_len = lengths[0, 0]
    rows = global_rows(perm_row, jnp.arange(group, dtype=jnp.int32))
    position = rows - jnp.where(rows >= first_len, first_len, 0)
    freqs = jnp.exp(jnp.arange(HEAD // 2, dtype=f32) * (-2.0 * math.log(10000.0) / HEAD))
    angle = position.astype(f32)[:, None] * freqs[None, :]
    cosine, sine = (jnp.cos(angle), jnp.sin(angle))
    resid_all = token_all.astype(f32)
    normed_all = resid_all * lax.rsqrt(
        jnp.mean(resid_all * resid_all, axis=-1, keepdims=True) + EPSILON
    )
    hidden_all = (normed_all * gain_one_f).astype(bf16)
    qkv = jnp.dot(hidden_all, wqkv, preferred_element_type=f32)
    queries = rotate(
        qkv[:, :width].reshape(group, repeat, HEAD), cosine[:, None], sine[:, None]
    ).astype(bf16)
    keys = rotate(qkv[:, width : width + HEAD], cosine, sine).astype(bf16)
    values = qkv[:, width + HEAD :].astype(bf16)
    mask = allowed(rows, rows, first_len)[None]
    scores = (
        jnp.einsum("qrd,kd->rqk", queries, keys, preferred_element_type=f32) * softmax_scale
    )
    scores = jnp.where(mask, scores, NEGATIVE)
    highest = jnp.max(scores, axis=-1)
    weights = jnp.exp(scores - highest[..., None])
    total = jnp.sum(weights, axis=-1)
    attended = (
        jnp.einsum("rqk,kd->rqd", weights.astype(bf16), values, preferred_element_type=f32)
        / total[..., None]
    )
    log_total = highest + jnp.log(total)
    attended_b = attended.transpose(1, 0, 2).reshape(group, width).astype(bf16)
    branch = lax.psum_scatter(
        jnp.dot(attended_b, wo, preferred_element_type=f32).astype(bf16),
        ctx_axes,
        scatter_dimension=0,
        tiled=True,
    )
    resid = tokens[0].astype(f32)
    middle = resid + branch.astype(f32)
    scale_two = lax.rsqrt(jnp.mean(middle * middle, axis=-1, keepdims=True) + EPSILON)
    normed_two = middle * scale_two
    hidden_two = (normed_two * gain_two_f).astype(bf16)

    hidden_blocks = lax.all_gather(hidden_two, tok_axes, axis=0)
    blocks = hidden_blocks.shape[0]
    held = 3
    base = lax.axis_index("exp") * EXP_DEV + (units * z_index) // 2
    shift = (units * z_index) % 2
    logits = jnp.einsum("btd,de->bte", hidden_blocks, weight_r, preferred_element_type=f32)
    picks = route_blocks[..., None] == jnp.arange(experts, dtype=jnp.int32)
    selected = jnp.sum(jnp.where(picks, logits[:, :, None, :], 0.0), axis=-1)
    gates_blocks = jax.nn.softmax(selected, axis=-1).astype(bf16).astype(f32)
    held_ids = base + jnp.arange(held, dtype=jnp.int32)
    held_picks = route_blocks[..., None] == held_ids
    gate_held = jnp.sum(jnp.where(held_picks, gates_blocks[..., None], 0.0), axis=2)
    hit = jnp.any(held_picks, axis=2)
    lower = jnp.tril(jnp.ones((count, count), bf16))
    rank = jnp.einsum("ts,bse->bte", lower, hit.astype(bf16), preferred_element_type=f32)
    pairs = blocks // 2
    side = jnp.arange(2, dtype=jnp.int32)
    held_first = lambda a: a.reshape(pairs, 2, count, held).transpose(0, 3, 1, 2)
    here = (
        held_first(hit)[:, :, None, None]
        & (
            held_first(rank)[:, :, None, None]
            == (jnp.arange(slots, dtype=f32) + 1.0)[None, None, None, :, None, None]
        )
        & (side[:, None] == side[None, :])[None, None, :, None, :, None]
    )
    spread = here.astype(bf16).reshape(pairs, held * 2 * slots, 2 * count)
    slot_gate = jnp.sum(
        jnp.where(here, held_first(gate_held)[:, :, None, None], 0.0), axis=(-2, -1)
    )
    slot_gate = slot_gate.transpose(1, 0, 2, 3).reshape(held, blocks * slots, 1)

    def to_rows(a):
        rows = jnp.einsum(
            "prt,ptd->prd", spread, a.reshape(pairs, 2 * count, D), preferred_element_type=f32
        )
        return rows.astype(bf16).reshape(pairs, held, 2 * slots, D)

    def to_tokens(rows):
        a = jnp.einsum(
            "prt,prd->ptd",
            spread,
            rows.reshape(pairs, held * 2 * slots, -1),
            preferred_element_type=f32,
        )
        return a.astype(bf16).reshape(blocks, count, -1)

    meta = jnp.stack([shift, z_index, y_index, base]).astype(jnp.int32)
    made, back, *grads = run_experts(
        meta, to_rows(hidden_blocks), to_rows(upstream_blocks), slot_gate, parts
    )
    back = lax.psum_scatter(to_tokens(back), tok_axes, scatter_dimension=0, tiled=False)
    back = back.astype(f32)
    mixture = lax.psum_scatter(to_tokens(made), tok_axes, scatter_dimension=0, tiled=False)
    output = (middle + mixture.astype(f32)).astype(bf16)
    back_rows, dgate_own = back[:, :D], back[:, D : D + experts]

    sums = [None] * 4
    for s in (3, 2, 1, 0):
        other = lax.ppermute(grads[4 + s], "y", swap_y)
        sums[s] = (grads[s].astype(f32) + other.astype(f32)).astype(bf16)
        if s:
            sums[s] = lax.ppermute(sums[s], "z", swap_z[s])
    grad_expert_in, grad_expert_out = place_units(z_index, jnp.concatenate(sums), units)
    grad_expert_in = grad_expert_in.transpose(1, 0, 2)
    grad_expert_out = grad_expert_out.transpose(1, 0, 2)

    chosen = routes[0]
    own_picks = chosen[:, :, None] == jnp.arange(experts, dtype=jnp.int32)[None, None, :]
    own_logits = jnp.dot(hidden_two, weight_r, preferred_element_type=f32)
    own_selected = jnp.sum(jnp.where(own_picks, own_logits[:, None, :], 0.0), axis=-1)
    gates = jax.nn.softmax(own_selected, axis=-1)
    gate_grad = jnp.sum(jnp.where(own_picks, dgate_own[:, None, :], 0.0), axis=-1)
    select_grad = gates * (gate_grad - jnp.sum(gates * gate_grad, axis=-1, keepdims=True))
    logit_grad = jnp.sum(jnp.where(own_picks, select_grad[:, :, None], 0.0), axis=1).astype(bf16)
    grad_router = contract_rows(hidden_two, logit_grad)
    grad_norm_two = back_rows + contract_cols(logit_grad, weight_r)
    grad_gain_two = jnp.sum(grad_norm_two * normed_two, axis=0)
    small_grads = jnp.concatenate(
        [grad_router, grad_gain_two[:, None], jnp.zeros((D, 128 - experts - 1), f32)], axis=1
    )
    small_grads = lax.psum_scatter(small_grads, all_axes, scatter_dimension=0, tiled=True)
    upstream = cotangent[0].astype(f32)
    scaled_two = grad_norm_two * gain_two_f
    grad_middle = upstream + scale_two * (
        scaled_two - normed_two * jnp.mean(scaled_two * normed_two, axis=-1, keepdims=True)
    )

    branch_all = lax.all_gather(grad_middle.astype(bf16), ctx_axes, axis=0, tiled=True)
    grad_wo = contract_rows(attended_b, branch_all).astype(bf16)
    grad_wo = lax.psum_scatter(grad_wo, "exp", scatter_dimension=0, tiled=True).astype(f32)
    grad_heads = contract_cols(branch_all, wo).astype(bf16).reshape(group, repeat, HEAD)
    grad_heads = grad_heads.transpose(1, 0, 2)
    drift = jnp.sum(grad_heads.astype(f32) * attended, axis=-1)
    scores = (
        jnp.einsum("qrd,kd->rqk", queries, keys, preferred_element_type=f32) * softmax_scale
    )
    weights = jnp.where(mask, jnp.exp(scores - log_total[..., None]), 0.0)
    prob_grad = jnp.einsum("rqd,kd->rqk", grad_heads, values, preferred_element_type=f32)
    score_grad = (weights * (prob_grad - drift[..., None])).astype(bf16)
    query_grad = (
        jnp.einsum("rqk,kd->qrd", score_grad, keys, preferred_element_type=f32) * softmax_scale
    )
    value_grad = jnp.einsum(
        "rqk,rqd->kd", weights.astype(bf16), grad_heads, preferred_element_type=f32
    )
    key_grad = (
        jnp.einsum("rqk,qrd->kd", score_grad, queries, preferred_element_type=f32) * softmax_scale
    )
    grad_qkv = jnp.concatenate(
        [
            rotate(query_grad, cosine[:, None], -sine[:, None]).reshape(group, width),
            rotate(key_grad, cosine, -sine),
            value_grad,
        ],
        axis=-1,
    ).astype(bf16)
    grad_hidden = lax.psum_scatter(
        contract_cols(grad_qkv, wqkv).astype(bf16), ctx_axes, scatter_dimension=0, tiled=True
    ).astype(f32)
    grad_wqkv = contract_rows(hidden_all, grad_qkv).astype(bf16)
    grad_wqkv = grad_wqkv.reshape(n_ctx, n_exp, own, width + 2 * HEAD).transpose(1, 0, 2, 3)
    grad_wqkv = lax.psum_scatter(grad_wqkv, "exp", scatter_dimension=0, tiled=False)
    grad_wqkv = lax.all_to_all(grad_wqkv, ctx_axes, split_axis=0, concat_axis=0, tiled=True)
    grad_wqkv = grad_wqkv.astype(f32)
    grad_q = grad_wqkv[:, :, :width].transpose(1, 0, 2).reshape(own, HEADS * HEAD)
    grad_k = grad_wqkv[:, :, width : width + HEAD].transpose(1, 0, 2).reshape(own, KV_HEADS * HEAD)
    grad_v = grad_wqkv[:, :, width + HEAD :].transpose(1, 0, 2).reshape(own, KV_HEADS * HEAD)
    grad_gain_one = jnp.sum(
        grad_wqkv.transpose(1, 0, 2) * own_qkv.astype(f32), axis=(1, 2)
    ) / norm_attn.astype(bf16).astype(f32)
    scale_one = lax.rsqrt(jnp.mean(resid * resid, axis=-1, keepdims=True) + EPSILON)
    normed_one = resid * scale_one
    scaled_one = grad_hidden * gain_one_f
    grad_tokens = grad_middle + scale_one * (
        scaled_one - normed_one * jnp.mean(scaled_one * normed_one, axis=-1, keepdims=True)
    )
    return (
        output[None],
        grad_tokens[None],
        grad_gain_one,
        grad_q,
        grad_k,
        grad_v,
        grad_wo,
        small_grads[:, :experts],
        small_grads[:, experts],
        grad_expert_in,
        grad_expert_out,
    )


def solution(mesh):
    ctx, exp = mesh.shape["ctx"], mesh.shape["exp"]
    if ctx == KV_HEADS and exp * EXP_DEV == 40:
        inner = jax.sharding.Mesh(mesh.devices.reshape(ctx // 2, 2, exp), ("z", "y", "exp"))
        body, ctx_name, both = body_heads, ("z", "y"), ("z", "y", "exp")
    else:
        inner, body, ctx_name, both = mesh, body_general, "ctx", ("ctx", "exp")
    token = P("exp", ctx_name, None)
    group = P("exp", None)
    expert = P(ctx_name, "exp", None)
    rows, gain = P(both, None), P(both)
    in_specs = (token, token, group, group, token, gain) + (rows,) * 5 + (gain, expert, expert)
    out_specs = (token, token, gain) + (rows,) * 5 + (gain, expert, expert)
    return jax.shard_map(
        body, mesh=inner, in_specs=in_specs, out_specs=out_specs, check_vma=False
    )
```

```python
import math

import jax
import jax.numpy as jnp
from jax import lax
from jax.experimental import pallas as pl
from jax.experimental.pallas import tpu as pltpu
from jax.sharding import PartitionSpec as P

D = 1536
HEADS = 24
KV_HEADS = 8
HEAD = 64
HID = 512
TOP = 8
EXP_DEV = 10
SPAN = 64


EPSILON = 1e-06
NEGATIVE = -1e30


def global_rows(perm_row, rows):
    slots = rows // SPAN
    match = slots[:, None] == jnp.arange(perm_row.shape[0], dtype=jnp.int32)[None, :]
    spans = jnp.sum(jnp.where(match, perm_row[None, :], 0), axis=1)
    return spans * SPAN + rows % SPAN


def rotary(tensor, position, sign):
    half = HEAD // 2
    freqs = jnp.exp(jnp.arange(half, dtype=jnp.float32) * (-2.0 * math.log(10000.0) / HEAD))
    angle = position.astype(jnp.float32)[:, None] * freqs[None, :]
    cosine = jnp.cos(angle)[:, None, :]
    sine = sign * jnp.sin(angle)[:, None, :]
    first, second = (tensor[..., :half], tensor[..., half:])
    return jnp.concatenate(
        [first * cosine - second * sine, second * cosine + first * sine], axis=-1
    )


def allowed(query_rows, key_rows, first_len):
    later = key_rows[None, :] <= query_rows[:, None]
    same_seq = (key_rows[None, :] >= first_len) == (query_rows[:, None] >= first_len)
    return later & same_seq


def contract_rows(left, right):
    return lax.dot_general(
        left, right, (((0,), (0,)), ((), ())), preferred_element_type=jnp.float32
    )


def contract_cols(left, right):
    return lax.dot_general(
        left, right, (((1,), (1,)), ((), ())), preferred_element_type=jnp.float32
    )


def block_grads(
    query_block,
    grad_block,
    lse_block,
    drift_block,
    query_rows,
    key_block,
    value_block,
    key_rows,
    first_len,
):
    softmax_scale = HEAD ** (-0.5)
    scores = (
        jnp.einsum("qgrd,kgd->grqk", query_block, key_block, preferred_element_type=jnp.float32)
        * softmax_scale
    )
    mask = allowed(query_rows, key_rows, first_len)[None, None]
    weights = jnp.where(mask, jnp.exp(scores - lse_block.transpose(1, 2, 0)[..., None]), 0.0)
    prob_grad = jnp.einsum(
        "qgrd,kgd->grqk", grad_block, value_block, preferred_element_type=jnp.float32
    )
    score_grad = (weights * (prob_grad - drift_block.transpose(1, 2, 0)[..., None])).astype(
        jnp.bfloat16
    )
    query_grad = None
    key_grad = None
    value_grad = None
    query_grad = (
        jnp.einsum("grqk,kgd->qgrd", score_grad, key_block, preferred_element_type=jnp.float32)
        * softmax_scale
    )
    value_grad = jnp.einsum(
        "grqk,qgrd->kgd",
        weights.astype(jnp.bfloat16),
        grad_block,
        preferred_element_type=jnp.float32,
    )
    key_grad = (
        jnp.einsum("grqk,qgrd->kgd", score_grad, query_block, preferred_element_type=jnp.float32)
        * softmax_scale
    )
    return (query_grad, key_grad, value_grad)


def body_general(
    tokens,
    cotangent,
    lengths,
    span_perm,
    routes,
    norm_attn,
    attn_q,
    attn_k,
    attn_v,
    attn_o,
    router,
    norm_moe,
    expert_in,
    expert_out,
):
    count = tokens.shape[1]
    repeat = HEADS // KV_HEADS
    experts = EXP_DEV * lax.axis_size("exp")
    capacity = count * TOP * 3 // (2 * experts)
    softmax_scale = HEAD ** (-0.5)
    perm_row = span_perm[0]
    first_len = lengths[0, 0]
    query_rows = global_rows(
        perm_row, lax.axis_index("ctx") * count + jnp.arange(count, dtype=jnp.int32)
    )
    position = query_rows - jnp.where(query_rows >= first_len, first_len, 0)
    gathered = (
        lax.all_gather(norm_attn.astype(jnp.bfloat16), ("ctx", "exp"), axis=0, tiled=True),
        lax.all_gather(attn_q.astype(jnp.bfloat16), ("ctx", "exp"), axis=0, tiled=True),
        lax.all_gather(attn_k.astype(jnp.bfloat16), ("ctx", "exp"), axis=0, tiled=True),
        lax.all_gather(attn_v.astype(jnp.bfloat16), ("ctx", "exp"), axis=0, tiled=True),
        lax.all_gather(attn_o.astype(jnp.bfloat16), ("ctx", "exp"), axis=0, tiled=True),
        lax.all_gather(router.astype(jnp.bfloat16), ("ctx", "exp"), axis=0, tiled=True),
        lax.all_gather(norm_moe.astype(jnp.bfloat16), ("ctx", "exp"), axis=0, tiled=True),
    )
    gain_one, weight_q, weight_k, weight_v, weight_o, weight_r, gain_two = gathered
    weight_in, weight_out = (
        lax.all_gather(expert_in.astype(jnp.bfloat16), "ctx", axis=0, tiled=True),
        lax.all_gather(expert_out.astype(jnp.bfloat16), "ctx", axis=0, tiled=True),
    )
    gain_one_f = gain_one.astype(jnp.float32)
    gain_two_f = gain_two.astype(jnp.float32)
    resid = tokens[0].astype(jnp.float32)
    scale_one = lax.rsqrt(jnp.mean(resid * resid, axis=-1, keepdims=True) + EPSILON)
    normed_one = resid * scale_one
    hidden_one = (normed_one * gain_one_f).astype(jnp.bfloat16)
    query_pre = jnp.dot(hidden_one, weight_q, preferred_element_type=jnp.float32).reshape(
        count, HEADS, HEAD
    )
    queries = (
        rotary(query_pre, position, 1.0).astype(jnp.bfloat16).reshape(count, KV_HEADS, repeat, HEAD)
    )
    key_pre = jnp.dot(hidden_one, weight_k, preferred_element_type=jnp.float32).reshape(
        count, KV_HEADS, HEAD
    )
    keys = rotary(key_pre, position, 1.0).astype(jnp.bfloat16)
    values = (
        jnp.dot(hidden_one, weight_v, preferred_element_type=jnp.float32)
        .astype(jnp.bfloat16)
        .reshape(count, KV_HEADS, HEAD)
    )
    start_state = (
        jnp.full((KV_HEADS, repeat, count), NEGATIVE, jnp.float32),
        jnp.zeros((KV_HEADS, repeat, count), jnp.float32),
        jnp.zeros((KV_HEADS, repeat, count, HEAD), jnp.float32),
    )
    carry = start_state
    key_piece = lax.all_gather(keys, "ctx", axis=0, tiled=True)
    value_piece = lax.all_gather(values, "ctx", axis=0, tiled=True)
    size = key_piece.shape[0]
    block = math.gcd(size, 512)
    number = size // block
    key_blocks = key_piece.reshape(number, block, KV_HEADS, HEAD)
    value_blocks = value_piece.reshape(number, block, KV_HEADS, HEAD)
    offsets = jnp.arange(size, dtype=jnp.int32).reshape(number, block)

    def forward_step(state, inputs):
        highest, total, accum = state
        key_block, value_block, offset = inputs
        key_rows = global_rows(perm_row, offset)
        scores = (
            jnp.einsum("qgrd,kgd->grqk", queries, key_block, preferred_element_type=jnp.float32)
            * softmax_scale
        )
        mask = allowed(query_rows, key_rows, first_len)[None, None]
        scores = jnp.where(mask, scores, NEGATIVE)
        newmax = jnp.maximum(highest, jnp.max(scores, axis=-1))
        weights = jnp.where(mask, jnp.exp(scores - newmax[..., None]), 0.0)
        factor = jnp.exp(highest - newmax)
        total = total * factor + jnp.sum(weights, axis=-1)
        accum = accum * factor[..., None] + jnp.einsum(
            "grqk,kgd->grqd",
            weights.astype(jnp.bfloat16),
            value_block,
            preferred_element_type=jnp.float32,
        )
        return ((newmax, total, accum), None)

    carry, _ = lax.scan(forward_step, carry, (key_blocks, value_blocks, offsets))
    highest, total, accum = carry
    log_total = (highest + jnp.log(total)).transpose(2, 0, 1)
    attended = (accum / total[..., None]).transpose(2, 0, 1, 3)
    attended_b = attended.reshape(count, HEADS * HEAD).astype(jnp.bfloat16)
    middle = resid + jnp.dot(attended_b, weight_o, preferred_element_type=jnp.float32)
    scale_two = lax.rsqrt(jnp.mean(middle * middle, axis=-1, keepdims=True) + EPSILON)
    normed_two = middle * scale_two
    hidden_two = (normed_two * gain_two_f).astype(jnp.bfloat16)
    logits = jnp.dot(hidden_two, weight_r, preferred_element_type=jnp.float32)
    chosen = routes[0]
    picks = chosen[:, :, None] == jnp.arange(experts, dtype=jnp.int32)[None, None, :]
    selected = jnp.sum(jnp.where(picks, logits[:, None, :], 0.0), axis=-1)
    gates = jax.nn.softmax(selected, axis=-1)
    gates_b = gates.astype(jnp.bfloat16)
    flat_picks = picks.reshape(count * TOP, experts).astype(jnp.int32)
    placed = jnp.sum((jnp.cumsum(flat_picks, axis=0) - 1) * flat_picks, axis=-1)
    column = chosen.reshape(-1) * capacity + placed
    hits = (
        column.reshape(count, TOP)[:, :, None]
        == jnp.arange(experts * capacity, dtype=jnp.int32)[None, None, :]
    )
    spread = jnp.any(hits, axis=1).astype(jnp.bfloat16)
    weighted = jnp.sum(
        jnp.where(hits, gates_b.astype(jnp.float32)[:, :, None], 0.0), axis=1
    ).astype(jnp.bfloat16)
    outgoing = contract_rows(spread, hidden_two).astype(jnp.bfloat16).reshape(experts, capacity, D)
    incoming = lax.all_to_all(outgoing, "exp", split_axis=0, concat_axis=1, tiled=True)
    gate_up = jnp.einsum("erd,dec->erc", incoming, weight_in, preferred_element_type=jnp.float32)
    gate_part = gate_up[..., :HID]
    up_part = gate_up[..., HID:]
    sigmoid_gate = jax.nn.sigmoid(gate_part)
    silu_gate = gate_part * sigmoid_gate
    activated = (silu_gate * up_part).astype(jnp.bfloat16)
    produced = jnp.einsum(
        "erh,deh->erd", activated, weight_out, preferred_element_type=jnp.float32
    ).astype(jnp.bfloat16)
    returned = lax.all_to_all(produced, "exp", split_axis=1, concat_axis=0, tiled=True).reshape(
        experts * capacity, D
    )
    mixture = jnp.dot(weighted, returned, preferred_element_type=jnp.float32)
    output = (middle + mixture).astype(jnp.bfloat16)
    upstream = cotangent[0].astype(jnp.float32)
    upstream_b = upstream.astype(jnp.bfloat16)
    sent_grad = (
        contract_rows(weighted, upstream_b).astype(jnp.bfloat16).reshape(experts, capacity, D)
    )
    grad_in = lax.all_to_all(sent_grad, "exp", split_axis=0, concat_axis=1, tiled=True)
    picked = jnp.take(returned, column, axis=0).reshape(count, TOP, D)
    gate_grad = jnp.einsum("tkd,td->tk", picked, upstream_b, preferred_element_type=jnp.float32)
    grad_act = (
        jnp.einsum("erd,deh->erh", grad_in, weight_out, preferred_element_type=jnp.float32)
        .astype(jnp.bfloat16)
        .astype(jnp.float32)
    )
    grad_gate = grad_act * up_part * (sigmoid_gate * (1.0 + gate_part * (1.0 - sigmoid_gate)))
    grad_up = grad_act * silu_gate
    grad_gu = jnp.concatenate([grad_gate, grad_up], axis=-1).astype(jnp.bfloat16)
    grad_weight_out = jnp.einsum(
        "erd,erh->deh", grad_in, activated, preferred_element_type=jnp.float32
    )
    grad_weight_in = jnp.einsum(
        "erd,erc->dec", incoming, grad_gu, preferred_element_type=jnp.float32
    )
    grad_rows = jnp.einsum(
        "erc,dec->erd", grad_gu, weight_in, preferred_element_type=jnp.float32
    ).astype(jnp.bfloat16)
    back_rows = lax.all_to_all(grad_rows, "exp", split_axis=1, concat_axis=0, tiled=True).reshape(
        experts * capacity, D
    )
    expert_sums = (
        lax.psum_scatter(
            grad_weight_in.astype(jnp.bfloat16), "ctx", scatter_dimension=0, tiled=True
        ).astype(jnp.float32),
        lax.psum_scatter(
            grad_weight_out.astype(jnp.bfloat16), "ctx", scatter_dimension=0, tiled=True
        ).astype(jnp.float32),
    )
    centered = gate_grad - jnp.sum(gates * gate_grad, axis=-1, keepdims=True)
    select_grad = gates * centered
    logit_grad = jnp.sum(jnp.where(picks, select_grad[:, :, None], 0.0), axis=1).astype(
        jnp.bfloat16
    )
    grad_router = contract_rows(hidden_two, logit_grad)
    grad_norm_two = jnp.dot(spread, back_rows, preferred_element_type=jnp.float32) + contract_cols(
        logit_grad, weight_r
    )
    grad_gain_two = jnp.sum(grad_norm_two * normed_two, axis=0)
    scaled_two = grad_norm_two * gain_two_f
    grad_middle = upstream + scale_two * (
        scaled_two - normed_two * jnp.mean(scaled_two * normed_two, axis=-1, keepdims=True)
    )
    branch_grad = grad_middle.astype(jnp.bfloat16)
    grad_weight_o = contract_rows(attended_b, branch_grad)
    grad_heads = (
        contract_cols(branch_grad, weight_o)
        .astype(jnp.bfloat16)
        .reshape(count, KV_HEADS, repeat, HEAD)
    )
    drift = jnp.sum(grad_heads.astype(jnp.float32) * attended, axis=-1)
    query_acc = jnp.zeros((count, KV_HEADS, repeat, HEAD), jnp.float32)
    key_piece = lax.all_gather(keys, "ctx", axis=0, tiled=True)
    value_piece = lax.all_gather(values, "ctx", axis=0, tiled=True)
    size = key_piece.shape[0]
    block = math.gcd(size, 512)
    number = size // block
    key_blocks = key_piece.reshape(number, block, KV_HEADS, HEAD)
    value_blocks = value_piece.reshape(number, block, KV_HEADS, HEAD)
    offsets = jnp.arange(size, dtype=jnp.int32).reshape(number, block)

    def backward_step(acc, inputs):
        key_block, value_block, offset = inputs
        part_q, part_k, part_v = block_grads(
            queries,
            grad_heads,
            log_total,
            drift,
            query_rows,
            key_block,
            value_block,
            global_rows(perm_row, offset),
            first_len,
        )
        joined = jnp.concatenate(
            [part_k.reshape(block, KV_HEADS * HEAD), part_v.reshape(block, KV_HEADS * HEAD)],
            axis=-1,
        )
        return (acc + part_q, joined)

    query_acc, joined_parts = lax.scan(
        backward_step, query_acc, (key_blocks, value_blocks, offsets)
    )
    pair_acc = joined_parts.reshape(size, 2 * KV_HEADS * HEAD)
    query_grad, pair_acc = (query_acc, pair_acc)
    pair_own = lax.psum_scatter(
        pair_acc.astype(jnp.bfloat16), "ctx", scatter_dimension=0, tiled=True
    ).astype(jnp.float32)
    key_grad = pair_own[:, : KV_HEADS * HEAD].reshape(count, KV_HEADS, HEAD)
    value_grad = pair_own[:, KV_HEADS * HEAD :].reshape(count, KV_HEADS, HEAD)
    query_grad_b = (
        rotary(query_grad.reshape(count, HEADS, HEAD), position, -1.0)
        .astype(jnp.bfloat16)
        .reshape(count, HEADS * HEAD)
    )
    key_grad_b = (
        rotary(key_grad, position, -1.0).astype(jnp.bfloat16).reshape(count, KV_HEADS * HEAD)
    )
    value_grad_b = value_grad.astype(jnp.bfloat16).reshape(count, KV_HEADS * HEAD)
    grad_weight_q = contract_rows(hidden_one, query_grad_b)
    grad_weight_k = contract_rows(hidden_one, key_grad_b)
    grad_weight_v = contract_rows(hidden_one, value_grad_b)
    grad_hidden_one = (
        contract_cols(query_grad_b, weight_q)
        + contract_cols(key_grad_b, weight_k)
        + contract_cols(value_grad_b, weight_v)
    )
    grad_gain_one = jnp.sum(grad_hidden_one * normed_one, axis=0)
    scaled_one = grad_hidden_one * gain_one_f
    grad_tokens = grad_middle + scale_one * (
        scaled_one - normed_one * jnp.mean(scaled_one * normed_one, axis=-1, keepdims=True)
    )
    attn_sums = (
        lax.psum_scatter(grad_gain_one, ("ctx", "exp"), scatter_dimension=0, tiled=True),
        lax.psum_scatter(grad_weight_q, ("ctx", "exp"), scatter_dimension=0, tiled=True),
        lax.psum_scatter(grad_weight_k, ("ctx", "exp"), scatter_dimension=0, tiled=True),
        lax.psum_scatter(grad_weight_v, ("ctx", "exp"), scatter_dimension=0, tiled=True),
        lax.psum_scatter(grad_weight_o, ("ctx", "exp"), scatter_dimension=0, tiled=True),
        lax.psum_scatter(grad_router, ("ctx", "exp"), scatter_dimension=0, tiled=True),
        lax.psum_scatter(grad_gain_two, ("ctx", "exp"), scatter_dimension=0, tiled=True),
    )
    return (
        output[None],
        grad_tokens[None],
        attn_sums[0],
        attn_sums[1],
        attn_sums[2],
        attn_sums[3],
        attn_sums[4],
        attn_sums[5],
        attn_sums[6],
        expert_sums[0],
        expert_sums[1],
    )


def rotate(tensor, cosine, sine):
    half = HEAD // 2
    first, second = (tensor[..., :half], tensor[..., half:])
    return jnp.concatenate(
        [first * cosine - second * sine, second * cosine + first * sine], axis=-1
    )


def unit_kernel(first_ref, gate_ref, up_ref, down_ref, unit_ref):
    half = gate_ref.shape[-1]
    unit_ref[0, :, :half] = gate_ref[0].astype(unit_ref.dtype)
    unit_ref[0, :, half : 2 * half] = up_ref[0].astype(unit_ref.dtype)
    unit_ref[0, :, 2 * half :] = down_ref[0].astype(unit_ref.dtype)


def take_units(first, number, win, wout):
    depth, half = win.shape[1], HID // 2
    return pl.pallas_call(
        unit_kernel,
        grid_spec=pltpu.PrefetchScalarGridSpec(
            num_scalar_prefetch=1,
            grid=(number,),
            in_specs=[
                pl.BlockSpec(
                    (1, depth, half), lambda j, f: ((f[0] + j) // 2, 0, lax.rem(f[0] + j, 2))
                ),
                pl.BlockSpec(
                    (1, depth, half), lambda j, f: ((f[0] + j) // 2, 0, 2 + lax.rem(f[0] + j, 2))
                ),
                pl.BlockSpec(
                    (1, depth, half), lambda j, f: ((f[0] + j) // 2, 0, lax.rem(f[0] + j, 2))
                ),
            ],
            out_specs=pl.BlockSpec((1, depth, 3 * half), lambda j, f: (j, 0, 0)),
        ),
        out_shape=jax.ShapeDtypeStruct((number, depth, 3 * half), jnp.bfloat16),
        name="take_units",
    )(first.reshape(1), win, win, wout)


def dispatch_kernel(base, hid_ref, mark_ref, router_ref, rows_ref, up_ref, gate_ref, spread_ref, gates_ref):
    bf16, f32 = jnp.bfloat16, jnp.float32
    count = hid_ref.shape[1]
    _, held, rows, _ = rows_ref.shape
    slots = rows // 2
    both = 2 * count
    x = hid_ref[...].reshape(both, D)
    logits = jnp.dot(x, router_ref[...], preferred_element_type=f32)
    routes = mark_ref[:, :, D:].reshape(both, 128).astype(f32)
    lane = lax.broadcasted_iota(jnp.int32, (both, 128), 1).astype(f32)
    picks = jnp.zeros((both, 128), f32)
    for i in range(TOP):
        picks = jnp.where(routes[:, i : i + 1] == lane, 1.0, picks)
    masked = jnp.where(picks > 0.0, logits, NEGATIVE)
    top = jnp.max(masked, axis=-1, keepdims=True)
    gates = jnp.where(picks > 0.0, jnp.exp(masked - top), 0.0)
    gates = gates / jnp.sum(gates, axis=-1, keepdims=True)
    gates_ref[...] = gates.reshape(2, count, 128)
    which = lax.broadcasted_iota(jnp.int32, (8, 128), 0)
    columns = lax.broadcasted_iota(jnp.int32, (8, 128), 1)
    chosen = jnp.where(columns == which + base[0], 1.0, 0.0).astype(bf16)
    hit = contract_cols(chosen, picks.astype(bf16))
    gate = contract_cols(chosen, gates.astype(bf16))
    earlier = lax.broadcasted_iota(jnp.int32, (both, both), 0)
    later = lax.broadcasted_iota(jnp.int32, (both, both), 1)
    upto = jnp.where((earlier <= later) & (earlier // count == later // count), 1.0, 0.0)
    rank = jnp.dot(hit.astype(bf16), upto.astype(bf16), preferred_element_type=f32)
    row = lax.broadcasted_iota(jnp.int32, (rows, both), 0)
    token = lax.broadcasted_iota(jnp.int32, (rows, both), 1)
    side = row // slots
    wanted = jnp.where(side == token // count, row - side * slots + 1, -1).astype(f32)
    for e in range(held):
        here = jnp.where((rank[e : e + 1] == wanted) & (hit[e : e + 1] > 0.0), 1.0, 0.0)
        gate_ref[0, e] = jnp.sum(here * gate[e : e + 1], axis=-1, keepdims=True)
        here = here.astype(bf16)
        spread_ref[0, e * rows : (e + 1) * rows, :] = here
        rows_ref[0, e] = jnp.dot(here, x, preferred_element_type=f32).astype(bf16)
        up_ref[0, e] = jnp.dot(
            here, mark_ref[:, :, :D].reshape(both, D), preferred_element_type=f32
        ).astype(bf16)


def dispatch(base, hidden, marked, router, held, slots):
    blocks, count, _ = hidden.shape
    pairs = blocks // 2
    bf16, f32 = jnp.bfloat16, jnp.float32
    pair = lambda *shape: pl.BlockSpec((1,) + shape, lambda p, b: (p,) + (0,) * len(shape))
    two = lambda width: pl.BlockSpec((2, count, width), lambda p, b: (p, 0, 0))
    return pl.pallas_call(
        dispatch_kernel,
        grid_spec=pltpu.PrefetchScalarGridSpec(
            num_scalar_prefetch=1,
            grid=(pairs,),
            in_specs=[two(D), two(D + 128), pl.BlockSpec((D, 128), lambda p, b: (0, 0))],
            out_specs=[
                pair(held, 2 * slots, D),
                pair(held, 2 * slots, D),
                pair(held, 2 * slots, 1),
                pair(held * 2 * slots, 2 * count),
                two(128),
            ],
        ),
        out_shape=[
            jax.ShapeDtypeStruct((pairs, held, 2 * slots, D), bf16),
            jax.ShapeDtypeStruct((pairs, held, 2 * slots, D), bf16),
            jax.ShapeDtypeStruct((pairs, held, 2 * slots, 1), f32),
            jax.ShapeDtypeStruct((pairs, held * 2 * slots, 2 * count), bf16),
            jax.ShapeDtypeStruct((blocks, count, 128), f32),
        ],
        compiler_params=pltpu.CompilerParams(vmem_limit_bytes=48 * 2**20),
        name="dispatch",
    )(base.reshape(1).astype(jnp.int32), hidden, marked, router)


def expert_kernel(depth, meta, x_ref, g_ref, gate_ref, *refs):
    parts, (y_ref, d_ref), outs = refs[:8], refs[8:10], refs[10:18]
    weight, du_ref, act_ref = refs[18:]
    bf16, f32 = jnp.bfloat16, jnp.float32
    j = pl.program_id(0)
    shift, z, y, base = meta[0], meta[1], meta[2], meta[3]
    half = HID // 2
    offsets = [
        pl.multiple_of(((z ^ (i % 4)) * 2 + (y ^ (i // 4))) * depth, 64) for i in range(8)
    ]
    for part, offset in zip(parts, offsets):
        weight[pl.ds(offset, depth), :] = part[0] if len(part.shape) == 3 else part[0, 0]
    expert = base + (j + shift) // 2
    first = jnp.logical_or(j == 0, lax.rem(j + shift, 2) == 0)
    keep = jnp.where(first, 0.0, 1.0)
    pairs, _, rows, _ = x_ref.shape
    step = 2

    def forward(i, carry):
        at = pl.ds(i * step, step)
        flat = pl.ds(pl.multiple_of(i * step * rows, 32), step * rows)
        x = x_ref[at, 0].reshape(step * rows, D)
        g = g_ref[at, 0].reshape(step * rows, D)
        gate = gate_ref[at, 0].reshape(step * rows, 1)
        u = jnp.dot(x, weight[:, : 2 * half], preferred_element_type=f32)
        raw = jnp.dot(g, weight[:, 2 * half :], preferred_element_type=f32)
        u1, u2 = u[:, :half], u[:, half:]
        sig = jax.nn.sigmoid(u1)
        silu = u1 * sig
        act = (silu * u2).astype(bf16).astype(f32)
        dgate = jnp.sum(raw * act, axis=-1, keepdims=True)
        dact = raw * gate
        du1 = dact * u2 * (sig * (1.0 + u1 * (1.0 - sig)))
        du = jnp.concatenate([du1, dact * silu], axis=-1).astype(bf16)
        act_gated = (act * gate).astype(bf16)
        du_ref[flat, :] = du
        act_ref[flat, :] = act_gated
        made = contract_cols(act_gated, weight[:, 2 * half :])
        back = contract_cols(du, weight[:, : 2 * half])
        lane = lax.broadcasted_iota(jnp.int32, (step * rows, 128), 1)
        tail = jnp.where(lane == expert, dgate, 0.0)

        @pl.when(first)
        def _():
            y_ref[at, 0] = made.astype(bf16).reshape(step, rows, D)
            d_ref[at, 0, :, :D] = back.astype(bf16).reshape(step, rows, D)
            d_ref[at, 0, :, D:] = tail.astype(bf16).reshape(step, rows, 128)

        @pl.when(jnp.logical_not(first))
        def _():
            old_y = y_ref[at, 0].reshape(step * rows, D).astype(f32)
            y_ref[at, 0] = (made + old_y).astype(bf16).reshape(step, rows, D)
            old_d = d_ref[at, 0].reshape(step * rows, D + 128).astype(f32)
            d_ref[at, 0, :, :D] = (back + old_d[:, :D]).astype(bf16).reshape(step, rows, D)
            d_ref[at, 0, :, D:] = (tail + old_d[:, D:]).astype(bf16).reshape(step, rows, 128)

        return carry

    lax.fori_loop(0, pairs // step, forward, 0)

    def gradient(i, carry):
        at = pl.ds(pl.multiple_of(i * 256, 256), 256)
        x = x_ref[:, 0, :, at].reshape(pairs * rows, 256)
        g = g_ref[:, 0, :, at].reshape(pairs * rows, 256)
        weight[at, : 2 * half] = contract_rows(x, du_ref[...]).astype(bf16)
        weight[at, 2 * half :] = contract_rows(g, act_ref[...]).astype(bf16)
        return carry

    lax.fori_loop(0, D // 256, gradient, 0)
    for out, offset in zip(outs, offsets):
        out[0] = weight[pl.ds(offset, depth), :]


def run_experts(meta, row_in, row_up, slot_gate, own_part, near_parts, far_parts):
    pairs, held, rows, _ = row_in.shape
    units, depth, columns = own_part.shape
    held_block = lambda width: pl.BlockSpec(
        (pairs, 1, rows, width), lambda j, m: (0, (j + m[0]) // 2, 0, 0)
    )
    unit_block = pl.BlockSpec((1, depth, columns), lambda j, m: (j, 0, 0))

    def part_block(i):
        return pl.BlockSpec((1, 1, depth, columns), lambda j, m: (i, j, 0, 0))

    bf16 = jnp.bfloat16
    total = units * pairs * rows * D * columns * 6
    return pl.pallas_call(
        lambda *refs: expert_kernel(depth, *refs),
        grid_spec=pltpu.PrefetchScalarGridSpec(
            num_scalar_prefetch=1,
            grid=(units,),
            in_specs=[
                held_block(D),
                held_block(D),
                held_block(1),
                unit_block,
            ]
            + [part_block(i) for i in (0, 1, 2, 0, 1, 2, 3)],
            out_specs=[held_block(D), held_block(D + 128)] + [unit_block] * 8,
            scratch_shapes=[
                pltpu.VMEM((D, columns), bf16),
                pltpu.VMEM((pairs * rows, HID), bf16),
                pltpu.VMEM((pairs * rows, HID // 2), bf16),
            ],
        ),
        out_shape=[
            jax.ShapeDtypeStruct((pairs, held, rows, D), bf16),
            jax.ShapeDtypeStruct((pairs, held, rows, D + 128), bf16),
        ]
        + [jax.ShapeDtypeStruct((units, depth, columns), bf16)] * 8,
        compiler_params=pltpu.CompilerParams(vmem_limit_bytes=56 * 2**20),
        cost_estimate=pl.CostEstimate(
            flops=total, bytes_accessed=60 * 2**20, transcendentals=units * pairs * rows * HID
        ),
        name="experts",
    )(meta, row_in, row_up, slot_gate, own_part, *[near_parts] * 3, *[far_parts] * 4)


def spread_kernel(z_ref, low_ref, high_ref, in_ref, out_ref):
    half = low_ref.shape[-1] // 3
    for h, ref in enumerate((low_ref, high_ref)):
        for p in range(2):
            at = p * 2 * half + h * half
            in_ref[0, :, at : at + half] = ref[0, :, p * half : (p + 1) * half].astype(in_ref.dtype)
        out_ref[0, :, h * half : (h + 1) * half] = ref[0, :, 2 * half :].astype(out_ref.dtype)


def place_units(z_index, units, number):
    depth, columns = units.shape[1:]

    def pick(h):
        def index(i, z):
            unit = 2 * i + h
            return ((unit // number) ^ z[0]) * number + lax.rem(unit, number), 0, 0

        return pl.BlockSpec((1, depth, columns), index)

    return pl.pallas_call(
        spread_kernel,
        grid_spec=pltpu.PrefetchScalarGridSpec(
            num_scalar_prefetch=1,
            grid=(EXP_DEV,),
            in_specs=[pick(0), pick(1)],
            out_specs=[
                pl.BlockSpec((1, depth, 2 * HID), lambda i, z: (i, 0, 0)),
                pl.BlockSpec((1, depth, HID), lambda i, z: (i, 0, 0)),
            ],
        ),
        out_shape=[
            jax.ShapeDtypeStruct((EXP_DEV, depth, 2 * HID), jnp.float32),
            jax.ShapeDtypeStruct((EXP_DEV, depth, HID), jnp.float32),
        ],
        name="place_units",
    )(z_index.reshape(1), units, units)


MESH = pl.DeviceIdType.MESH


def greet(peers):
    barrier = pltpu.get_barrier_semaphore()
    for peer in peers:
        pl.semaphore_signal(barrier, inc=1, device_id=peer, device_id_type=MESH)
    pl.semaphore_wait(barrier, len(peers))


def send(src, dst, sems, at, peer):
    copy = pltpu.make_async_remote_copy(
        src_ref=src,
        dst_ref=dst,
        send_sem=sems[0].at[at],
        recv_sem=sems[1].at[at],
        device_id=peer,
        device_id_type=MESH,
    )
    copy.start()
    return copy


def dma_pair(number):
    return [pltpu.SemaphoreType.DMA((number,)), pltpu.SemaphoreType.DMA((number,))]


def z_peers():
    z = lax.axis_index("z")
    return [{"z": z ^ s} for s in (3, 2, 1)]


def siblings(axes):
    return [{a: 1 - lax.axis_index(a)} for a in axes]


class Scatter:
    def __init__(self, part, axes, chunks, refs):
        self.part, self.axes, self.chunks = part, axes, chunks
        depth = len(axes)
        self.own, self.came = refs[0], refs[1 : 1 + depth]
        self.sums, self.far = refs[1 + depth : 1 + 2 * depth], refs[1 + 2 * depth]
        self.load_sem = refs[2 + 2 * depth]
        sems = refs[3 + 2 * depth :]
        self.sems = [sems[2 * i : 2 * i + 2] for i in range(depth + 1)]
        self.z = lax.axis_index("z")
        self.mine = [lax.axis_index(a) for a in axes]
        self.rows = part.shape[-2] // chunks
        self.flying = [[None] * chunks for _ in axes]
        self.over_z = [None] * chunks

    @staticmethod
    def scratch(part, axes, chunks):
        n_z, rows, width, kind = part.shape[0], part.shape[-2], part.shape[-1], part.dtype
        depth = len(axes)

        def buffer(i):
            return pltpu.VMEM((chunks, n_z) + (2,) * i + (rows // chunks, width), kind)

        shapes = [buffer(depth - 1)] + [buffer(i) for i in range(depth)] * 2
        shapes += [pltpu.VMEM((chunks, n_z - 1, rows // chunks, width), kind)]
        shapes += [pltpu.SemaphoreType.DMA((chunks,))]
        for _ in range(depth):
            shapes += dma_pair(chunks)
        return shapes + dma_pair(chunks * (n_z - 1))

    def start(self):
        level = len(self.axes) - 1
        lead = (slice(None),) * len(self.axes)
        mine = self.mine[-1]
        self.loads = []
        for c in range(self.chunks):
            at = pl.ds(c * self.rows, self.rows)
            self.flying[level][c] = send(
                self.part.at[lead + (1 - mine, at)],
                self.came[level].at[c],
                self.sems[level],
                c,
                {self.axes[-1]: 1 - mine},
            )
            load = pltpu.make_async_copy(
                self.part.at[lead + (mine, at)], self.own.at[c], self.load_sem.at[c]
            )
            load.start()
            self.loads.append(load)

    def fold(self, level, c):
        self.flying[level][c].wait_recv()
        if level == len(self.axes) - 1:
            self.loads[c].wait()
            held = self.own[c]
        else:
            held = self.sums[level + 1][
                (c,) + (slice(None),) * (level + 1) + (self.mine[level],)
            ]
        total = held.astype(jnp.float32) + self.came[level][c].astype(jnp.float32)
        self.sums[level][c] = total.astype(held.dtype)
        if level > 0:
            mine = self.mine[level - 1]
            self.flying[level - 1][c] = send(
                self.sums[level].at[(c,) + (slice(None),) * level + (1 - mine,)],
                self.came[level - 1].at[c],
                self.sems[level - 1],
                c,
                {self.axes[level - 1]: 1 - mine},
            )
        else:
            self.over_z[c] = [
                send(
                    self.sums[0].at[c, self.z ^ s],
                    self.far.at[c, s - 1],
                    self.sems[-1],
                    c * 3 + s - 1,
                    {"z": self.z ^ s},
                )
                for s in (3, 2, 1)
            ]

    def total(self, c):
        for copy in self.over_z[c]:
            copy.wait_recv()
        total = self.sums[0][c, self.z].astype(jnp.float32)
        for s in range(3):
            total = total + self.far[c, s].astype(jnp.float32)
        return total

    def run(self, use):
        depth = len(self.axes)
        for step in range(self.chunks + depth):
            for level in range(depth - 1, -1, -1):
                c = step - (depth - 1 - level)
                if 0 <= c < self.chunks:
                    self.fold(level, c)
            c = step - depth
            if 0 <= c < self.chunks:
                use(c, pl.ds(c * self.rows, self.rows), self.total(c))

    def finish(self):
        for copy in sum(self.flying + self.over_z, []):
            copy.wait_send()


class Gather:
    def __init__(self, own, out, axes, chunks, refs):
        self.own, self.out, self.axes, self.chunks = own, out, axes, chunks
        self.keep_sem = refs[0]
        self.sems = [refs[1 + 2 * i : 3 + 2 * i] for i in range(len(axes) + 1)]
        self.z = lax.axis_index("z")
        self.mine = tuple(lax.axis_index(a) for a in axes)
        self.rows = own.shape[0] // chunks
        self.keeps, self.over_z, self.over = [], {}, [{} for _ in axes]

    @staticmethod
    def scratch(axes, chunks):
        shapes = [pltpu.SemaphoreType.DMA((chunks,))] + dma_pair(3 * chunks)
        for i in range(len(axes)):
            shapes += dma_pair(4 * 2**i * chunks)
        return shapes

    def pass_on(self, level, c, s, flips, src):
        at = pl.ds(c * self.rows, self.rows)
        places = tuple(
            1 - m if i < len(flips) and flips[i] else m for i, m in enumerate(self.mine)
        )
        where = self.out.at[(self.z ^ s,) + places + (at,)]
        number = s
        for f in flips:
            number = number * 2 + f
        axis = self.axes[level]
        self.over[level][c, s, flips] = send(
            where if src is None else src,
            where,
            self.sems[level + 1],
            number * self.chunks + c,
            {axis: 1 - self.mine[level]},
        )

    def start(self, c):
        at = pl.ds(c * self.rows, self.rows)
        own, place = self.own.at[at], self.out.at[(self.z,) + self.mine + (at,)]
        for s in (3, 2, 1):
            self.over_z[c, s] = send(
                own, place, self.sems[0], (s - 1) * self.chunks + c, {"z": self.z ^ s}
            )
        for level in range(len(self.axes)):
            self.pass_on(level, c, 0, (0,) * level, own)
        keep = pltpu.make_async_copy(own, place, self.keep_sem.at[c])
        keep.start()
        self.keeps.append(keep)

    def forward(self, c):
        for s in (1, 2, 3):
            self.over_z[c, s].wait_recv()
            for level in range(len(self.axes)):
                self.pass_on(level, c, s, (0,) * level, None)

    def spread(self, c):
        for level in range(len(self.axes) - 1):
            for (chunk, s, flips), copy in list(self.over[level].items()):
                if chunk == c:
                    copy.wait_recv()
                    for later in range(level + 1, len(self.axes)):
                        self.pass_on(
                            later, c, s, flips + (1,) + (0,) * (later - level - 1), None
                        )

    def finish(self):
        for keep in self.keeps:
            keep.wait()
        for copy in self.over[-1].values():
            copy.wait_recv()
        for copies in [self.over_z] + self.over:
            for copy in copies.values():
                copy.wait_send()


VMEM_SPEC = pl.BlockSpec(memory_space=pltpu.VMEM)
ANY_SPEC = pl.BlockSpec(memory_space=pl.ANY)


def exchange(kernel, name, number, inputs, specs, outs, out_specs, scratch):
    sizes = [len(inputs), len(outs)] + [len(s) for s in scratch]

    def run(*refs):
        groups, at = [], 0
        for size in sizes:
            groups.append(refs[at : at + size])
            at += size
        kernel(*groups)

    return pl.pallas_call(
        run,
        out_shape=outs,
        in_specs=specs,
        out_specs=out_specs,
        scratch_shapes=sum(scratch, []),
        compiler_params=pltpu.CompilerParams(
            collective_id=number, has_side_effects=True, vmem_limit_bytes=48 * 2**20
        ),
        name=name,
    )(*inputs)


def share_inputs(tokens, slices, wo, units):
    count, own = tokens.shape[0], wo.shape[0]
    number = units[0].shape[0]
    columns = slices.shape[-1]
    chunks = 2

    def kernel(ins, outs, token_refs, other):
        tok, cut, wo_ref, unit_refs = ins[0], ins[1], ins[2], ins[3:]
        tok_out, cut_out, wo_out, near_out, far_out = outs
        keep, ctx_sems, exp_sems, wo_sems = other[0], other[1:3], other[3:5], other[5:7]
        near_sems, far_sems = other[7:9], other[9:11]
        z, y, x, k = (lax.axis_index(a) for a in ("z", "y", "x", "k"))
        ctx_peers = [
            ((z ^ s, y ^ t), s * 2 + t) for s in (3, 2, 1, 0) for t in (1, 0) if s or t
        ]
        exp_peers = [((x ^ a, k ^ b), a * 2 + b) for a in (1, 0) for b in (1, 0) if a or b]
        greet(
            [{"z": p, "y": q} for (p, q), _ in ctx_peers]
            + [{"x": p, "k": q} for (p, q), _ in exp_peers]
        )
        gather = Gather(tok, tok_out, ("y",), chunks, token_refs)
        over_ctx = [
            send(cut.at[p, q], cut_out.at[z, y, x, k], ctx_sems, i - 1, {"z": p, "y": q})
            for (p, q), i in ctx_peers
        ]
        for c in range(chunks):
            gather.start(c)
        over_wo = [
            send(wo_ref, wo_out.at[x, k], wo_sems, i - 1, {"x": p, "k": q})
            for (p, q), i in exp_peers
        ]
        over_near, over_far = {}, []
        for j in range(number):
            for i in (3, 2, 1):
                over_near[i, j] = send(
                    unit_refs[i].at[j],
                    near_out.at[i - 1, j],
                    near_sems,
                    (i - 1) * number + j,
                    {"z": z ^ i},
                )
            over_far.append(
                send(unit_refs[0].at[j], far_out.at[0, j], far_sems, j, {"y": 1 - y})
            )
        keeps = [
            pltpu.make_async_copy(cut.at[z, y], cut_out.at[z, y, x, k], keep.at[0]),
            pltpu.make_async_copy(wo_ref, wo_out.at[x, k], keep.at[1]),
        ]
        for copy in keeps:
            copy.start()
        for copy in over_ctx:
            copy.wait_recv()
        keeps[0].wait()
        mine = cut_out.at[:, :, x, k]
        over_exp = [
            send(mine, mine, exp_sems, i - 1, {"x": p, "k": q}) for (p, q), i in exp_peers
        ]
        for c in range(chunks):
            gather.forward(c)
        for j in range(number):
            for i in (1, 2, 3):
                over_near[i, j].wait_recv()
                over_far.append(
                    send(
                        near_out.at[i - 1, j],
                        far_out.at[i, j],
                        far_sems,
                        i * number + j,
                        {"y": 1 - y},
                    )
                )
        for copy in over_exp + over_wo + over_far:
            copy.wait_recv()
        keeps[1].wait()
        gather.finish()
        for copy in over_ctx + over_exp + over_wo + list(over_near.values()) + over_far:
            copy.wait_send()

    bf16 = jnp.bfloat16
    return exchange(
        kernel,
        "share_inputs",
        1,
        (tokens, slices, wo, *units),
        [ANY_SPEC] * 7,
        [
            jax.ShapeDtypeStruct((4, 2, count, D), bf16),
            jax.ShapeDtypeStruct((4, 2, 2, 2, own, columns), bf16),
            jax.ShapeDtypeStruct((2, 2, own, D), bf16),
            jax.ShapeDtypeStruct((3,) + units[0].shape, bf16),
            jax.ShapeDtypeStruct((4,) + units[0].shape, bf16),
        ],
        [ANY_SPEC] * 5,
        [
            Gather.scratch(("y",), chunks),
            [pltpu.SemaphoreType.DMA((2,))]
            + dma_pair(7)
            + dma_pair(3)
            + dma_pair(3)
            + dma_pair(3 * number)
            + dma_pair(4 * number),
        ],
    )


def middle_step(part, tokens, marked, gain):
    count, chunks, wide = tokens.shape[0], 4, marked.shape[-1]
    bf16, f32 = jnp.bfloat16, jnp.float32

    def kernel(ins, outs, scatter_refs, hidden_refs, marked_refs, own):
        part_ref, tok, marked_ref, gain_ref = ins
        middle_ref, hidden_out, marked_out = outs
        greet(z_peers() + siblings(("y", "x", "k")))
        scatter = Scatter(part_ref, ("y",), chunks, scatter_refs)
        hidden = Gather(own[0], hidden_out, ("x", "k"), chunks, hidden_refs)
        other = Gather(marked_ref, marked_out, ("x", "k"), 1, marked_refs)
        scatter.start()
        other.start(0)

        def use(c, at, total):
            middle = tok[at, :].astype(f32) + total
            middle_ref[at, :] = middle
            scale = lax.rsqrt(jnp.mean(middle * middle, axis=-1, keepdims=True) + EPSILON)
            own[0][at, :] = (middle * scale * gain_ref[...]).astype(bf16)
            hidden.start(c)

        scatter.run(use)
        other.forward(0)
        for c in range(chunks):
            hidden.forward(c)
            if c == 0:
                other.spread(0)
            hidden.spread(c)
        other.finish()
        hidden.finish()
        scatter.finish()

    blocks = (4, 2, 2, count)
    return exchange(
        kernel,
        "middle_step",
        2,
        (part, tokens, marked, gain),
        [ANY_SPEC, VMEM_SPEC, ANY_SPEC, VMEM_SPEC],
        [
            jax.ShapeDtypeStruct((count, D), f32),
            jax.ShapeDtypeStruct(blocks + (D,), bf16),
            jax.ShapeDtypeStruct(blocks + (wide,), bf16),
        ],
        [VMEM_SPEC, ANY_SPEC, ANY_SPEC],
        [
            Scatter.scratch(part, ("y",), chunks),
            Gather.scratch(("x", "k"), chunks),
            Gather.scratch(("x", "k"), 1),
            [pltpu.VMEM((count, D), bf16)],
        ],
    )


def router_step(part, middle, cotangent, gates, router, gain):
    count, chunks = middle.shape[0], 4
    bf16, f32 = jnp.bfloat16, jnp.float32

    def kernel(ins, outs, scatter_refs, gather_refs, own):
        part_ref, middle_ref, up_ref, gates_ref, router_ref, gain_ref = ins
        logit_ref, gain_out, grad_ref, branch_out = outs
        greet(z_peers() + siblings(("y", "x", "k")))
        scatter = Scatter(part_ref, ("x", "k"), chunks, scatter_refs)
        gather = Gather(own[0], branch_out, ("y",), chunks, gather_refs)
        scatter.start()
        gain_out[...] = jnp.zeros_like(gain_out)

        def use(c, at, total):
            gate, gate_grad = gates_ref[at, :], total[:, D:]
            inner = jnp.sum(gate * gate_grad, axis=-1, keepdims=True)
            logit_grad = (gate * (gate_grad - inner)).astype(bf16)
            logit_ref[at, :] = logit_grad
            grad = total[:, :D] + contract_cols(logit_grad, router_ref[...])
            middle = middle_ref[at, :]
            scale = lax.rsqrt(jnp.mean(middle * middle, axis=-1, keepdims=True) + EPSILON)
            normed = middle * scale
            gain_out[...] += jnp.sum(grad * normed, axis=0, keepdims=True)
            scaled = grad * gain_ref[...]
            result = up_ref[at, :].astype(f32) + scale * (
                scaled - normed * jnp.mean(scaled * normed, axis=-1, keepdims=True)
            )
            grad_ref[at, :] = result
            own[0][at, :] = result.astype(bf16)
            gather.start(c)

        scatter.run(use)
        for c in range(chunks):
            gather.forward(c)
        gather.finish()
        scatter.finish()

    return exchange(
        kernel,
        "router_step",
        3,
        (part, middle, cotangent, gates, router, gain),
        [ANY_SPEC] + [VMEM_SPEC] * 5,
        [
            jax.ShapeDtypeStruct((count, 128), bf16),
            jax.ShapeDtypeStruct((1, D), f32),
            jax.ShapeDtypeStruct((count, D), f32),
            jax.ShapeDtypeStruct((4, 2, count, D), bf16),
        ],
        [VMEM_SPEC] * 3 + [ANY_SPEC],
        [
            Scatter.scratch(part, ("x", "k"), chunks),
            Gather.scratch(("y",), chunks),
            [pltpu.VMEM((count, D), bf16)],
        ],
    )


def last_step(part, mixed, tokens, middle, grad_middle, gain, qkv_part, wo_part, small_part):
    count, chunks = tokens.shape[0], 4
    own, columns = qkv_part.shape[-2:]
    bf16, f32 = jnp.bfloat16, jnp.float32

    def kernel(ins, outs, part_refs, mixed_refs, other):
        part_ref, mixed_ref, tok, middle_ref, grad_ref, gain_ref, qkv, wo, small = ins
        out_ref, tokens_ref, qkv_out, wo_out, small_out = outs
        qkv_came, qkv_sum, wo_came, small_came = other[:4]
        sems = [other[4 + 2 * i : 6 + 2 * i] for i in range(4)]
        names = ("z", "y", "x", "k")
        z, y, x, k = (lax.axis_index(a) for a in names)
        everyone = [
            ((z ^ (i // 8), y ^ (i // 4 % 2), x ^ (i // 2 % 2), k ^ (i % 2)), i)
            for i in range(31, 0, -1)
        ]
        of_ctx = [(p, i // 4) for p, i in everyone if i % 4 == 0]
        of_exp = [(p, i) for p, i in everyone if i < 4]
        place = lambda p: dict(zip(names, p))
        greet([place(p) for p, _ in everyone])
        first = Scatter(part_ref, ("y",), chunks, part_refs)
        second = Scatter(mixed_ref, ("x", "k"), chunks, mixed_refs)
        first.start()
        second.start()
        over_qkv = [
            send(qkv.at[p[2], p[3]], qkv_came.at[i - 1], sems[0], i - 1, place(p))
            for p, i in of_exp
        ]
        over_wo = [
            send(wo.at[p[2], p[3]], wo_came.at[i - 1], sems[1], i - 1, place(p))
            for p, i in of_exp
        ]

        def use_first(c, at, total):
            resid = tok[at, :].astype(f32)
            scale = lax.rsqrt(jnp.mean(resid * resid, axis=-1, keepdims=True) + EPSILON)
            normed = resid * scale
            scaled = total * gain_ref[...]
            tokens_ref[at, :] = grad_ref[at, :] + scale * (
                scaled - normed * jnp.mean(scaled * normed, axis=-1, keepdims=True)
            )

        def use_second(c, at, total):
            out_ref[at, :] = (middle_ref[at, :] + total).astype(bf16)

        first.run(use_first)
        total = qkv[x, k].astype(f32)
        for copy, (_, i) in zip(over_qkv, of_exp):
            copy.wait_recv()
            total = total + qkv_came[i - 1].astype(f32)
        qkv_sum[...] = total.astype(bf16)
        qkv_out[z, y] = qkv_sum[z, y]
        over_ctx = [
            send(qkv_sum.at[p[0], p[1]], qkv_out.at[z, y], sems[2], i - 1, place(p))
            for p, i in of_ctx
        ]
        over_small = [
            send(small.at[p], small_came.at[i - 1], sems[3], i - 1, place(p)) for p, i in everyone
        ]
        second.run(use_second)
        total = wo[x, k].astype(f32)
        for copy, (_, i) in zip(over_wo, of_exp):
            copy.wait_recv()
            total = total + wo_came[i - 1].astype(f32)
        wo_out[...] = total
        total = small[z, y, x, k].astype(f32)
        for copy, (_, i) in zip(over_small, everyone):
            copy.wait_recv()
            total = total + small_came[i - 1].astype(f32)
        small_out[...] = total
        for copy in over_ctx:
            copy.wait_recv()
        first.finish()
        second.finish()
        for copy in over_qkv + over_wo + over_ctx + over_small:
            copy.wait_send()

    return exchange(
        kernel,
        "last_step",
        4,
        (part, mixed, tokens, middle, grad_middle, gain, qkv_part, wo_part, small_part),
        [ANY_SPEC] * 2 + [VMEM_SPEC] * 7,
        [
            jax.ShapeDtypeStruct((count, D), bf16),
            jax.ShapeDtypeStruct((count, D), f32),
            jax.ShapeDtypeStruct((4, 2, own, columns), bf16),
            jax.ShapeDtypeStruct((own, D), f32),
            jax.ShapeDtypeStruct((own, 128), f32),
        ],
        [VMEM_SPEC] * 5,
        [
            Scatter.scratch(part, ("y",), chunks),
            Scatter.scratch(mixed, ("x", "k"), chunks),
            [
                pltpu.VMEM((3, 4, 2, own, columns), bf16),
                pltpu.VMEM((4, 2, own, columns), bf16),
                pltpu.VMEM((3, own, D), bf16),
                pltpu.VMEM((31, own, 128), bf16),
            ]
            + dma_pair(3)
            + dma_pair(3)
            + dma_pair(7)
            + dma_pair(31),
        ],
    )


def body_heads(
    tokens,
    cotangent,
    lengths,
    span_perm,
    routes,
    norm_attn,
    attn_q,
    attn_k,
    attn_v,
    attn_o,
    router,
    norm_moe,
    expert_in,
    expert_out,
):
    bf16, f32 = jnp.bfloat16, jnp.float32
    n_z, n_y = (lax.axis_size(a) for a in ("z", "y"))
    n_exp = lax.axis_size("x") * lax.axis_size("k")
    n_ctx = n_z * n_y
    exp_index = lax.axis_index("x") * lax.axis_size("k") + lax.axis_index("k")
    count = tokens.shape[1]
    group = count * n_ctx
    repeat = HEADS // KV_HEADS
    width = repeat * HEAD
    experts = EXP_DEV * n_exp
    capacity = count * TOP * 3 // (2 * experts)
    slots = -(-capacity // 8) * 8
    own = attn_q.shape[0]
    softmax_scale = HEAD ** (-0.5)
    z_index = lax.axis_index("z")

    units = 2 * EXP_DEV // n_z
    y_index = lax.axis_index("y")
    win = expert_in.transpose(1, 0, 2)
    wout = expert_out.transpose(1, 0, 2)
    swap_z = [[(i, i ^ s) for i in range(n_z)] for s in range(n_z)]
    swap_y = [(i, i ^ 1) for i in range(n_y)]
    near = [take_units(units * (z_index ^ s), units, win, wout) for s in range(4)]

    wq, wk, wv = (a.astype(bf16) for a in (attn_q, attn_k, attn_v))
    own_qkv = jnp.concatenate(
        [
            wq.reshape(own, n_ctx, width),
            wk.reshape(own, n_ctx, HEAD),
            wv.reshape(own, n_ctx, HEAD),
        ],
        axis=-1,
    )
    small = jnp.concatenate(
        [
            router.astype(bf16),
            norm_attn.astype(bf16)[:, None],
            norm_moe.astype(bf16)[:, None],
            jnp.zeros((own, 64 - experts - 2), bf16),
        ],
        axis=1,
    )
    slices = jnp.concatenate(
        [own_qkv.transpose(1, 0, 2), jnp.broadcast_to(small, (n_ctx, own, 64))], axis=-1
    )
    token_all, slices, wo, near_parts, far_parts = share_inputs(
        tokens[0], slices.reshape(n_z, n_y, own, -1), attn_o.astype(bf16), near
    )
    token_all = token_all.reshape(group, D)
    slices = slices.reshape(D, -1)
    wo = wo.reshape(width, D)
    wqkv, small = slices[:, : width + 2 * HEAD], slices[:, width + 2 * HEAD :]
    weight_r = jnp.concatenate([small[:, :experts], jnp.zeros((D, 128 - experts), bf16)], axis=1)
    gain_one_f = small[:, experts].astype(f32)[None, :]
    gain_two_f = small[:, experts + 1].astype(f32)[None, :]
    marked = jnp.concatenate(
        [cotangent[0], routes[0].astype(bf16), jnp.zeros((count, 128 - TOP), bf16)], axis=1
    )

    perm_row = span_perm[0]
    first_len = lengths[0, 0]
    rows = global_rows(perm_row, jnp.arange(group, dtype=jnp.int32))
    position = rows - jnp.where(rows >= first_len, first_len, 0)
    freqs = jnp.exp(jnp.arange(HEAD // 2, dtype=f32) * (-2.0 * math.log(10000.0) / HEAD))
    angle = position.astype(f32)[:, None] * freqs[None, :]
    cosine, sine = (jnp.cos(angle), jnp.sin(angle))
    resid_all = token_all.astype(f32)
    normed_all = resid_all * lax.rsqrt(
        jnp.mean(resid_all * resid_all, axis=-1, keepdims=True) + EPSILON
    )
    hidden_all = (normed_all * gain_one_f).astype(bf16)
    qkv = jnp.dot(hidden_all, wqkv, preferred_element_type=f32)
    queries = rotate(
        qkv[:, :width].reshape(group, repeat, HEAD), cosine[:, None], sine[:, None]
    ).astype(bf16)
    keys = rotate(qkv[:, width : width + HEAD], cosine, sine).astype(bf16)
    values = qkv[:, width + HEAD :].astype(bf16)
    mask = allowed(rows, rows, first_len)[None]
    scores = (
        jnp.einsum("qrd,kd->rqk", queries, keys, preferred_element_type=f32) * softmax_scale
    )
    scores = jnp.where(mask, scores, NEGATIVE)
    highest = jnp.max(scores, axis=-1)
    weights = jnp.exp(scores - highest[..., None])
    total = jnp.sum(weights, axis=-1)
    attended = (
        jnp.einsum("rqk,kd->rqd", weights.astype(bf16), values, preferred_element_type=f32)
        / total[..., None]
    )
    log_total = highest + jnp.log(total)
    attended_b = attended.transpose(1, 0, 2).reshape(group, width).astype(bf16)
    branch = jnp.dot(attended_b, wo, preferred_element_type=f32).astype(bf16)
    middle, hidden_blocks, marked_blocks = middle_step(
        branch.reshape(n_z, n_y, count, D), tokens[0], marked, gain_two_f
    )
    hidden_blocks = hidden_blocks.reshape(-1, count, D)
    marked_blocks = marked_blocks.reshape(-1, count, D + 128)

    blocks = hidden_blocks.shape[0]
    held = 3
    base = exp_index * EXP_DEV + (units * z_index) // 2
    shift = (units * z_index) % 2
    pairs = blocks // 2
    row_in, row_up, slot_gate, spread, gates_blocks = dispatch(
        base, hidden_blocks, marked_blocks, weight_r, held, slots
    )
    gates = lax.dynamic_index_in_dim(gates_blocks, z_index * n_exp + exp_index, 0, keepdims=False)

    def to_tokens(rows):
        a = jnp.einsum(
            "prt,prd->ptd",
            spread,
            rows.reshape(pairs, held * 2 * slots, -1),
            preferred_element_type=f32,
        )
        return a.astype(bf16).reshape(blocks, count, -1)

    meta = jnp.stack([shift, z_index, y_index, base]).astype(jnp.int32)
    made, back, *grads = run_experts(
        meta, row_in, row_up, slot_gate, near[0], near_parts, far_parts
    )
    logit_grad, grad_gain_two, grad_middle, branch_all = router_step(
        to_tokens(back).reshape(n_z, 2, 2, count, D + 128),
        middle,
        cotangent[0],
        gates,
        weight_r,
        gain_two_f,
    )
    branch_all = branch_all.reshape(group, D)

    swap_z = [[(i, i ^ s) for i in range(n_z)] for s in range(n_z)]
    swap_y = [(i, i ^ 1) for i in range(n_y)]
    sums = [None] * 4
    for s in (3, 2, 1, 0):
        other = lax.ppermute(grads[4 + s], "y", swap_y)
        sums[s] = (grads[s].astype(f32) + other.astype(f32)).astype(bf16)
    sums, branch_all = lax.optimization_barrier((sums, branch_all))
    for s in (3, 2, 1):
        sums[s] = lax.ppermute(sums[s], "z", swap_z[s])
    grad_expert_in, grad_expert_out = place_units(z_index, jnp.concatenate(sums), units)
    grad_expert_in = grad_expert_in.transpose(1, 0, 2)
    grad_expert_out = grad_expert_out.transpose(1, 0, 2)

    hidden_two = lax.dynamic_index_in_dim(
        hidden_blocks, z_index * n_exp + exp_index, 0, keepdims=False
    )
    small_grads = jnp.concatenate(
        [
            contract_rows(hidden_two, logit_grad)[:, : 128 - 1],
            grad_gain_two.reshape(D, 1),
        ],
        axis=1,
    )
    small_grads = small_grads.astype(bf16).reshape(n_z, n_y, 2, 2, own, 128)

    grad_wo = contract_rows(attended_b, branch_all).astype(bf16)
    grad_heads = contract_cols(branch_all, wo).astype(bf16).reshape(group, repeat, HEAD)
    grad_heads = grad_heads.transpose(1, 0, 2)
    drift = jnp.sum(grad_heads.astype(f32) * attended, axis=-1)
    scores = (
        jnp.einsum("qrd,kd->rqk", queries, keys, preferred_element_type=f32) * softmax_scale
    )
    weights = jnp.where(mask, jnp.exp(scores - log_total[..., None]), 0.0)
    prob_grad = jnp.einsum("rqd,kd->rqk", grad_heads, values, preferred_element_type=f32)
    score_grad = (weights * (prob_grad - drift[..., None])).astype(bf16)
    query_grad = (
        jnp.einsum("rqk,kd->qrd", score_grad, keys, preferred_element_type=f32) * softmax_scale
    )
    value_grad = jnp.einsum(
        "rqk,rqd->kd", weights.astype(bf16), grad_heads, preferred_element_type=f32
    )
    key_grad = (
        jnp.einsum("rqk,qrd->kd", score_grad, queries, preferred_element_type=f32) * softmax_scale
    )
    grad_qkv = jnp.concatenate(
        [
            rotate(query_grad, cosine[:, None], -sine[:, None]).reshape(group, width),
            rotate(key_grad, cosine, -sine),
            value_grad,
        ],
        axis=-1,
    ).astype(bf16)
    grad_hidden = contract_cols(grad_qkv, wqkv).astype(bf16).reshape(n_z, n_y, count, D)
    grad_wqkv = contract_rows(hidden_all, grad_qkv).astype(bf16)
    grad_wqkv = grad_wqkv.reshape(n_ctx, n_exp, own, width + 2 * HEAD).transpose(1, 0, 2, 3)
    output, grad_tokens, grad_wqkv, grad_wo, small_grads = last_step(
        grad_hidden,
        to_tokens(made).reshape(n_z, 2, 2, count, D),
        tokens[0],
        middle,
        grad_middle,
        gain_one_f,
        grad_wqkv.reshape(2, 2, n_z, n_y, own, width + 2 * HEAD),
        grad_wo.reshape(2, 2, own, D),
        small_grads,
    )
    grad_wqkv = grad_wqkv.reshape(n_ctx, own, width + 2 * HEAD).astype(f32)
    grad_q = grad_wqkv[:, :, :width].transpose(1, 0, 2).reshape(own, HEADS * HEAD)
    grad_k = grad_wqkv[:, :, width : width + HEAD].transpose(1, 0, 2).reshape(own, KV_HEADS * HEAD)
    grad_v = grad_wqkv[:, :, width + HEAD :].transpose(1, 0, 2).reshape(own, KV_HEADS * HEAD)
    grad_gain_one = jnp.sum(
        grad_wqkv.transpose(1, 0, 2) * own_qkv.astype(f32), axis=(1, 2)
    ) / norm_attn.astype(bf16).astype(f32)
    return (
        output[None],
        grad_tokens[None],
        grad_gain_one,
        grad_q,
        grad_k,
        grad_v,
        grad_wo,
        small_grads[:, :experts],
        small_grads[:, 127],
        grad_expert_in,
        grad_expert_out,
    )


def solution(mesh):
    ctx, exp = mesh.shape["ctx"], mesh.shape["exp"]
    if ctx == KV_HEADS and exp == 4:
        names = ("z", "y", "x", "k")
        inner = jax.sharding.Mesh(mesh.devices.reshape(4, 2, 2, 2), names)
        body, ctx_name, exp_name, both = body_heads, names[:2], names[2:], names
    else:
        inner, body, ctx_name, exp_name, both = mesh, body_general, "ctx", "exp", ("ctx", "exp")
    token = P(exp_name, ctx_name, None)
    group = P(exp_name, None)
    expert = P(ctx_name, exp_name, None)
    rows, gain = P(both, None), P(both)
    in_specs = (token, token, group, group, token, gain) + (rows,) * 5 + (gain, expert, expert)
    out_specs = (token, token, gain) + (rows,) * 5 + (gain, expert, expert)
    return jax.shard_map(
        body, mesh=inner, in_specs=in_specs, out_specs=out_specs, check_vma=False
    )
```

```python
import math

import jax
import jax.numpy as jnp
from jax import lax
from jax.experimental import pallas as pl
from jax.experimental.pallas import tpu as pltpu
from jax.sharding import PartitionSpec as P

D = 1536
HEADS = 24
KV_HEADS = 8
HEAD = 64
HID = 512
TOP = 8
EXP_DEV = 10
SPAN = 64


EPSILON = 1e-06
NEGATIVE = -1e30


def global_rows(perm_row, rows):
    slots = rows // SPAN
    match = slots[:, None] == jnp.arange(perm_row.shape[0], dtype=jnp.int32)[None, :]
    spans = jnp.sum(jnp.where(match, perm_row[None, :], 0), axis=1)
    return spans * SPAN + rows % SPAN


def rotary(tensor, position, sign):
    half = HEAD // 2
    freqs = jnp.exp(jnp.arange(half, dtype=jnp.float32) * (-2.0 * math.log(10000.0) / HEAD))
    angle = position.astype(jnp.float32)[:, None] * freqs[None, :]
    cosine = jnp.cos(angle)[:, None, :]
    sine = sign * jnp.sin(angle)[:, None, :]
    first, second = (tensor[..., :half], tensor[..., half:])
    return jnp.concatenate(
        [first * cosine - second * sine, second * cosine + first * sine], axis=-1
    )


def allowed(query_rows, key_rows, first_len):
    later = key_rows[None, :] <= query_rows[:, None]
    same_seq = (key_rows[None, :] >= first_len) == (query_rows[:, None] >= first_len)
    return later & same_seq


def contract_rows(left, right):
    return lax.dot_general(
        left, right, (((0,), (0,)), ((), ())), preferred_element_type=jnp.float32
    )


def contract_cols(left, right):
    return lax.dot_general(
        left, right, (((1,), (1,)), ((), ())), preferred_element_type=jnp.float32
    )


def block_grads(
    query_block,
    grad_block,
    lse_block,
    drift_block,
    query_rows,
    key_block,
    value_block,
    key_rows,
    first_len,
):
    softmax_scale = HEAD ** (-0.5)
    scores = (
        jnp.einsum("qgrd,kgd->grqk", query_block, key_block, preferred_element_type=jnp.float32)
        * softmax_scale
    )
    mask = allowed(query_rows, key_rows, first_len)[None, None]
    weights = jnp.where(mask, jnp.exp(scores - lse_block.transpose(1, 2, 0)[..., None]), 0.0)
    prob_grad = jnp.einsum(
        "qgrd,kgd->grqk", grad_block, value_block, preferred_element_type=jnp.float32
    )
    score_grad = (weights * (prob_grad - drift_block.transpose(1, 2, 0)[..., None])).astype(
        jnp.bfloat16
    )
    query_grad = None
    key_grad = None
    value_grad = None
    query_grad = (
        jnp.einsum("grqk,kgd->qgrd", score_grad, key_block, preferred_element_type=jnp.float32)
        * softmax_scale
    )
    value_grad = jnp.einsum(
        "grqk,qgrd->kgd",
        weights.astype(jnp.bfloat16),
        grad_block,
        preferred_element_type=jnp.float32,
    )
    key_grad = (
        jnp.einsum("grqk,qgrd->kgd", score_grad, query_block, preferred_element_type=jnp.float32)
        * softmax_scale
    )
    return (query_grad, key_grad, value_grad)


def body_general(
    tokens,
    cotangent,
    lengths,
    span_perm,
    routes,
    norm_attn,
    attn_q,
    attn_k,
    attn_v,
    attn_o,
    router,
    norm_moe,
    expert_in,
    expert_out,
):
    count = tokens.shape[1]
    repeat = HEADS // KV_HEADS
    experts = EXP_DEV * lax.axis_size("exp")
    capacity = count * TOP * 3 // (2 * experts)
    softmax_scale = HEAD ** (-0.5)
    perm_row = span_perm[0]
    first_len = lengths[0, 0]
    query_rows = global_rows(
        perm_row, lax.axis_index("ctx") * count + jnp.arange(count, dtype=jnp.int32)
    )
    position = query_rows - jnp.where(query_rows >= first_len, first_len, 0)
    gathered = (
        lax.all_gather(norm_attn.astype(jnp.bfloat16), ("ctx", "exp"), axis=0, tiled=True),
        lax.all_gather(attn_q.astype(jnp.bfloat16), ("ctx", "exp"), axis=0, tiled=True),
        lax.all_gather(attn_k.astype(jnp.bfloat16), ("ctx", "exp"), axis=0, tiled=True),
        lax.all_gather(attn_v.astype(jnp.bfloat16), ("ctx", "exp"), axis=0, tiled=True),
        lax.all_gather(attn_o.astype(jnp.bfloat16), ("ctx", "exp"), axis=0, tiled=True),
        lax.all_gather(router.astype(jnp.bfloat16), ("ctx", "exp"), axis=0, tiled=True),
        lax.all_gather(norm_moe.astype(jnp.bfloat16), ("ctx", "exp"), axis=0, tiled=True),
    )
    gain_one, weight_q, weight_k, weight_v, weight_o, weight_r, gain_two = gathered
    weight_in, weight_out = (
        lax.all_gather(expert_in.astype(jnp.bfloat16), "ctx", axis=0, tiled=True),
        lax.all_gather(expert_out.astype(jnp.bfloat16), "ctx", axis=0, tiled=True),
    )
    gain_one_f = gain_one.astype(jnp.float32)
    gain_two_f = gain_two.astype(jnp.float32)
    resid = tokens[0].astype(jnp.float32)
    scale_one = lax.rsqrt(jnp.mean(resid * resid, axis=-1, keepdims=True) + EPSILON)
    normed_one = resid * scale_one
    hidden_one = (normed_one * gain_one_f).astype(jnp.bfloat16)
    query_pre = jnp.dot(hidden_one, weight_q, preferred_element_type=jnp.float32).reshape(
        count, HEADS, HEAD
    )
    queries = (
        rotary(query_pre, position, 1.0).astype(jnp.bfloat16).reshape(count, KV_HEADS, repeat, HEAD)
    )
    key_pre = jnp.dot(hidden_one, weight_k, preferred_element_type=jnp.float32).reshape(
        count, KV_HEADS, HEAD
    )
    keys = rotary(key_pre, position, 1.0).astype(jnp.bfloat16)
    values = (
        jnp.dot(hidden_one, weight_v, preferred_element_type=jnp.float32)
        .astype(jnp.bfloat16)
        .reshape(count, KV_HEADS, HEAD)
    )
    start_state = (
        jnp.full((KV_HEADS, repeat, count), NEGATIVE, jnp.float32),
        jnp.zeros((KV_HEADS, repeat, count), jnp.float32),
        jnp.zeros((KV_HEADS, repeat, count, HEAD), jnp.float32),
    )
    carry = start_state
    key_piece = lax.all_gather(keys, "ctx", axis=0, tiled=True)
    value_piece = lax.all_gather(values, "ctx", axis=0, tiled=True)
    size = key_piece.shape[0]
    block = math.gcd(size, 512)
    number = size // block
    key_blocks = key_piece.reshape(number, block, KV_HEADS, HEAD)
    value_blocks = value_piece.reshape(number, block, KV_HEADS, HEAD)
    offsets = jnp.arange(size, dtype=jnp.int32).reshape(number, block)

    def forward_step(state, inputs):
        highest, total, accum = state
        key_block, value_block, offset = inputs
        key_rows = global_rows(perm_row, offset)
        scores = (
            jnp.einsum("qgrd,kgd->grqk", queries, key_block, preferred_element_type=jnp.float32)
            * softmax_scale
        )
        mask = allowed(query_rows, key_rows, first_len)[None, None]
        scores = jnp.where(mask, scores, NEGATIVE)
        newmax = jnp.maximum(highest, jnp.max(scores, axis=-1))
        weights = jnp.where(mask, jnp.exp(scores - newmax[..., None]), 0.0)
        factor = jnp.exp(highest - newmax)
        total = total * factor + jnp.sum(weights, axis=-1)
        accum = accum * factor[..., None] + jnp.einsum(
            "grqk,kgd->grqd",
            weights.astype(jnp.bfloat16),
            value_block,
            preferred_element_type=jnp.float32,
        )
        return ((newmax, total, accum), None)

    carry, _ = lax.scan(forward_step, carry, (key_blocks, value_blocks, offsets))
    highest, total, accum = carry
    log_total = (highest + jnp.log(total)).transpose(2, 0, 1)
    attended = (accum / total[..., None]).transpose(2, 0, 1, 3)
    attended_b = attended.reshape(count, HEADS * HEAD).astype(jnp.bfloat16)
    middle = resid + jnp.dot(attended_b, weight_o, preferred_element_type=jnp.float32)
    scale_two = lax.rsqrt(jnp.mean(middle * middle, axis=-1, keepdims=True) + EPSILON)
    normed_two = middle * scale_two
    hidden_two = (normed_two * gain_two_f).astype(jnp.bfloat16)
    logits = jnp.dot(hidden_two, weight_r, preferred_element_type=jnp.float32)
    chosen = routes[0]
    picks = chosen[:, :, None] == jnp.arange(experts, dtype=jnp.int32)[None, None, :]
    selected = jnp.sum(jnp.where(picks, logits[:, None, :], 0.0), axis=-1)
    gates = jax.nn.softmax(selected, axis=-1)
    gates_b = gates.astype(jnp.bfloat16)
    flat_picks = picks.reshape(count * TOP, experts).astype(jnp.int32)
    placed = jnp.sum((jnp.cumsum(flat_picks, axis=0) - 1) * flat_picks, axis=-1)
    column = chosen.reshape(-1) * capacity + placed
    hits = (
        column.reshape(count, TOP)[:, :, None]
        == jnp.arange(experts * capacity, dtype=jnp.int32)[None, None, :]
    )
    spread = jnp.any(hits, axis=1).astype(jnp.bfloat16)
    weighted = jnp.sum(
        jnp.where(hits, gates_b.astype(jnp.float32)[:, :, None], 0.0), axis=1
    ).astype(jnp.bfloat16)
    outgoing = contract_rows(spread, hidden_two).astype(jnp.bfloat16).reshape(experts, capacity, D)
    incoming = lax.all_to_all(outgoing, "exp", split_axis=0, concat_axis=1, tiled=True)
    gate_up = jnp.einsum("erd,dec->erc", incoming, weight_in, preferred_element_type=jnp.float32)
    gate_part = gate_up[..., :HID]
    up_part = gate_up[..., HID:]
    sigmoid_gate = jax.nn.sigmoid(gate_part)
    silu_gate = gate_part * sigmoid_gate
    activated = (silu_gate * up_part).astype(jnp.bfloat16)
    produced = jnp.einsum(
        "erh,deh->erd", activated, weight_out, preferred_element_type=jnp.float32
    ).astype(jnp.bfloat16)
    returned = lax.all_to_all(produced, "exp", split_axis=1, concat_axis=0, tiled=True).reshape(
        experts * capacity, D
    )
    mixture = jnp.dot(weighted, returned, preferred_element_type=jnp.float32)
    output = (middle + mixture).astype(jnp.bfloat16)
    upstream = cotangent[0].astype(jnp.float32)
    upstream_b = upstream.astype(jnp.bfloat16)
    sent_grad = (
        contract_rows(weighted, upstream_b).astype(jnp.bfloat16).reshape(experts, capacity, D)
    )
    grad_in = lax.all_to_all(sent_grad, "exp", split_axis=0, concat_axis=1, tiled=True)
    picked = jnp.take(returned, column, axis=0).reshape(count, TOP, D)
    gate_grad = jnp.einsum("tkd,td->tk", picked, upstream_b, preferred_element_type=jnp.float32)
    grad_act = (
        jnp.einsum("erd,deh->erh", grad_in, weight_out, preferred_element_type=jnp.float32)
        .astype(jnp.bfloat16)
        .astype(jnp.float32)
    )
    grad_gate = grad_act * up_part * (sigmoid_gate * (1.0 + gate_part * (1.0 - sigmoid_gate)))
    grad_up = grad_act * silu_gate
    grad_gu = jnp.concatenate([grad_gate, grad_up], axis=-1).astype(jnp.bfloat16)
    grad_weight_out = jnp.einsum(
        "erd,erh->deh", grad_in, activated, preferred_element_type=jnp.float32
    )
    grad_weight_in = jnp.einsum(
        "erd,erc->dec", incoming, grad_gu, preferred_element_type=jnp.float32
    )
    grad_rows = jnp.einsum(
        "erc,dec->erd", grad_gu, weight_in, preferred_element_type=jnp.float32
    ).astype(jnp.bfloat16)
    back_rows = lax.all_to_all(grad_rows, "exp", split_axis=1, concat_axis=0, tiled=True).reshape(
        experts * capacity, D
    )
    expert_sums = (
        lax.psum_scatter(
            grad_weight_in.astype(jnp.bfloat16), "ctx", scatter_dimension=0, tiled=True
        ).astype(jnp.float32),
        lax.psum_scatter(
            grad_weight_out.astype(jnp.bfloat16), "ctx", scatter_dimension=0, tiled=True
        ).astype(jnp.float32),
    )
    centered = gate_grad - jnp.sum(gates * gate_grad, axis=-1, keepdims=True)
    select_grad = gates * centered
    logit_grad = jnp.sum(jnp.where(picks, select_grad[:, :, None], 0.0), axis=1).astype(
        jnp.bfloat16
    )
    grad_router = contract_rows(hidden_two, logit_grad)
    grad_norm_two = jnp.dot(spread, back_rows, preferred_element_type=jnp.float32) + contract_cols(
        logit_grad, weight_r
    )
    grad_gain_two = jnp.sum(grad_norm_two * normed_two, axis=0)
    scaled_two = grad_norm_two * gain_two_f
    grad_middle = upstream + scale_two * (
        scaled_two - normed_two * jnp.mean(scaled_two * normed_two, axis=-1, keepdims=True)
    )
    branch_grad = grad_middle.astype(jnp.bfloat16)
    grad_weight_o = contract_rows(attended_b, branch_grad)
    grad_heads = (
        contract_cols(branch_grad, weight_o)
        .astype(jnp.bfloat16)
        .reshape(count, KV_HEADS, repeat, HEAD)
    )
    drift = jnp.sum(grad_heads.astype(jnp.float32) * attended, axis=-1)
    query_acc = jnp.zeros((count, KV_HEADS, repeat, HEAD), jnp.float32)
    key_piece = lax.all_gather(keys, "ctx", axis=0, tiled=True)
    value_piece = lax.all_gather(values, "ctx", axis=0, tiled=True)
    size = key_piece.shape[0]
    block = math.gcd(size, 512)
    number = size // block
    key_blocks = key_piece.reshape(number, block, KV_HEADS, HEAD)
    value_blocks = value_piece.reshape(number, block, KV_HEADS, HEAD)
    offsets = jnp.arange(size, dtype=jnp.int32).reshape(number, block)

    def backward_step(acc, inputs):
        key_block, value_block, offset = inputs
        part_q, part_k, part_v = block_grads(
            queries,
            grad_heads,
            log_total,
            drift,
            query_rows,
            key_block,
            value_block,
            global_rows(perm_row, offset),
            first_len,
        )
        joined = jnp.concatenate(
            [part_k.reshape(block, KV_HEADS * HEAD), part_v.reshape(block, KV_HEADS * HEAD)],
            axis=-1,
        )
        return (acc + part_q, joined)

    query_acc, joined_parts = lax.scan(
        backward_step, query_acc, (key_blocks, value_blocks, offsets)
    )
    pair_acc = joined_parts.reshape(size, 2 * KV_HEADS * HEAD)
    query_grad, pair_acc = (query_acc, pair_acc)
    pair_own = lax.psum_scatter(
        pair_acc.astype(jnp.bfloat16), "ctx", scatter_dimension=0, tiled=True
    ).astype(jnp.float32)
    key_grad = pair_own[:, : KV_HEADS * HEAD].reshape(count, KV_HEADS, HEAD)
    value_grad = pair_own[:, KV_HEADS * HEAD :].reshape(count, KV_HEADS, HEAD)
    query_grad_b = (
        rotary(query_grad.reshape(count, HEADS, HEAD), position, -1.0)
        .astype(jnp.bfloat16)
        .reshape(count, HEADS * HEAD)
    )
    key_grad_b = (
        rotary(key_grad, position, -1.0).astype(jnp.bfloat16).reshape(count, KV_HEADS * HEAD)
    )
    value_grad_b = value_grad.astype(jnp.bfloat16).reshape(count, KV_HEADS * HEAD)
    grad_weight_q = contract_rows(hidden_one, query_grad_b)
    grad_weight_k = contract_rows(hidden_one, key_grad_b)
    grad_weight_v = contract_rows(hidden_one, value_grad_b)
    grad_hidden_one = (
        contract_cols(query_grad_b, weight_q)
        + contract_cols(key_grad_b, weight_k)
        + contract_cols(value_grad_b, weight_v)
    )
    grad_gain_one = jnp.sum(grad_hidden_one * normed_one, axis=0)
    scaled_one = grad_hidden_one * gain_one_f
    grad_tokens = grad_middle + scale_one * (
        scaled_one - normed_one * jnp.mean(scaled_one * normed_one, axis=-1, keepdims=True)
    )
    attn_sums = (
        lax.psum_scatter(grad_gain_one, ("ctx", "exp"), scatter_dimension=0, tiled=True),
        lax.psum_scatter(grad_weight_q, ("ctx", "exp"), scatter_dimension=0, tiled=True),
        lax.psum_scatter(grad_weight_k, ("ctx", "exp"), scatter_dimension=0, tiled=True),
        lax.psum_scatter(grad_weight_v, ("ctx", "exp"), scatter_dimension=0, tiled=True),
        lax.psum_scatter(grad_weight_o, ("ctx", "exp"), scatter_dimension=0, tiled=True),
        lax.psum_scatter(grad_router, ("ctx", "exp"), scatter_dimension=0, tiled=True),
        lax.psum_scatter(grad_gain_two, ("ctx", "exp"), scatter_dimension=0, tiled=True),
    )
    return (
        output[None],
        grad_tokens[None],
        attn_sums[0],
        attn_sums[1],
        attn_sums[2],
        attn_sums[3],
        attn_sums[4],
        attn_sums[5],
        attn_sums[6],
        expert_sums[0],
        expert_sums[1],
    )


def rotate(tensor, cosine, sine):
    half = HEAD // 2
    first, second = (tensor[..., :half], tensor[..., half:])
    return jnp.concatenate(
        [first * cosine - second * sine, second * cosine + first * sine], axis=-1
    )


def dispatch_kernel(base, hid_ref, mark_ref, router_ref, rows_ref, up_ref, gate_ref, spread_ref, gates_ref):
    bf16, f32 = jnp.bfloat16, jnp.float32
    count = hid_ref.shape[1]
    _, held, rows, _ = rows_ref.shape
    slots = rows // 2
    both = 2 * count
    x = hid_ref[...].reshape(both, D)
    logits = jnp.dot(x, router_ref[...], preferred_element_type=f32)
    routes = mark_ref[:, :, D:].reshape(both, 128).astype(f32)
    lane = lax.broadcasted_iota(jnp.int32, (both, 128), 1).astype(f32)
    picks = jnp.zeros((both, 128), f32)
    for i in range(TOP):
        picks = jnp.where(routes[:, i : i + 1] == lane, 1.0, picks)
    masked = jnp.where(picks > 0.0, logits, NEGATIVE)
    top = jnp.max(masked, axis=-1, keepdims=True)
    gates = jnp.where(picks > 0.0, jnp.exp(masked - top), 0.0)
    gates = gates / jnp.sum(gates, axis=-1, keepdims=True)
    gates_ref[...] = gates.reshape(2, count, 128)
    which = lax.broadcasted_iota(jnp.int32, (8, 128), 0)
    columns = lax.broadcasted_iota(jnp.int32, (8, 128), 1)
    chosen = jnp.where(columns == which + base[0], 1.0, 0.0).astype(bf16)
    hit = contract_cols(chosen, picks.astype(bf16))
    gate = contract_cols(chosen, gates.astype(bf16))
    earlier = lax.broadcasted_iota(jnp.int32, (both, both), 0)
    later = lax.broadcasted_iota(jnp.int32, (both, both), 1)
    upto = jnp.where((earlier <= later) & (earlier // count == later // count), 1.0, 0.0)
    rank = jnp.dot(hit.astype(bf16), upto.astype(bf16), preferred_element_type=f32)
    row = lax.broadcasted_iota(jnp.int32, (rows, both), 0)
    token = lax.broadcasted_iota(jnp.int32, (rows, both), 1)
    side = row // slots
    wanted = jnp.where(side == token // count, row - side * slots + 1, -1).astype(f32)
    for e in range(held):
        here = jnp.where((rank[e : e + 1] == wanted) & (hit[e : e + 1] > 0.0), 1.0, 0.0)
        gate_ref[0, e] = jnp.sum(here * gate[e : e + 1], axis=-1, keepdims=True)
        here = here.astype(bf16)
        spread_ref[0, e * rows : (e + 1) * rows, :] = here
        rows_ref[0, e] = jnp.dot(here, x, preferred_element_type=f32).astype(bf16)
        up_ref[0, e] = jnp.dot(
            here, mark_ref[:, :, :D].reshape(both, D), preferred_element_type=f32
        ).astype(bf16)


def dispatch(base, hidden, marked, router, held, slots):
    blocks, count, _ = hidden.shape
    pairs = blocks // 2
    bf16, f32 = jnp.bfloat16, jnp.float32
    pair = lambda *shape: pl.BlockSpec((1,) + shape, lambda p, b: (p,) + (0,) * len(shape))
    two = lambda width: pl.BlockSpec((2, count, width), lambda p, b: (p, 0, 0))
    return pl.pallas_call(
        dispatch_kernel,
        grid_spec=pltpu.PrefetchScalarGridSpec(
            num_scalar_prefetch=1,
            grid=(pairs,),
            in_specs=[two(D), two(D + 128), pl.BlockSpec((D, 128), lambda p, b: (0, 0))],
            out_specs=[
                pair(held, 2 * slots, D),
                pair(held, 2 * slots, D),
                pair(held, 2 * slots, 1),
                pair(held * 2 * slots, 2 * count),
                two(128),
            ],
        ),
        out_shape=[
            jax.ShapeDtypeStruct((pairs, held, 2 * slots, D), bf16),
            jax.ShapeDtypeStruct((pairs, held, 2 * slots, D), bf16),
            jax.ShapeDtypeStruct((pairs, held, 2 * slots, 1), f32),
            jax.ShapeDtypeStruct((pairs, held * 2 * slots, 2 * count), bf16),
            jax.ShapeDtypeStruct((blocks, count, 128), f32),
        ],
        compiler_params=pltpu.CompilerParams(vmem_limit_bytes=48 * 2**20),
        name="dispatch",
    )(base.reshape(1).astype(jnp.int32), hidden, marked, router)


def expert_kernel(depth, meta, x_ref, g_ref, gate_ref, *refs):
    parts, (y_ref, d_ref), outs = refs[:8], refs[8:10], refs[10:18]
    weight, du_ref, act_ref = refs[18:]
    bf16, f32 = jnp.bfloat16, jnp.float32
    j = pl.program_id(0)
    shift, z, y, base = meta[0], meta[1], meta[2], meta[3]
    half = HID // 2
    offsets = [
        pl.multiple_of(((z ^ (i % 4)) * 2 + (y ^ (i // 4))) * depth, 64) for i in range(8)
    ]
    for part, offset in zip(parts, offsets):
        weight[pl.ds(offset, depth), :] = part[0]
    expert = base + (j + shift) // 2
    first = jnp.logical_or(j == 0, lax.rem(j + shift, 2) == 0)
    keep = jnp.where(first, 0.0, 1.0)
    pairs, _, rows, _ = x_ref.shape
    step = 2

    def forward(i, carry):
        at = pl.ds(i * step, step)
        flat = pl.ds(pl.multiple_of(i * step * rows, 32), step * rows)
        x = x_ref[at, 0].reshape(step * rows, D)
        g = g_ref[at, 0].reshape(step * rows, D)
        gate = gate_ref[at, 0].reshape(step * rows, 1)
        u = jnp.dot(x, weight[:, : 2 * half], preferred_element_type=f32)
        raw = jnp.dot(g, weight[:, 2 * half :], preferred_element_type=f32)
        u1, u2 = u[:, :half], u[:, half:]
        sig = jax.nn.sigmoid(u1)
        silu = u1 * sig
        act = (silu * u2).astype(bf16).astype(f32)
        dgate = jnp.sum(raw * act, axis=-1, keepdims=True)
        dact = raw * gate
        du1 = dact * u2 * (sig * (1.0 + u1 * (1.0 - sig)))
        du = jnp.concatenate([du1, dact * silu], axis=-1).astype(bf16)
        act_gated = (act * gate).astype(bf16)
        du_ref[flat, :] = du
        act_ref[flat, :] = act_gated
        made = contract_cols(act_gated, weight[:, 2 * half :])
        back = contract_cols(du, weight[:, : 2 * half])
        lane = lax.broadcasted_iota(jnp.int32, (step * rows, 128), 1)
        tail = jnp.where(lane == expert, dgate, 0.0)

        @pl.when(first)
        def _():
            y_ref[at, 0] = made.astype(bf16).reshape(step, rows, D)
            d_ref[at, 0, :, :D] = back.astype(bf16).reshape(step, rows, D)
            d_ref[at, 0, :, D:] = tail.astype(bf16).reshape(step, rows, 128)

        @pl.when(jnp.logical_not(first))
        def _():
            old_y = y_ref[at, 0].reshape(step * rows, D).astype(f32)
            y_ref[at, 0] = (made + old_y).astype(bf16).reshape(step, rows, D)
            old_d = d_ref[at, 0].reshape(step * rows, D + 128).astype(f32)
            d_ref[at, 0, :, :D] = (back + old_d[:, :D]).astype(bf16).reshape(step, rows, D)
            d_ref[at, 0, :, D:] = (tail + old_d[:, D:]).astype(bf16).reshape(step, rows, 128)

        return carry

    lax.fori_loop(0, pairs // step, forward, 0)

    def gradient(i, carry):
        at = pl.ds(pl.multiple_of(i * 256, 256), 256)
        x = x_ref[:, 0, :, at].reshape(pairs * rows, 256)
        g = g_ref[:, 0, :, at].reshape(pairs * rows, 256)
        weight[at, : 2 * half] = contract_rows(x, du_ref[...]).astype(bf16)
        weight[at, 2 * half :] = contract_rows(g, act_ref[...]).astype(bf16)
        return carry

    lax.fori_loop(0, D // 256, gradient, 0)
    for out, offset in zip(outs, offsets):
        out[0] = weight[pl.ds(offset, depth), :]


def run_experts(meta, row_in, row_up, slot_gate, parts):
    pairs, held, rows, _ = row_in.shape
    units, depth, columns = parts[0].shape
    held_block = lambda width: pl.BlockSpec(
        (pairs, 1, rows, width), lambda j, m: (0, (j + m[0]) // 2, 0, 0)
    )
    unit_block = pl.BlockSpec((1, depth, columns), lambda j, m: (j, 0, 0))
    bf16 = jnp.bfloat16
    total = units * pairs * rows * D * columns * 6
    return pl.pallas_call(
        lambda *refs: expert_kernel(depth, *refs),
        grid_spec=pltpu.PrefetchScalarGridSpec(
            num_scalar_prefetch=1,
            grid=(units,),
            in_specs=[
                held_block(D),
                held_block(D),
                held_block(1),
            ]
            + [unit_block] * 8,
            out_specs=[held_block(D), held_block(D + 128)] + [unit_block] * 8,
            scratch_shapes=[
                pltpu.VMEM((D, columns), bf16),
                pltpu.VMEM((pairs * rows, HID), bf16),
                pltpu.VMEM((pairs * rows, HID // 2), bf16),
            ],
        ),
        out_shape=[
            jax.ShapeDtypeStruct((pairs, held, rows, D), bf16),
            jax.ShapeDtypeStruct((pairs, held, rows, D + 128), bf16),
        ]
        + [jax.ShapeDtypeStruct((units, depth, columns), bf16)] * 8,
        compiler_params=pltpu.CompilerParams(vmem_limit_bytes=56 * 2**20),
        cost_estimate=pl.CostEstimate(
            flops=total, bytes_accessed=60 * 2**20, transcendentals=units * pairs * rows * HID
        ),
        name="experts",
    )(meta, row_in, row_up, slot_gate, *parts)


def spread_kernel(z_ref, low_ref, high_ref, in_ref, out_ref):
    half = low_ref.shape[-1] // 3
    for h, ref in enumerate((low_ref, high_ref)):
        for p in range(2):
            at = p * 2 * half + h * half
            in_ref[0, :, at : at + half] = ref[0, :, p * half : (p + 1) * half].astype(in_ref.dtype)
        out_ref[0, :, h * half : (h + 1) * half] = ref[0, :, 2 * half :].astype(out_ref.dtype)


def place_units(z_index, units, number):
    depth, columns = units.shape[1:]

    def pick(h):
        def index(i, z):
            unit = 2 * i + h
            return ((unit // number) ^ z[0]) * number + lax.rem(unit, number), 0, 0

        return pl.BlockSpec((1, depth, columns), index)

    return pl.pallas_call(
        spread_kernel,
        grid_spec=pltpu.PrefetchScalarGridSpec(
            num_scalar_prefetch=1,
            grid=(EXP_DEV,),
            in_specs=[pick(0), pick(1)],
            out_specs=[
                pl.BlockSpec((1, depth, 2 * HID), lambda i, z: (i, 0, 0)),
                pl.BlockSpec((1, depth, HID), lambda i, z: (i, 0, 0)),
            ],
        ),
        out_shape=[
            jax.ShapeDtypeStruct((EXP_DEV, depth, 2 * HID), jnp.float32),
            jax.ShapeDtypeStruct((EXP_DEV, depth, HID), jnp.float32),
        ],
        name="place_units",
    )(z_index.reshape(1), units, units)


MESH = pl.DeviceIdType.MESH


def greet(peers):
    barrier = pltpu.get_barrier_semaphore()
    for peer in peers:
        pl.semaphore_signal(barrier, inc=1, device_id=peer, device_id_type=MESH)
    pl.semaphore_wait(barrier, len(peers))


def send(src, dst, sems, at, peer):
    copy = pltpu.make_async_remote_copy(
        src_ref=src,
        dst_ref=dst,
        send_sem=sems[0].at[at],
        recv_sem=sems[1].at[at],
        device_id=peer,
        device_id_type=MESH,
    )
    copy.start()
    return copy


def dma_pair(number):
    return [pltpu.SemaphoreType.DMA((number,)), pltpu.SemaphoreType.DMA((number,))]


def z_peers():
    z = lax.axis_index("z")
    return [{"z": z ^ s} for s in (3, 2, 1)]


def siblings(axes):
    return [{a: 1 - lax.axis_index(a)} for a in axes]


class Scatter:
    def __init__(self, part, axes, chunks, refs):
        self.part, self.axes, self.chunks = part, axes, chunks
        depth = len(axes)
        self.own, self.came = refs[0], refs[1 : 1 + depth]
        self.sums = refs[1 + depth : 1 + 2 * depth]
        self.turn, self.line, self.result, self.load_sem = refs[1 + 2 * depth : 5 + 2 * depth]
        sems = refs[5 + 2 * depth :]
        self.sems = [sems[2 * i : 2 * i + 2] for i in range(depth + 1)]
        self.z = lax.axis_index("z")
        self.mine = [lax.axis_index(a) for a in axes]
        self.rows = part.shape[-2] // chunks
        self.flying = [[None] * chunks for _ in axes]

    @staticmethod
    def scratch(part, axes, chunks):
        n_z, rows, width, kind = part.shape[0], part.shape[-2], part.shape[-1], part.dtype
        depth = len(axes)

        def buffer(i):
            return pltpu.VMEM((chunks, n_z) + (2,) * i + (rows // chunks, width), kind)

        shapes = [buffer(depth - 1)] + [buffer(i) for i in range(depth)] * 2
        shapes += [buffer(0), pltpu.VMEM((chunks, n_z + 1, rows // chunks, width), kind)]
        shapes += [pltpu.VMEM((rows // chunks, width), jnp.float32)]
        shapes += [pltpu.SemaphoreType.DMA((chunks,))]
        for _ in range(depth):
            shapes += dma_pair(chunks)
        return shapes + dma_pair(chunks * (n_z + 1))

    def start(self):
        level = len(self.axes) - 1
        lead = (slice(None),) * len(self.axes)
        mine = self.mine[-1]
        self.loads = []
        for c in range(self.chunks):
            at = pl.ds(c * self.rows, self.rows)
            self.flying[level][c] = send(
                self.part.at[lead + (1 - mine, at)],
                self.came[level].at[c],
                self.sems[level],
                c,
                {self.axes[-1]: 1 - mine},
            )
            load = pltpu.make_async_copy(
                self.part.at[lead + (mine, at)], self.own.at[c], self.load_sem.at[c]
            )
            load.start()
            self.loads.append(load)

    def fold(self, level, c):
        self.flying[level][c].wait_recv()
        if level == len(self.axes) - 1:
            self.loads[c].wait()
            held = self.own[c]
        else:
            held = self.sums[level + 1][
                (c,) + (slice(None),) * (level + 1) + (self.mine[level],)
            ]
        total = held.astype(jnp.float32) + self.came[level][c].astype(jnp.float32)
        self.sums[level][c] = total.astype(held.dtype)
        if level > 0:
            mine = self.mine[level - 1]
            self.flying[level - 1][c] = send(
                self.sums[level].at[(c,) + (slice(None),) * level + (1 - mine,)],
                self.came[level - 1].at[c],
                self.sems[level - 1],
                c,
                {self.axes[level - 1]: 1 - mine},
            )

    def along(self, c, w, up):
        slot = w + 1 if up else w
        return pltpu.make_async_remote_copy(
            src_ref=self.turn.at[c, w],
            dst_ref=self.line.at[c, slot],
            send_sem=self.sems[-1][0].at[w * self.chunks + c],
            recv_sem=self.sems[-1][1].at[slot * self.chunks + c],
            device_id={"z": self.z + 1 if up else self.z - 1},
            device_id_type=MESH,
        )

    def steps(self):
        return [(3, True), (0, False), (2, True), (1, False), (1, True), (2, False)]

    def relay(self, c):
        z = self.z
        for w, up in self.steps():
            slot = w + 1 if up else w

            @pl.when((z < w) if up else (z > w))
            def _(w=w, up=up, slot=slot):
                inner = (z > 0) if up else (z < 3)

                @pl.when(inner)
                def _():
                    self.along(c, w, up).wait_recv()
                    total = self.sums[0][c, w].astype(jnp.float32) + self.line[c, slot].astype(
                        jnp.float32
                    )
                    self.turn[c, w] = total.astype(self.turn.dtype)

                @pl.when(jnp.logical_not(inner))
                def _():
                    self.turn[c, w] = self.sums[0][c, w]

                self.along(c, w, up).start()

    def total(self, c):
        z = self.z
        self.result[...] = self.sums[0][c, z].astype(jnp.float32)
        for up in (True, False):

            @pl.when((z > 0) if up else (z < 3))
            def _(up=up):
                self.along(c, z, up).wait_recv()
                self.result[...] += self.line[c, z + 1 if up else z].astype(jnp.float32)

        return self.result[...]

    lag = 2

    def length(self):
        return self.chunks + len(self.axes) + self.lag

    def advance(self, step, use):
        depth = len(self.axes)
        for level in range(depth - 1, -1, -1):
            c = step - (depth - 1 - level)
            if 0 <= c < self.chunks:
                self.fold(level, c)
        c = step - (depth - 1)
        if 0 <= c < self.chunks:
            self.relay(c)
        c = step - depth - self.lag + 1
        if 0 <= c < self.chunks:
            use(c, pl.ds(c * self.rows, self.rows), self.total(c))

    def run(self, use):
        for step in range(self.length()):
            self.advance(step, use)

    def finish(self):
        for copy in sum(self.flying, []):
            copy.wait_send()
        for c in range(self.chunks):
            for w, up in self.steps():

                @pl.when((self.z < w) if up else (self.z > w))
                def _(w=w, up=up, c=c):
                    self.along(c, w, up).wait_send()


class Gather:
    def __init__(self, own, out, axes, chunks, refs):
        self.own, self.out, self.axes, self.chunks = own, out, axes, chunks
        self.keep_sem = refs[0]
        self.sems = [refs[1 + 2 * i : 3 + 2 * i] for i in range(len(axes) + 1)]
        self.z = lax.axis_index("z")
        self.mine = tuple(lax.axis_index(a) for a in axes)
        self.rows = own.shape[0] // chunks
        self.keeps = []

    @staticmethod
    def scratch(axes, chunks):
        shapes = [pltpu.SemaphoreType.DMA((chunks,)), *dma_pair(8 * chunks)]
        for i in range(len(axes)):
            shapes += dma_pair(4 * 2**i * chunks)
        return shapes

    def block(self, c, w, flips):
        places = tuple(
            1 - m if i < len(flips) and flips[i] else m for i, m in enumerate(self.mine)
        )
        return self.out.at[(w,) + places + (pl.ds(c * self.rows, self.rows),)]

    def along(self, c, w, up, own=False):
        where = self.block(c, w, ())
        return pltpu.make_async_remote_copy(
            src_ref=self.own.at[pl.ds(c * self.rows, self.rows)] if own else where,
            dst_ref=where,
            send_sem=self.sems[0][0].at[(w * 2 + int(up)) * self.chunks + c],
            recv_sem=self.sems[0][1].at[w * self.chunks + c],
            device_id={"z": self.z + 1 if up else self.z - 1},
            device_id_type=MESH,
        )

    def across(self, level, c, w, flips, own=False):
        where = self.block(c, w, flips)
        number = w
        for f in flips:
            number = number * 2 + f
        at = number * self.chunks + c
        return pltpu.make_async_remote_copy(
            src_ref=self.own.at[pl.ds(c * self.rows, self.rows)] if own else where,
            dst_ref=where,
            send_sem=self.sems[level + 1][0].at[at],
            recv_sem=self.sems[level + 1][1].at[at],
            device_id={self.axes[level]: 1 - self.mine[level]},
            device_id_type=MESH,
        )

    def start(self, c):
        z = self.z
        for up in (True, False):

            @pl.when((z < 3) if up else (z > 0))
            def _(up=up):
                self.along(c, z, up, own=True).start()

        for level in range(len(self.axes)):
            self.across(level, c, z, (0,) * level, own=True).start()
        keep = pltpu.make_async_copy(
            self.own.at[pl.ds(c * self.rows, self.rows)], self.block(c, z, ()), self.keep_sem.at[c]
        )
        keep.start()
        self.keeps.append(keep)

    def forward(self, c, hops=(1, 2, 3)):
        z = self.z
        for t in hops:
            for up in (True, False):

                @pl.when((z >= t) if up else (z + t <= 3))
                def _(t=t, up=up):
                    w = z - t if up else z + t
                    self.along(c, w, up).wait_recv()

                    @pl.when((z < 3) if up else (z > 0))
                    def _():
                        self.along(c, w, up).start()

                    for level in range(len(self.axes)):
                        self.across(level, c, w, (0,) * level).start()

    def flips(self, level):
        return [tuple((i >> b) & 1 for b in range(level)) for i in range(2**level)]

    def spread(self, c):
        for level in range(len(self.axes) - 1):
            for s in range(4):
                for flips in self.flips(level):
                    w = self.z ^ s
                    turned = flips + (1,)
                    self.across(level, c, w, flips).wait_recv()
                    for later in range(level + 1, len(self.axes)):
                        self.across(later, c, w, turned + (0,) * (later - level - 1)).start()

    def finish(self):
        z, last = self.z, len(self.axes) - 1
        for keep in self.keeps:
            keep.wait()
        for c in range(self.chunks):
            for s in range(4):
                for flips in self.flips(last):
                    self.across(last, c, z ^ s, flips).wait_recv()
                for level in range(last + 1):
                    for flips in self.flips(level):
                        self.across(level, c, z ^ s, flips).wait_send()
            for t in (0, 1, 2, 3):
                for up in (True, False):
                    here = ((z >= t) & (z < 3)) if up else ((z + t <= 3) & (z > 0))

                    @pl.when(here)
                    def _(t=t, up=up, c=c):
                        self.along(c, z - t if up else z + t, up).wait_send()


VMEM_SPEC = pl.BlockSpec(memory_space=pltpu.VMEM)
ANY_SPEC = pl.BlockSpec(memory_space=pl.ANY)


def exchange(kernel, name, number, inputs, specs, outs, out_specs, scratch):
    sizes = [len(inputs), len(outs)] + [len(s) for s in scratch]

    def run(*refs):
        groups, at = [], 0
        for size in sizes:
            groups.append(refs[at : at + size])
            at += size
        kernel(*groups)

    return pl.pallas_call(
        run,
        out_shape=outs,
        in_specs=specs,
        out_specs=out_specs,
        scratch_shapes=sum(scratch, []),
        compiler_params=pltpu.CompilerParams(
            collective_id=number, has_side_effects=True, vmem_limit_bytes=48 * 2**20
        ),
        name=name,
    )(*inputs)


def share_inputs(tokens, slices, wo, marked, win, wout):
    count, own = tokens.shape[0], wo.shape[0]
    columns, wide = slices.shape[-1], marked.shape[-1]
    depth, half = win.shape[1], HID // 2
    number = 2 * win.shape[0] // 4
    chunks = 2
    bf16 = jnp.bfloat16

    def kernel(ins, outs, token_refs, wo_refs, marked_refs, other):
        tok, cut, wo_ref, marked_ref, win_ref, wout_ref = ins
        tok_out, cut_out, wo_out, marked_out = outs[:4]
        near, far = outs[4:8], outs[8:12]
        keep, ctx_sems, exp_sems = other[0], other[1:3], other[3:5]
        near_sems, far_sems, win_in, wout_in, unit = other[5:7], other[7:9], *other[9:12]
        z, y, x, k = (lax.axis_index(a) for a in ("z", "y", "x", "k"))
        loads = [
            pltpu.make_async_copy(win_ref, win_in, keep.at[1]),
            pltpu.make_async_copy(wout_ref, wout_in, keep.at[2]),
        ]
        for copy in loads:
            copy.start()
        exp_peers = [((x ^ a, k ^ b), a * 2 + b) for a in (1, 0) for b in (1, 0) if a or b]
        greet(
            [{"z": p, "y": q} for p, q, _ in ctx_peers()]
            + [{"x": p, "k": q} for (p, q), _ in exp_peers]
        )
        gather = Gather(tok, tok_out, ("y",), chunks, token_refs)
        whole = Gather(wo_ref, wo_out, ("y", "x", "k"), 1, wo_refs)
        other_rows = Gather(marked_ref, marked_out, ("x", "k"), 1, marked_refs)
        over_ctx = [
            send(cut.at[p, q], cut_out.at[z, y, x, k], ctx_sems, i - 1, {"z": p, "y": q})
            for p, q, i in ctx_peers()
        ]
        whole.start(0)
        for c in range(chunks):
            gather.start(c)
        other_rows.start(0)
        copy_own = pltpu.make_async_copy(cut.at[z, y], cut_out.at[z, y, x, k], keep.at[0])
        copy_own.start()

        def over_z(i, j):
            return pltpu.make_async_remote_copy(
                src_ref=unit.at[i, j],
                dst_ref=near[i].at[j],
                send_sem=near_sems[0].at[i * number + j],
                recv_sem=near_sems[1].at[i * number + j],
                device_id={"z": z ^ i},
                device_id_type=MESH,
            )

        def over_y(i, j):
            return pltpu.make_async_remote_copy(
                src_ref=near[i].at[j] if i else unit.at[0, j],
                dst_ref=far[i].at[j],
                send_sem=far_sems[0].at[i * number + j],
                recv_sem=far_sems[1].at[i * number + j],
                device_id={"y": 1 - y},
                device_id_type=MESH,
            )

        def own_unit(j):
            return pltpu.make_async_copy(unit.at[0, j], near[0].at[j], keep.at[3 + j])

        def convert(j):
            for i in range(4):
                index = number * (z ^ i) + j
                e, h = index // 2, lax.rem(index, 2)
                first = pl.ds(pl.multiple_of(h * half, half), half)
                second = pl.ds(pl.multiple_of(HID + h * half, half), half)
                unit[i, j, :, :half] = win_in[e, :, first].astype(bf16)
                unit[i, j, :, half : 2 * half] = win_in[e, :, second].astype(bf16)
                unit[i, j, :, 2 * half :] = wout_in[e, :, first].astype(bf16)

        def send_units(j):
            for i in (3, 2, 1):
                over_z(i, j).start()

        def pass_units(j):
            for i in (1, 2, 3):
                over_z(i, j).wait_recv()
                over_y(i, j).start()

        for copy in loads:
            copy.wait()
        convert(0)
        send_units(0)
        for j in range(number):
            if j:
                convert(j)
            own_unit(j).start()
            over_y(0, j).start()
        for t in (1, 2, 3):
            whole.forward(0, (t,))
            for c in range(chunks):
                gather.forward(c, (t,))
            other_rows.forward(0, (t,))
            send_units(t)
            if t == 1:
                for copy in over_ctx:
                    copy.wait_recv()
                copy_own.wait()
                mine = cut_out.at[:, :, x, k]
                over_exp = [
                    send(mine, mine, exp_sems, i - 1, {"x": p, "k": q})
                    for (p, q), i in exp_peers
                ]
            pass_units(t - 1)
        for j in range(4, number):
            send_units(j)
        whole.spread(0)
        other_rows.spread(0)
        for j in range(3, number):
            pass_units(j)
        for copy in over_exp:
            copy.wait_recv()
        gather.finish()
        whole.finish()
        other_rows.finish()
        for copy in over_ctx + over_exp:
            copy.wait_send()
        for j in range(number):
            own_unit(j).wait()
            for i in range(4):
                over_y(i, j).wait_recv()
                over_y(i, j).wait_send()
                if i:
                    over_z(i, j).wait_send()

    units = jax.ShapeDtypeStruct((number, depth, 3 * half), bf16)
    outs = exchange(
        kernel,
        "share_inputs",
        1,
        (tokens, slices, wo, marked, win, wout),
        [ANY_SPEC] * 6,
        [
            jax.ShapeDtypeStruct((4, 2, count, D), bf16),
            jax.ShapeDtypeStruct((4, 2, 2, 2, own, columns), bf16),
            jax.ShapeDtypeStruct((4, 2, 2, 2, own, D), bf16),
            jax.ShapeDtypeStruct((4, 2, 2, count, wide), bf16),
        ]
        + [units] * 8,
        [ANY_SPEC] * 12,
        [
            Gather.scratch(("y",), chunks),
            Gather.scratch(("y", "x", "k"), 1),
            Gather.scratch(("x", "k"), 1),
            [pltpu.SemaphoreType.DMA((3 + number,))]
            + dma_pair(7)
            + dma_pair(3)
            + dma_pair(4 * number)
            + dma_pair(4 * number)
            + [
                pltpu.VMEM(win.shape, jnp.float32),
                pltpu.VMEM(wout.shape, jnp.float32),
                pltpu.VMEM((4, number, depth, 3 * half), bf16),
            ],
        ],
    )
    return (*outs[:4], list(outs[4:]))


def ctx_peers():
    z, y = lax.axis_index("z"), lax.axis_index("y")
    return [(z ^ (i // 2), y ^ (i % 2), i) for i in range(7, 0, -1)]


def middle_step(heads, tokens, wo, gain):
    count, chunks = tokens.shape[0], 4
    width = heads.shape[-1]
    bf16, f32 = jnp.bfloat16, jnp.float32

    def kernel(ins, outs, hidden_refs, other):
        heads_ref, tok, wo_ref, gain_ref = ins
        attended_ref, middle_ref, hidden_out = outs
        own, sems = other[0], other[1:3]
        z, y = lax.axis_index("z"), lax.axis_index("y")
        greet(
            [{"z": p, "y": q} for p, q, _ in ctx_peers()] + siblings(("x", "k"))
        )
        hidden = Gather(own, hidden_out, ("x", "k"), chunks, hidden_refs)
        copies = [
            send(heads_ref.at[p, q], attended_ref.at[z, y], sems, i - 1, {"z": p, "y": q})
            for p, q, i in ctx_peers()
        ]
        attended_ref[z, y] = heads_ref[z, y]
        for copy in copies:
            copy.wait_recv()
        step = count // chunks
        for c in range(chunks):
            at = pl.ds(c * step, step)
            middle = tok[at, :].astype(f32)
            for i in range(8):
                middle = middle + jnp.dot(
                    attended_ref[i // 2, i % 2, at, :],
                    wo_ref[i * width : (i + 1) * width, :],
                    preferred_element_type=f32,
                )
            middle_ref[at, :] = middle
            scale = lax.rsqrt(jnp.mean(middle * middle, axis=-1, keepdims=True) + EPSILON)
            own[at, :] = (middle * scale * gain_ref[...]).astype(bf16)
            hidden.start(c)
        for c in range(chunks):
            hidden.forward(c)
            hidden.spread(c)
        hidden.finish()
        for copy in copies:
            copy.wait_send()

    return exchange(
        kernel,
        "middle_step",
        2,
        (heads, tokens, wo, gain),
        [VMEM_SPEC] * 4,
        [
            jax.ShapeDtypeStruct((4, 2, count, width), bf16),
            jax.ShapeDtypeStruct((count, D), f32),
            jax.ShapeDtypeStruct((4, 2, 2, count, D), bf16),
        ],
        [VMEM_SPEC, VMEM_SPEC, ANY_SPEC],
        [
            Gather.scratch(("x", "k"), chunks),
            [pltpu.VMEM((count, D), bf16)] + dma_pair(7),
        ],
    )


def router_step(part, middle, cotangent, gates, router, gain, wo, bulk):
    count, chunks = middle.shape[0], 4
    width = wo.shape[0] // 8
    bf16, f32 = jnp.bfloat16, jnp.float32

    def kernel(ins, outs, scatter_refs, other):
        part_ref, middle_ref, up_ref, gates_ref, router_ref, gain_ref, wo_ref = ins[:7]
        logit_ref, gain_out, grad_ref, heads_out = outs[:4]
        turned, sems, bulk_sems = other[0], other[1:3], other[3:5]
        z, y = lax.axis_index("z"), lax.axis_index("y")
        greet([{"z": p, "y": q} for p, q, _ in ctx_peers()] + siblings(("x", "k")))
        scatter = Scatter(part_ref, ("x", "k"), chunks, scatter_refs)
        copies = []
        scatter.start()
        bulk_copies = [
            send(a, b, bulk_sems, i, {"y": 1 - y})
            for i, (a, b) in enumerate(zip(ins[7:], outs[4:]))
        ]
        gain_out[...] = jnp.zeros_like(gain_out)

        def use(c, at, total):
            gate, gate_grad = gates_ref[at, :], total[:, D:]
            inner = jnp.sum(gate * gate_grad, axis=-1, keepdims=True)
            logit_grad = (gate * (gate_grad - inner)).astype(bf16)
            logit_ref[at, :] = logit_grad
            grad = total[:, :D] + contract_cols(logit_grad, router_ref[...])
            middle = middle_ref[at, :]
            scale = lax.rsqrt(jnp.mean(middle * middle, axis=-1, keepdims=True) + EPSILON)
            normed = middle * scale
            gain_out[...] += jnp.sum(grad * normed, axis=0, keepdims=True)
            scaled = grad * gain_ref[...]
            result = up_ref[at, :].astype(f32) + scale * (
                scaled - normed * jnp.mean(scaled * normed, axis=-1, keepdims=True)
            )
            grad_ref[at, :] = result
            down = result.astype(bf16)
            for i in range(8):
                turned[i // 2, i % 2, at, :] = contract_cols(
                    down, wo_ref[i * width : (i + 1) * width, :]
                ).astype(bf16)
            for p, q, i in ctx_peers():
                copies.append(
                    send(
                        turned.at[p, q, at],
                        heads_out.at[z, y, at],
                        sems,
                        (i - 1) * chunks + c,
                        {"z": p, "y": q},
                    )
                )
            heads_out[z, y, at, :] = turned[z, y, at, :]

        scatter.run(use)
        for copy in copies + bulk_copies:
            copy.wait_recv()
        for copy in copies + bulk_copies:
            copy.wait_send()
        scatter.finish()

    return exchange(
        kernel,
        "router_step",
        3,
        (part, middle, cotangent, gates, router, gain, wo, *bulk),
        [ANY_SPEC] + [VMEM_SPEC] * 6 + [ANY_SPEC] * len(bulk),
        [
            jax.ShapeDtypeStruct((count, 128), bf16),
            jax.ShapeDtypeStruct((1, D), f32),
            jax.ShapeDtypeStruct((count, D), f32),
            jax.ShapeDtypeStruct((4, 2, count, width), bf16),
        ]
        + [jax.ShapeDtypeStruct(a.shape, a.dtype) for a in bulk],
        [VMEM_SPEC] * 4 + [ANY_SPEC] * len(bulk),
        [
            Scatter.scratch(part, ("x", "k"), chunks),
            [pltpu.VMEM((4, 2, count, width), bf16)] + dma_pair(7 * chunks) + dma_pair(len(bulk)),
        ],
    )


def last_step(
    part, mixed, tokens, middle, grad_middle, gain, qkv_part, wo_part, small_part, bulk
):
    count, chunks = tokens.shape[0], 4
    own, columns = qkv_part.shape[-2:]
    bf16, f32 = jnp.bfloat16, jnp.float32

    def kernel(ins, outs, part_refs, mixed_refs, wo_refs, other):
        part_ref, mixed_ref, tok, middle_ref, grad_ref, gain_ref, qkv, wo, small = ins[:9]
        out_ref, tokens_ref, qkv_out, wo_out, small_out = outs[:5]
        qkv_came, qkv_sum, small_came = other[:3]
        sems = [other[3 + 2 * i : 5 + 2 * i] for i in range(4)]
        names = ("z", "y", "x", "k")
        z, y, x, k = (lax.axis_index(a) for a in names)
        everyone = [
            ((z ^ (i // 8), y ^ (i // 4 % 2), x ^ (i // 2 % 2), k ^ (i % 2)), i)
            for i in range(31, 0, -1)
        ]
        of_ctx = [(p, i // 4) for p, i in everyone if i % 4 == 0]
        of_exp = [(p, i) for p, i in everyone if i < 4]
        place = lambda p: dict(zip(names, p))
        greet([place(p) for p, _ in everyone])
        first = Scatter(part_ref, ("y",), chunks, part_refs)
        second = Scatter(mixed_ref, ("x", "k"), chunks, mixed_refs)
        third = Scatter(wo, ("y", "x", "k"), 1, wo_refs)
        first.start()
        second.start()
        third.start()
        over_qkv = [
            send(qkv.at[p[2], p[3]], qkv_came.at[i - 1], sems[0], i - 1, place(p))
            for p, i in of_exp
        ]
        def use_first(c, at, total):
            resid = tok[at, :].astype(f32)
            scale = lax.rsqrt(jnp.mean(resid * resid, axis=-1, keepdims=True) + EPSILON)
            normed = resid * scale
            scaled = total * gain_ref[...]
            tokens_ref[at, :] = grad_ref[at, :] + scale * (
                scaled - normed * jnp.mean(scaled * normed, axis=-1, keepdims=True)
            )

        def use_third(c, at, total):
            wo_out[at, :] = total

        def use_second(c, at, total):
            out_ref[at, :] = (middle_ref[at, :] + total).astype(bf16)

        number = bulk[0].shape[0]
        waiting = [(i, j) for j in range(number) for i in (0, 1, 2)]
        over = [{"z": z ^ 2}, {"z": z ^ 1}, {"y": 1 - y}]
        over_bulk = []

        def send_bulk(most):
            for i, j in waiting[:most]:
                over_bulk.append(
                    send(
                        ins[9 + i].at[j],
                        outs[5 + i].at[j],
                        sems[3],
                        i * number + j,
                        over[i],
                    )
                )
            del waiting[:most]

        for step in range(second.length()):
            second.advance(step, use_second)
            if step < first.length():
                first.advance(step, use_first)
            if step < third.length():
                third.advance(step, use_third)
            if step == 1:
                total = qkv[x, k].astype(f32)
                for copy, (_, i) in zip(over_qkv, of_exp):
                    copy.wait_recv()
                    total = total + qkv_came[i - 1].astype(f32)
                qkv_sum[...] = total.astype(bf16)
                qkv_out[z, y] = qkv_sum[z, y]
                over_ctx = [
                    send(qkv_sum.at[p[0], p[1]], qkv_out.at[z, y], sems[1], i - 1, place(p))
                    for p, i in of_ctx
                ]
                over_small = [
                    send(small.at[p], small_came.at[i - 1], sems[2], i - 1, place(p))
                    for p, i in everyone
                ]
            if step >= 2:
                send_bulk(3)
        send_bulk(len(waiting))
        total = small[z, y, x, k].astype(f32)
        for copy, (_, i) in zip(over_small, everyone):
            copy.wait_recv()
            total = total + small_came[i - 1].astype(f32)
        small_out[...] = total
        for copy in over_ctx + over_bulk:
            copy.wait_recv()
        first.finish()
        second.finish()
        third.finish()
        for copy in over_qkv + over_ctx + over_small + over_bulk:
            copy.wait_send()

    return exchange(
        kernel,
        "last_step",
        4,
        (part, mixed, tokens, middle, grad_middle, gain, qkv_part, wo_part, small_part, *bulk),
        [ANY_SPEC] * 2 + [VMEM_SPEC] * 5 + [ANY_SPEC, VMEM_SPEC] + [ANY_SPEC] * len(bulk),
        [
            jax.ShapeDtypeStruct((count, D), bf16),
            jax.ShapeDtypeStruct((count, D), f32),
            jax.ShapeDtypeStruct((4, 2, own, columns), bf16),
            jax.ShapeDtypeStruct((own, D), f32),
            jax.ShapeDtypeStruct((own, 128), f32),
        ]
        + [jax.ShapeDtypeStruct(a.shape, a.dtype) for a in bulk],
        [VMEM_SPEC] * 5 + [ANY_SPEC] * len(bulk),
        [
            Scatter.scratch(part, ("y",), chunks),
            Scatter.scratch(mixed, ("x", "k"), chunks),
            Scatter.scratch(wo_part, ("y", "x", "k"), 1),
            [
                pltpu.VMEM((3, 4, 2, own, columns), bf16),
                pltpu.VMEM((4, 2, own, columns), bf16),
                pltpu.VMEM((31, own, 128), bf16),
            ]
            + dma_pair(3)
            + dma_pair(7)
            + dma_pair(31)
            + dma_pair(len(bulk) * bulk[0].shape[0]),
        ],
    )


def body_heads(
    tokens,
    cotangent,
    lengths,
    span_perm,
    routes,
    norm_attn,
    attn_q,
    attn_k,
    attn_v,
    attn_o,
    router,
    norm_moe,
    expert_in,
    expert_out,
):
    bf16, f32 = jnp.bfloat16, jnp.float32
    n_z, n_y = (lax.axis_size(a) for a in ("z", "y"))
    n_exp = lax.axis_size("x") * lax.axis_size("k")
    n_ctx = n_z * n_y
    exp_index = lax.axis_index("x") * lax.axis_size("k") + lax.axis_index("k")
    count = tokens.shape[1]
    group = count * n_ctx
    repeat = HEADS // KV_HEADS
    width = repeat * HEAD
    experts = EXP_DEV * n_exp
    capacity = count * TOP * 3 // (2 * experts)
    slots = -(-capacity // 8) * 8
    own = attn_q.shape[0]
    softmax_scale = HEAD ** (-0.5)
    z_index = lax.axis_index("z")

    units = 2 * EXP_DEV // n_z
    y_index = lax.axis_index("y")
    win = expert_in.transpose(1, 0, 2)
    wout = expert_out.transpose(1, 0, 2)
    swap_z = [[(i, i ^ s) for i in range(n_z)] for s in range(n_z)]
    swap_y = [(i, i ^ 1) for i in range(n_y)]
    swap_z = [[(i, i ^ s) for i in range(n_z)] for s in range(n_z)]
    swap_y = [(i, i ^ 1) for i in range(n_y)]

    wq, wk, wv = (a.astype(bf16) for a in (attn_q, attn_k, attn_v))
    own_qkv = jnp.concatenate(
        [
            wq.reshape(own, n_ctx, width),
            wk.reshape(own, n_ctx, HEAD),
            wv.reshape(own, n_ctx, HEAD),
        ],
        axis=-1,
    )
    small = jnp.concatenate(
        [
            router.astype(bf16),
            norm_attn.astype(bf16)[:, None],
            norm_moe.astype(bf16)[:, None],
            jnp.zeros((own, 64 - experts - 2), bf16),
        ],
        axis=1,
    )
    slices = jnp.concatenate(
        [own_qkv.transpose(1, 0, 2), jnp.broadcast_to(small, (n_ctx, own, 64))], axis=-1
    )
    marked = jnp.concatenate(
        [cotangent[0], routes[0].astype(bf16), jnp.zeros((count, 128 - TOP), bf16)], axis=1
    )
    token_all, slices, wo, marked_blocks, parts = share_inputs(
        tokens[0], slices.reshape(n_z, n_y, own, -1), attn_o.astype(bf16), marked, win, wout
    )
    token_all = token_all.reshape(group, D)
    slices = slices.reshape(D, -1)
    wo = wo.reshape(HEADS * HEAD, D)
    wqkv, small = slices[:, : width + 2 * HEAD], slices[:, width + 2 * HEAD :]
    weight_r = jnp.concatenate([small[:, :experts], jnp.zeros((D, 128 - experts), bf16)], axis=1)
    gain_one_f = small[:, experts].astype(f32)[None, :]
    gain_two_f = small[:, experts + 1].astype(f32)[None, :]

    perm_row = span_perm[0]
    first_len = lengths[0, 0]
    rows = global_rows(perm_row, jnp.arange(group, dtype=jnp.int32))
    position = rows - jnp.where(rows >= first_len, first_len, 0)
    freqs = jnp.exp(jnp.arange(HEAD // 2, dtype=f32) * (-2.0 * math.log(10000.0) / HEAD))
    angle = position.astype(f32)[:, None] * freqs[None, :]
    cosine, sine = (jnp.cos(angle), jnp.sin(angle))
    resid_all = token_all.astype(f32)
    normed_all = resid_all * lax.rsqrt(
        jnp.mean(resid_all * resid_all, axis=-1, keepdims=True) + EPSILON
    )
    hidden_all = (normed_all * gain_one_f).astype(bf16)
    qkv = jnp.dot(hidden_all, wqkv, preferred_element_type=f32)
    queries = rotate(
        qkv[:, :width].reshape(group, repeat, HEAD), cosine[:, None], sine[:, None]
    ).astype(bf16)
    keys = rotate(qkv[:, width : width + HEAD], cosine, sine).astype(bf16)
    values = qkv[:, width + HEAD :].astype(bf16)
    mask = allowed(rows, rows, first_len)[None]
    scores = (
        jnp.einsum("qrd,kd->rqk", queries, keys, preferred_element_type=f32) * softmax_scale
    )
    scores = jnp.where(mask, scores, NEGATIVE)
    highest = jnp.max(scores, axis=-1)
    weights = jnp.exp(scores - highest[..., None])
    total = jnp.sum(weights, axis=-1)
    attended = (
        jnp.einsum("rqk,kd->rqd", weights.astype(bf16), values, preferred_element_type=f32)
        / total[..., None]
    )
    log_total = highest + jnp.log(total)
    attended_b = attended.transpose(1, 0, 2).reshape(group, width).astype(bf16)
    own_attended, middle, hidden_blocks = middle_step(
        attended_b.reshape(n_z, n_y, count, width), tokens[0], wo, gain_two_f
    )
    hidden_blocks = hidden_blocks.reshape(-1, count, D)
    marked_blocks = marked_blocks.reshape(-1, count, D + 128)

    blocks = hidden_blocks.shape[0]
    held = 3
    base = exp_index * EXP_DEV + (units * z_index) // 2
    shift = (units * z_index) % 2
    pairs = blocks // 2
    row_in, row_up, slot_gate, spread, gates_blocks = dispatch(
        base, hidden_blocks, marked_blocks, weight_r, held, slots
    )
    gates = lax.dynamic_index_in_dim(gates_blocks, z_index * n_exp + exp_index, 0, keepdims=False)

    def to_tokens(rows):
        a = jnp.einsum(
            "prt,prd->ptd",
            spread,
            rows.reshape(pairs, held * 2 * slots, -1),
            preferred_element_type=f32,
        )
        return a.astype(bf16).reshape(blocks, count, -1)

    meta = jnp.stack([shift, z_index, y_index, base]).astype(jnp.int32)
    made, back, *grads = run_experts(
        meta, row_in, row_up, slot_gate, parts
    )
    logit_grad, grad_gain_two, grad_middle, grad_heads, *others = router_step(
        to_tokens(back).reshape(n_z, 2, 2, count, D + 128),
        middle,
        cotangent[0],
        gates,
        weight_r,
        gain_two_f,
        wo,
        grads[6:8],
    )

    grads[5], grad_heads = lax.optimization_barrier((grads[5], grad_heads))
    others = [grads[4], lax.ppermute(grads[5], "y", swap_y)] + others
    add = lambda a, b: (a.astype(f32) + b.astype(f32)).astype(bf16)
    sums = [None, None, add(grads[2], others[2]), add(grads[3], others[3])]
    sums[3], sums[2], grad_heads = lax.optimization_barrier((sums[3], sums[2], grad_heads))
    sums[3] = lax.ppermute(sums[3], "z", swap_z[3])

    hidden_two = lax.dynamic_index_in_dim(
        hidden_blocks, z_index * n_exp + exp_index, 0, keepdims=False
    )
    small_grads = jnp.concatenate(
        [
            contract_rows(hidden_two, logit_grad)[:, : 128 - 1],
            grad_gain_two.reshape(D, 1),
        ],
        axis=1,
    )
    small_grads = small_grads.astype(bf16).reshape(n_z, n_y, 2, 2, own, 128)

    grad_wo = jnp.einsum(
        "cth,td->chd",
        own_attended.reshape(n_ctx, count, width),
        grad_middle.astype(bf16),
        preferred_element_type=f32,
    ).astype(bf16)
    grad_heads = grad_heads.reshape(group, repeat, HEAD)
    grad_heads = grad_heads.transpose(1, 0, 2)
    drift = jnp.sum(grad_heads.astype(f32) * attended, axis=-1)
    scores = (
        jnp.einsum("qrd,kd->rqk", queries, keys, preferred_element_type=f32) * softmax_scale
    )
    weights = jnp.where(mask, jnp.exp(scores - log_total[..., None]), 0.0)
    prob_grad = jnp.einsum("rqd,kd->rqk", grad_heads, values, preferred_element_type=f32)
    score_grad = (weights * (prob_grad - drift[..., None])).astype(bf16)
    query_grad = (
        jnp.einsum("rqk,kd->qrd", score_grad, keys, preferred_element_type=f32) * softmax_scale
    )
    value_grad = jnp.einsum(
        "rqk,rqd->kd", weights.astype(bf16), grad_heads, preferred_element_type=f32
    )
    key_grad = (
        jnp.einsum("rqk,qrd->kd", score_grad, queries, preferred_element_type=f32) * softmax_scale
    )
    grad_qkv = jnp.concatenate(
        [
            rotate(query_grad, cosine[:, None], -sine[:, None]).reshape(group, width),
            rotate(key_grad, cosine, -sine),
            value_grad,
        ],
        axis=-1,
    ).astype(bf16)
    grad_hidden = contract_cols(grad_qkv, wqkv).astype(bf16).reshape(n_z, n_y, count, D)
    grad_wqkv = contract_rows(hidden_all, grad_qkv).astype(bf16)
    grad_wqkv = grad_wqkv.reshape(n_ctx, n_exp, own, width + 2 * HEAD).transpose(1, 0, 2, 3)
    sums[1] = add(grads[1], others[1])
    grad_hidden, sums[1:] = lax.optimization_barrier((grad_hidden, sums[1:]))
    output, grad_tokens, grad_wqkv, grad_wo, small_grads, *bulk = last_step(
        grad_hidden,
        to_tokens(made).reshape(n_z, 2, 2, count, D),
        tokens[0],
        middle,
        grad_middle,
        gain_one_f,
        grad_wqkv.reshape(2, 2, n_z, n_y, own, width + 2 * HEAD),
        grad_wo.reshape(n_z, n_y, 2, 2, own, D),
        small_grads,
        [sums[2], sums[1], others[0]],
    )
    sums[2], sums[1], sums[0] = bulk[0], bulk[1], add(grads[0], bulk[2])
    grad_expert_in, grad_expert_out = place_units(z_index, jnp.concatenate(sums), units)
    grad_expert_in = grad_expert_in.transpose(1, 0, 2)
    grad_expert_out = grad_expert_out.transpose(1, 0, 2)
    grad_wqkv = grad_wqkv.reshape(n_ctx, own, width + 2 * HEAD).astype(f32)
    grad_q = grad_wqkv[:, :, :width].transpose(1, 0, 2).reshape(own, HEADS * HEAD)
    grad_k = grad_wqkv[:, :, width : width + HEAD].transpose(1, 0, 2).reshape(own, KV_HEADS * HEAD)
    grad_v = grad_wqkv[:, :, width + HEAD :].transpose(1, 0, 2).reshape(own, KV_HEADS * HEAD)
    grad_gain_one = jnp.sum(
        grad_wqkv.transpose(1, 0, 2) * own_qkv.astype(f32), axis=(1, 2)
    ) / norm_attn.astype(bf16).astype(f32)
    return (
        output[None],
        grad_tokens[None],
        grad_gain_one,
        grad_q,
        grad_k,
        grad_v,
        grad_wo,
        small_grads[:, :experts],
        small_grads[:, 127],
        grad_expert_in,
        grad_expert_out,
    )


def solution(mesh):
    ctx, exp = mesh.shape["ctx"], mesh.shape["exp"]
    if ctx == KV_HEADS and exp == 4:
        names = ("z", "y", "x", "k")
        inner = jax.sharding.Mesh(mesh.devices.reshape(4, 2, 2, 2), names)
        body, ctx_name, exp_name, both = body_heads, names[:2], names[2:], names
    else:
        inner, body, ctx_name, exp_name, both = mesh, body_general, "ctx", "exp", ("ctx", "exp")
    token = P(exp_name, ctx_name, None)
    group = P(exp_name, None)
    expert = P(ctx_name, exp_name, None)
    rows, gain = P(both, None), P(both)
    in_specs = (token, token, group, group, token, gain) + (rows,) * 5 + (gain, expert, expert)
    out_specs = (token, token, gain) + (rows,) * 5 + (gain, expert, expert)
    return jax.shard_map(
        body, mesh=inner, in_specs=in_specs, out_specs=out_specs, check_vma=False
    )
```

```python
import math

import jax
import jax.numpy as jnp
from jax import lax
from jax.experimental import pallas as pl
from jax.experimental.pallas import tpu as pltpu
from jax.sharding import PartitionSpec as P

D = 1536
HEADS = 24
KV_HEADS = 8
HEAD = 64
HID = 512
TOP = 8
EXP_DEV = 10
SPAN = 64


EPSILON = 1e-06
NEGATIVE = -1e30


def global_rows(perm_row, rows):
    slots = rows // SPAN
    match = slots[:, None] == jnp.arange(perm_row.shape[0], dtype=jnp.int32)[None, :]
    spans = jnp.sum(jnp.where(match, perm_row[None, :], 0), axis=1)
    return spans * SPAN + rows % SPAN


def rotary(tensor, position, sign):
    half = HEAD // 2
    freqs = jnp.exp(jnp.arange(half, dtype=jnp.float32) * (-2.0 * math.log(10000.0) / HEAD))
    angle = position.astype(jnp.float32)[:, None] * freqs[None, :]
    cosine = jnp.cos(angle)[:, None, :]
    sine = sign * jnp.sin(angle)[:, None, :]
    first, second = (tensor[..., :half], tensor[..., half:])
    return jnp.concatenate(
        [first * cosine - second * sine, second * cosine + first * sine], axis=-1
    )


def allowed(query_rows, key_rows, first_len):
    later = key_rows[None, :] <= query_rows[:, None]
    same_seq = (key_rows[None, :] >= first_len) == (query_rows[:, None] >= first_len)
    return later & same_seq


def contract_rows(left, right):
    return lax.dot_general(
        left, right, (((0,), (0,)), ((), ())), preferred_element_type=jnp.float32
    )


def contract_cols(left, right):
    return lax.dot_general(
        left, right, (((1,), (1,)), ((), ())), preferred_element_type=jnp.float32
    )


def block_grads(
    query_block,
    grad_block,
    lse_block,
    drift_block,
    query_rows,
    key_block,
    value_block,
    key_rows,
    first_len,
):
    softmax_scale = HEAD ** (-0.5)
    scores = (
        jnp.einsum("qgrd,kgd->grqk", query_block, key_block, preferred_element_type=jnp.float32)
        * softmax_scale
    )
    mask = allowed(query_rows, key_rows, first_len)[None, None]
    weights = jnp.where(mask, jnp.exp(scores - lse_block.transpose(1, 2, 0)[..., None]), 0.0)
    prob_grad = jnp.einsum(
        "qgrd,kgd->grqk", grad_block, value_block, preferred_element_type=jnp.float32
    )
    score_grad = (weights * (prob_grad - drift_block.transpose(1, 2, 0)[..., None])).astype(
        jnp.bfloat16
    )
    query_grad = None
    key_grad = None
    value_grad = None
    query_grad = (
        jnp.einsum("grqk,kgd->qgrd", score_grad, key_block, preferred_element_type=jnp.float32)
        * softmax_scale
    )
    value_grad = jnp.einsum(
        "grqk,qgrd->kgd",
        weights.astype(jnp.bfloat16),
        grad_block,
        preferred_element_type=jnp.float32,
    )
    key_grad = (
        jnp.einsum("grqk,qgrd->kgd", score_grad, query_block, preferred_element_type=jnp.float32)
        * softmax_scale
    )
    return (query_grad, key_grad, value_grad)


def body_general(
    tokens,
    cotangent,
    lengths,
    span_perm,
    routes,
    norm_attn,
    attn_q,
    attn_k,
    attn_v,
    attn_o,
    router,
    norm_moe,
    expert_in,
    expert_out,
):
    count = tokens.shape[1]
    repeat = HEADS // KV_HEADS
    experts = EXP_DEV * lax.axis_size("exp")
    capacity = count * TOP * 3 // (2 * experts)
    softmax_scale = HEAD ** (-0.5)
    perm_row = span_perm[0]
    first_len = lengths[0, 0]
    query_rows = global_rows(
        perm_row, lax.axis_index("ctx") * count + jnp.arange(count, dtype=jnp.int32)
    )
    position = query_rows - jnp.where(query_rows >= first_len, first_len, 0)
    gathered = (
        lax.all_gather(norm_attn.astype(jnp.bfloat16), ("ctx", "exp"), axis=0, tiled=True),
        lax.all_gather(attn_q.astype(jnp.bfloat16), ("ctx", "exp"), axis=0, tiled=True),
        lax.all_gather(attn_k.astype(jnp.bfloat16), ("ctx", "exp"), axis=0, tiled=True),
        lax.all_gather(attn_v.astype(jnp.bfloat16), ("ctx", "exp"), axis=0, tiled=True),
        lax.all_gather(attn_o.astype(jnp.bfloat16), ("ctx", "exp"), axis=0, tiled=True),
        lax.all_gather(router.astype(jnp.bfloat16), ("ctx", "exp"), axis=0, tiled=True),
        lax.all_gather(norm_moe.astype(jnp.bfloat16), ("ctx", "exp"), axis=0, tiled=True),
    )
    gain_one, weight_q, weight_k, weight_v, weight_o, weight_r, gain_two = gathered
    weight_in, weight_out = (
        lax.all_gather(expert_in.astype(jnp.bfloat16), "ctx", axis=0, tiled=True),
        lax.all_gather(expert_out.astype(jnp.bfloat16), "ctx", axis=0, tiled=True),
    )
    gain_one_f = gain_one.astype(jnp.float32)
    gain_two_f = gain_two.astype(jnp.float32)
    resid = tokens[0].astype(jnp.float32)
    scale_one = lax.rsqrt(jnp.mean(resid * resid, axis=-1, keepdims=True) + EPSILON)
    normed_one = resid * scale_one
    hidden_one = (normed_one * gain_one_f).astype(jnp.bfloat16)
    query_pre = jnp.dot(hidden_one, weight_q, preferred_element_type=jnp.float32).reshape(
        count, HEADS, HEAD
    )
    queries = (
        rotary(query_pre, position, 1.0).astype(jnp.bfloat16).reshape(count, KV_HEADS, repeat, HEAD)
    )
    key_pre = jnp.dot(hidden_one, weight_k, preferred_element_type=jnp.float32).reshape(
        count, KV_HEADS, HEAD
    )
    keys = rotary(key_pre, position, 1.0).astype(jnp.bfloat16)
    values = (
        jnp.dot(hidden_one, weight_v, preferred_element_type=jnp.float32)
        .astype(jnp.bfloat16)
        .reshape(count, KV_HEADS, HEAD)
    )
    start_state = (
        jnp.full((KV_HEADS, repeat, count), NEGATIVE, jnp.float32),
        jnp.zeros((KV_HEADS, repeat, count), jnp.float32),
        jnp.zeros((KV_HEADS, repeat, count, HEAD), jnp.float32),
    )
    carry = start_state
    key_piece = lax.all_gather(keys, "ctx", axis=0, tiled=True)
    value_piece = lax.all_gather(values, "ctx", axis=0, tiled=True)
    size = key_piece.shape[0]
    block = math.gcd(size, 512)
    number = size // block
    key_blocks = key_piece.reshape(number, block, KV_HEADS, HEAD)
    value_blocks = value_piece.reshape(number, block, KV_HEADS, HEAD)
    offsets = jnp.arange(size, dtype=jnp.int32).reshape(number, block)

    def forward_step(state, inputs):
        highest, total, accum = state
        key_block, value_block, offset = inputs
        key_rows = global_rows(perm_row, offset)
        scores = (
            jnp.einsum("qgrd,kgd->grqk", queries, key_block, preferred_element_type=jnp.float32)
            * softmax_scale
        )
        mask = allowed(query_rows, key_rows, first_len)[None, None]
        scores = jnp.where(mask, scores, NEGATIVE)
        newmax = jnp.maximum(highest, jnp.max(scores, axis=-1))
        weights = jnp.where(mask, jnp.exp(scores - newmax[..., None]), 0.0)
        factor = jnp.exp(highest - newmax)
        total = total * factor + jnp.sum(weights, axis=-1)
        accum = accum * factor[..., None] + jnp.einsum(
            "grqk,kgd->grqd",
            weights.astype(jnp.bfloat16),
            value_block,
            preferred_element_type=jnp.float32,
        )
        return ((newmax, total, accum), None)

    carry, _ = lax.scan(forward_step, carry, (key_blocks, value_blocks, offsets))
    highest, total, accum = carry
    log_total = (highest + jnp.log(total)).transpose(2, 0, 1)
    attended = (accum / total[..., None]).transpose(2, 0, 1, 3)
    attended_b = attended.reshape(count, HEADS * HEAD).astype(jnp.bfloat16)
    middle = resid + jnp.dot(attended_b, weight_o, preferred_element_type=jnp.float32)
    scale_two = lax.rsqrt(jnp.mean(middle * middle, axis=-1, keepdims=True) + EPSILON)
    normed_two = middle * scale_two
    hidden_two = (normed_two * gain_two_f).astype(jnp.bfloat16)
    logits = jnp.dot(hidden_two, weight_r, preferred_element_type=jnp.float32)
    chosen = routes[0]
    picks = chosen[:, :, None] == jnp.arange(experts, dtype=jnp.int32)[None, None, :]
    selected = jnp.sum(jnp.where(picks, logits[:, None, :], 0.0), axis=-1)
    gates = jax.nn.softmax(selected, axis=-1)
    gates_b = gates.astype(jnp.bfloat16)
    flat_picks = picks.reshape(count * TOP, experts).astype(jnp.int32)
    placed = jnp.sum((jnp.cumsum(flat_picks, axis=0) - 1) * flat_picks, axis=-1)
    column = chosen.reshape(-1) * capacity + placed
    hits = (
        column.reshape(count, TOP)[:, :, None]
        == jnp.arange(experts * capacity, dtype=jnp.int32)[None, None, :]
    )
    spread = jnp.any(hits, axis=1).astype(jnp.bfloat16)
    weighted = jnp.sum(
        jnp.where(hits, gates_b.astype(jnp.float32)[:, :, None], 0.0), axis=1
    ).astype(jnp.bfloat16)
    outgoing = contract_rows(spread, hidden_two).astype(jnp.bfloat16).reshape(experts, capacity, D)
    incoming = lax.all_to_all(outgoing, "exp", split_axis=0, concat_axis=1, tiled=True)
    gate_up = jnp.einsum("erd,dec->erc", incoming, weight_in, preferred_element_type=jnp.float32)
    gate_part = gate_up[..., :HID]
    up_part = gate_up[..., HID:]
    sigmoid_gate = jax.nn.sigmoid(gate_part)
    silu_gate = gate_part * sigmoid_gate
    activated = (silu_gate * up_part).astype(jnp.bfloat16)
    produced = jnp.einsum(
        "erh,deh->erd", activated, weight_out, preferred_element_type=jnp.float32
    ).astype(jnp.bfloat16)
    returned = lax.all_to_all(produced, "exp", split_axis=1, concat_axis=0, tiled=True).reshape(
        experts * capacity, D
    )
    mixture = jnp.dot(weighted, returned, preferred_element_type=jnp.float32)
    output = (middle + mixture).astype(jnp.bfloat16)
    upstream = cotangent[0].astype(jnp.float32)
    upstream_b = upstream.astype(jnp.bfloat16)
    sent_grad = (
        contract_rows(weighted, upstream_b).astype(jnp.bfloat16).reshape(experts, capacity, D)
    )
    grad_in = lax.all_to_all(sent_grad, "exp", split_axis=0, concat_axis=1, tiled=True)
    picked = jnp.take(returned, column, axis=0).reshape(count, TOP, D)
    gate_grad = jnp.einsum("tkd,td->tk", picked, upstream_b, preferred_element_type=jnp.float32)
    grad_act = (
        jnp.einsum("erd,deh->erh", grad_in, weight_out, preferred_element_type=jnp.float32)
        .astype(jnp.bfloat16)
        .astype(jnp.float32)
    )
    grad_gate = grad_act * up_part * (sigmoid_gate * (1.0 + gate_part * (1.0 - sigmoid_gate)))
    grad_up = grad_act * silu_gate
    grad_gu = jnp.concatenate([grad_gate, grad_up], axis=-1).astype(jnp.bfloat16)
    grad_weight_out = jnp.einsum(
        "erd,erh->deh", grad_in, activated, preferred_element_type=jnp.float32
    )
    grad_weight_in = jnp.einsum(
        "erd,erc->dec", incoming, grad_gu, preferred_element_type=jnp.float32
    )
    grad_rows = jnp.einsum(
        "erc,dec->erd", grad_gu, weight_in, preferred_element_type=jnp.float32
    ).astype(jnp.bfloat16)
    back_rows = lax.all_to_all(grad_rows, "exp", split_axis=1, concat_axis=0, tiled=True).reshape(
        experts * capacity, D
    )
    expert_sums = (
        lax.psum_scatter(
            grad_weight_in.astype(jnp.bfloat16), "ctx", scatter_dimension=0, tiled=True
        ).astype(jnp.float32),
        lax.psum_scatter(
            grad_weight_out.astype(jnp.bfloat16), "ctx", scatter_dimension=0, tiled=True
        ).astype(jnp.float32),
    )
    centered = gate_grad - jnp.sum(gates * gate_grad, axis=-1, keepdims=True)
    select_grad = gates * centered
    logit_grad = jnp.sum(jnp.where(picks, select_grad[:, :, None], 0.0), axis=1).astype(
        jnp.bfloat16
    )
    grad_router = contract_rows(hidden_two, logit_grad)
    grad_norm_two = jnp.dot(spread, back_rows, preferred_element_type=jnp.float32) + contract_cols(
        logit_grad, weight_r
    )
    grad_gain_two = jnp.sum(grad_norm_two * normed_two, axis=0)
    scaled_two = grad_norm_two * gain_two_f
    grad_middle = upstream + scale_two * (
        scaled_two - normed_two * jnp.mean(scaled_two * normed_two, axis=-1, keepdims=True)
    )
    branch_grad = grad_middle.astype(jnp.bfloat16)
    grad_weight_o = contract_rows(attended_b, branch_grad)
    grad_heads = (
        contract_cols(branch_grad, weight_o)
        .astype(jnp.bfloat16)
        .reshape(count, KV_HEADS, repeat, HEAD)
    )
    drift = jnp.sum(grad_heads.astype(jnp.float32) * attended, axis=-1)
    query_acc = jnp.zeros((count, KV_HEADS, repeat, HEAD), jnp.float32)
    key_piece = lax.all_gather(keys, "ctx", axis=0, tiled=True)
    value_piece = lax.all_gather(values, "ctx", axis=0, tiled=True)
    size = key_piece.shape[0]
    block = math.gcd(size, 512)
    number = size // block
    key_blocks = key_piece.reshape(number, block, KV_HEADS, HEAD)
    value_blocks = value_piece.reshape(number, block, KV_HEADS, HEAD)
    offsets = jnp.arange(size, dtype=jnp.int32).reshape(number, block)

    def backward_step(acc, inputs):
        key_block, value_block, offset = inputs
        part_q, part_k, part_v = block_grads(
            queries,
            grad_heads,
            log_total,
            drift,
            query_rows,
            key_block,
            value_block,
            global_rows(perm_row, offset),
            first_len,
        )
        joined = jnp.concatenate(
            [part_k.reshape(block, KV_HEADS * HEAD), part_v.reshape(block, KV_HEADS * HEAD)],
            axis=-1,
        )
        return (acc + part_q, joined)

    query_acc, joined_parts = lax.scan(
        backward_step, query_acc, (key_blocks, value_blocks, offsets)
    )
    pair_acc = joined_parts.reshape(size, 2 * KV_HEADS * HEAD)
    query_grad, pair_acc = (query_acc, pair_acc)
    pair_own = lax.psum_scatter(
        pair_acc.astype(jnp.bfloat16), "ctx", scatter_dimension=0, tiled=True
    ).astype(jnp.float32)
    key_grad = pair_own[:, : KV_HEADS * HEAD].reshape(count, KV_HEADS, HEAD)
    value_grad = pair_own[:, KV_HEADS * HEAD :].reshape(count, KV_HEADS, HEAD)
    query_grad_b = (
        rotary(query_grad.reshape(count, HEADS, HEAD), position, -1.0)
        .astype(jnp.bfloat16)
        .reshape(count, HEADS * HEAD)
    )
    key_grad_b = (
        rotary(key_grad, position, -1.0).astype(jnp.bfloat16).reshape(count, KV_HEADS * HEAD)
    )
    value_grad_b = value_grad.astype(jnp.bfloat16).reshape(count, KV_HEADS * HEAD)
    grad_weight_q = contract_rows(hidden_one, query_grad_b)
    grad_weight_k = contract_rows(hidden_one, key_grad_b)
    grad_weight_v = contract_rows(hidden_one, value_grad_b)
    grad_hidden_one = (
        contract_cols(query_grad_b, weight_q)
        + contract_cols(key_grad_b, weight_k)
        + contract_cols(value_grad_b, weight_v)
    )
    grad_gain_one = jnp.sum(grad_hidden_one * normed_one, axis=0)
    scaled_one = grad_hidden_one * gain_one_f
    grad_tokens = grad_middle + scale_one * (
        scaled_one - normed_one * jnp.mean(scaled_one * normed_one, axis=-1, keepdims=True)
    )
    attn_sums = (
        lax.psum_scatter(grad_gain_one, ("ctx", "exp"), scatter_dimension=0, tiled=True),
        lax.psum_scatter(grad_weight_q, ("ctx", "exp"), scatter_dimension=0, tiled=True),
        lax.psum_scatter(grad_weight_k, ("ctx", "exp"), scatter_dimension=0, tiled=True),
        lax.psum_scatter(grad_weight_v, ("ctx", "exp"), scatter_dimension=0, tiled=True),
        lax.psum_scatter(grad_weight_o, ("ctx", "exp"), scatter_dimension=0, tiled=True),
        lax.psum_scatter(grad_router, ("ctx", "exp"), scatter_dimension=0, tiled=True),
        lax.psum_scatter(grad_gain_two, ("ctx", "exp"), scatter_dimension=0, tiled=True),
    )
    return (
        output[None],
        grad_tokens[None],
        attn_sums[0],
        attn_sums[1],
        attn_sums[2],
        attn_sums[3],
        attn_sums[4],
        attn_sums[5],
        attn_sums[6],
        expert_sums[0],
        expert_sums[1],
    )


def rotate(tensor, cosine, sine):
    half = HEAD // 2
    first, second = (tensor[..., :half], tensor[..., half:])
    return jnp.concatenate(
        [first * cosine - second * sine, second * cosine + first * sine], axis=-1
    )


def dispatch_kernel(base, hid_ref, mark_ref, router_ref, rows_ref, up_ref, gate_ref, spread_ref, gates_ref):
    bf16, f32 = jnp.bfloat16, jnp.float32
    count = hid_ref.shape[1]
    _, held, rows, _ = rows_ref.shape
    slots = rows // 2
    both = 2 * count
    x = hid_ref[...].reshape(both, D)
    logits = jnp.dot(x, router_ref[...], preferred_element_type=f32)
    routes = mark_ref[:, :, D:].reshape(both, 128).astype(f32)
    lane = lax.broadcasted_iota(jnp.int32, (both, 128), 1).astype(f32)
    picks = jnp.zeros((both, 128), f32)
    for i in range(TOP):
        picks = jnp.where(routes[:, i : i + 1] == lane, 1.0, picks)
    masked = jnp.where(picks > 0.0, logits, NEGATIVE)
    top = jnp.max(masked, axis=-1, keepdims=True)
    gates = jnp.where(picks > 0.0, jnp.exp(masked - top), 0.0)
    gates = gates / jnp.sum(gates, axis=-1, keepdims=True)
    gates_ref[...] = gates.reshape(2, count, 128)
    which = lax.broadcasted_iota(jnp.int32, (8, 128), 0)
    columns = lax.broadcasted_iota(jnp.int32, (8, 128), 1)
    chosen = jnp.where(columns == which + base[0], 1.0, 0.0).astype(bf16)
    hit = contract_cols(chosen, picks.astype(bf16))
    gate = contract_cols(chosen, gates.astype(bf16))
    earlier = lax.broadcasted_iota(jnp.int32, (both, both), 0)
    later = lax.broadcasted_iota(jnp.int32, (both, both), 1)
    upto = jnp.where((earlier <= later) & (earlier // count == later // count), 1.0, 0.0)
    rank = jnp.dot(hit.astype(bf16), upto.astype(bf16), preferred_element_type=f32)
    row = lax.broadcasted_iota(jnp.int32, (rows, both), 0)
    token = lax.broadcasted_iota(jnp.int32, (rows, both), 1)
    side = row // slots
    wanted = jnp.where(side == token // count, row - side * slots + 1, -1).astype(f32)
    for e in range(held):
        here = jnp.where((rank[e : e + 1] == wanted) & (hit[e : e + 1] > 0.0), 1.0, 0.0)
        gate_ref[0, e] = jnp.sum(here * gate[e : e + 1], axis=-1, keepdims=True)
        here = here.astype(bf16)
        spread_ref[0, e * rows : (e + 1) * rows, :] = here
        rows_ref[0, e] = jnp.dot(here, x, preferred_element_type=f32).astype(bf16)
        up_ref[0, e] = jnp.dot(
            here, mark_ref[:, :, :D].reshape(both, D), preferred_element_type=f32
        ).astype(bf16)


def dispatch(base, hidden, marked, router, held, slots):
    blocks, count, _ = hidden.shape
    pairs = blocks // 2
    bf16, f32 = jnp.bfloat16, jnp.float32
    pair = lambda *shape: pl.BlockSpec((1,) + shape, lambda p, b: (p,) + (0,) * len(shape))
    two = lambda width: pl.BlockSpec((2, count, width), lambda p, b: (p, 0, 0))
    return pl.pallas_call(
        dispatch_kernel,
        grid_spec=pltpu.PrefetchScalarGridSpec(
            num_scalar_prefetch=1,
            grid=(pairs,),
            in_specs=[two(D), two(D + 128), pl.BlockSpec((D, 128), lambda p, b: (0, 0))],
            out_specs=[
                pair(held, 2 * slots, D),
                pair(held, 2 * slots, D),
                pair(held, 2 * slots, 1),
                pair(held * 2 * slots, 2 * count),
                two(128),
            ],
        ),
        out_shape=[
            jax.ShapeDtypeStruct((pairs, held, 2 * slots, D), bf16),
            jax.ShapeDtypeStruct((pairs, held, 2 * slots, D), bf16),
            jax.ShapeDtypeStruct((pairs, held, 2 * slots, 1), f32),
            jax.ShapeDtypeStruct((pairs, held * 2 * slots, 2 * count), bf16),
            jax.ShapeDtypeStruct((blocks, count, 128), f32),
        ],
        compiler_params=pltpu.CompilerParams(vmem_limit_bytes=48 * 2**20),
        name="dispatch",
    )(base.reshape(1).astype(jnp.int32), hidden, marked, router)


def expert_kernel(depth, meta, x_ref, g_ref, gate_ref, *refs):
    parts, (y_ref, d_ref), outs = refs[:8], refs[8:10], refs[10:18]
    weight, du_ref, act_ref = refs[18:]
    bf16, f32 = jnp.bfloat16, jnp.float32
    j = pl.program_id(0)
    shift, z, y, base = meta[0], meta[1], meta[2], meta[3]
    half = HID // 2
    offsets = [
        pl.multiple_of(((z ^ (i % 4)) * 2 + (y ^ (i // 4))) * depth, 64) for i in range(8)
    ]
    for part, offset in zip(parts, offsets):
        weight[pl.ds(offset, depth), :] = part[0]
    expert = base + (j + shift) // 2
    first = jnp.logical_or(j == 0, lax.rem(j + shift, 2) == 0)
    keep = jnp.where(first, 0.0, 1.0)
    pairs, _, rows, _ = x_ref.shape
    step = 4

    def forward(i, carry):
        at = pl.ds(i * step, step)
        flat = pl.ds(pl.multiple_of(i * step * rows, 32), step * rows)
        x = x_ref[at, 0].reshape(step * rows, D)
        g = g_ref[at, 0].reshape(step * rows, D)
        gate = gate_ref[at, 0].reshape(step * rows, 1)
        u = jnp.dot(x, weight[:, : 2 * half], preferred_element_type=f32)
        raw = jnp.dot(g, weight[:, 2 * half :], preferred_element_type=f32)
        u1, u2 = u[:, :half], u[:, half:]
        sig = jax.nn.sigmoid(u1)
        silu = u1 * sig
        act = (silu * u2).astype(bf16).astype(f32)
        dgate = jnp.sum(raw * act, axis=-1, keepdims=True)
        dact = raw * gate
        du1 = dact * u2 * (sig * (1.0 + u1 * (1.0 - sig)))
        du = jnp.concatenate([du1, dact * silu], axis=-1).astype(bf16)
        act_gated = (act * gate).astype(bf16)
        du_ref[flat, :] = du
        act_ref[flat, :] = act_gated
        made = contract_cols(act_gated, weight[:, 2 * half :])
        back = contract_cols(du, weight[:, : 2 * half])
        lane = lax.broadcasted_iota(jnp.int32, (step * rows, 128), 1)
        tail = jnp.where(lane == expert, dgate, 0.0)

        @pl.when(first)
        def _():
            y_ref[at, 0] = made.astype(bf16).reshape(step, rows, D)
            d_ref[at, 0, :, :D] = back.astype(bf16).reshape(step, rows, D)
            d_ref[at, 0, :, D:] = tail.astype(bf16).reshape(step, rows, 128)

        @pl.when(jnp.logical_not(first))
        def _():
            old_y = y_ref[at, 0].reshape(step * rows, D).astype(f32)
            y_ref[at, 0] = (made + old_y).astype(bf16).reshape(step, rows, D)
            old_d = d_ref[at, 0].reshape(step * rows, D + 128).astype(f32)
            d_ref[at, 0, :, :D] = (back + old_d[:, :D]).astype(bf16).reshape(step, rows, D)
            d_ref[at, 0, :, D:] = (tail + old_d[:, D:]).astype(bf16).reshape(step, rows, 128)

        return carry

    lax.fori_loop(0, pairs // step, forward, 0)

    wide = D // 2

    def gradient(i, carry):
        at = pl.ds(pl.multiple_of(i * wide, wide), wide)
        x = x_ref[:, 0, :, at].reshape(pairs * rows, wide)
        g = g_ref[:, 0, :, at].reshape(pairs * rows, wide)
        weight[at, : 2 * half] = contract_rows(x, du_ref[...]).astype(bf16)
        weight[at, 2 * half :] = contract_rows(g, act_ref[...]).astype(bf16)
        return carry

    lax.fori_loop(0, D // wide, gradient, 0)
    for out, offset in zip(outs, offsets):
        out[0] = weight[pl.ds(offset, depth), :]


def run_experts(meta, row_in, row_up, slot_gate, parts):
    pairs, held, rows, _ = row_in.shape
    units, depth, columns = parts[0].shape
    held_block = lambda width: pl.BlockSpec(
        (pairs, 1, rows, width), lambda j, m: (0, (j + m[0]) // 2, 0, 0)
    )
    unit_block = pl.BlockSpec((1, depth, columns), lambda j, m: (j, 0, 0))
    bf16 = jnp.bfloat16
    total = units * pairs * rows * D * columns * 6
    return pl.pallas_call(
        lambda *refs: expert_kernel(depth, *refs),
        grid_spec=pltpu.PrefetchScalarGridSpec(
            num_scalar_prefetch=1,
            grid=(units,),
            in_specs=[
                held_block(D),
                held_block(D),
                held_block(1),
            ]
            + [unit_block] * 8,
            out_specs=[held_block(D), held_block(D + 128)] + [unit_block] * 8,
            scratch_shapes=[
                pltpu.VMEM((D, columns), bf16),
                pltpu.VMEM((pairs * rows, HID), bf16),
                pltpu.VMEM((pairs * rows, HID // 2), bf16),
            ],
        ),
        out_shape=[
            jax.ShapeDtypeStruct((pairs, held, rows, D), bf16),
            jax.ShapeDtypeStruct((pairs, held, rows, D + 128), bf16),
        ]
        + [jax.ShapeDtypeStruct((units, depth, columns), bf16)] * 8,
        compiler_params=pltpu.CompilerParams(vmem_limit_bytes=56 * 2**20),
        cost_estimate=pl.CostEstimate(
            flops=total, bytes_accessed=60 * 2**20, transcendentals=units * pairs * rows * HID
        ),
        name="experts",
    )(meta, row_in, row_up, slot_gate, *parts)


def place_kernel(number, z_ref, *refs):
    in_ref, out_ref = refs[10:]
    half = refs[0].shape[-1] // 3
    for h in range(2):
        source = ((2 * pl.program_id(0) + h) // number) ^ z_ref[0]
        first, other, *rest = refs[5 * h : 5 * h + 5]
        for i, group in enumerate([(first, other)] + [(ref,) for ref in rest]):

            @pl.when(source == i)
            def _(h=h, group=group):
                total = group[0][0].astype(jnp.float32)
                for ref in group[1:]:
                    total = total + ref[0].astype(jnp.float32)
                in_ref[0, :, h * half : (h + 1) * half] = total[:, :half]
                in_ref[0, :, HID + h * half : HID + (h + 1) * half] = total[:, half : 2 * half]
                out_ref[0, :, h * half : (h + 1) * half] = total[:, 2 * half :]


def place_units(z_index, first, other, near, mid, far):
    number, depth, columns = first.shape

    def block(i, h):
        def index(e, z):
            unit = 2 * e + h
            return jnp.where((unit // number) ^ z[0] == i, lax.rem(unit, number), 0), 0, 0

        return pl.BlockSpec((1, depth, columns), index)

    return pl.pallas_call(
        lambda *refs: place_kernel(number, *refs),
        grid_spec=pltpu.PrefetchScalarGridSpec(
            num_scalar_prefetch=1,
            grid=(EXP_DEV,),
            in_specs=[block(i, h) for h in range(2) for i in (0, 0, 1, 2, 3)],
            out_specs=[
                pl.BlockSpec((1, depth, 2 * HID), lambda e, z: (e, 0, 0)),
                pl.BlockSpec((1, depth, HID), lambda e, z: (e, 0, 0)),
            ],
        ),
        out_shape=[
            jax.ShapeDtypeStruct((EXP_DEV, depth, 2 * HID), jnp.float32),
            jax.ShapeDtypeStruct((EXP_DEV, depth, HID), jnp.float32),
        ],
        name="place_units",
    )(z_index.reshape(1), *[first, other, near, mid, far] * 2)


MESH = pl.DeviceIdType.MESH


def greet(peers):
    barrier = pltpu.get_barrier_semaphore()
    for peer in peers:
        pl.semaphore_signal(barrier, inc=1, device_id=peer, device_id_type=MESH)
    pl.semaphore_wait(barrier, len(peers))


def send(src, dst, sems, at, peer):
    copy = pltpu.make_async_remote_copy(
        src_ref=src,
        dst_ref=dst,
        send_sem=sems[0].at[at],
        recv_sem=sems[1].at[at],
        device_id=peer,
        device_id_type=MESH,
    )
    copy.start()
    return copy


def dma_pair(number):
    return [pltpu.SemaphoreType.DMA((number,)), pltpu.SemaphoreType.DMA((number,))]


def z_peers():
    z = lax.axis_index("z")
    return [{"z": z ^ s} for s in (3, 2, 1)]


def siblings(axes):
    return [{a: 1 - lax.axis_index(a)} for a in axes]


class Scatter:
    def __init__(self, part, axes, chunks, refs, direct=False):
        self.part, self.axes, self.chunks, self.direct = part, axes, chunks, direct
        depth = len(axes)
        self.own, self.came = refs[0], refs[1 : 1 + depth]
        self.sums = refs[1 + depth : 1 + 2 * depth]
        self.turn, self.line, self.result, self.load_sem = refs[1 + 2 * depth : 5 + 2 * depth]
        sems = refs[5 + 2 * depth :]
        self.sems = [sems[2 * i : 2 * i + 2] for i in range(depth + 1)]
        self.z = lax.axis_index("z")
        self.mine = [lax.axis_index(a) for a in axes]
        self.rows = part.shape[-2] // chunks
        self.flying = [[None] * chunks for _ in axes]

    @staticmethod
    def scratch(part, axes, chunks):
        n_z, rows, width, kind = part.shape[0], part.shape[-2], part.shape[-1], part.dtype
        depth = len(axes)

        def buffer(i):
            return pltpu.VMEM((chunks, n_z) + (2,) * i + (rows // chunks, width), kind)

        shapes = [buffer(depth - 1)] + [buffer(i) for i in range(depth)] * 2
        shapes += [buffer(0), pltpu.VMEM((chunks, n_z + 1, rows // chunks, width), kind)]
        shapes += [pltpu.VMEM((rows // chunks, width), jnp.float32)]
        shapes += [pltpu.SemaphoreType.DMA((chunks,))]
        for _ in range(depth):
            shapes += dma_pair(chunks)
        return shapes + dma_pair(chunks * (n_z + 1))

    def start(self):
        level = len(self.axes) - 1
        lead = (slice(None),) * len(self.axes)
        mine = self.mine[-1]
        self.loads = []
        for c in range(self.chunks):
            at = pl.ds(c * self.rows, self.rows)
            self.flying[level][c] = send(
                self.part.at[lead + (1 - mine, at)],
                self.came[level].at[c],
                self.sems[level],
                c,
                {self.axes[-1]: 1 - mine},
            )
            load = pltpu.make_async_copy(
                self.part.at[lead + (mine, at)], self.own.at[c], self.load_sem.at[c]
            )
            load.start()
            self.loads.append(load)

    def fold(self, level, c):
        self.flying[level][c].wait_recv()
        if level == len(self.axes) - 1:
            self.loads[c].wait()
            held = self.own[c]
        else:
            held = self.sums[level + 1][
                (c,) + (slice(None),) * (level + 1) + (self.mine[level],)
            ]
        total = held.astype(jnp.float32) + self.came[level][c].astype(jnp.float32)
        self.sums[level][c] = total.astype(held.dtype)
        if level > 0:
            mine = self.mine[level - 1]
            self.flying[level - 1][c] = send(
                self.sums[level].at[(c,) + (slice(None),) * level + (1 - mine,)],
                self.came[level - 1].at[c],
                self.sems[level - 1],
                c,
                {self.axes[level - 1]: 1 - mine},
            )

    def along(self, c, w, up):
        slot = w + 1 if up else w
        return pltpu.make_async_remote_copy(
            src_ref=self.turn.at[c, w],
            dst_ref=self.line.at[c, slot],
            send_sem=self.sems[-1][0].at[w * self.chunks + c],
            recv_sem=self.sems[-1][1].at[slot * self.chunks + c],
            device_id={"z": self.z + 1 if up else self.z - 1},
            device_id_type=MESH,
        )

    def steps(self):
        return [(3, True), (0, False), (2, True), (1, False), (1, True), (2, False)]

    def over_z(self, c, s):
        return pltpu.make_async_remote_copy(
            src_ref=self.sums[0].at[c, self.z ^ s],
            dst_ref=self.line.at[c, s],
            send_sem=self.sems[-1][0].at[s * self.chunks + c],
            recv_sem=self.sems[-1][1].at[s * self.chunks + c],
            device_id={"z": self.z ^ s},
            device_id_type=MESH,
        )

    def relay(self, c):
        z = self.z
        if self.direct:
            for s in (3, 2, 1):
                self.over_z(c, s).start()
            return
        for w, up in self.steps():
            slot = w + 1 if up else w

            @pl.when((z < w) if up else (z > w))
            def _(w=w, up=up, slot=slot):
                inner = (z > 0) if up else (z < 3)

                @pl.when(inner)
                def _():
                    self.along(c, w, up).wait_recv()
                    total = self.sums[0][c, w].astype(jnp.float32) + self.line[c, slot].astype(
                        jnp.float32
                    )
                    self.turn[c, w] = total.astype(self.turn.dtype)

                @pl.when(jnp.logical_not(inner))
                def _():
                    self.turn[c, w] = self.sums[0][c, w]

                self.along(c, w, up).start()

    def total(self, c):
        z = self.z
        if self.direct:
            total = self.sums[0][c, z].astype(jnp.float32)
            for s in (1, 2, 3):
                self.over_z(c, s).wait_recv()
                total = total + self.line[c, s].astype(jnp.float32)
            return total
        self.result[...] = self.sums[0][c, z].astype(jnp.float32)
        for up in (True, False):

            @pl.when((z > 0) if up else (z < 3))
            def _(up=up):
                self.along(c, z, up).wait_recv()
                self.result[...] += self.line[c, z + 1 if up else z].astype(jnp.float32)

        return self.result[...]

    lag = 1

    def length(self):
        return self.chunks + len(self.axes) + self.lag

    def advance(self, step, use):
        depth = len(self.axes)
        for level in range(depth - 1, -1, -1):
            c = step - (depth - 1 - level)
            if 0 <= c < self.chunks:
                self.fold(level, c)
        c = step - (depth - 1)
        if 0 <= c < self.chunks:
            self.relay(c)
        c = step - depth - self.lag + 1
        if 0 <= c < self.chunks:
            use(c, pl.ds(c * self.rows, self.rows), self.total(c))

    def run(self, use):
        for step in range(self.length()):
            self.advance(step, use)

    def finish(self):
        for copy in sum(self.flying, []):
            copy.wait_send()
        for c in range(self.chunks):
            if self.direct:
                for s in (1, 2, 3):
                    self.over_z(c, s).wait_send()
                continue
            for w, up in self.steps():

                @pl.when((self.z < w) if up else (self.z > w))
                def _(w=w, up=up, c=c):
                    self.along(c, w, up).wait_send()


class Gather:
    def __init__(self, own, out, axes, chunks, refs, direct=False):
        self.own, self.out, self.axes, self.chunks, self.direct = own, out, axes, chunks, direct
        self.keep_sem = refs[0]
        self.sems = [refs[1 + 2 * i : 3 + 2 * i] for i in range(len(axes) + 1)]
        self.z = lax.axis_index("z")
        self.mine = tuple(lax.axis_index(a) for a in axes)
        self.rows = own.shape[0] // chunks
        self.keeps = []

    @staticmethod
    def scratch(axes, chunks):
        shapes = [pltpu.SemaphoreType.DMA((chunks,)), *dma_pair(8 * chunks)]
        for i in range(len(axes)):
            shapes += dma_pair(4 * 2**i * chunks)
        return shapes

    def block(self, c, w, flips):
        places = tuple(
            1 - m if i < len(flips) and flips[i] else m for i, m in enumerate(self.mine)
        )
        return self.out.at[(w,) + places + (pl.ds(c * self.rows, self.rows),)]

    def along(self, c, w, up, own=False):
        where = self.block(c, w, ())
        return pltpu.make_async_remote_copy(
            src_ref=self.own.at[pl.ds(c * self.rows, self.rows)] if own else where,
            dst_ref=where,
            send_sem=self.sems[0][0].at[(w * 2 + int(up)) * self.chunks + c],
            recv_sem=self.sems[0][1].at[w * self.chunks + c],
            device_id={"z": self.z + 1 if up else self.z - 1},
            device_id_type=MESH,
        )

    def across(self, level, c, w, flips, own=False):
        where = self.block(c, w, flips)
        number = w
        for f in flips:
            number = number * 2 + f
        at = number * self.chunks + c
        return pltpu.make_async_remote_copy(
            src_ref=self.own.at[pl.ds(c * self.rows, self.rows)] if own else where,
            dst_ref=where,
            send_sem=self.sems[level + 1][0].at[at],
            recv_sem=self.sems[level + 1][1].at[at],
            device_id={self.axes[level]: 1 - self.mine[level]},
            device_id_type=MESH,
        )

    def over_z(self, c, s):
        where = self.block(c, self.z, ())
        return pltpu.make_async_remote_copy(
            src_ref=self.own.at[pl.ds(c * self.rows, self.rows)],
            dst_ref=where,
            send_sem=self.sems[0][0].at[s * self.chunks + c],
            recv_sem=self.sems[0][1].at[s * self.chunks + c],
            device_id={"z": self.z ^ s},
            device_id_type=MESH,
        )

    def start(self, c):
        z = self.z
        for s in (3, 2, 1) if self.direct else ():
            self.over_z(c, s).start()
        for up in () if self.direct else (True, False):

            @pl.when((z < 3) if up else (z > 0))
            def _(up=up):
                self.along(c, z, up, own=True).start()

        for level in range(len(self.axes)):
            self.across(level, c, z, (0,) * level, own=True).start()
        keep = pltpu.make_async_copy(
            self.own.at[pl.ds(c * self.rows, self.rows)], self.block(c, z, ()), self.keep_sem.at[c]
        )
        keep.start()
        self.keeps.append(keep)

    def forward(self, c, hops=(1, 2, 3)):
        z = self.z
        for s in hops if self.direct else ():
            self.over_z(c, s).wait_recv()
            for level in range(len(self.axes)):
                self.across(level, c, z ^ s, (0,) * level).start()
        for t in () if self.direct else hops:
            for up in (True, False):

                @pl.when((z >= t) if up else (z + t <= 3))
                def _(t=t, up=up):
                    w = z - t if up else z + t
                    self.along(c, w, up).wait_recv()

                    @pl.when((z < 3) if up else (z > 0))
                    def _():
                        self.along(c, w, up).start()

                    for level in range(len(self.axes)):
                        self.across(level, c, w, (0,) * level).start()

    def flips(self, level):
        return [tuple((i >> b) & 1 for b in range(level)) for i in range(2**level)]

    def spread(self, c):
        for level in range(len(self.axes) - 1):
            for s in range(4):
                for flips in self.flips(level):
                    w = self.z ^ s
                    turned = flips + (1,)
                    self.across(level, c, w, flips).wait_recv()
                    for later in range(level + 1, len(self.axes)):
                        self.across(later, c, w, turned + (0,) * (later - level - 1)).start()

    def finish(self):
        z, last = self.z, len(self.axes) - 1
        for keep in self.keeps:
            keep.wait()
        for c in range(self.chunks):
            for s in range(4):
                for flips in self.flips(last):
                    self.across(last, c, z ^ s, flips).wait_recv()
                for level in range(last + 1):
                    for flips in self.flips(level):
                        self.across(level, c, z ^ s, flips).wait_send()
            for s in (1, 2, 3) if self.direct else ():
                self.over_z(c, s).wait_send()
            for t in () if self.direct else (0, 1, 2, 3):
                for up in (True, False):
                    here = ((z >= t) & (z < 3)) if up else ((z + t <= 3) & (z > 0))

                    @pl.when(here)
                    def _(t=t, up=up, c=c):
                        self.along(c, z - t if up else z + t, up).wait_send()


VMEM_SPEC = pl.BlockSpec(memory_space=pltpu.VMEM)
ANY_SPEC = pl.BlockSpec(memory_space=pl.ANY)


def exchange(kernel, name, number, inputs, specs, outs, out_specs, scratch):
    sizes = [len(inputs), len(outs)] + [len(s) for s in scratch]

    def run(*refs):
        groups, at = [], 0
        for size in sizes:
            groups.append(refs[at : at + size])
            at += size
        kernel(*groups)

    return pl.pallas_call(
        run,
        out_shape=outs,
        in_specs=specs,
        out_specs=out_specs,
        scratch_shapes=sum(scratch, []),
        compiler_params=pltpu.CompilerParams(
            collective_id=number, has_side_effects=True, vmem_limit_bytes=48 * 2**20
        ),
        name=name,
    )(*inputs)


def share_inputs(tokens, slices, wo, marked, win, wout):
    count, own = tokens.shape[0], wo.shape[0]
    columns, wide = slices.shape[-1], marked.shape[-1]
    depth, half = win.shape[1], HID // 2
    number = 2 * win.shape[0] // 4
    chunks = 2
    bf16 = jnp.bfloat16

    def kernel(ins, outs, token_refs, wo_refs, marked_refs, other):
        tok, cut, wo_ref, marked_ref, win_ref, wout_ref = ins
        tok_out, cut_out, wo_out, marked_out = outs[:4]
        near, far = outs[4:8], outs[8:12]
        keep, ctx_sems, exp_sems = other[0], other[1:3], other[3:5]
        near_sems, far_sems, win_in, wout_in, unit = other[5:7], other[7:9], *other[9:12]
        z, y, x, k = (lax.axis_index(a) for a in ("z", "y", "x", "k"))
        loads = [
            pltpu.make_async_copy(win_ref, win_in, keep.at[1]),
            pltpu.make_async_copy(wout_ref, wout_in, keep.at[2]),
        ]
        for copy in loads:
            copy.start()
        exp_peers = [((x ^ a, k ^ b), a * 2 + b) for a in (1, 0) for b in (1, 0) if a or b]
        greet(
            [{"z": p, "y": q} for p, q, _ in ctx_peers()]
            + [{"x": p, "k": q} for (p, q), _ in exp_peers]
        )
        gather = Gather(tok, tok_out, ("y",), chunks, token_refs)
        whole = Gather(wo_ref, wo_out, ("y", "x", "k"), 1, wo_refs)
        other_rows = Gather(marked_ref, marked_out, ("x", "k"), 1, marked_refs)
        over_ctx = [
            send(cut.at[p, q], cut_out.at[z, y, x, k], ctx_sems, i - 1, {"z": p, "y": q})
            for p, q, i in ctx_peers()
        ]
        whole.start(0)
        for c in range(chunks):
            gather.start(c)
        other_rows.start(0)
        copy_own = pltpu.make_async_copy(cut.at[z, y], cut_out.at[z, y, x, k], keep.at[0])
        copy_own.start()

        def over_z(i, j):
            return pltpu.make_async_remote_copy(
                src_ref=unit.at[i, j],
                dst_ref=near[i].at[j],
                send_sem=near_sems[0].at[i * number + j],
                recv_sem=near_sems[1].at[i * number + j],
                device_id={"z": z ^ i},
                device_id_type=MESH,
            )

        def over_y(i, j):
            return pltpu.make_async_remote_copy(
                src_ref=near[i].at[j] if i else unit.at[0, j],
                dst_ref=far[i].at[j],
                send_sem=far_sems[0].at[i * number + j],
                recv_sem=far_sems[1].at[i * number + j],
                device_id={"y": 1 - y},
                device_id_type=MESH,
            )

        def own_unit(j):
            return pltpu.make_async_copy(unit.at[0, j], near[0].at[j], keep.at[3 + j])

        def convert(j):
            for i in range(4):
                index = number * (z ^ i) + j
                e, h = index // 2, lax.rem(index, 2)
                first = pl.ds(pl.multiple_of(h * half, half), half)
                second = pl.ds(pl.multiple_of(HID + h * half, half), half)
                unit[i, j, :, :half] = win_in[e, :, first].astype(bf16)
                unit[i, j, :, half : 2 * half] = win_in[e, :, second].astype(bf16)
                unit[i, j, :, 2 * half :] = wout_in[e, :, first].astype(bf16)

        def send_units(j):
            for i in (3, 2, 1):
                over_z(i, j).start()

        def pass_units(j):
            for i in (1, 2, 3):
                over_z(i, j).wait_recv()
                over_y(i, j).start()

        for copy in loads:
            copy.wait()
        convert(0)
        send_units(0)
        for j in range(number):
            if j:
                convert(j)
            own_unit(j).start()
            over_y(0, j).start()
        for t in (1, 2, 3):
            whole.forward(0, (t,))
            for c in range(chunks):
                gather.forward(c, (t,))
            other_rows.forward(0, (t,))
            send_units(t)
            if t == 1:
                for copy in over_ctx:
                    copy.wait_recv()
                copy_own.wait()
                mine = cut_out.at[:, :, x, k]
                over_exp = [
                    send(mine, mine, exp_sems, i - 1, {"x": p, "k": q})
                    for (p, q), i in exp_peers
                ]
            pass_units(t - 1)
        for j in range(4, number):
            send_units(j)
        whole.spread(0)
        other_rows.spread(0)
        for j in range(3, number):
            pass_units(j)
        for copy in over_exp:
            copy.wait_recv()
        gather.finish()
        whole.finish()
        other_rows.finish()
        for copy in over_ctx + over_exp:
            copy.wait_send()
        for j in range(number):
            own_unit(j).wait()
            for i in range(4):
                over_y(i, j).wait_recv()
                over_y(i, j).wait_send()
                if i:
                    over_z(i, j).wait_send()

    units = jax.ShapeDtypeStruct((number, depth, 3 * half), bf16)
    outs = exchange(
        kernel,
        "share_inputs",
        1,
        (tokens, slices, wo, marked, win, wout),
        [ANY_SPEC] * 6,
        [
            jax.ShapeDtypeStruct((4, 2, count, D), bf16),
            jax.ShapeDtypeStruct((4, 2, 2, 2, own, columns), bf16),
            jax.ShapeDtypeStruct((4, 2, 2, 2, own, D), bf16),
            jax.ShapeDtypeStruct((4, 2, 2, count, wide), bf16),
        ]
        + [units] * 8,
        [ANY_SPEC] * 12,
        [
            Gather.scratch(("y",), chunks),
            Gather.scratch(("y", "x", "k"), 1),
            Gather.scratch(("x", "k"), 1),
            [pltpu.SemaphoreType.DMA((3 + number,))]
            + dma_pair(7)
            + dma_pair(3)
            + dma_pair(4 * number)
            + dma_pair(4 * number)
            + [
                pltpu.VMEM(win.shape, jnp.float32),
                pltpu.VMEM(wout.shape, jnp.float32),
                pltpu.VMEM((4, number, depth, 3 * half), bf16),
            ],
        ],
    )
    return (*outs[:4], list(outs[4:]))


def ctx_peers():
    z, y = lax.axis_index("z"), lax.axis_index("y")
    return [(z ^ (i // 2), y ^ (i % 2), i) for i in range(7, 0, -1)]


def middle_step(heads, tokens, wo, gain):
    count, chunks = tokens.shape[0], 2
    width = heads.shape[-1]
    bf16, f32 = jnp.bfloat16, jnp.float32

    def kernel(ins, outs, hidden_refs, other):
        heads_ref, tok, wo_ref, gain_ref = ins
        attended_ref, middle_ref, hidden_out = outs
        own, sems = other[0], other[1:3]
        z, y = lax.axis_index("z"), lax.axis_index("y")
        greet(
            [{"z": p, "y": q} for p, q, _ in ctx_peers()] + siblings(("x", "k"))
        )
        hidden = Gather(own, hidden_out, ("x", "k"), chunks, hidden_refs)
        copies = [
            send(heads_ref.at[p, q], attended_ref.at[z, y], sems, i - 1, {"z": p, "y": q})
            for p, q, i in ctx_peers()
        ]
        attended_ref[z, y] = heads_ref[z, y]
        for copy in copies:
            copy.wait_recv()
        step = count // chunks
        middle = tok[...].astype(f32)
        for i in range(8):
            middle = middle + jnp.dot(
                attended_ref[i // 2, i % 2],
                wo_ref[i * width : (i + 1) * width, :],
                preferred_element_type=f32,
            )
        middle_ref[...] = middle
        for c in range(chunks):
            at = pl.ds(c * step, step)
            middle = middle_ref[at, :]
            scale = lax.rsqrt(jnp.mean(middle * middle, axis=-1, keepdims=True) + EPSILON)
            own[at, :] = (middle * scale * gain_ref[...]).astype(bf16)
            hidden.start(c)
        for c in range(chunks):
            hidden.forward(c)
            hidden.spread(c)
        hidden.finish()
        for copy in copies:
            copy.wait_send()

    return exchange(
        kernel,
        "middle_step",
        2,
        (heads, tokens, wo, gain),
        [VMEM_SPEC] * 4,
        [
            jax.ShapeDtypeStruct((4, 2, count, width), bf16),
            jax.ShapeDtypeStruct((count, D), f32),
            jax.ShapeDtypeStruct((4, 2, 2, count, D), bf16),
        ],
        [VMEM_SPEC, VMEM_SPEC, ANY_SPEC],
        [
            Gather.scratch(("x", "k"), chunks),
            [pltpu.VMEM((count, D), bf16)] + dma_pair(7),
        ],
    )


def router_step(part, mixed, middle, cotangent, gates, router, gain, wo, bulk, added):
    count, chunks = middle.shape[0], 4
    width, (number, depth, _) = wo.shape[0] // 8, added.shape
    bf16, f32 = jnp.bfloat16, jnp.float32

    def kernel(ins, outs, scatter_refs, mixed_refs, other):
        part_ref, mixed_ref, middle_ref, up_ref, gates_ref, router_ref, gain_ref, wo_ref = ins[:8]
        logit_ref, gain_out, grad_ref, heads_out, out_ref = outs[:5]
        turned, sems, bulk_sems, first_sems, far_sems = other[0], *(
            other[i : i + 2] for i in (1, 3, 5, 7)
        )
        own_unit, came_unit, load_sem = other[9:12]
        bulk_in, bulk_out, added_ref = ins[8:-1], outs[6:], ins[-1]
        far_out = outs[5]
        z, y = lax.axis_index("z"), lax.axis_index("y")
        load = pltpu.make_async_copy(added_ref, own_unit, load_sem.at[0])
        load.start()
        greet([{"z": p, "y": q} for p, q, _ in ctx_peers()] + siblings(("x", "k")))
        scatter = Scatter(part_ref, ("x", "k"), chunks, scatter_refs)
        mixture = Scatter(mixed_ref, ("x", "k"), chunks, mixed_refs)
        copies = []
        scatter.start()
        mixture.start()
        pieces = 2 * number
        piece = lambda ref, j: ref.at[j // 2, pl.ds(j % 2 * (depth // 2), depth // 2)]
        over_first = [
            send(piece(bulk_in[0], j), piece(came_unit, j), first_sems, j, {"y": 1 - y})
            for j in range(pieces)
        ]
        over_far = []
        bulk_copies = [send(bulk_in[1], bulk_out[0], bulk_sems, 0, {"y": 1 - y})]
        load.wait()

        def send_far(j):
            over_first[j].wait_recv()
            mine = piece(own_unit, j)
            total = mine[...].astype(f32) + piece(came_unit, j)[...].astype(f32)
            mine[...] = total.astype(bf16)
            over_far.append(send(mine, piece(far_out, j), far_sems, j, {"z": z ^ 3}))

        gain_out[...] = jnp.zeros_like(gain_out)

        def use(c, at, total):
            gate, gate_grad = gates_ref[at, :], total[:, D:]
            inner = jnp.sum(gate * gate_grad, axis=-1, keepdims=True)
            logit_grad = (gate * (gate_grad - inner)).astype(bf16)
            logit_ref[at, :] = logit_grad
            grad = total[:, :D] + contract_cols(logit_grad, router_ref[...])
            middle = middle_ref[at, :]
            scale = lax.rsqrt(jnp.mean(middle * middle, axis=-1, keepdims=True) + EPSILON)
            normed = middle * scale
            gain_out[...] += jnp.sum(grad * normed, axis=0, keepdims=True)
            scaled = grad * gain_ref[...]
            result = up_ref[at, :].astype(f32) + scale * (
                scaled - normed * jnp.mean(scaled * normed, axis=-1, keepdims=True)
            )
            grad_ref[at, :] = result

        def to_heads():
            down = grad_ref[...].astype(bf16)
            for i in range(8):
                turned[i // 2, i % 2] = contract_cols(
                    down, wo_ref[i * width : (i + 1) * width, :]
                ).astype(bf16)
            for p, q, i in ctx_peers():
                copies.append(
                    send(
                        turned.at[p, q], heads_out.at[z, y], sems, i - 1, {"z": p, "y": q}
                    )
                )
            heads_out[z, y] = turned[z, y]

        def use_mixture(c, at, total):
            out_ref[at, :] = (middle_ref[at, :] + total).astype(bf16)

        behind = 3
        plan = [[0], [1, 2], [3], [4], [5], [6], [7], [8], [9], []]
        for step in range(scatter.length() + behind):
            if step < scatter.length():
                scatter.advance(step, use)
            if step == scatter.length() - 1:
                to_heads()
            if step >= behind:
                mixture.advance(step - behind, use_mixture)
            for j in plan[step]:
                send_far(j)
        for copy in copies + bulk_copies + over_far:
            copy.wait_recv()
        for copy in copies + bulk_copies + over_first + over_far:
            copy.wait_send()
        scatter.finish()
        mixture.finish()

    return exchange(
        kernel,
        "router_step",
        3,
        (part, mixed, middle, cotangent, gates, router, gain, wo, *bulk, added),
        [ANY_SPEC] * 2 + [VMEM_SPEC] * 6 + [ANY_SPEC] * 3,
        [
            jax.ShapeDtypeStruct((count, 128), bf16),
            jax.ShapeDtypeStruct((1, D), f32),
            jax.ShapeDtypeStruct((count, D), f32),
            jax.ShapeDtypeStruct((4, 2, count, width), bf16),
            jax.ShapeDtypeStruct((count, D), bf16),
        ]
        + [jax.ShapeDtypeStruct(added.shape, bf16)] * 2,
        [VMEM_SPEC] * 5 + [ANY_SPEC] * 2,
        [
            Scatter.scratch(part, ("x", "k"), chunks),
            Scatter.scratch(mixed, ("x", "k"), chunks),
            [pltpu.VMEM((4, 2, count, width), bf16)] + dma_pair(7) + dma_pair(1) + dma_pair(2 * number) * 2
            + [pltpu.VMEM(added.shape, bf16)] * 2 + [pltpu.SemaphoreType.DMA((1,))],
        ],
    )


def last_step(
    part, tokens, grad_middle, gain, qkv_part, wo_part, small_part, bulk
):
    count, chunks = tokens.shape[0], 4
    own, columns = qkv_part.shape[-2:]
    bf16, f32 = jnp.bfloat16, jnp.float32

    def kernel(ins, outs, part_refs, wo_refs, other):
        part_ref, tok, grad_ref, gain_ref, qkv, wo, small = ins[:7]
        tokens_ref, qkv_out, wo_out, small_out = outs[:4]
        qkv_came, qkv_sum, small_came = other[:3]
        sems = [other[3 + 2 * i : 5 + 2 * i] for i in range(4)]
        names = ("z", "y", "x", "k")
        z, y, x, k = (lax.axis_index(a) for a in names)
        everyone = [
            ((z ^ (i // 8), y ^ (i // 4 % 2), x ^ (i // 2 % 2), k ^ (i % 2)), i)
            for i in range(31, 0, -1)
        ]
        of_ctx = [(p, i // 4) for p, i in everyone if i % 4 == 0]
        of_exp = [(p, i) for p, i in everyone if i < 4]
        place = lambda p: dict(zip(names, p))
        greet([place(p) for p, _ in everyone])
        first = Scatter(part_ref, ("y",), chunks, part_refs)
        third = Scatter(wo, ("y", "x", "k"), 3, wo_refs, True)
        first.start()
        third.start()
        over_qkv = [
            send(qkv.at[p[2], p[3]], qkv_came.at[i - 1], sems[0], i - 1, place(p))
            for p, i in of_exp
        ]
        def use_first(c, at, total):
            resid = tok[at, :].astype(f32)
            scale = lax.rsqrt(jnp.mean(resid * resid, axis=-1, keepdims=True) + EPSILON)
            normed = resid * scale
            scaled = total * gain_ref[...]
            tokens_ref[at, :] = grad_ref[at, :] + scale * (
                scaled - normed * jnp.mean(scaled * normed, axis=-1, keepdims=True)
            )

        def use_third(c, at, total):
            wo_out[at, :] = total

        number = bulk[0].shape[0]
        waiting = [(i, j) for j in range(number) for i in range(len(bulk))]
        over = [{"z": z ^ 1}, {"y": 1 - y}]
        over_bulk = []

        def send_bulk(most):
            for i, j in waiting[:most]:
                over_bulk.append(
                    send(
                        ins[7 + i].at[j],
                        outs[4 + i].at[j],
                        sems[3],
                        i * number + j,
                        over[i],
                    )
                )
            del waiting[:most]

        for step in range(third.length()):
            if step < first.length():
                first.advance(step, use_first)
            if step < third.length():
                third.advance(step, use_third)
            if step == 1:
                total = qkv[x, k].astype(f32)
                for copy, (_, i) in zip(over_qkv, of_exp):
                    copy.wait_recv()
                    total = total + qkv_came[i - 1].astype(f32)
                qkv_sum[...] = total.astype(bf16)
                qkv_out[z, y] = qkv_sum[z, y]
                over_ctx = [
                    send(qkv_sum.at[p[0], p[1]], qkv_out.at[z, y], sems[1], i - 1, place(p))
                    for p, i in of_ctx
                ]
                over_small = [
                    send(small.at[p], small_came.at[i - 1], sems[2], i - 1, place(p))
                    for p, i in everyone
                ]
            if step >= 2:
                send_bulk(2)
        send_bulk(len(waiting))
        total = small[z, y, x, k].astype(f32)
        for copy, (_, i) in zip(over_small, everyone):
            copy.wait_recv()
            total = total + small_came[i - 1].astype(f32)
        small_out[...] = total
        for copy in over_ctx + over_bulk:
            copy.wait_recv()
        first.finish()
        third.finish()
        for copy in over_qkv + over_ctx + over_small + over_bulk:
            copy.wait_send()

    return exchange(
        kernel,
        "last_step",
        4,
        (part, tokens, grad_middle, gain, qkv_part, wo_part, small_part, *bulk),
        [ANY_SPEC] + [VMEM_SPEC] * 4 + [ANY_SPEC, VMEM_SPEC] + [ANY_SPEC] * len(bulk),
        [
            jax.ShapeDtypeStruct((count, D), f32),
            jax.ShapeDtypeStruct((4, 2, own, columns), bf16),
            jax.ShapeDtypeStruct((own, D), f32),
            jax.ShapeDtypeStruct((own, 128), f32),
        ]
        + [jax.ShapeDtypeStruct(a.shape, a.dtype) for a in bulk],
        [VMEM_SPEC] * 4 + [ANY_SPEC] * len(bulk),
        [
            Scatter.scratch(part, ("y",), chunks),
            Scatter.scratch(wo_part, ("y", "x", "k"), 3),
            [
                pltpu.VMEM((3, 4, 2, own, columns), bf16),
                pltpu.VMEM((4, 2, own, columns), bf16),
                pltpu.VMEM((31, own, 128), bf16),
            ]
            + dma_pair(3)
            + dma_pair(7)
            + dma_pair(31)
            + dma_pair(len(bulk) * bulk[0].shape[0]),
        ],
    )


def pick(rows, columns, kind, test):
    row = lax.broadcasted_iota(jnp.int32, (rows, columns), 0)
    column = lax.broadcasted_iota(jnp.int32, (rows, columns), 1)
    return jnp.where(test(row, column), 1.0, 0.0).astype(kind)


def half_swap():
    to_first = pick(256, 256, jnp.float32, lambda r, c: (c % HEAD < HEAD // 2) & (r == c + HEAD // 2))
    to_second = pick(
        256, 256, jnp.float32, lambda r, c: (c % HEAD >= HEAD // 2) & (r + HEAD // 2 == c)
    )
    return to_second - to_first


def twice(a):
    return jnp.concatenate([a, a], axis=-1)


def exact_dot(left, right):
    return jnp.dot(
        left, right, preferred_element_type=jnp.float32, precision=lax.Precision.HIGHEST
    )


def attention_forward_kernel(
    tok, weight, gain, cosine, sine, rows, starts, key_rows, hidden, qk, keys, values, out, lse
):
    bf16, f32 = jnp.bfloat16, jnp.float32
    swap = half_swap()
    width = out.shape[-1]
    to_keys = pick(256, 256, bf16, lambda r, c: (c < width) & (r - width == c % HEAD))
    to_values = pick(128, 256, bf16, lambda r, c: (c < width) & (r == c % HEAD))
    block = 256
    steps = tok.shape[0] // block

    def project(b, carry):
        at = pl.ds(pl.multiple_of(b * block, block), block)
        x = tok[at, :].astype(f32)
        normed = x * lax.rsqrt(jnp.mean(x * x, axis=-1, keepdims=True) + EPSILON)
        h = (normed * gain[...]).astype(bf16)
        hidden[at, :] = h
        t = jnp.dot(h, weight[...], preferred_element_type=f32)
        u = t[:, :256]
        turned = (u * twice(cosine[at, :]) + exact_dot(u, swap) * twice(sine[at, :])).astype(bf16)
        qk[at, :] = turned
        keys[at, :] = jnp.dot(turned, to_keys, preferred_element_type=f32).astype(bf16)
        values[at, :] = jnp.dot(
            t[:, 256:].astype(bf16), to_values, preferred_element_type=f32
        ).astype(bf16)
        return carry

    lax.fori_loop(0, steps, project, 0)
    head = lax.broadcasted_iota(jnp.int32, (block, 256), 1) // HEAD
    lane = lax.broadcasted_iota(jnp.int32, (block, 128), 1)

    def attend(b, carry):
        at = pl.ds(pl.multiple_of(b * block, block), block)
        mask = (key_rows[...] <= rows[at, :]) & (key_rows[...] >= starts[at, :])
        result = jnp.zeros((block, 256), f32)
        logs = jnp.zeros((block, 128), f32)
        for h in range(HEADS // KV_HEADS):
            query = jnp.where(head == h, qk[at, :], jnp.zeros((), bf16))
            scores = contract_cols(query, keys[...]) * HEAD ** (-0.5)
            scores = jnp.where(mask, scores, NEGATIVE)
            top = jnp.max(scores, axis=-1, keepdims=True)
            weights = jnp.exp(scores - top)
            total = jnp.sum(weights, axis=-1, keepdims=True)
            mixed = jnp.dot(weights.astype(bf16), values[...], preferred_element_type=f32)
            result = jnp.where(head == h, mixed / total, result)
            logs = jnp.where(lane == h, top + jnp.log(total), logs)
        out[at, :] = result[:, :width].astype(bf16)
        lse[at, :] = logs
        return carry

    lax.fori_loop(0, steps, attend, 0)


def attention_forward(tokens, weight, gain, cosine, sine, rows, starts):
    count, width = tokens.shape[0], HEADS // KV_HEADS * HEAD
    bf16, f32 = jnp.bfloat16, jnp.float32
    shape = jax.ShapeDtypeStruct
    return pl.pallas_call(
        attention_forward_kernel,
        in_specs=[VMEM_SPEC] * 8,
        out_specs=[VMEM_SPEC] * 6,
        out_shape=[shape((count, D), bf16)]
        + [shape((count, 256), bf16)] * 3
        + [shape((count, width), bf16), shape((count, 128), f32)],
        compiler_params=pltpu.CompilerParams(vmem_limit_bytes=48 * 2**20),
        name="attention_forward",
    )(tokens, weight, gain, cosine, sine, rows[:, None], starts[:, None], rows[None, :])


def attention_backward_kernel(
    hidden, qk, keys, values, lse, upstream, weight, cosine, sine, rows, starts, key_rows,
    weight_grad, hidden_grad, grads, query_grad, key_grad, value_grad, up
):
    bf16, f32 = jnp.bfloat16, jnp.float32
    width = upstream.shape[-1]
    scale = HEAD ** (-0.5)
    block = 256
    steps = hidden.shape[0] // block
    head = lax.broadcasted_iota(jnp.int32, (block, 256), 1) // HEAD
    lane = lax.broadcasted_iota(jnp.int32, (block, 128), 1)
    up[...] = jnp.zeros_like(up)
    up[:, :width] = upstream[...]
    key_grad[...] = jnp.zeros_like(key_grad)
    value_grad[...] = jnp.zeros_like(value_grad)

    def attend(b, carry):
        at = pl.ds(pl.multiple_of(b * block, block), block)
        mask = (key_rows[...] <= rows[at, :]) & (key_rows[...] >= starts[at, :])
        logs = lse[at, :]
        result = jnp.zeros((block, 256), f32)
        for h in range(HEADS // KV_HEADS):
            zero = jnp.zeros((), bf16)
            query = jnp.where(head == h, qk[at, :], zero)
            grad = jnp.where(head == h, up[at, :], zero)
            log = jnp.sum(jnp.where(lane == h, logs, 0.0), axis=-1, keepdims=True)
            scores = contract_cols(query, keys[...]) * scale
            weights = jnp.where(mask, jnp.exp(scores - log), 0.0)
            prob_grad = contract_cols(grad, values[...])
            drift = jnp.sum(weights * prob_grad, axis=-1, keepdims=True)
            score_grad = (weights * (prob_grad - drift)).astype(bf16)
            part = jnp.dot(score_grad, keys[...], preferred_element_type=f32)
            result = jnp.where(head == h, part, result)
            key_grad[...] += contract_rows(score_grad, query)
            value_grad[...] += contract_rows(weights.astype(bf16), grad)
        query_grad[at, :] = result
        return carry

    lax.fori_loop(0, steps, attend, 0)
    swap = half_swap()
    from_keys = pick(256, 256, f32, lambda r, c: (r < width) & (c - width == r % HEAD))
    from_values = pick(256, 128, f32, lambda r, c: (r < width) & (c == r % HEAD))

    def turn(b, carry):
        at = pl.ds(pl.multiple_of(b * block, block), block)
        t = jnp.where(head < HEADS // KV_HEADS, query_grad[at, :], 0.0)
        t = (t + exact_dot(key_grad[at, :], from_keys)) * scale
        grads[at, :256] = (
            t * twice(cosine[at, :]) - exact_dot(t, swap) * twice(sine[at, :])
        ).astype(bf16)
        grads[at, 256:] = exact_dot(value_grad[at, :], from_values).astype(bf16)
        hidden_grad[at, :] = contract_cols(grads[at, :], weight[...]).astype(bf16)
        return carry

    lax.fori_loop(0, steps, turn, 0)
    parts, places, own, columns = weight_grad.shape
    for i in range(places // 2):
        deep = 2 * parts * own
        part = contract_rows(hidden[:, i * deep : (i + 1) * deep], grads[...]).astype(bf16)
        for j in range(2 * parts):
            weight_grad[j % parts, 2 * i + j // parts] = part[j * own : (j + 1) * own, :columns]


def attention_backward(hidden, qk, keys, values, lse, upstream, weight, cosine, sine, rows, starts, own):
    count = hidden.shape[0]
    bf16, f32 = jnp.bfloat16, jnp.float32
    shape = jax.ShapeDtypeStruct
    return pl.pallas_call(
        attention_backward_kernel,
        in_specs=[VMEM_SPEC] * 12,
        out_specs=[VMEM_SPEC] * 2,
        out_shape=[
            shape((4, D // own // 4, own, upstream.shape[-1] + 2 * HEAD), bf16),
            shape((count, D), bf16),
        ],
        scratch_shapes=[
            pltpu.VMEM((count, 384), bf16),
            pltpu.VMEM((count, 256), f32),
            pltpu.VMEM((count, 256), f32),
            pltpu.VMEM((count, 256), f32),
            pltpu.VMEM((count, 256), bf16),
        ],
        compiler_params=pltpu.CompilerParams(vmem_limit_bytes=48 * 2**20),
        name="attention_backward",
    )(
        hidden, qk, keys, values, lse, upstream, weight, cosine, sine,
        rows[:, None], starts[:, None], rows[None, :],
    )


def body_heads(
    tokens,
    cotangent,
    lengths,
    span_perm,
    routes,
    norm_attn,
    attn_q,
    attn_k,
    attn_v,
    attn_o,
    router,
    norm_moe,
    expert_in,
    expert_out,
):
    bf16, f32 = jnp.bfloat16, jnp.float32
    n_z, n_y = (lax.axis_size(a) for a in ("z", "y"))
    n_exp = lax.axis_size("x") * lax.axis_size("k")
    n_ctx = n_z * n_y
    exp_index = lax.axis_index("x") * lax.axis_size("k") + lax.axis_index("k")
    count = tokens.shape[1]
    group = count * n_ctx
    repeat = HEADS // KV_HEADS
    width = repeat * HEAD
    experts = EXP_DEV * n_exp
    capacity = count * TOP * 3 // (2 * experts)
    slots = -(-capacity // 8) * 8
    own = attn_q.shape[0]
    softmax_scale = HEAD ** (-0.5)
    z_index = lax.axis_index("z")

    units = 2 * EXP_DEV // n_z
    y_index = lax.axis_index("y")
    win = expert_in.transpose(1, 0, 2)
    wout = expert_out.transpose(1, 0, 2)
    swap_z = [[(i, i ^ s) for i in range(n_z)] for s in range(n_z)]
    swap_y = [(i, i ^ 1) for i in range(n_y)]
    swap_z = [[(i, i ^ s) for i in range(n_z)] for s in range(n_z)]
    swap_y = [(i, i ^ 1) for i in range(n_y)]

    wq, wk, wv = (a.astype(bf16) for a in (attn_q, attn_k, attn_v))
    own_qkv = jnp.concatenate(
        [
            wq.reshape(own, n_ctx, width),
            wk.reshape(own, n_ctx, HEAD),
            wv.reshape(own, n_ctx, HEAD),
        ],
        axis=-1,
    )
    small = jnp.concatenate(
        [
            router.astype(bf16),
            norm_attn.astype(bf16)[:, None],
            norm_moe.astype(bf16)[:, None],
            jnp.zeros((own, 64 - experts - 2), bf16),
        ],
        axis=1,
    )
    slices = jnp.concatenate(
        [own_qkv.transpose(1, 0, 2), jnp.broadcast_to(small, (n_ctx, own, 64))], axis=-1
    )
    marked = jnp.concatenate(
        [cotangent[0], routes[0].astype(bf16), jnp.zeros((count, 128 - TOP), bf16)], axis=1
    )
    token_all, slices, wo, marked_blocks, parts = share_inputs(
        tokens[0], slices.reshape(n_z, n_y, own, -1), attn_o.astype(bf16), marked, win, wout
    )
    token_all = token_all.reshape(group, D)
    slices = slices.reshape(D, -1)
    wo = wo.reshape(HEADS * HEAD, D)
    small = slices[:, width + 2 * HEAD :]
    weight_r = jnp.concatenate([small[:, :experts], jnp.zeros((D, 128 - experts), bf16)], axis=1)
    gain_one_f = small[:, experts].astype(f32)[None, :]
    gain_two_f = small[:, experts + 1].astype(f32)[None, :]

    perm_row = span_perm[0]
    first_len = lengths[0, 0]
    rows = global_rows(perm_row, jnp.arange(group, dtype=jnp.int32))
    starts = jnp.where(rows >= first_len, first_len, 0)
    freqs = jnp.exp(
        (jnp.arange(128) % (HEAD // 2)).astype(f32) * (-2.0 * math.log(10000.0) / HEAD)
    )
    angle = (rows - starts).astype(f32)[:, None] * freqs[None, :]
    cosine, sine = jnp.cos(angle), jnp.sin(angle)
    hidden_all, queries, keys, values, attended_b, log_total = attention_forward(
        token_all, slices, gain_one_f, cosine, sine, rows, starts
    )
    own_attended, middle, hidden_blocks = middle_step(
        attended_b.reshape(n_z, n_y, count, width), tokens[0], wo, gain_two_f
    )
    hidden_blocks = hidden_blocks.reshape(-1, count, D)
    marked_blocks = marked_blocks.reshape(-1, count, D + 128)

    blocks = hidden_blocks.shape[0]
    held = 3
    base = exp_index * EXP_DEV + (units * z_index) // 2
    shift = (units * z_index) % 2
    pairs = blocks // 2
    row_in, row_up, slot_gate, spread, gates_blocks = dispatch(
        base, hidden_blocks, marked_blocks, weight_r, held, slots
    )
    gates = lax.dynamic_index_in_dim(gates_blocks, z_index * n_exp + exp_index, 0, keepdims=False)

    def to_tokens(rows):
        a = jnp.einsum(
            "prt,prd->ptd",
            spread,
            rows.reshape(pairs, held * 2 * slots, -1),
            preferred_element_type=f32,
        )
        return a.astype(bf16).reshape(blocks, count, -1)

    meta = jnp.stack([shift, z_index, y_index, base]).astype(jnp.int32)
    made, back, *grads = run_experts(
        meta, row_in, row_up, slot_gate, parts
    )
    logit_grad, grad_gain_two, grad_middle, grad_heads, output, far_sum, other = router_step(
        to_tokens(back).reshape(n_z, 2, 2, count, D + 128),
        to_tokens(made).reshape(n_z, 2, 2, count, D),
        middle,
        cotangent[0],
        gates,
        weight_r,
        gain_two_f,
        wo,
        [grads[7], grads[6]],
        grads[3],
    )

    add = lambda a, b: (a.astype(f32) + b.astype(f32)).astype(bf16)
    sums = [None, None, add(grads[2], other), far_sum]
    sums[2], grads[5], grad_heads = lax.optimization_barrier((sums[2], grads[5], grad_heads))
    sums[2] = lax.ppermute(sums[2], "z", swap_z[2])
    other = lax.ppermute(grads[5], "y", swap_y)

    hidden_two = lax.dynamic_index_in_dim(
        hidden_blocks, z_index * n_exp + exp_index, 0, keepdims=False
    )
    small_grads = jnp.concatenate(
        [
            contract_rows(hidden_two, logit_grad)[:, : 128 - 1],
            grad_gain_two.reshape(D, 1),
        ],
        axis=1,
    )
    small_grads = small_grads.astype(bf16).reshape(n_z, n_y, 2, 2, own, 128)

    grad_wo = jnp.einsum(
        "cth,td->chd",
        own_attended.reshape(n_ctx, count, width),
        grad_middle.astype(bf16),
        preferred_element_type=f32,
    ).astype(bf16)
    grad_wqkv, grad_hidden = attention_backward(
        hidden_all,
        queries,
        keys,
        values,
        log_total,
        grad_heads.reshape(group, width),
        slices,
        cosine,
        sine,
        rows,
        starts,
        own,
    )
    grad_hidden = grad_hidden.reshape(n_z, n_y, count, D)
    sums[1] = add(grads[1], other)
    sums[1], grad_hidden = lax.optimization_barrier((sums[1], grad_hidden))
    grad_tokens, grad_wqkv, grad_wo, small_grads, *bulk = last_step(
        grad_hidden,
        tokens[0],
        grad_middle,
        gain_one_f,
        grad_wqkv.reshape(2, 2, n_z, n_y, own, width + 2 * HEAD),
        grad_wo.reshape(n_z, n_y, 2, 2, own, D),
        small_grads,
        [sums[1], grads[4]],
    )
    grad_expert_in, grad_expert_out = place_units(
        z_index, grads[0], bulk[1], bulk[0], sums[2], sums[3]
    )
    grad_expert_in = grad_expert_in.transpose(1, 0, 2)
    grad_expert_out = grad_expert_out.transpose(1, 0, 2)
    grad_wqkv = grad_wqkv.reshape(n_ctx, own, width + 2 * HEAD).astype(f32)
    grad_q = grad_wqkv[:, :, :width].transpose(1, 0, 2).reshape(own, HEADS * HEAD)
    grad_k = grad_wqkv[:, :, width : width + HEAD].transpose(1, 0, 2).reshape(own, KV_HEADS * HEAD)
    grad_v = grad_wqkv[:, :, width + HEAD :].transpose(1, 0, 2).reshape(own, KV_HEADS * HEAD)
    grad_gain_one = jnp.sum(
        grad_wqkv.transpose(1, 0, 2) * own_qkv.astype(f32), axis=(1, 2)
    ) / norm_attn.astype(bf16).astype(f32)
    return (
        output[None],
        grad_tokens[None],
        grad_gain_one,
        grad_q,
        grad_k,
        grad_v,
        grad_wo,
        small_grads[:, :experts],
        small_grads[:, 127],
        grad_expert_in,
        grad_expert_out,
    )


def solution(mesh):
    ctx, exp = mesh.shape["ctx"], mesh.shape["exp"]
    if ctx == KV_HEADS and exp == 4:
        names = ("z", "y", "x", "k")
        inner = jax.sharding.Mesh(mesh.devices.reshape(4, 2, 2, 2), names)
        body, ctx_name, exp_name, both = body_heads, names[:2], names[2:], names
    else:
        inner, body, ctx_name, exp_name, both = mesh, body_general, "ctx", "exp", ("ctx", "exp")
    token = P(exp_name, ctx_name, None)
    group = P(exp_name, None)
    expert = P(ctx_name, exp_name, None)
    rows, gain = P(both, None), P(both)
    in_specs = (token, token, group, group, token, gain) + (rows,) * 5 + (gain, expert, expert)
    out_specs = (token, token, gain) + (rows,) * 5 + (gain, expert, expert)
    return jax.shard_map(
        body, mesh=inner, in_specs=in_specs, out_specs=out_specs, check_vma=False
    )
```

```python
import math

import jax
import jax.numpy as jnp
from jax import lax
from jax.experimental import pallas as pl
from jax.experimental.pallas import tpu as pltpu
from jax.sharding import PartitionSpec as P

D = 1536
HEADS = 24
KV_HEADS = 8
HEAD = 64
HID = 512
TOP = 8
EXP_DEV = 10
SPAN = 64


EPSILON = 1e-06
LATE = 2
NEGATIVE = -1e30


def global_rows(perm_row, rows):
    slots = rows // SPAN
    match = slots[:, None] == jnp.arange(perm_row.shape[0], dtype=jnp.int32)[None, :]
    spans = jnp.sum(jnp.where(match, perm_row[None, :], 0), axis=1)
    return spans * SPAN + rows % SPAN


def rotary(tensor, position, sign):
    half = HEAD // 2
    freqs = jnp.exp(jnp.arange(half, dtype=jnp.float32) * (-2.0 * math.log(10000.0) / HEAD))
    angle = position.astype(jnp.float32)[:, None] * freqs[None, :]
    cosine = jnp.cos(angle)[:, None, :]
    sine = sign * jnp.sin(angle)[:, None, :]
    first, second = (tensor[..., :half], tensor[..., half:])
    return jnp.concatenate(
        [first * cosine - second * sine, second * cosine + first * sine], axis=-1
    )


def allowed(query_rows, key_rows, first_len):
    later = key_rows[None, :] <= query_rows[:, None]
    same_seq = (key_rows[None, :] >= first_len) == (query_rows[:, None] >= first_len)
    return later & same_seq


def contract_rows(left, right):
    return lax.dot_general(
        left, right, (((0,), (0,)), ((), ())), preferred_element_type=jnp.float32
    )


def contract_cols(left, right):
    return lax.dot_general(
        left, right, (((1,), (1,)), ((), ())), preferred_element_type=jnp.float32
    )


def block_grads(
    query_block,
    grad_block,
    lse_block,
    drift_block,
    query_rows,
    key_block,
    value_block,
    key_rows,
    first_len,
):
    softmax_scale = HEAD ** (-0.5)
    scores = (
        jnp.einsum("qgrd,kgd->grqk", query_block, key_block, preferred_element_type=jnp.float32)
        * softmax_scale
    )
    mask = allowed(query_rows, key_rows, first_len)[None, None]
    weights = jnp.where(mask, jnp.exp(scores - lse_block.transpose(1, 2, 0)[..., None]), 0.0)
    prob_grad = jnp.einsum(
        "qgrd,kgd->grqk", grad_block, value_block, preferred_element_type=jnp.float32
    )
    score_grad = (weights * (prob_grad - drift_block.transpose(1, 2, 0)[..., None])).astype(
        jnp.bfloat16
    )
    query_grad = None
    key_grad = None
    value_grad = None
    query_grad = (
        jnp.einsum("grqk,kgd->qgrd", score_grad, key_block, preferred_element_type=jnp.float32)
        * softmax_scale
    )
    value_grad = jnp.einsum(
        "grqk,qgrd->kgd",
        weights.astype(jnp.bfloat16),
        grad_block,
        preferred_element_type=jnp.float32,
    )
    key_grad = (
        jnp.einsum("grqk,qgrd->kgd", score_grad, query_block, preferred_element_type=jnp.float32)
        * softmax_scale
    )
    return (query_grad, key_grad, value_grad)


def body_general(
    tokens,
    cotangent,
    lengths,
    span_perm,
    routes,
    norm_attn,
    attn_q,
    attn_k,
    attn_v,
    attn_o,
    router,
    norm_moe,
    expert_in,
    expert_out,
):
    count = tokens.shape[1]
    repeat = HEADS // KV_HEADS
    experts = EXP_DEV * lax.axis_size("exp")
    capacity = count * TOP * 3 // (2 * experts)
    softmax_scale = HEAD ** (-0.5)
    perm_row = span_perm[0]
    first_len = lengths[0, 0]
    query_rows = global_rows(
        perm_row, lax.axis_index("ctx") * count + jnp.arange(count, dtype=jnp.int32)
    )
    position = query_rows - jnp.where(query_rows >= first_len, first_len, 0)
    gathered = (
        lax.all_gather(norm_attn.astype(jnp.bfloat16), ("ctx", "exp"), axis=0, tiled=True),
        lax.all_gather(attn_q.astype(jnp.bfloat16), ("ctx", "exp"), axis=0, tiled=True),
        lax.all_gather(attn_k.astype(jnp.bfloat16), ("ctx", "exp"), axis=0, tiled=True),
        lax.all_gather(attn_v.astype(jnp.bfloat16), ("ctx", "exp"), axis=0, tiled=True),
        lax.all_gather(attn_o.astype(jnp.bfloat16), ("ctx", "exp"), axis=0, tiled=True),
        lax.all_gather(router.astype(jnp.bfloat16), ("ctx", "exp"), axis=0, tiled=True),
        lax.all_gather(norm_moe.astype(jnp.bfloat16), ("ctx", "exp"), axis=0, tiled=True),
    )
    gain_one, weight_q, weight_k, weight_v, weight_o, weight_r, gain_two = gathered
    weight_in, weight_out = (
        lax.all_gather(expert_in.astype(jnp.bfloat16), "ctx", axis=0, tiled=True),
        lax.all_gather(expert_out.astype(jnp.bfloat16), "ctx", axis=0, tiled=True),
    )
    gain_one_f = gain_one.astype(jnp.float32)
    gain_two_f = gain_two.astype(jnp.float32)
    resid = tokens[0].astype(jnp.float32)
    scale_one = lax.rsqrt(jnp.mean(resid * resid, axis=-1, keepdims=True) + EPSILON)
    normed_one = resid * scale_one
    hidden_one = (normed_one * gain_one_f).astype(jnp.bfloat16)
    query_pre = jnp.dot(hidden_one, weight_q, preferred_element_type=jnp.float32).reshape(
        count, HEADS, HEAD
    )
    queries = (
        rotary(query_pre, position, 1.0).astype(jnp.bfloat16).reshape(count, KV_HEADS, repeat, HEAD)
    )
    key_pre = jnp.dot(hidden_one, weight_k, preferred_element_type=jnp.float32).reshape(
        count, KV_HEADS, HEAD
    )
    keys = rotary(key_pre, position, 1.0).astype(jnp.bfloat16)
    values = (
        jnp.dot(hidden_one, weight_v, preferred_element_type=jnp.float32)
        .astype(jnp.bfloat16)
        .reshape(count, KV_HEADS, HEAD)
    )
    start_state = (
        jnp.full((KV_HEADS, repeat, count), NEGATIVE, jnp.float32),
        jnp.zeros((KV_HEADS, repeat, count), jnp.float32),
        jnp.zeros((KV_HEADS, repeat, count, HEAD), jnp.float32),
    )
    carry = start_state
    key_piece = lax.all_gather(keys, "ctx", axis=0, tiled=True)
    value_piece = lax.all_gather(values, "ctx", axis=0, tiled=True)
    size = key_piece.shape[0]
    block = math.gcd(size, 512)
    number = size // block
    key_blocks = key_piece.reshape(number, block, KV_HEADS, HEAD)
    value_blocks = value_piece.reshape(number, block, KV_HEADS, HEAD)
    offsets = jnp.arange(size, dtype=jnp.int32).reshape(number, block)

    def forward_step(state, inputs):
        highest, total, accum = state
        key_block, value_block, offset = inputs
        key_rows = global_rows(perm_row, offset)
        scores = (
            jnp.einsum("qgrd,kgd->grqk", queries, key_block, preferred_element_type=jnp.float32)
            * softmax_scale
        )
        mask = allowed(query_rows, key_rows, first_len)[None, None]
        scores = jnp.where(mask, scores, NEGATIVE)
        newmax = jnp.maximum(highest, jnp.max(scores, axis=-1))
        weights = jnp.where(mask, jnp.exp(scores - newmax[..., None]), 0.0)
        factor = jnp.exp(highest - newmax)
        total = total * factor + jnp.sum(weights, axis=-1)
        accum = accum * factor[..., None] + jnp.einsum(
            "grqk,kgd->grqd",
            weights.astype(jnp.bfloat16),
            value_block,
            preferred_element_type=jnp.float32,
        )
        return ((newmax, total, accum), None)

    carry, _ = lax.scan(forward_step, carry, (key_blocks, value_blocks, offsets))
    highest, total, accum = carry
    log_total = (highest + jnp.log(total)).transpose(2, 0, 1)
    attended = (accum / total[..., None]).transpose(2, 0, 1, 3)
    attended_b = attended.reshape(count, HEADS * HEAD).astype(jnp.bfloat16)
    middle = resid + jnp.dot(attended_b, weight_o, preferred_element_type=jnp.float32)
    scale_two = lax.rsqrt(jnp.mean(middle * middle, axis=-1, keepdims=True) + EPSILON)
    normed_two = middle * scale_two
    hidden_two = (normed_two * gain_two_f).astype(jnp.bfloat16)
    logits = jnp.dot(hidden_two, weight_r, preferred_element_type=jnp.float32)
    chosen = routes[0]
    picks = chosen[:, :, None] == jnp.arange(experts, dtype=jnp.int32)[None, None, :]
    selected = jnp.sum(jnp.where(picks, logits[:, None, :], 0.0), axis=-1)
    gates = jax.nn.softmax(selected, axis=-1)
    gates_b = gates.astype(jnp.bfloat16)
    flat_picks = picks.reshape(count * TOP, experts).astype(jnp.int32)
    placed = jnp.sum((jnp.cumsum(flat_picks, axis=0) - 1) * flat_picks, axis=-1)
    column = chosen.reshape(-1) * capacity + placed
    hits = (
        column.reshape(count, TOP)[:, :, None]
        == jnp.arange(experts * capacity, dtype=jnp.int32)[None, None, :]
    )
    spread = jnp.any(hits, axis=1).astype(jnp.bfloat16)
    weighted = jnp.sum(
        jnp.where(hits, gates_b.astype(jnp.float32)[:, :, None], 0.0), axis=1
    ).astype(jnp.bfloat16)
    outgoing = contract_rows(spread, hidden_two).astype(jnp.bfloat16).reshape(experts, capacity, D)
    incoming = lax.all_to_all(outgoing, "exp", split_axis=0, concat_axis=1, tiled=True)
    gate_up = jnp.einsum("erd,dec->erc", incoming, weight_in, preferred_element_type=jnp.float32)
    gate_part = gate_up[..., :HID]
    up_part = gate_up[..., HID:]
    sigmoid_gate = jax.nn.sigmoid(gate_part)
    silu_gate = gate_part * sigmoid_gate
    activated = (silu_gate * up_part).astype(jnp.bfloat16)
    produced = jnp.einsum(
        "erh,deh->erd", activated, weight_out, preferred_element_type=jnp.float32
    ).astype(jnp.bfloat16)
    returned = lax.all_to_all(produced, "exp", split_axis=1, concat_axis=0, tiled=True).reshape(
        experts * capacity, D
    )
    mixture = jnp.dot(weighted, returned, preferred_element_type=jnp.float32)
    output = (middle + mixture).astype(jnp.bfloat16)
    upstream = cotangent[0].astype(jnp.float32)
    upstream_b = upstream.astype(jnp.bfloat16)
    sent_grad = (
        contract_rows(weighted, upstream_b).astype(jnp.bfloat16).reshape(experts, capacity, D)
    )
    grad_in = lax.all_to_all(sent_grad, "exp", split_axis=0, concat_axis=1, tiled=True)
    picked = jnp.take(returned, column, axis=0).reshape(count, TOP, D)
    gate_grad = jnp.einsum("tkd,td->tk", picked, upstream_b, preferred_element_type=jnp.float32)
    grad_act = (
        jnp.einsum("erd,deh->erh", grad_in, weight_out, preferred_element_type=jnp.float32)
        .astype(jnp.bfloat16)
        .astype(jnp.float32)
    )
    grad_gate = grad_act * up_part * (sigmoid_gate * (1.0 + gate_part * (1.0 - sigmoid_gate)))
    grad_up = grad_act * silu_gate
    grad_gu = jnp.concatenate([grad_gate, grad_up], axis=-1).astype(jnp.bfloat16)
    grad_weight_out = jnp.einsum(
        "erd,erh->deh", grad_in, activated, preferred_element_type=jnp.float32
    )
    grad_weight_in = jnp.einsum(
        "erd,erc->dec", incoming, grad_gu, preferred_element_type=jnp.float32
    )
    grad_rows = jnp.einsum(
        "erc,dec->erd", grad_gu, weight_in, preferred_element_type=jnp.float32
    ).astype(jnp.bfloat16)
    back_rows = lax.all_to_all(grad_rows, "exp", split_axis=1, concat_axis=0, tiled=True).reshape(
        experts * capacity, D
    )
    expert_sums = (
        lax.psum_scatter(
            grad_weight_in.astype(jnp.bfloat16), "ctx", scatter_dimension=0, tiled=True
        ).astype(jnp.float32),
        lax.psum_scatter(
            grad_weight_out.astype(jnp.bfloat16), "ctx", scatter_dimension=0, tiled=True
        ).astype(jnp.float32),
    )
    centered = gate_grad - jnp.sum(gates * gate_grad, axis=-1, keepdims=True)
    select_grad = gates * centered
    logit_grad = jnp.sum(jnp.where(picks, select_grad[:, :, None], 0.0), axis=1).astype(
        jnp.bfloat16
    )
    grad_router = contract_rows(hidden_two, logit_grad)
    grad_norm_two = jnp.dot(spread, back_rows, preferred_element_type=jnp.float32) + contract_cols(
        logit_grad, weight_r
    )
    grad_gain_two = jnp.sum(grad_norm_two * normed_two, axis=0)
    scaled_two = grad_norm_two * gain_two_f
    grad_middle = upstream + scale_two * (
        scaled_two - normed_two * jnp.mean(scaled_two * normed_two, axis=-1, keepdims=True)
    )
    branch_grad = grad_middle.astype(jnp.bfloat16)
    grad_weight_o = contract_rows(attended_b, branch_grad)
    grad_heads = (
        contract_cols(branch_grad, weight_o)
        .astype(jnp.bfloat16)
        .reshape(count, KV_HEADS, repeat, HEAD)
    )
    drift = jnp.sum(grad_heads.astype(jnp.float32) * attended, axis=-1)
    query_acc = jnp.zeros((count, KV_HEADS, repeat, HEAD), jnp.float32)
    key_piece = lax.all_gather(keys, "ctx", axis=0, tiled=True)
    value_piece = lax.all_gather(values, "ctx", axis=0, tiled=True)
    size = key_piece.shape[0]
    block = math.gcd(size, 512)
    number = size // block
    key_blocks = key_piece.reshape(number, block, KV_HEADS, HEAD)
    value_blocks = value_piece.reshape(number, block, KV_HEADS, HEAD)
    offsets = jnp.arange(size, dtype=jnp.int32).reshape(number, block)

    def backward_step(acc, inputs):
        key_block, value_block, offset = inputs
        part_q, part_k, part_v = block_grads(
            queries,
            grad_heads,
            log_total,
            drift,
            query_rows,
            key_block,
            value_block,
            global_rows(perm_row, offset),
            first_len,
        )
        joined = jnp.concatenate(
            [part_k.reshape(block, KV_HEADS * HEAD), part_v.reshape(block, KV_HEADS * HEAD)],
            axis=-1,
        )
        return (acc + part_q, joined)

    query_acc, joined_parts = lax.scan(
        backward_step, query_acc, (key_blocks, value_blocks, offsets)
    )
    pair_acc = joined_parts.reshape(size, 2 * KV_HEADS * HEAD)
    query_grad, pair_acc = (query_acc, pair_acc)
    pair_own = lax.psum_scatter(
        pair_acc.astype(jnp.bfloat16), "ctx", scatter_dimension=0, tiled=True
    ).astype(jnp.float32)
    key_grad = pair_own[:, : KV_HEADS * HEAD].reshape(count, KV_HEADS, HEAD)
    value_grad = pair_own[:, KV_HEADS * HEAD :].reshape(count, KV_HEADS, HEAD)
    query_grad_b = (
        rotary(query_grad.reshape(count, HEADS, HEAD), position, -1.0)
        .astype(jnp.bfloat16)
        .reshape(count, HEADS * HEAD)
    )
    key_grad_b = (
        rotary(key_grad, position, -1.0).astype(jnp.bfloat16).reshape(count, KV_HEADS * HEAD)
    )
    value_grad_b = value_grad.astype(jnp.bfloat16).reshape(count, KV_HEADS * HEAD)
    grad_weight_q = contract_rows(hidden_one, query_grad_b)
    grad_weight_k = contract_rows(hidden_one, key_grad_b)
    grad_weight_v = contract_rows(hidden_one, value_grad_b)
    grad_hidden_one = (
        contract_cols(query_grad_b, weight_q)
        + contract_cols(key_grad_b, weight_k)
        + contract_cols(value_grad_b, weight_v)
    )
    grad_gain_one = jnp.sum(grad_hidden_one * normed_one, axis=0)
    scaled_one = grad_hidden_one * gain_one_f
    grad_tokens = grad_middle + scale_one * (
        scaled_one - normed_one * jnp.mean(scaled_one * normed_one, axis=-1, keepdims=True)
    )
    attn_sums = (
        lax.psum_scatter(grad_gain_one, ("ctx", "exp"), scatter_dimension=0, tiled=True),
        lax.psum_scatter(grad_weight_q, ("ctx", "exp"), scatter_dimension=0, tiled=True),
        lax.psum_scatter(grad_weight_k, ("ctx", "exp"), scatter_dimension=0, tiled=True),
        lax.psum_scatter(grad_weight_v, ("ctx", "exp"), scatter_dimension=0, tiled=True),
        lax.psum_scatter(grad_weight_o, ("ctx", "exp"), scatter_dimension=0, tiled=True),
        lax.psum_scatter(grad_router, ("ctx", "exp"), scatter_dimension=0, tiled=True),
        lax.psum_scatter(grad_gain_two, ("ctx", "exp"), scatter_dimension=0, tiled=True),
    )
    return (
        output[None],
        grad_tokens[None],
        attn_sums[0],
        attn_sums[1],
        attn_sums[2],
        attn_sums[3],
        attn_sums[4],
        attn_sums[5],
        attn_sums[6],
        expert_sums[0],
        expert_sums[1],
    )


def rotate(tensor, cosine, sine):
    half = HEAD // 2
    first, second = (tensor[..., :half], tensor[..., half:])
    return jnp.concatenate(
        [first * cosine - second * sine, second * cosine + first * sine], axis=-1
    )


def dispatch_kernel(base, hid_ref, mark_ref, router_ref, rows_ref, up_ref, gate_ref, spread_ref, gates_ref):
    bf16, f32 = jnp.bfloat16, jnp.float32
    count = hid_ref.shape[1]
    _, held, rows, _ = rows_ref.shape
    slots = rows // 2
    both = 2 * count
    x = hid_ref[...].reshape(both, D)
    logits = jnp.dot(x, router_ref[...], preferred_element_type=f32)
    routes = mark_ref[:, :, D:].reshape(both, 128).astype(f32)
    lane = lax.broadcasted_iota(jnp.int32, (both, 128), 1).astype(f32)
    picks = jnp.zeros((both, 128), f32)
    for i in range(TOP):
        picks = jnp.where(routes[:, i : i + 1] == lane, 1.0, picks)
    masked = jnp.where(picks > 0.0, logits, NEGATIVE)
    top = jnp.max(masked, axis=-1, keepdims=True)
    gates = jnp.where(picks > 0.0, jnp.exp(masked - top), 0.0)
    gates = gates / jnp.sum(gates, axis=-1, keepdims=True)
    gates_ref[...] = gates.reshape(2, count, 128)
    which = lax.broadcasted_iota(jnp.int32, (8, 128), 0)
    columns = lax.broadcasted_iota(jnp.int32, (8, 128), 1)
    chosen = jnp.where(columns == which + base[0], 1.0, 0.0).astype(bf16)
    hit = contract_cols(chosen, picks.astype(bf16))
    gate = contract_cols(chosen, gates.astype(bf16))
    earlier = lax.broadcasted_iota(jnp.int32, (both, both), 0)
    later = lax.broadcasted_iota(jnp.int32, (both, both), 1)
    upto = jnp.where((earlier <= later) & (earlier // count == later // count), 1.0, 0.0)
    rank = jnp.dot(hit.astype(bf16), upto.astype(bf16), preferred_element_type=f32)
    row = lax.broadcasted_iota(jnp.int32, (rows, both), 0)
    token = lax.broadcasted_iota(jnp.int32, (rows, both), 1)
    side = row // slots
    wanted = jnp.where(side == token // count, row - side * slots + 1, -1).astype(f32)
    for e in range(held):
        here = jnp.where((rank[e : e + 1] == wanted) & (hit[e : e + 1] > 0.0), 1.0, 0.0)
        gate_ref[0, e] = jnp.sum(here * gate[e : e + 1], axis=-1, keepdims=True)
        here = here.astype(bf16)
        spread_ref[0, e * rows : (e + 1) * rows, :] = here
        rows_ref[0, e] = jnp.dot(here, x, preferred_element_type=f32).astype(bf16)
        up_ref[0, e] = jnp.dot(
            here, mark_ref[:, :, :D].reshape(both, D), preferred_element_type=f32
        ).astype(bf16)


def dispatch(base, hidden, marked, router, held, slots):
    blocks, count, _ = hidden.shape
    pairs = blocks // 2
    bf16, f32 = jnp.bfloat16, jnp.float32
    pair = lambda *shape: pl.BlockSpec((1,) + shape, lambda p, b: (p,) + (0,) * len(shape))
    two = lambda width: pl.BlockSpec((2, count, width), lambda p, b: (p, 0, 0))
    return pl.pallas_call(
        dispatch_kernel,
        grid_spec=pltpu.PrefetchScalarGridSpec(
            num_scalar_prefetch=1,
            grid=(pairs,),
            in_specs=[two(D), two(D + 128), pl.BlockSpec((D, 128), lambda p, b: (0, 0))],
            out_specs=[
                pair(held, 2 * slots, D),
                pair(held, 2 * slots, D),
                pair(held, 2 * slots, 1),
                pair(held * 2 * slots, 2 * count),
                two(128),
            ],
        ),
        out_shape=[
            jax.ShapeDtypeStruct((pairs, held, 2 * slots, D), bf16),
            jax.ShapeDtypeStruct((pairs, held, 2 * slots, D), bf16),
            jax.ShapeDtypeStruct((pairs, held, 2 * slots, 1), f32),
            jax.ShapeDtypeStruct((pairs, held * 2 * slots, 2 * count), bf16),
            jax.ShapeDtypeStruct((blocks, count, 128), f32),
        ],
        compiler_params=pltpu.CompilerParams(vmem_limit_bytes=48 * 2**20),
        name="dispatch",
    )(base.reshape(1).astype(jnp.int32), hidden, marked, router)


def expert_kernel(depth, meta, x_ref, g_ref, gate_ref, *refs):
    parts, (y_ref, d_ref), outs = refs[:10], refs[10:12], refs[12:20]
    weight, du_ref, act_ref = refs[20:]
    bf16, f32 = jnp.bfloat16, jnp.float32
    j = pl.program_id(0)
    shift, z, y, base = meta[0], meta[1], meta[2], meta[3]
    half = HID // 2
    offsets = [
        pl.multiple_of(((z ^ (i % 4)) * 2 + (y ^ (i // 4))) * depth, 64) for i in range(8)
    ]
    cut = pl.num_programs(0) - LATE
    for i, offset in enumerate(offsets):
        group = parts[i // 4 * 5 + i % 4 : i // 4 * 5 + i % 4 + (2 if i % 4 == 3 else 1)]
        for part, here in zip(group, (j < cut, j >= cut) if len(group) > 1 else (j >= 0,)):

            @pl.when(here)
            def _(part=part, offset=offset):
                weight[pl.ds(offset, depth), :] = part[0]

    expert = base + (j + shift) // 2
    first = jnp.logical_or(j == 0, lax.rem(j + shift, 2) == 0)
    keep = jnp.where(first, 0.0, 1.0)
    pairs, _, rows, _ = x_ref.shape
    step = 4

    def forward(i, carry):
        at = pl.ds(i * step, step)
        flat = pl.ds(pl.multiple_of(i * step * rows, 32), step * rows)
        x = x_ref[at, 0].reshape(step * rows, D)
        g = g_ref[at, 0].reshape(step * rows, D)
        gate = gate_ref[at, 0].reshape(step * rows, 1)
        u = jnp.dot(x, weight[:, : 2 * half], preferred_element_type=f32)
        raw = jnp.dot(g, weight[:, 2 * half :], preferred_element_type=f32)
        u1, u2 = u[:, :half], u[:, half:]
        sig = jax.nn.sigmoid(u1)
        silu = u1 * sig
        act = (silu * u2).astype(bf16).astype(f32)
        dgate = jnp.sum(raw * act, axis=-1, keepdims=True)
        dact = raw * gate
        du1 = dact * u2 * (sig * (1.0 + u1 * (1.0 - sig)))
        du = jnp.concatenate([du1, dact * silu], axis=-1).astype(bf16)
        act_gated = (act * gate).astype(bf16)
        du_ref[flat, :] = du
        act_ref[flat, :] = act_gated
        made = contract_cols(act_gated, weight[:, 2 * half :])
        back = contract_cols(du, weight[:, : 2 * half])
        lane = lax.broadcasted_iota(jnp.int32, (step * rows, 128), 1)
        tail = jnp.where(lane == expert, dgate, 0.0)

        @pl.when(first)
        def _():
            y_ref[at, 0] = made.astype(bf16).reshape(step, rows, D)
            d_ref[at, 0, :, :D] = back.astype(bf16).reshape(step, rows, D)
            d_ref[at, 0, :, D:] = tail.astype(bf16).reshape(step, rows, 128)

        @pl.when(jnp.logical_not(first))
        def _():
            old_y = y_ref[at, 0].reshape(step * rows, D).astype(f32)
            y_ref[at, 0] = (made + old_y).astype(bf16).reshape(step, rows, D)
            old_d = d_ref[at, 0].reshape(step * rows, D + 128).astype(f32)
            d_ref[at, 0, :, :D] = (back + old_d[:, :D]).astype(bf16).reshape(step, rows, D)
            d_ref[at, 0, :, D:] = (tail + old_d[:, D:]).astype(bf16).reshape(step, rows, 128)

        return carry

    lax.fori_loop(0, pairs // step, forward, 0)

    wide = D // 2

    def gradient(i, carry):
        at = pl.ds(pl.multiple_of(i * wide, wide), wide)
        x = x_ref[:, 0, :, at].reshape(pairs * rows, wide)
        g = g_ref[:, 0, :, at].reshape(pairs * rows, wide)
        weight[at, : 2 * half] = contract_rows(x, du_ref[...]).astype(bf16)
        weight[at, 2 * half :] = contract_rows(g, act_ref[...]).astype(bf16)
        return carry

    lax.fori_loop(0, D // wide, gradient, 0)
    for out, offset in zip(outs, offsets):
        out[0] = weight[pl.ds(offset, depth), :]


def run_experts(meta, row_in, row_up, slot_gate, parts):
    pairs, held, rows, _ = row_in.shape
    units, depth, columns = parts[0].shape
    held_block = lambda width: pl.BlockSpec(
        (pairs, 1, rows, width), lambda j, m: (0, (j + m[0]) // 2, 0, 0)
    )
    unit_block = pl.BlockSpec((1, depth, columns), lambda j, m: (j, 0, 0))
    cut = units - LATE
    early_block = pl.BlockSpec((1, depth, columns), lambda j, m: (jnp.minimum(j, cut - 1), 0, 0))
    late_block = pl.BlockSpec((1, depth, columns), lambda j, m: (jnp.maximum(j - cut, 0), 0, 0))
    bf16 = jnp.bfloat16
    total = units * pairs * rows * D * columns * 6
    return pl.pallas_call(
        lambda *refs: expert_kernel(depth, *refs),
        grid_spec=pltpu.PrefetchScalarGridSpec(
            num_scalar_prefetch=1,
            grid=(units,),
            in_specs=[
                held_block(D),
                held_block(D),
                held_block(1),
            ]
            + [unit_block, unit_block, unit_block, early_block, late_block] * 2,
            out_specs=[held_block(D), held_block(D + 128)] + [unit_block] * 8,
            scratch_shapes=[
                pltpu.VMEM((D, columns), bf16),
                pltpu.VMEM((pairs * rows, HID), bf16),
                pltpu.VMEM((pairs * rows, HID // 2), bf16),
            ],
        ),
        out_shape=[
            jax.ShapeDtypeStruct((pairs, held, rows, D), bf16),
            jax.ShapeDtypeStruct((pairs, held, rows, D + 128), bf16),
        ]
        + [jax.ShapeDtypeStruct((units, depth, columns), bf16)] * 8,
        compiler_params=pltpu.CompilerParams(vmem_limit_bytes=56 * 2**20),
        cost_estimate=pl.CostEstimate(
            flops=total, bytes_accessed=60 * 2**20, transcendentals=units * pairs * rows * HID
        ),
        name="experts",
    )(meta, row_in, row_up, slot_gate, *parts)


def place_kernel(number, z_ref, *refs):
    in_ref, out_ref = refs[12:]
    half = refs[0].shape[-1] // 3
    for h in range(2):
        unit = 2 * pl.program_id(0) + h
        source = (unit // number) ^ z_ref[0]
        late = (source == 3) & (lax.rem(unit, number) >= number - LATE)
        source = jnp.where(late, 4, source)
        first, other, *rest = refs[6 * h : 6 * h + 6]
        for i, group in enumerate([(first, other)] + [(ref,) for ref in rest]):

            @pl.when(source == i)
            def _(h=h, group=group):
                total = group[0][0].astype(jnp.float32)
                for ref in group[1:]:
                    total = total + ref[0].astype(jnp.float32)
                in_ref[0, :, h * half : (h + 1) * half] = total[:, :half]
                in_ref[0, :, HID + h * half : HID + (h + 1) * half] = total[:, half : 2 * half]
                out_ref[0, :, h * half : (h + 1) * half] = total[:, 2 * half :]


def place_units(z_index, first, other, near, mid, far, late):
    number, depth, columns = first.shape

    def block(i, h):
        low, most = {3: (0, number - LATE - 1), 4: (number - LATE, LATE - 1)}.get(i, (0, number - 1))

        def index(e, z):
            unit = 2 * e + h
            at = jnp.clip(lax.rem(unit, number) - low, 0, most)
            return jnp.where((unit // number) ^ z[0] == min(i, 3), at, 0), 0, 0

        return pl.BlockSpec((1, depth, columns), index)

    return pl.pallas_call(
        lambda *refs: place_kernel(number, *refs),
        grid_spec=pltpu.PrefetchScalarGridSpec(
            num_scalar_prefetch=1,
            grid=(EXP_DEV,),
            in_specs=[block(i, h) for h in range(2) for i in (0, 0, 1, 2, 3, 4)],
            out_specs=[
                pl.BlockSpec((1, depth, 2 * HID), lambda e, z: (e, 0, 0)),
                pl.BlockSpec((1, depth, HID), lambda e, z: (e, 0, 0)),
            ],
        ),
        out_shape=[
            jax.ShapeDtypeStruct((EXP_DEV, depth, 2 * HID), jnp.float32),
            jax.ShapeDtypeStruct((EXP_DEV, depth, HID), jnp.float32),
        ],
        name="place_units",
    )(z_index.reshape(1), *[first, other, near, mid, far, late] * 2)


MESH = pl.DeviceIdType.MESH


def greet(peers):
    barrier = pltpu.get_barrier_semaphore()
    for peer in peers:
        pl.semaphore_signal(barrier, inc=1, device_id=peer, device_id_type=MESH)
    pl.semaphore_wait(barrier, len(peers))


def send(src, dst, sems, at, peer):
    copy = pltpu.make_async_remote_copy(
        src_ref=src,
        dst_ref=dst,
        send_sem=sems[0].at[at],
        recv_sem=sems[1].at[at],
        device_id=peer,
        device_id_type=MESH,
    )
    copy.start()
    return copy


def dma_pair(number):
    return [pltpu.SemaphoreType.DMA((number,)), pltpu.SemaphoreType.DMA((number,))]


def z_peers():
    z = lax.axis_index("z")
    return [{"z": z ^ s} for s in (3, 2, 1)]


def siblings(axes):
    return [{a: 1 - lax.axis_index(a)} for a in axes]


class Scatter:
    def __init__(self, part, axes, chunks, refs, direct=False):
        self.part, self.axes, self.chunks, self.direct = part, axes, chunks, direct
        depth = len(axes)
        self.own, self.came = refs[0], refs[1 : 1 + depth]
        self.sums = refs[1 + depth : 1 + 2 * depth]
        self.turn, self.line, self.result, self.load_sem = refs[1 + 2 * depth : 5 + 2 * depth]
        sems = refs[5 + 2 * depth :]
        self.sems = [sems[2 * i : 2 * i + 2] for i in range(depth + 1)]
        self.z = lax.axis_index("z")
        self.mine = [lax.axis_index(a) for a in axes]
        self.rows = part.shape[-2] // chunks
        self.flying = [[None] * chunks for _ in axes]

    @staticmethod
    def scratch(part, axes, chunks):
        n_z, rows, width, kind = part.shape[0], part.shape[-2], part.shape[-1], part.dtype
        depth = len(axes)

        def buffer(i):
            return pltpu.VMEM((chunks, n_z) + (2,) * i + (rows // chunks, width), kind)

        shapes = [buffer(depth - 1)] + [buffer(i) for i in range(depth)] * 2
        shapes += [buffer(0), pltpu.VMEM((chunks, n_z + 1, rows // chunks, width), kind)]
        shapes += [pltpu.VMEM((rows // chunks, width), jnp.float32)]
        shapes += [pltpu.SemaphoreType.DMA((chunks,))]
        for _ in range(depth):
            shapes += dma_pair(chunks)
        return shapes + dma_pair(chunks * (n_z + 1))

    def start(self):
        level = len(self.axes) - 1
        lead = (slice(None),) * len(self.axes)
        mine = self.mine[-1]
        self.loads = []
        for c in range(self.chunks):
            at = pl.ds(c * self.rows, self.rows)
            self.flying[level][c] = send(
                self.part.at[lead + (1 - mine, at)],
                self.came[level].at[c],
                self.sems[level],
                c,
                {self.axes[-1]: 1 - mine},
            )
            load = pltpu.make_async_copy(
                self.part.at[lead + (mine, at)], self.own.at[c], self.load_sem.at[c]
            )
            load.start()
            self.loads.append(load)

    def fold(self, level, c):
        self.flying[level][c].wait_recv()
        if level == len(self.axes) - 1:
            self.loads[c].wait()
            held = self.own[c]
        else:
            held = self.sums[level + 1][
                (c,) + (slice(None),) * (level + 1) + (self.mine[level],)
            ]
        total = held.astype(jnp.float32) + self.came[level][c].astype(jnp.float32)
        self.sums[level][c] = total.astype(held.dtype)
        if level > 0:
            mine = self.mine[level - 1]
            self.flying[level - 1][c] = send(
                self.sums[level].at[(c,) + (slice(None),) * level + (1 - mine,)],
                self.came[level - 1].at[c],
                self.sems[level - 1],
                c,
                {self.axes[level - 1]: 1 - mine},
            )

    def along(self, c, w, up):
        slot = w + 1 if up else w
        return pltpu.make_async_remote_copy(
            src_ref=self.turn.at[c, w],
            dst_ref=self.line.at[c, slot],
            send_sem=self.sems[-1][0].at[w * self.chunks + c],
            recv_sem=self.sems[-1][1].at[slot * self.chunks + c],
            device_id={"z": self.z + 1 if up else self.z - 1},
            device_id_type=MESH,
        )

    def steps(self):
        return [(3, True), (0, False), (2, True), (1, False), (1, True), (2, False)]

    def over_z(self, c, s):
        return pltpu.make_async_remote_copy(
            src_ref=self.sums[0].at[c, self.z ^ s],
            dst_ref=self.line.at[c, s],
            send_sem=self.sems[-1][0].at[s * self.chunks + c],
            recv_sem=self.sems[-1][1].at[s * self.chunks + c],
            device_id={"z": self.z ^ s},
            device_id_type=MESH,
        )

    def relay(self, c):
        z = self.z
        if self.direct:
            for s in (3, 2, 1):
                self.over_z(c, s).start()
            return
        for w, up in self.steps():
            slot = w + 1 if up else w

            @pl.when((z < w) if up else (z > w))
            def _(w=w, up=up, slot=slot):
                inner = (z > 0) if up else (z < 3)

                @pl.when(inner)
                def _():
                    self.along(c, w, up).wait_recv()
                    total = self.sums[0][c, w].astype(jnp.float32) + self.line[c, slot].astype(
                        jnp.float32
                    )
                    self.turn[c, w] = total.astype(self.turn.dtype)

                @pl.when(jnp.logical_not(inner))
                def _():
                    self.turn[c, w] = self.sums[0][c, w]

                self.along(c, w, up).start()

    def total(self, c):
        z = self.z
        if self.direct:
            total = self.sums[0][c, z].astype(jnp.float32)
            for s in (1, 2, 3):
                self.over_z(c, s).wait_recv()
                total = total + self.line[c, s].astype(jnp.float32)
            return total
        self.result[...] = self.sums[0][c, z].astype(jnp.float32)
        for up in (True, False):

            @pl.when((z > 0) if up else (z < 3))
            def _(up=up):
                self.along(c, z, up).wait_recv()
                self.result[...] += self.line[c, z + 1 if up else z].astype(jnp.float32)

        return self.result[...]

    lag = 1

    def length(self):
        return self.chunks + len(self.axes) + self.lag

    def advance(self, step, use):
        depth = len(self.axes)
        for level in range(depth - 1, -1, -1):
            c = step - (depth - 1 - level)
            if 0 <= c < self.chunks:
                self.fold(level, c)
        c = step - (depth - 1)
        if 0 <= c < self.chunks:
            self.relay(c)
        c = step - depth - self.lag + 1
        if 0 <= c < self.chunks:
            use(c, pl.ds(c * self.rows, self.rows), self.total(c))

    def run(self, use):
        for step in range(self.length()):
            self.advance(step, use)

    def finish(self):
        for copy in sum(self.flying, []):
            copy.wait_send()
        for c in range(self.chunks):
            if self.direct:
                for s in (1, 2, 3):
                    self.over_z(c, s).wait_send()
                continue
            for w, up in self.steps():

                @pl.when((self.z < w) if up else (self.z > w))
                def _(w=w, up=up, c=c):
                    self.along(c, w, up).wait_send()


class Gather:
    def __init__(self, own, out, axes, chunks, refs, direct=False):
        self.own, self.out, self.axes, self.chunks, self.direct = own, out, axes, chunks, direct
        self.keep_sem = refs[0]
        self.sems = [refs[1 + 2 * i : 3 + 2 * i] for i in range(len(axes) + 1)]
        self.z = lax.axis_index("z")
        self.mine = tuple(lax.axis_index(a) for a in axes)
        self.rows = own.shape[0] // chunks
        self.keeps = []

    @staticmethod
    def scratch(axes, chunks):
        shapes = [pltpu.SemaphoreType.DMA((chunks,)), *dma_pair(8 * chunks)]
        for i in range(len(axes)):
            shapes += dma_pair(4 * 2**i * chunks)
        return shapes

    def block(self, c, w, flips):
        places = tuple(
            1 - m if i < len(flips) and flips[i] else m for i, m in enumerate(self.mine)
        )
        return self.out.at[(w,) + places + (pl.ds(c * self.rows, self.rows),)]

    def along(self, c, w, up, own=False):
        where = self.block(c, w, ())
        return pltpu.make_async_remote_copy(
            src_ref=self.own.at[pl.ds(c * self.rows, self.rows)] if own else where,
            dst_ref=where,
            send_sem=self.sems[0][0].at[(w * 2 + int(up)) * self.chunks + c],
            recv_sem=self.sems[0][1].at[w * self.chunks + c],
            device_id={"z": self.z + 1 if up else self.z - 1},
            device_id_type=MESH,
        )

    def across(self, level, c, w, flips, own=False):
        where = self.block(c, w, flips)
        number = w
        for f in flips:
            number = number * 2 + f
        at = number * self.chunks + c
        return pltpu.make_async_remote_copy(
            src_ref=self.own.at[pl.ds(c * self.rows, self.rows)] if own else where,
            dst_ref=where,
            send_sem=self.sems[level + 1][0].at[at],
            recv_sem=self.sems[level + 1][1].at[at],
            device_id={self.axes[level]: 1 - self.mine[level]},
            device_id_type=MESH,
        )

    def over_z(self, c, s):
        where = self.block(c, self.z, ())
        return pltpu.make_async_remote_copy(
            src_ref=self.own.at[pl.ds(c * self.rows, self.rows)],
            dst_ref=where,
            send_sem=self.sems[0][0].at[s * self.chunks + c],
            recv_sem=self.sems[0][1].at[s * self.chunks + c],
            device_id={"z": self.z ^ s},
            device_id_type=MESH,
        )

    def start(self, c):
        z = self.z
        for s in (3, 2, 1) if self.direct else ():
            self.over_z(c, s).start()
        for up in () if self.direct else (True, False):

            @pl.when((z < 3) if up else (z > 0))
            def _(up=up):
                self.along(c, z, up, own=True).start()

        for level in range(len(self.axes)):
            self.across(level, c, z, (0,) * level, own=True).start()
        keep = pltpu.make_async_copy(
            self.own.at[pl.ds(c * self.rows, self.rows)], self.block(c, z, ()), self.keep_sem.at[c]
        )
        keep.start()
        self.keeps.append(keep)

    def forward(self, c, hops=(1, 2, 3)):
        z = self.z
        for s in hops if self.direct else ():
            self.over_z(c, s).wait_recv()
            for level in range(len(self.axes)):
                self.across(level, c, z ^ s, (0,) * level).start()
        for t in () if self.direct else hops:
            for up in (True, False):

                @pl.when((z >= t) if up else (z + t <= 3))
                def _(t=t, up=up):
                    w = z - t if up else z + t
                    self.along(c, w, up).wait_recv()

                    @pl.when((z < 3) if up else (z > 0))
                    def _():
                        self.along(c, w, up).start()

                    for level in range(len(self.axes)):
                        self.across(level, c, w, (0,) * level).start()

    def flips(self, level):
        return [tuple((i >> b) & 1 for b in range(level)) for i in range(2**level)]

    def spread(self, c):
        for level in range(len(self.axes) - 1):
            for s in range(4):
                for flips in self.flips(level):
                    w = self.z ^ s
                    turned = flips + (1,)
                    self.across(level, c, w, flips).wait_recv()
                    for later in range(level + 1, len(self.axes)):
                        self.across(later, c, w, turned + (0,) * (later - level - 1)).start()

    def finish(self):
        z, last = self.z, len(self.axes) - 1
        for keep in self.keeps:
            keep.wait()
        for c in range(self.chunks):
            for s in range(4):
                for flips in self.flips(last):
                    self.across(last, c, z ^ s, flips).wait_recv()
                for level in range(last + 1):
                    for flips in self.flips(level):
                        self.across(level, c, z ^ s, flips).wait_send()
            for s in (1, 2, 3) if self.direct else ():
                self.over_z(c, s).wait_send()
            for t in () if self.direct else (0, 1, 2, 3):
                for up in (True, False):
                    here = ((z >= t) & (z < 3)) if up else ((z + t <= 3) & (z > 0))

                    @pl.when(here)
                    def _(t=t, up=up, c=c):
                        self.along(c, z - t if up else z + t, up).wait_send()


VMEM_SPEC = pl.BlockSpec(memory_space=pltpu.VMEM)
ANY_SPEC = pl.BlockSpec(memory_space=pl.ANY)


def exchange(kernel, name, number, inputs, specs, outs, out_specs, scratch):
    sizes = [len(inputs), len(outs)] + [len(s) for s in scratch]

    def run(*refs):
        groups, at = [], 0
        for size in sizes:
            groups.append(refs[at : at + size])
            at += size
        kernel(*groups)

    return pl.pallas_call(
        run,
        out_shape=outs,
        in_specs=specs,
        out_specs=out_specs,
        scratch_shapes=sum(scratch, []),
        compiler_params=pltpu.CompilerParams(
            collective_id=number, has_side_effects=True, vmem_limit_bytes=48 * 2**20
        ),
        name=name,
    )(*inputs)


def share_inputs(tokens, slices, wo, marked, win, wout):
    count, own = tokens.shape[0], wo.shape[0]
    columns, wide = slices.shape[-1], marked.shape[-1]
    depth, half = win.shape[1], HID // 2
    number = 2 * win.shape[0] // 4
    early = number - LATE
    chunks = 2
    bf16 = jnp.bfloat16

    def kernel(ins, outs, token_refs, wo_refs, marked_refs, other):
        tok, cut, wo_ref, marked_ref, win_ref, wout_ref = ins
        tok_out, cut_out, wo_out, marked_out = outs[:4]
        near, far, late = outs[4:8], (outs[8], None, *outs[9:11]), outs[11]
        keep, ctx_sems, exp_sems = other[0], other[1:3], other[3:5]
        near_sems, far_sems, win_in, wout_in, unit = other[5:7], other[7:9], *other[9:12]
        z, y, x, k = (lax.axis_index(a) for a in ("z", "y", "x", "k"))
        loads = [
            pltpu.make_async_copy(win_ref, win_in, keep.at[1]),
            pltpu.make_async_copy(wout_ref, wout_in, keep.at[2]),
        ]
        for copy in loads:
            copy.start()
        exp_peers = [((x ^ a, k ^ b), a * 2 + b) for a in (1, 0) for b in (1, 0) if a or b]
        greet(
            [{"z": p, "y": q} for p, q, _ in ctx_peers()]
            + [{"x": p, "k": q} for (p, q), _ in exp_peers]
        )
        gather = Gather(tok, tok_out, ("y",), chunks, token_refs)
        whole = Gather(wo_ref, wo_out, ("y", "x", "k"), 1, wo_refs)
        other_rows = Gather(marked_ref, marked_out, ("x", "k"), 1, marked_refs)
        over_ctx = [
            send(cut.at[p, q], cut_out.at[z, y, x, k], ctx_sems, i - 1, {"z": p, "y": q})
            for p, q, i in ctx_peers()
        ]
        whole.start(0)
        for c in range(chunks):
            gather.start(c)
        other_rows.start(0)
        copy_own = pltpu.make_async_copy(cut.at[z, y], cut_out.at[z, y, x, k], keep.at[0])
        copy_own.start()

        def over_z(i, j):
            return pltpu.make_async_remote_copy(
                src_ref=unit.at[i, j],
                dst_ref=near[i].at[j],
                send_sem=near_sems[0].at[i * number + j],
                recv_sem=near_sems[1].at[i * number + j],
                device_id={"z": z ^ i},
                device_id_type=MESH,
            )

        def over_y(i, j):
            return pltpu.make_async_remote_copy(
                src_ref=near[i].at[j] if i else unit.at[0, j],
                dst_ref=far[i].at[j],
                send_sem=far_sems[0].at[i * number + j],
                recv_sem=far_sems[1].at[i * number + j],
                device_id={"y": 1 - y},
                device_id_type=MESH,
            )

        def own_unit(j):
            return pltpu.make_async_copy(unit.at[0, j], near[0].at[j], keep.at[3 + j])

        def late_unit(j):
            return pltpu.make_async_copy(unit.at[3, j], late.at[j - early], keep.at[3 + number + j])

        def convert(j):
            for i in range(4):
                index = number * (z ^ i) + j
                e, h = index // 2, lax.rem(index, 2)
                first = pl.ds(pl.multiple_of(h * half, half), half)
                second = pl.ds(pl.multiple_of(HID + h * half, half), half)
                unit[i, j, :, :half] = win_in[e, :, first].astype(bf16)
                unit[i, j, :, half : 2 * half] = win_in[e, :, second].astype(bf16)
                unit[i, j, :, 2 * half :] = wout_in[e, :, first].astype(bf16)

        def send_units(j):
            for i in (3, 2, 1) if j < early else (2, 1):
                over_z(i, j).start()

        def pass_units(j):
            for i in (2, 3) if j < early else (2,):
                over_z(i, j).wait_recv()
                over_y(i, j).start()

        for copy in loads:
            copy.wait()
        convert(0)
        send_units(0)
        for j in range(number):
            if j:
                convert(j)
            own_unit(j).start()
            if j >= early:
                late_unit(j).start()
            over_y(0, j).start()
        for t in (1, 2, 3):
            whole.forward(0, (t,))
            for c in range(chunks):
                gather.forward(c, (t,))
            other_rows.forward(0, (t,))
            send_units(t)
            if t == 1:
                for copy in over_ctx:
                    copy.wait_recv()
                copy_own.wait()
                mine = cut_out.at[:, :, x, k]
                over_exp = [
                    send(mine, mine, exp_sems, i - 1, {"x": p, "k": q})
                    for (p, q), i in exp_peers
                ]
            pass_units(t - 1)
        for j in range(4, number):
            send_units(j)
        whole.spread(0)
        other_rows.spread(0)
        for j in range(3, number):
            pass_units(j)
        for copy in over_exp:
            copy.wait_recv()
        gather.finish()
        whole.finish()
        other_rows.finish()
        for copy in over_ctx + over_exp:
            copy.wait_send()
        for j in range(number):
            own_unit(j).wait()
            if j >= early:
                late_unit(j).wait()
            for i in range(4):
                if i == 3 and j >= early:
                    continue
                if i == 1:
                    over_z(i, j).wait_recv()
                else:
                    over_y(i, j).wait_recv()
                    over_y(i, j).wait_send()
                if i:
                    over_z(i, j).wait_send()

    units, most, few = (
        jax.ShapeDtypeStruct((n, depth, 3 * half), bf16) for n in (number, early, LATE)
    )
    outs = exchange(
        kernel,
        "share_inputs",
        1,
        (tokens, slices, wo, marked, win, wout),
        [ANY_SPEC] * 6,
        [
            jax.ShapeDtypeStruct((4, 2, count, D), bf16),
            jax.ShapeDtypeStruct((4, 2, 2, 2, own, columns), bf16),
            jax.ShapeDtypeStruct((4, 2, 2, 2, own, D), bf16),
            jax.ShapeDtypeStruct((4, 2, 2, count, wide), bf16),
        ]
        + [units] * 3
        + [most, units, units, most, few],
        [ANY_SPEC] * 12,
        [
            Gather.scratch(("y",), chunks),
            Gather.scratch(("y", "x", "k"), 1),
            Gather.scratch(("x", "k"), 1),
            [pltpu.SemaphoreType.DMA((3 + 2 * number,))]
            + dma_pair(7)
            + dma_pair(3)
            + dma_pair(4 * number)
            + dma_pair(4 * number)
            + [
                pltpu.VMEM(win.shape, jnp.float32),
                pltpu.VMEM(wout.shape, jnp.float32),
                pltpu.VMEM((4, number, depth, 3 * half), bf16),
            ],
        ],
    )
    return (*outs[:4], outs[4:8], outs[8:11], outs[11])


def ctx_peers():
    z, y = lax.axis_index("z"), lax.axis_index("y")
    return [(z ^ (i // 2), y ^ (i % 2), i) for i in range(7, 0, -1)]


def middle_step(heads, tokens, wo, gain, bulk):
    count, chunks = tokens.shape[0], 2
    width = heads.shape[-1]
    bf16, f32 = jnp.bfloat16, jnp.float32

    def kernel(ins, outs, hidden_refs, other):
        heads_ref, tok, wo_ref, gain_ref = ins[:4]
        attended_ref, middle_ref, hidden_out = outs[:3]
        own, sems, bulk_sems = other[0], other[1:3], other[3:5]
        z, y = lax.axis_index("z"), lax.axis_index("y")
        greet(
            [{"z": p, "y": q} for p, q, _ in ctx_peers()] + siblings(("x", "k"))
        )
        hidden = Gather(own, hidden_out, ("x", "k"), chunks, hidden_refs)
        copies = [
            send(heads_ref.at[p, q], attended_ref.at[z, y], sems, i - 1, {"z": p, "y": q})
            for p, q, i in ctx_peers()
        ]
        attended_ref[z, y] = heads_ref[z, y]
        bulk_copies = [
            send(a, b, bulk_sems, i, {"y": 1 - y}) for i, (a, b) in enumerate(zip(ins[4:], outs[3:]))
        ]
        for copy in copies:
            copy.wait_recv()
        step = count // chunks
        middle = tok[...].astype(f32)
        for i in range(8):
            middle = middle + jnp.dot(
                attended_ref[i // 2, i % 2],
                wo_ref[i * width : (i + 1) * width, :],
                preferred_element_type=f32,
            )
        middle_ref[...] = middle
        for c in range(chunks):
            at = pl.ds(c * step, step)
            middle = middle_ref[at, :]
            scale = lax.rsqrt(jnp.mean(middle * middle, axis=-1, keepdims=True) + EPSILON)
            own[at, :] = (middle * scale * gain_ref[...]).astype(bf16)
            hidden.start(c)
        for c in range(chunks):
            hidden.forward(c)
            hidden.spread(c)
        hidden.finish()
        for copy in bulk_copies:
            copy.wait_recv()
        for copy in copies + bulk_copies:
            copy.wait_send()

    return exchange(
        kernel,
        "middle_step",
        2,
        (heads, tokens, wo, gain, *bulk),
        [VMEM_SPEC] * 4 + [ANY_SPEC] * len(bulk),
        [
            jax.ShapeDtypeStruct((4, 2, count, width), bf16),
            jax.ShapeDtypeStruct((count, D), f32),
            jax.ShapeDtypeStruct((4, 2, 2, count, D), bf16),
        ]
        + [jax.ShapeDtypeStruct(a.shape, a.dtype) for a in bulk],
        [VMEM_SPEC, VMEM_SPEC, ANY_SPEC] + [ANY_SPEC] * len(bulk),
        [
            Gather.scratch(("x", "k"), chunks),
            [pltpu.VMEM((count, D), bf16)] + dma_pair(7) + dma_pair(len(bulk)),
        ],
    )


def router_step(part, mixed, middle, cotangent, gates, router, gain, wo, bulk, added):
    count, chunks = middle.shape[0], 4
    width, (number, depth, _) = wo.shape[0] // 8, added.shape
    early = number - LATE
    bf16, f32 = jnp.bfloat16, jnp.float32

    def kernel(ins, outs, scatter_refs, mixed_refs, other):
        part_ref, mixed_ref, middle_ref, up_ref, gates_ref, router_ref, gain_ref, wo_ref = ins[:8]
        logit_ref, gain_out, grad_ref, heads_out, out_ref = outs[:5]
        turned, sems, bulk_sems, first_sems, far_sems = other[0], *(
            other[i : i + 2] for i in (1, 3, 5, 7)
        )
        own_unit, came_unit, load_sem = other[9:12]
        bulk_in, bulk_out, added_ref = ins[8:-1], outs[6:], ins[-1]
        far_out = outs[5]
        z, y = lax.axis_index("z"), lax.axis_index("y")
        load = pltpu.make_async_copy(added_ref.at[pl.ds(0, early)], own_unit, load_sem.at[0])
        load.start()
        greet([{"z": p, "y": q} for p, q, _ in ctx_peers()] + siblings(("x", "k")))
        scatter = Scatter(part_ref, ("x", "k"), chunks, scatter_refs)
        mixture = Scatter(mixed_ref, ("x", "k"), chunks, mixed_refs)
        copies = []
        scatter.start()
        mixture.start()
        pieces = 2 * early
        piece = lambda ref, j: ref.at[j // 2, pl.ds(j % 2 * (depth // 2), depth // 2)]
        over_first = [
            send(piece(bulk_in[0], j), piece(came_unit, j), first_sems, j, {"y": 1 - y})
            for j in range(pieces)
        ]
        over_far = []
        bulk_copies = [
            send(
                bulk_in[0].at[pl.ds(early, number - early)], bulk_out[0], bulk_sems, 0, {"y": 1 - y}
            ),
            send(bulk_in[1], bulk_out[1], bulk_sems, 1, {"y": 1 - y}),
        ]
        load.wait()

        def send_far(j):
            over_first[j].wait_recv()
            mine = piece(own_unit, j)
            total = mine[...].astype(f32) + piece(came_unit, j)[...].astype(f32)
            mine[...] = total.astype(bf16)
            over_far.append(send(mine, piece(far_out, j), far_sems, j, {"z": z ^ 3}))

        gain_out[...] = jnp.zeros_like(gain_out)

        def use(c, at, total):
            gate, gate_grad = gates_ref[at, :], total[:, D:]
            inner = jnp.sum(gate * gate_grad, axis=-1, keepdims=True)
            logit_grad = (gate * (gate_grad - inner)).astype(bf16)
            logit_ref[at, :] = logit_grad
            grad = total[:, :D] + contract_cols(logit_grad, router_ref[...])
            middle = middle_ref[at, :]
            scale = lax.rsqrt(jnp.mean(middle * middle, axis=-1, keepdims=True) + EPSILON)
            normed = middle * scale
            gain_out[...] += jnp.sum(grad * normed, axis=0, keepdims=True)
            scaled = grad * gain_ref[...]
            result = up_ref[at, :].astype(f32) + scale * (
                scaled - normed * jnp.mean(scaled * normed, axis=-1, keepdims=True)
            )
            grad_ref[at, :] = result

        def to_heads():
            down = grad_ref[...].astype(bf16)
            for i in range(8):
                turned[i // 2, i % 2] = contract_cols(
                    down, wo_ref[i * width : (i + 1) * width, :]
                ).astype(bf16)
            for p, q, i in ctx_peers():
                copies.append(
                    send(
                        turned.at[p, q], heads_out.at[z, y], sems, i - 1, {"z": p, "y": q}
                    )
                )
            heads_out[z, y] = turned[z, y]
            bulk_copies.append(send(bulk_in[2], bulk_out[2], bulk_sems, 2, {"y": 1 - y}))

        def use_mixture(c, at, total):
            out_ref[at, :] = (middle_ref[at, :] + total).astype(bf16)

        behind = 3
        plan = [[0, 1], [2], [3], [4], [5]] + [[]] * 5
        for step in range(scatter.length() + behind):
            if step < scatter.length():
                scatter.advance(step, use)
            if step == scatter.length() - 1:
                to_heads()
            if step >= behind:
                mixture.advance(step - behind, use_mixture)
            for j in plan[step]:
                send_far(j)
        for copy in copies + bulk_copies + over_far:
            copy.wait_recv()
        for copy in copies + bulk_copies + over_first + over_far:
            copy.wait_send()
        scatter.finish()
        mixture.finish()

    return exchange(
        kernel,
        "router_step",
        3,
        (part, mixed, middle, cotangent, gates, router, gain, wo, *bulk, added),
        [ANY_SPEC] * 2 + [VMEM_SPEC] * 6 + [ANY_SPEC] * 4,
        [
            jax.ShapeDtypeStruct((count, 128), bf16),
            jax.ShapeDtypeStruct((1, D), f32),
            jax.ShapeDtypeStruct((count, D), f32),
            jax.ShapeDtypeStruct((4, 2, count, width), bf16),
            jax.ShapeDtypeStruct((count, D), bf16),
        ]
        + [
            jax.ShapeDtypeStruct((n, *added.shape[1:]), bf16)
            for n in (early, number - early, number, number)
        ],
        [VMEM_SPEC] * 5 + [ANY_SPEC] * 4,
        [
            Scatter.scratch(part, ("x", "k"), chunks),
            Scatter.scratch(mixed, ("x", "k"), chunks),
            [pltpu.VMEM((4, 2, count, width), bf16)] + dma_pair(7) + dma_pair(3) + dma_pair(2 * early) * 2
            + [pltpu.VMEM((early, *added.shape[1:]), bf16)] * 2 + [pltpu.SemaphoreType.DMA((1,))],
        ],
    )


def last_step(
    part, tokens, grad_middle, gain, qkv_part, wo_part, small_part
):
    count, chunks = tokens.shape[0], 4
    own, columns = qkv_part.shape[-2:]
    bf16, f32 = jnp.bfloat16, jnp.float32

    def kernel(ins, outs, part_refs, wo_refs, other):
        part_ref, tok, grad_ref, gain_ref, qkv, wo, small = ins
        tokens_ref, qkv_out, wo_out, small_out = outs
        qkv_came, qkv_sum, small_came = other[:3]
        sems = [other[3 + 2 * i : 5 + 2 * i] for i in range(3)]
        names = ("z", "y", "x", "k")
        z, y, x, k = (lax.axis_index(a) for a in names)
        everyone = [
            ((z ^ (i // 8), y ^ (i // 4 % 2), x ^ (i // 2 % 2), k ^ (i % 2)), i)
            for i in range(31, 0, -1)
        ]
        of_ctx = [(p, i // 4) for p, i in everyone if i % 4 == 0]
        of_exp = [(p, i) for p, i in everyone if i < 4]
        place = lambda p: dict(zip(names, p))
        greet([place(p) for p, _ in everyone])
        first = Scatter(part_ref, ("y",), chunks, part_refs)
        third = Scatter(wo, ("y", "x", "k"), 3, wo_refs, True)
        first.start()
        third.start()
        over_qkv = [
            send(qkv.at[p[2], p[3]], qkv_came.at[i - 1], sems[0], i - 1, place(p))
            for p, i in of_exp
        ]
        def use_first(c, at, total):
            resid = tok[at, :].astype(f32)
            scale = lax.rsqrt(jnp.mean(resid * resid, axis=-1, keepdims=True) + EPSILON)
            normed = resid * scale
            scaled = total * gain_ref[...]
            tokens_ref[at, :] = grad_ref[at, :] + scale * (
                scaled - normed * jnp.mean(scaled * normed, axis=-1, keepdims=True)
            )

        def use_third(c, at, total):
            wo_out[at, :] = total

        for step in range(third.length()):
            if step < first.length():
                first.advance(step, use_first)
            if step < third.length():
                third.advance(step, use_third)
            if step == 1:
                total = qkv[x, k].astype(f32)
                for copy, (_, i) in zip(over_qkv, of_exp):
                    copy.wait_recv()
                    total = total + qkv_came[i - 1].astype(f32)
                qkv_sum[...] = total.astype(bf16)
                qkv_out[z, y] = qkv_sum[z, y]
                over_ctx = [
                    send(qkv_sum.at[p[0], p[1]], qkv_out.at[z, y], sems[1], i - 1, place(p))
                    for p, i in of_ctx
                ]
                over_small = [
                    send(small.at[p], small_came.at[i - 1], sems[2], i - 1, place(p))
                    for p, i in everyone
                ]
        total = small[z, y, x, k].astype(f32)
        for copy, (_, i) in zip(over_small, everyone):
            copy.wait_recv()
            total = total + small_came[i - 1].astype(f32)
        small_out[...] = total
        for copy in over_ctx:
            copy.wait_recv()
        first.finish()
        third.finish()
        for copy in over_qkv + over_ctx + over_small:
            copy.wait_send()

    return exchange(
        kernel,
        "last_step",
        4,
        (part, tokens, grad_middle, gain, qkv_part, wo_part, small_part),
        [ANY_SPEC] + [VMEM_SPEC] * 4 + [ANY_SPEC, VMEM_SPEC],
        [
            jax.ShapeDtypeStruct((count, D), f32),
            jax.ShapeDtypeStruct((4, 2, own, columns), bf16),
            jax.ShapeDtypeStruct((own, D), f32),
            jax.ShapeDtypeStruct((own, 128), f32),
        ],
        [VMEM_SPEC] * 4,
        [
            Scatter.scratch(part, ("y",), chunks),
            Scatter.scratch(wo_part, ("y", "x", "k"), 3),
            [
                pltpu.VMEM((3, 4, 2, own, columns), bf16),
                pltpu.VMEM((4, 2, own, columns), bf16),
                pltpu.VMEM((31, own, 128), bf16),
            ]
            + dma_pair(3)
            + dma_pair(7)
            + dma_pair(31),
        ],
    )


def pick(rows, columns, kind, test):
    row = lax.broadcasted_iota(jnp.int32, (rows, columns), 0)
    column = lax.broadcasted_iota(jnp.int32, (rows, columns), 1)
    return jnp.where(test(row, column), 1.0, 0.0).astype(kind)


def half_swap():
    to_first = pick(256, 256, jnp.float32, lambda r, c: (c % HEAD < HEAD // 2) & (r == c + HEAD // 2))
    to_second = pick(
        256, 256, jnp.float32, lambda r, c: (c % HEAD >= HEAD // 2) & (r + HEAD // 2 == c)
    )
    return to_second - to_first


def twice(a):
    return jnp.concatenate([a, a], axis=-1)


def exact_dot(left, right):
    return jnp.dot(
        left, right, preferred_element_type=jnp.float32, precision=lax.Precision.HIGHEST
    )


def attention_forward_kernel(
    tok, weight, gain, cosine, sine, rows, starts, key_rows, hidden, qk, keys, values, out, lse
):
    bf16, f32 = jnp.bfloat16, jnp.float32
    swap = half_swap()
    width = out.shape[-1]
    to_keys = pick(256, 256, bf16, lambda r, c: (c < width) & (r - width == c % HEAD))
    to_values = pick(128, 256, bf16, lambda r, c: (c < width) & (r == c % HEAD))
    block = 256
    steps = tok.shape[0] // block

    def project(b, carry):
        at = pl.ds(pl.multiple_of(b * block, block), block)
        x = tok[at, :].astype(f32)
        normed = x * lax.rsqrt(jnp.mean(x * x, axis=-1, keepdims=True) + EPSILON)
        h = (normed * gain[...]).astype(bf16)
        hidden[at, :] = h
        t = jnp.dot(h, weight[...], preferred_element_type=f32)
        u = t[:, :256]
        turned = (u * twice(cosine[at, :]) + exact_dot(u, swap) * twice(sine[at, :])).astype(bf16)
        qk[at, :] = turned
        keys[at, :] = jnp.dot(turned, to_keys, preferred_element_type=f32).astype(bf16)
        values[at, :] = jnp.dot(
            t[:, 256:].astype(bf16), to_values, preferred_element_type=f32
        ).astype(bf16)
        return carry

    lax.fori_loop(0, steps, project, 0)
    head = lax.broadcasted_iota(jnp.int32, (block, 256), 1) // HEAD
    lane = lax.broadcasted_iota(jnp.int32, (block, 128), 1)

    def attend(b, carry):
        at = pl.ds(pl.multiple_of(b * block, block), block)
        mask = (key_rows[...] <= rows[at, :]) & (key_rows[...] >= starts[at, :])
        result = jnp.zeros((block, 256), f32)
        logs = jnp.zeros((block, 128), f32)
        for h in range(HEADS // KV_HEADS):
            query = jnp.where(head == h, qk[at, :], jnp.zeros((), bf16))
            scores = contract_cols(query, keys[...]) * HEAD ** (-0.5)
            scores = jnp.where(mask, scores, NEGATIVE)
            top = jnp.max(scores, axis=-1, keepdims=True)
            weights = jnp.exp(scores - top)
            total = jnp.sum(weights, axis=-1, keepdims=True)
            mixed = jnp.dot(weights.astype(bf16), values[...], preferred_element_type=f32)
            result = jnp.where(head == h, mixed / total, result)
            logs = jnp.where(lane == h, top + jnp.log(total), logs)
        out[at, :] = result[:, :width].astype(bf16)
        lse[at, :] = logs
        return carry

    lax.fori_loop(0, steps, attend, 0)


def attention_forward(tokens, weight, gain, cosine, sine, rows, starts):
    count, width = tokens.shape[0], HEADS // KV_HEADS * HEAD
    bf16, f32 = jnp.bfloat16, jnp.float32
    shape = jax.ShapeDtypeStruct
    return pl.pallas_call(
        attention_forward_kernel,
        in_specs=[VMEM_SPEC] * 8,
        out_specs=[VMEM_SPEC] * 6,
        out_shape=[shape((count, D), bf16)]
        + [shape((count, 256), bf16)] * 3
        + [shape((count, width), bf16), shape((count, 128), f32)],
        compiler_params=pltpu.CompilerParams(vmem_limit_bytes=48 * 2**20),
        name="attention_forward",
    )(tokens, weight, gain, cosine, sine, rows[:, None], starts[:, None], rows[None, :])


def attention_backward_kernel(
    hidden, qk, keys, values, lse, upstream, weight, cosine, sine, rows, starts, key_rows,
    weight_grad, hidden_grad, grads, query_grad, key_grad, value_grad, up
):
    bf16, f32 = jnp.bfloat16, jnp.float32
    width = upstream.shape[-1]
    scale = HEAD ** (-0.5)
    block = 256
    steps = hidden.shape[0] // block
    head = lax.broadcasted_iota(jnp.int32, (block, 256), 1) // HEAD
    lane = lax.broadcasted_iota(jnp.int32, (block, 128), 1)
    up[...] = jnp.zeros_like(up)
    up[:, :width] = upstream[...]
    key_grad[...] = jnp.zeros_like(key_grad)
    value_grad[...] = jnp.zeros_like(value_grad)

    def attend(b, carry):
        at = pl.ds(pl.multiple_of(b * block, block), block)
        mask = (key_rows[...] <= rows[at, :]) & (key_rows[...] >= starts[at, :])
        logs = lse[at, :]
        result = jnp.zeros((block, 256), f32)
        for h in range(HEADS // KV_HEADS):
            zero = jnp.zeros((), bf16)
            query = jnp.where(head == h, qk[at, :], zero)
            grad = jnp.where(head == h, up[at, :], zero)
            log = jnp.sum(jnp.where(lane == h, logs, 0.0), axis=-1, keepdims=True)
            scores = contract_cols(query, keys[...]) * scale
            weights = jnp.where(mask, jnp.exp(scores - log), 0.0)
            prob_grad = contract_cols(grad, values[...])
            drift = jnp.sum(weights * prob_grad, axis=-1, keepdims=True)
            score_grad = (weights * (prob_grad - drift)).astype(bf16)
            part = jnp.dot(score_grad, keys[...], preferred_element_type=f32)
            result = jnp.where(head == h, part, result)
            key_grad[...] += contract_rows(score_grad, query)
            value_grad[...] += contract_rows(weights.astype(bf16), grad)
        query_grad[at, :] = result
        return carry

    lax.fori_loop(0, steps, attend, 0)
    swap = half_swap()
    from_keys = pick(256, 256, f32, lambda r, c: (r < width) & (c - width == r % HEAD))
    from_values = pick(256, 128, f32, lambda r, c: (r < width) & (c == r % HEAD))

    def turn(b, carry):
        at = pl.ds(pl.multiple_of(b * block, block), block)
        t = jnp.where(head < HEADS // KV_HEADS, query_grad[at, :], 0.0)
        t = (t + exact_dot(key_grad[at, :], from_keys)) * scale
        grads[at, :256] = (
            t * twice(cosine[at, :]) - exact_dot(t, swap) * twice(sine[at, :])
        ).astype(bf16)
        grads[at, 256:] = exact_dot(value_grad[at, :], from_values).astype(bf16)
        hidden_grad[at, :] = contract_cols(grads[at, :], weight[...]).astype(bf16)
        return carry

    lax.fori_loop(0, steps, turn, 0)
    parts, places, own, columns = weight_grad.shape
    for i in range(places // 2):
        deep = 2 * parts * own
        part = contract_rows(hidden[:, i * deep : (i + 1) * deep], grads[...]).astype(bf16)
        for j in range(2 * parts):
            weight_grad[j % parts, 2 * i + j // parts] = part[j * own : (j + 1) * own, :columns]


def attention_backward(hidden, qk, keys, values, lse, upstream, weight, cosine, sine, rows, starts, own):
    count = hidden.shape[0]
    bf16, f32 = jnp.bfloat16, jnp.float32
    shape = jax.ShapeDtypeStruct
    return pl.pallas_call(
        attention_backward_kernel,
        in_specs=[VMEM_SPEC] * 12,
        out_specs=[VMEM_SPEC] * 2,
        out_shape=[
            shape((4, D // own // 4, own, upstream.shape[-1] + 2 * HEAD), bf16),
            shape((count, D), bf16),
        ],
        scratch_shapes=[
            pltpu.VMEM((count, 384), bf16),
            pltpu.VMEM((count, 256), f32),
            pltpu.VMEM((count, 256), f32),
            pltpu.VMEM((count, 256), f32),
            pltpu.VMEM((count, 256), bf16),
        ],
        compiler_params=pltpu.CompilerParams(vmem_limit_bytes=48 * 2**20),
        name="attention_backward",
    )(
        hidden, qk, keys, values, lse, upstream, weight, cosine, sine,
        rows[:, None], starts[:, None], rows[None, :],
    )


def body_heads(
    tokens,
    cotangent,
    lengths,
    span_perm,
    routes,
    norm_attn,
    attn_q,
    attn_k,
    attn_v,
    attn_o,
    router,
    norm_moe,
    expert_in,
    expert_out,
):
    bf16, f32 = jnp.bfloat16, jnp.float32
    n_z, n_y = (lax.axis_size(a) for a in ("z", "y"))
    n_exp = lax.axis_size("x") * lax.axis_size("k")
    n_ctx = n_z * n_y
    exp_index = lax.axis_index("x") * lax.axis_size("k") + lax.axis_index("k")
    count = tokens.shape[1]
    group = count * n_ctx
    repeat = HEADS // KV_HEADS
    width = repeat * HEAD
    experts = EXP_DEV * n_exp
    capacity = count * TOP * 3 // (2 * experts)
    slots = -(-capacity // 8) * 8
    own = attn_q.shape[0]
    softmax_scale = HEAD ** (-0.5)
    z_index = lax.axis_index("z")

    units = 2 * EXP_DEV // n_z
    y_index = lax.axis_index("y")
    win = expert_in.transpose(1, 0, 2)
    wout = expert_out.transpose(1, 0, 2)
    swap_z = [[(i, i ^ s) for i in range(n_z)] for s in range(n_z)]
    swap_y = [(i, i ^ 1) for i in range(n_y)]
    swap_z = [[(i, i ^ s) for i in range(n_z)] for s in range(n_z)]
    swap_y = [(i, i ^ 1) for i in range(n_y)]

    wq, wk, wv = (a.astype(bf16) for a in (attn_q, attn_k, attn_v))
    own_qkv = jnp.concatenate(
        [
            wq.reshape(own, n_ctx, width),
            wk.reshape(own, n_ctx, HEAD),
            wv.reshape(own, n_ctx, HEAD),
        ],
        axis=-1,
    )
    small = jnp.concatenate(
        [
            router.astype(bf16),
            norm_attn.astype(bf16)[:, None],
            norm_moe.astype(bf16)[:, None],
            jnp.zeros((own, 64 - experts - 2), bf16),
        ],
        axis=1,
    )
    slices = jnp.concatenate(
        [own_qkv.transpose(1, 0, 2), jnp.broadcast_to(small, (n_ctx, own, 64))], axis=-1
    )
    marked = jnp.concatenate(
        [cotangent[0], routes[0].astype(bf16), jnp.zeros((count, 128 - TOP), bf16)], axis=1
    )
    token_all, slices, wo, marked_blocks, near, far, late = share_inputs(
        tokens[0], slices.reshape(n_z, n_y, own, -1), attn_o.astype(bf16), marked, win, wout
    )
    late = lax.ppermute(late, "z", swap_z[3])
    token_all = token_all.reshape(group, D)
    slices = slices.reshape(D, -1)
    wo = wo.reshape(HEADS * HEAD, D)
    small = slices[:, width + 2 * HEAD :]
    weight_r = jnp.concatenate([small[:, :experts], jnp.zeros((D, 128 - experts), bf16)], axis=1)
    gain_one_f = small[:, experts].astype(f32)[None, :]
    gain_two_f = small[:, experts + 1].astype(f32)[None, :]

    perm_row = span_perm[0]
    first_len = lengths[0, 0]
    rows = global_rows(perm_row, jnp.arange(group, dtype=jnp.int32))
    starts = jnp.where(rows >= first_len, first_len, 0)
    freqs = jnp.exp(
        (jnp.arange(128) % (HEAD // 2)).astype(f32) * (-2.0 * math.log(10000.0) / HEAD)
    )
    angle = (rows - starts).astype(f32)[:, None] * freqs[None, :]
    cosine, sine = jnp.cos(angle), jnp.sin(angle)
    hidden_all, queries, keys, values, attended_b, log_total = attention_forward(
        token_all, slices, gain_one_f, cosine, sine, rows, starts
    )
    own_attended, middle, hidden_blocks, *passed = middle_step(
        attended_b.reshape(n_z, n_y, count, width), tokens[0], wo, gain_two_f, [near[1], late]
    )
    parts = [*near, late, far[0], passed[0], far[1], far[2], passed[1]]
    hidden_blocks = hidden_blocks.reshape(-1, count, D)
    marked_blocks = marked_blocks.reshape(-1, count, D + 128)

    blocks = hidden_blocks.shape[0]
    held = 3
    base = exp_index * EXP_DEV + (units * z_index) // 2
    shift = (units * z_index) % 2
    pairs = blocks // 2
    row_in, row_up, slot_gate, spread, gates_blocks = dispatch(
        base, hidden_blocks, marked_blocks, weight_r, held, slots
    )
    gates = lax.dynamic_index_in_dim(gates_blocks, z_index * n_exp + exp_index, 0, keepdims=False)

    def to_tokens(rows):
        a = jnp.einsum(
            "prt,prd->ptd",
            spread,
            rows.reshape(pairs, held * 2 * slots, -1),
            preferred_element_type=f32,
        )
        return a.astype(bf16).reshape(blocks, count, -1)

    meta = jnp.stack([shift, z_index, y_index, base]).astype(jnp.int32)
    made, back, *grads = run_experts(
        meta, row_in, row_up, slot_gate, parts
    )
    logit_grad, grad_gain_two, grad_middle, grad_heads, output, far_sum, *others = router_step(
        to_tokens(back).reshape(n_z, 2, 2, count, D + 128),
        to_tokens(made).reshape(n_z, 2, 2, count, D),
        middle,
        cotangent[0],
        gates,
        weight_r,
        gain_two_f,
        wo,
        [grads[7], grads[6], grads[5]],
        grads[3],
    )

    add = lambda a, b: (a.astype(f32) + b.astype(f32)).astype(bf16)
    late_sum, mid_sum = add(grads[3][-LATE:], others[0]), add(grads[2], others[1])
    late_sum, mid_sum, grads[4], grad_heads = lax.optimization_barrier(
        (late_sum, mid_sum, grads[4], grad_heads)
    )
    late_sum = lax.ppermute(late_sum, "z", swap_z[3])
    mid_sum = lax.ppermute(mid_sum, "z", swap_z[2])
    other = lax.ppermute(grads[4], "y", swap_y)
    near_sum = lax.ppermute(add(grads[1], others[2]), "z", swap_z[1])

    hidden_two = lax.dynamic_index_in_dim(
        hidden_blocks, z_index * n_exp + exp_index, 0, keepdims=False
    )
    small_grads = jnp.concatenate(
        [
            contract_rows(hidden_two, logit_grad)[:, : 128 - 1],
            grad_gain_two.reshape(D, 1),
        ],
        axis=1,
    )
    small_grads = small_grads.astype(bf16).reshape(n_z, n_y, 2, 2, own, 128)

    grad_wo = jnp.einsum(
        "cth,td->chd",
        own_attended.reshape(n_ctx, count, width),
        grad_middle.astype(bf16),
        preferred_element_type=f32,
    ).astype(bf16)
    grad_wqkv, grad_hidden = attention_backward(
        hidden_all,
        queries,
        keys,
        values,
        log_total,
        grad_heads.reshape(group, width),
        slices,
        cosine,
        sine,
        rows,
        starts,
        own,
    )
    grad_hidden = grad_hidden.reshape(n_z, n_y, count, D)
    grad_tokens, grad_wqkv, grad_wo, small_grads = last_step(
        grad_hidden,
        tokens[0],
        grad_middle,
        gain_one_f,
        grad_wqkv.reshape(2, 2, n_z, n_y, own, width + 2 * HEAD),
        grad_wo.reshape(n_z, n_y, 2, 2, own, D),
        small_grads,
    )
    grad_expert_in, grad_expert_out = place_units(
        z_index, grads[0], other, near_sum, mid_sum, far_sum, late_sum
    )
    grad_expert_in = grad_expert_in.transpose(1, 0, 2)
    grad_expert_out = grad_expert_out.transpose(1, 0, 2)
    grad_wqkv = grad_wqkv.reshape(n_ctx, own, width + 2 * HEAD).astype(f32)
    grad_q = grad_wqkv[:, :, :width].transpose(1, 0, 2).reshape(own, HEADS * HEAD)
    grad_k = grad_wqkv[:, :, width : width + HEAD].transpose(1, 0, 2).reshape(own, KV_HEADS * HEAD)
    grad_v = grad_wqkv[:, :, width + HEAD :].transpose(1, 0, 2).reshape(own, KV_HEADS * HEAD)
    grad_gain_one = jnp.sum(
        grad_wqkv.transpose(1, 0, 2) * own_qkv.astype(f32), axis=(1, 2)
    ) / norm_attn.astype(bf16).astype(f32)
    return (
        output[None],
        grad_tokens[None],
        grad_gain_one,
        grad_q,
        grad_k,
        grad_v,
        grad_wo,
        small_grads[:, :experts],
        small_grads[:, 127],
        grad_expert_in,
        grad_expert_out,
    )


def solution(mesh):
    ctx, exp = mesh.shape["ctx"], mesh.shape["exp"]
    if ctx == KV_HEADS and exp == 4:
        names = ("z", "y", "x", "k")
        inner = jax.sharding.Mesh(mesh.devices.reshape(4, 2, 2, 2), names)
        body, ctx_name, exp_name, both = body_heads, names[:2], names[2:], names
    else:
        inner, body, ctx_name, exp_name, both = mesh, body_general, "ctx", "exp", ("ctx", "exp")
    token = P(exp_name, ctx_name, None)
    group = P(exp_name, None)
    expert = P(ctx_name, exp_name, None)
    rows, gain = P(both, None), P(both)
    in_specs = (token, token, group, group, token, gain) + (rows,) * 5 + (gain, expert, expert)
    out_specs = (token, token, gain) + (rows,) * 5 + (gain, expert, expert)
    return jax.shard_map(
        body, mesh=inner, in_specs=in_specs, out_specs=out_specs, check_vma=False
    )
```

```python
import math

import jax
import jax.numpy as jnp
from jax import lax
from jax.experimental import pallas as pl
from jax.experimental.pallas import tpu as pltpu
from jax.sharding import PartitionSpec as P

D = 1536
HEADS = 24
KV_HEADS = 8
HEAD = 64
HID = 512
TOP = 8
EXP_DEV = 10
SPAN = 64


EPSILON = 1e-06
LATE = 2
NEGATIVE = -1e30


def global_rows(perm_row, rows):
    slots = rows // SPAN
    match = slots[:, None] == jnp.arange(perm_row.shape[0], dtype=jnp.int32)[None, :]
    spans = jnp.sum(jnp.where(match, perm_row[None, :], 0), axis=1)
    return spans * SPAN + rows % SPAN


def rotary(tensor, position, sign):
    half = HEAD // 2
    freqs = jnp.exp(jnp.arange(half, dtype=jnp.float32) * (-2.0 * math.log(10000.0) / HEAD))
    angle = position.astype(jnp.float32)[:, None] * freqs[None, :]
    cosine = jnp.cos(angle)[:, None, :]
    sine = sign * jnp.sin(angle)[:, None, :]
    first, second = (tensor[..., :half], tensor[..., half:])
    return jnp.concatenate(
        [first * cosine - second * sine, second * cosine + first * sine], axis=-1
    )


def allowed(query_rows, key_rows, first_len):
    later = key_rows[None, :] <= query_rows[:, None]
    same_seq = (key_rows[None, :] >= first_len) == (query_rows[:, None] >= first_len)
    return later & same_seq


def contract_rows(left, right):
    return lax.dot_general(
        left, right, (((0,), (0,)), ((), ())), preferred_element_type=jnp.float32
    )


def contract_cols(left, right):
    return lax.dot_general(
        left, right, (((1,), (1,)), ((), ())), preferred_element_type=jnp.float32
    )


def block_grads(
    query_block,
    grad_block,
    lse_block,
    drift_block,
    query_rows,
    key_block,
    value_block,
    key_rows,
    first_len,
):
    softmax_scale = HEAD ** (-0.5)
    scores = (
        jnp.einsum("qgrd,kgd->grqk", query_block, key_block, preferred_element_type=jnp.float32)
        * softmax_scale
    )
    mask = allowed(query_rows, key_rows, first_len)[None, None]
    weights = jnp.where(mask, jnp.exp(scores - lse_block.transpose(1, 2, 0)[..., None]), 0.0)
    prob_grad = jnp.einsum(
        "qgrd,kgd->grqk", grad_block, value_block, preferred_element_type=jnp.float32
    )
    score_grad = (weights * (prob_grad - drift_block.transpose(1, 2, 0)[..., None])).astype(
        jnp.bfloat16
    )
    query_grad = None
    key_grad = None
    value_grad = None
    query_grad = (
        jnp.einsum("grqk,kgd->qgrd", score_grad, key_block, preferred_element_type=jnp.float32)
        * softmax_scale
    )
    value_grad = jnp.einsum(
        "grqk,qgrd->kgd",
        weights.astype(jnp.bfloat16),
        grad_block,
        preferred_element_type=jnp.float32,
    )
    key_grad = (
        jnp.einsum("grqk,qgrd->kgd", score_grad, query_block, preferred_element_type=jnp.float32)
        * softmax_scale
    )
    return (query_grad, key_grad, value_grad)


def body_general(
    tokens,
    cotangent,
    lengths,
    span_perm,
    routes,
    norm_attn,
    attn_q,
    attn_k,
    attn_v,
    attn_o,
    router,
    norm_moe,
    expert_in,
    expert_out,
):
    count = tokens.shape[1]
    repeat = HEADS // KV_HEADS
    experts = EXP_DEV * lax.axis_size("exp")
    capacity = count * TOP * 3 // (2 * experts)
    softmax_scale = HEAD ** (-0.5)
    perm_row = span_perm[0]
    first_len = lengths[0, 0]
    query_rows = global_rows(
        perm_row, lax.axis_index("ctx") * count + jnp.arange(count, dtype=jnp.int32)
    )
    position = query_rows - jnp.where(query_rows >= first_len, first_len, 0)
    gathered = (
        lax.all_gather(norm_attn.astype(jnp.bfloat16), ("ctx", "exp"), axis=0, tiled=True),
        lax.all_gather(attn_q.astype(jnp.bfloat16), ("ctx", "exp"), axis=0, tiled=True),
        lax.all_gather(attn_k.astype(jnp.bfloat16), ("ctx", "exp"), axis=0, tiled=True),
        lax.all_gather(attn_v.astype(jnp.bfloat16), ("ctx", "exp"), axis=0, tiled=True),
        lax.all_gather(attn_o.astype(jnp.bfloat16), ("ctx", "exp"), axis=0, tiled=True),
        lax.all_gather(router.astype(jnp.bfloat16), ("ctx", "exp"), axis=0, tiled=True),
        lax.all_gather(norm_moe.astype(jnp.bfloat16), ("ctx", "exp"), axis=0, tiled=True),
    )
    gain_one, weight_q, weight_k, weight_v, weight_o, weight_r, gain_two = gathered
    weight_in, weight_out = (
        lax.all_gather(expert_in.astype(jnp.bfloat16), "ctx", axis=0, tiled=True),
        lax.all_gather(expert_out.astype(jnp.bfloat16), "ctx", axis=0, tiled=True),
    )
    gain_one_f = gain_one.astype(jnp.float32)
    gain_two_f = gain_two.astype(jnp.float32)
    resid = tokens[0].astype(jnp.float32)
    scale_one = lax.rsqrt(jnp.mean(resid * resid, axis=-1, keepdims=True) + EPSILON)
    normed_one = resid * scale_one
    hidden_one = (normed_one * gain_one_f).astype(jnp.bfloat16)
    query_pre = jnp.dot(hidden_one, weight_q, preferred_element_type=jnp.float32).reshape(
        count, HEADS, HEAD
    )
    queries = (
        rotary(query_pre, position, 1.0).astype(jnp.bfloat16).reshape(count, KV_HEADS, repeat, HEAD)
    )
    key_pre = jnp.dot(hidden_one, weight_k, preferred_element_type=jnp.float32).reshape(
        count, KV_HEADS, HEAD
    )
    keys = rotary(key_pre, position, 1.0).astype(jnp.bfloat16)
    values = (
        jnp.dot(hidden_one, weight_v, preferred_element_type=jnp.float32)
        .astype(jnp.bfloat16)
        .reshape(count, KV_HEADS, HEAD)
    )
    start_state = (
        jnp.full((KV_HEADS, repeat, count), NEGATIVE, jnp.float32),
        jnp.zeros((KV_HEADS, repeat, count), jnp.float32),
        jnp.zeros((KV_HEADS, repeat, count, HEAD), jnp.float32),
    )
    carry = start_state
    key_piece = lax.all_gather(keys, "ctx", axis=0, tiled=True)
    value_piece = lax.all_gather(values, "ctx", axis=0, tiled=True)
    size = key_piece.shape[0]
    block = math.gcd(size, 512)
    number = size // block
    key_blocks = key_piece.reshape(number, block, KV_HEADS, HEAD)
    value_blocks = value_piece.reshape(number, block, KV_HEADS, HEAD)
    offsets = jnp.arange(size, dtype=jnp.int32).reshape(number, block)

    def forward_step(state, inputs):
        highest, total, accum = state
        key_block, value_block, offset = inputs
        key_rows = global_rows(perm_row, offset)
        scores = (
            jnp.einsum("qgrd,kgd->grqk", queries, key_block, preferred_element_type=jnp.float32)
            * softmax_scale
        )
        mask = allowed(query_rows, key_rows, first_len)[None, None]
        scores = jnp.where(mask, scores, NEGATIVE)
        newmax = jnp.maximum(highest, jnp.max(scores, axis=-1))
        weights = jnp.where(mask, jnp.exp(scores - newmax[..., None]), 0.0)
        factor = jnp.exp(highest - newmax)
        total = total * factor + jnp.sum(weights, axis=-1)
        accum = accum * factor[..., None] + jnp.einsum(
            "grqk,kgd->grqd",
            weights.astype(jnp.bfloat16),
            value_block,
            preferred_element_type=jnp.float32,
        )
        return ((newmax, total, accum), None)

    carry, _ = lax.scan(forward_step, carry, (key_blocks, value_blocks, offsets))
    highest, total, accum = carry
    log_total = (highest + jnp.log(total)).transpose(2, 0, 1)
    attended = (accum / total[..., None]).transpose(2, 0, 1, 3)
    attended_b = attended.reshape(count, HEADS * HEAD).astype(jnp.bfloat16)
    middle = resid + jnp.dot(attended_b, weight_o, preferred_element_type=jnp.float32)
    scale_two = lax.rsqrt(jnp.mean(middle * middle, axis=-1, keepdims=True) + EPSILON)
    normed_two = middle * scale_two
    hidden_two = (normed_two * gain_two_f).astype(jnp.bfloat16)
    logits = jnp.dot(hidden_two, weight_r, preferred_element_type=jnp.float32)
    chosen = routes[0]
    picks = chosen[:, :, None] == jnp.arange(experts, dtype=jnp.int32)[None, None, :]
    selected = jnp.sum(jnp.where(picks, logits[:, None, :], 0.0), axis=-1)
    gates = jax.nn.softmax(selected, axis=-1)
    gates_b = gates.astype(jnp.bfloat16)
    flat_picks = picks.reshape(count * TOP, experts).astype(jnp.int32)
    placed = jnp.sum((jnp.cumsum(flat_picks, axis=0) - 1) * flat_picks, axis=-1)
    column = chosen.reshape(-1) * capacity + placed
    hits = (
        column.reshape(count, TOP)[:, :, None]
        == jnp.arange(experts * capacity, dtype=jnp.int32)[None, None, :]
    )
    spread = jnp.any(hits, axis=1).astype(jnp.bfloat16)
    weighted = jnp.sum(
        jnp.where(hits, gates_b.astype(jnp.float32)[:, :, None], 0.0), axis=1
    ).astype(jnp.bfloat16)
    outgoing = contract_rows(spread, hidden_two).astype(jnp.bfloat16).reshape(experts, capacity, D)
    incoming = lax.all_to_all(outgoing, "exp", split_axis=0, concat_axis=1, tiled=True)
    gate_up = jnp.einsum("erd,dec->erc", incoming, weight_in, preferred_element_type=jnp.float32)
    gate_part = gate_up[..., :HID]
    up_part = gate_up[..., HID:]
    sigmoid_gate = jax.nn.sigmoid(gate_part)
    silu_gate = gate_part * sigmoid_gate
    activated = (silu_gate * up_part).astype(jnp.bfloat16)
    produced = jnp.einsum(
        "erh,deh->erd", activated, weight_out, preferred_element_type=jnp.float32
    ).astype(jnp.bfloat16)
    returned = lax.all_to_all(produced, "exp", split_axis=1, concat_axis=0, tiled=True).reshape(
        experts * capacity, D
    )
    mixture = jnp.dot(weighted, returned, preferred_element_type=jnp.float32)
    output = (middle + mixture).astype(jnp.bfloat16)
    upstream = cotangent[0].astype(jnp.float32)
    upstream_b = upstream.astype(jnp.bfloat16)
    sent_grad = (
        contract_rows(weighted, upstream_b).astype(jnp.bfloat16).reshape(experts, capacity, D)
    )
    grad_in = lax.all_to_all(sent_grad, "exp", split_axis=0, concat_axis=1, tiled=True)
    picked = jnp.take(returned, column, axis=0).reshape(count, TOP, D)
    gate_grad = jnp.einsum("tkd,td->tk", picked, upstream_b, preferred_element_type=jnp.float32)
    grad_act = (
        jnp.einsum("erd,deh->erh", grad_in, weight_out, preferred_element_type=jnp.float32)
        .astype(jnp.bfloat16)
        .astype(jnp.float32)
    )
    grad_gate = grad_act * up_part * (sigmoid_gate * (1.0 + gate_part * (1.0 - sigmoid_gate)))
    grad_up = grad_act * silu_gate
    grad_gu = jnp.concatenate([grad_gate, grad_up], axis=-1).astype(jnp.bfloat16)
    grad_weight_out = jnp.einsum(
        "erd,erh->deh", grad_in, activated, preferred_element_type=jnp.float32
    )
    grad_weight_in = jnp.einsum(
        "erd,erc->dec", incoming, grad_gu, preferred_element_type=jnp.float32
    )
    grad_rows = jnp.einsum(
        "erc,dec->erd", grad_gu, weight_in, preferred_element_type=jnp.float32
    ).astype(jnp.bfloat16)
    back_rows = lax.all_to_all(grad_rows, "exp", split_axis=1, concat_axis=0, tiled=True).reshape(
        experts * capacity, D
    )
    expert_sums = (
        lax.psum_scatter(
            grad_weight_in.astype(jnp.bfloat16), "ctx", scatter_dimension=0, tiled=True
        ).astype(jnp.float32),
        lax.psum_scatter(
            grad_weight_out.astype(jnp.bfloat16), "ctx", scatter_dimension=0, tiled=True
        ).astype(jnp.float32),
    )
    centered = gate_grad - jnp.sum(gates * gate_grad, axis=-1, keepdims=True)
    select_grad = gates * centered
    logit_grad = jnp.sum(jnp.where(picks, select_grad[:, :, None], 0.0), axis=1).astype(
        jnp.bfloat16
    )
    grad_router = contract_rows(hidden_two, logit_grad)
    grad_norm_two = jnp.dot(spread, back_rows, preferred_element_type=jnp.float32) + contract_cols(
        logit_grad, weight_r
    )
    grad_gain_two = jnp.sum(grad_norm_two * normed_two, axis=0)
    scaled_two = grad_norm_two * gain_two_f
    grad_middle = upstream + scale_two * (
        scaled_two - normed_two * jnp.mean(scaled_two * normed_two, axis=-1, keepdims=True)
    )
    branch_grad = grad_middle.astype(jnp.bfloat16)
    grad_weight_o = contract_rows(attended_b, branch_grad)
    grad_heads = (
        contract_cols(branch_grad, weight_o)
        .astype(jnp.bfloat16)
        .reshape(count, KV_HEADS, repeat, HEAD)
    )
    drift = jnp.sum(grad_heads.astype(jnp.float32) * attended, axis=-1)
    query_acc = jnp.zeros((count, KV_HEADS, repeat, HEAD), jnp.float32)
    key_piece = lax.all_gather(keys, "ctx", axis=0, tiled=True)
    value_piece = lax.all_gather(values, "ctx", axis=0, tiled=True)
    size = key_piece.shape[0]
    block = math.gcd(size, 512)
    number = size // block
    key_blocks = key_piece.reshape(number, block, KV_HEADS, HEAD)
    value_blocks = value_piece.reshape(number, block, KV_HEADS, HEAD)
    offsets = jnp.arange(size, dtype=jnp.int32).reshape(number, block)

    def backward_step(acc, inputs):
        key_block, value_block, offset = inputs
        part_q, part_k, part_v = block_grads(
            queries,
            grad_heads,
            log_total,
            drift,
            query_rows,
            key_block,
            value_block,
            global_rows(perm_row, offset),
            first_len,
        )
        joined = jnp.concatenate(
            [part_k.reshape(block, KV_HEADS * HEAD), part_v.reshape(block, KV_HEADS * HEAD)],
            axis=-1,
        )
        return (acc + part_q, joined)

    query_acc, joined_parts = lax.scan(
        backward_step, query_acc, (key_blocks, value_blocks, offsets)
    )
    pair_acc = joined_parts.reshape(size, 2 * KV_HEADS * HEAD)
    query_grad, pair_acc = (query_acc, pair_acc)
    pair_own = lax.psum_scatter(
        pair_acc.astype(jnp.bfloat16), "ctx", scatter_dimension=0, tiled=True
    ).astype(jnp.float32)
    key_grad = pair_own[:, : KV_HEADS * HEAD].reshape(count, KV_HEADS, HEAD)
    value_grad = pair_own[:, KV_HEADS * HEAD :].reshape(count, KV_HEADS, HEAD)
    query_grad_b = (
        rotary(query_grad.reshape(count, HEADS, HEAD), position, -1.0)
        .astype(jnp.bfloat16)
        .reshape(count, HEADS * HEAD)
    )
    key_grad_b = (
        rotary(key_grad, position, -1.0).astype(jnp.bfloat16).reshape(count, KV_HEADS * HEAD)
    )
    value_grad_b = value_grad.astype(jnp.bfloat16).reshape(count, KV_HEADS * HEAD)
    grad_weight_q = contract_rows(hidden_one, query_grad_b)
    grad_weight_k = contract_rows(hidden_one, key_grad_b)
    grad_weight_v = contract_rows(hidden_one, value_grad_b)
    grad_hidden_one = (
        contract_cols(query_grad_b, weight_q)
        + contract_cols(key_grad_b, weight_k)
        + contract_cols(value_grad_b, weight_v)
    )
    grad_gain_one = jnp.sum(grad_hidden_one * normed_one, axis=0)
    scaled_one = grad_hidden_one * gain_one_f
    grad_tokens = grad_middle + scale_one * (
        scaled_one - normed_one * jnp.mean(scaled_one * normed_one, axis=-1, keepdims=True)
    )
    attn_sums = (
        lax.psum_scatter(grad_gain_one, ("ctx", "exp"), scatter_dimension=0, tiled=True),
        lax.psum_scatter(grad_weight_q, ("ctx", "exp"), scatter_dimension=0, tiled=True),
        lax.psum_scatter(grad_weight_k, ("ctx", "exp"), scatter_dimension=0, tiled=True),
        lax.psum_scatter(grad_weight_v, ("ctx", "exp"), scatter_dimension=0, tiled=True),
        lax.psum_scatter(grad_weight_o, ("ctx", "exp"), scatter_dimension=0, tiled=True),
        lax.psum_scatter(grad_router, ("ctx", "exp"), scatter_dimension=0, tiled=True),
        lax.psum_scatter(grad_gain_two, ("ctx", "exp"), scatter_dimension=0, tiled=True),
    )
    return (
        output[None],
        grad_tokens[None],
        attn_sums[0],
        attn_sums[1],
        attn_sums[2],
        attn_sums[3],
        attn_sums[4],
        attn_sums[5],
        attn_sums[6],
        expert_sums[0],
        expert_sums[1],
    )


def rotate(tensor, cosine, sine):
    half = HEAD // 2
    first, second = (tensor[..., :half], tensor[..., half:])
    return jnp.concatenate(
        [first * cosine - second * sine, second * cosine + first * sine], axis=-1
    )


def dispatch_kernel(base, hid_ref, mark_ref, router_ref, rows_ref, up_ref, gate_ref, spread_ref, gates_ref):
    bf16, f32 = jnp.bfloat16, jnp.float32
    count = hid_ref.shape[1]
    _, held, rows, _ = rows_ref.shape
    slots = rows // 2
    both = 2 * count
    x = hid_ref[...].reshape(both, D)
    logits = jnp.dot(x, router_ref[...], preferred_element_type=f32)
    routes = mark_ref[:, :, D:].reshape(both, 128).astype(f32)
    lane = lax.broadcasted_iota(jnp.int32, (both, 128), 1).astype(f32)
    picks = jnp.zeros((both, 128), f32)
    for i in range(TOP):
        picks = jnp.where(routes[:, i : i + 1] == lane, 1.0, picks)
    masked = jnp.where(picks > 0.0, logits, NEGATIVE)
    top = jnp.max(masked, axis=-1, keepdims=True)
    gates = jnp.where(picks > 0.0, jnp.exp(masked - top), 0.0)
    gates = gates / jnp.sum(gates, axis=-1, keepdims=True)
    gates_ref[...] = gates.reshape(2, count, 128)
    which = lax.broadcasted_iota(jnp.int32, (8, 128), 0)
    columns = lax.broadcasted_iota(jnp.int32, (8, 128), 1)
    chosen = jnp.where(columns == which + base[0], 1.0, 0.0).astype(bf16)
    hit = contract_cols(chosen, picks.astype(bf16))
    gate = contract_cols(chosen, gates.astype(bf16))
    earlier = lax.broadcasted_iota(jnp.int32, (both, both), 0)
    later = lax.broadcasted_iota(jnp.int32, (both, both), 1)
    upto = jnp.where((earlier <= later) & (earlier // count == later // count), 1.0, 0.0)
    rank = jnp.dot(hit.astype(bf16), upto.astype(bf16), preferred_element_type=f32)
    row = lax.broadcasted_iota(jnp.int32, (rows, both), 0)
    token = lax.broadcasted_iota(jnp.int32, (rows, both), 1)
    side = row // slots
    wanted = jnp.where(side == token // count, row - side * slots + 1, -1).astype(f32)
    for e in range(held):
        here = jnp.where((rank[e : e + 1] == wanted) & (hit[e : e + 1] > 0.0), 1.0, 0.0)
        gate_ref[0, e] = jnp.sum(here * gate[e : e + 1], axis=-1, keepdims=True)
        here = here.astype(bf16)
        spread_ref[0, e * rows : (e + 1) * rows, :] = here
        rows_ref[0, e] = jnp.dot(here, x, preferred_element_type=f32).astype(bf16)
        up_ref[0, e] = jnp.dot(
            here, mark_ref[:, :, :D].reshape(both, D), preferred_element_type=f32
        ).astype(bf16)


def dispatch(base, hidden, marked, router, held, slots):
    blocks, count, _ = hidden.shape
    pairs = blocks // 2
    bf16, f32 = jnp.bfloat16, jnp.float32
    pair = lambda *shape: pl.BlockSpec((1,) + shape, lambda p, b: (p,) + (0,) * len(shape))
    two = lambda width: pl.BlockSpec((2, count, width), lambda p, b: (p, 0, 0))
    return pl.pallas_call(
        dispatch_kernel,
        grid_spec=pltpu.PrefetchScalarGridSpec(
            num_scalar_prefetch=1,
            grid=(pairs,),
            in_specs=[two(D), two(D + 128), pl.BlockSpec((D, 128), lambda p, b: (0, 0))],
            out_specs=[
                pair(held, 2 * slots, D),
                pair(held, 2 * slots, D),
                pair(held, 2 * slots, 1),
                pair(held * 2 * slots, 2 * count),
                two(128),
            ],
        ),
        out_shape=[
            jax.ShapeDtypeStruct((pairs, held, 2 * slots, D), bf16),
            jax.ShapeDtypeStruct((pairs, held, 2 * slots, D), bf16),
            jax.ShapeDtypeStruct((pairs, held, 2 * slots, 1), f32),
            jax.ShapeDtypeStruct((pairs, held * 2 * slots, 2 * count), bf16),
            jax.ShapeDtypeStruct((blocks, count, 128), f32),
        ],
        compiler_params=pltpu.CompilerParams(vmem_limit_bytes=48 * 2**20),
        name="dispatch",
    )(base.reshape(1).astype(jnp.int32), hidden, marked, router)


def combine_kernel(spread, made, back, made_out, back_out):
    for rows, out in ((made, made_out), (back, back_out)):
        width = rows.shape[-1]
        total = contract_rows(spread[0], rows[0].reshape(-1, width))
        out[...] = total.astype(out.dtype).reshape(out.shape)


def combine(spread, made, back):
    pairs, slots, both = spread.shape
    count = both // 2
    rows = lambda a: pl.BlockSpec((1, *a.shape[1:]), lambda p: (p,) + (0,) * (a.ndim - 1))
    return pl.pallas_call(
        combine_kernel,
        grid=(pairs,),
        in_specs=[rows(spread), rows(made), rows(back)],
        out_specs=[
            pl.BlockSpec((2, count, a.shape[-1]), lambda p: (p, 0, 0)) for a in (made, back)
        ],
        out_shape=[
            jax.ShapeDtypeStruct((2 * pairs, count, a.shape[-1]), jnp.bfloat16)
            for a in (made, back)
        ],
        compiler_params=pltpu.CompilerParams(vmem_limit_bytes=48 * 2**20),
        name="combine",
    )(spread, made, back)


def expert_kernel(depth, meta, x_ref, g_ref, gate_ref, *refs):
    parts, (y_ref, d_ref), outs = refs[:10], refs[10:12], refs[12:20]
    weight, du_ref, act_ref = refs[20:]
    bf16, f32 = jnp.bfloat16, jnp.float32
    j = pl.program_id(0)
    shift, z, y, base = meta[0], meta[1], meta[2], meta[3]
    half = HID // 2
    offsets = [
        pl.multiple_of(((z ^ (i % 4)) * 2 + (y ^ (i // 4))) * depth, 64) for i in range(8)
    ]
    cut = pl.num_programs(0) - LATE
    for i, offset in enumerate(offsets):
        group = parts[i // 4 * 5 + i % 4 : i // 4 * 5 + i % 4 + (2 if i % 4 == 3 else 1)]
        for part, here in zip(group, (j < cut, j >= cut) if len(group) > 1 else (j >= 0,)):

            @pl.when(here)
            def _(part=part, offset=offset):
                weight[pl.ds(offset, depth), :] = part[0]

    expert = base + (j + shift) // 2
    first = jnp.logical_or(j == 0, lax.rem(j + shift, 2) == 0)
    keep = jnp.where(first, 0.0, 1.0)
    pairs, _, rows, _ = x_ref.shape
    step = 4

    def forward(i, carry):
        at = pl.ds(i * step, step)
        flat = pl.ds(pl.multiple_of(i * step * rows, 32), step * rows)
        x = x_ref[at, 0].reshape(step * rows, D)
        g = g_ref[at, 0].reshape(step * rows, D)
        gate = gate_ref[at, 0].reshape(step * rows, 1)
        u = jnp.dot(x, weight[:, : 2 * half], preferred_element_type=f32)
        raw = jnp.dot(g, weight[:, 2 * half :], preferred_element_type=f32)
        u1, u2 = u[:, :half], u[:, half:]
        sig = jax.nn.sigmoid(u1)
        silu = u1 * sig
        act = (silu * u2).astype(bf16).astype(f32)
        dgate = jnp.sum(raw * act, axis=-1, keepdims=True)
        dact = raw * gate
        du1 = dact * u2 * (sig * (1.0 + u1 * (1.0 - sig)))
        du = jnp.concatenate([du1, dact * silu], axis=-1).astype(bf16)
        act_gated = (act * gate).astype(bf16)
        du_ref[flat, :] = du
        act_ref[flat, :] = act_gated
        made = contract_cols(act_gated, weight[:, 2 * half :])
        back = contract_cols(du, weight[:, : 2 * half])
        lane = lax.broadcasted_iota(jnp.int32, (step * rows, 128), 1)
        tail = jnp.where(lane == expert, dgate, 0.0)

        @pl.when(first)
        def _():
            y_ref[at, 0] = made.astype(bf16).reshape(step, rows, D)
            d_ref[at, 0, :, :D] = back.astype(bf16).reshape(step, rows, D)
            d_ref[at, 0, :, D:] = tail.astype(bf16).reshape(step, rows, 128)

        @pl.when(jnp.logical_not(first))
        def _():
            old_y = y_ref[at, 0].reshape(step * rows, D).astype(f32)
            y_ref[at, 0] = (made + old_y).astype(bf16).reshape(step, rows, D)
            old_d = d_ref[at, 0].reshape(step * rows, D + 128).astype(f32)
            d_ref[at, 0, :, :D] = (back + old_d[:, :D]).astype(bf16).reshape(step, rows, D)
            d_ref[at, 0, :, D:] = (tail + old_d[:, D:]).astype(bf16).reshape(step, rows, 128)

        return carry

    lax.fori_loop(0, pairs // step, forward, 0)

    wide = D // 2

    def gradient(i, carry):
        at = pl.ds(pl.multiple_of(i * wide, wide), wide)
        x = x_ref[:, 0, :, at].reshape(pairs * rows, wide)
        g = g_ref[:, 0, :, at].reshape(pairs * rows, wide)
        weight[at, : 2 * half] = contract_rows(x, du_ref[...]).astype(bf16)
        weight[at, 2 * half :] = contract_rows(g, act_ref[...]).astype(bf16)
        return carry

    lax.fori_loop(0, D // wide, gradient, 0)
    for out, offset in zip(outs, offsets):
        out[0] = weight[pl.ds(offset, depth), :]


def run_experts(meta, row_in, row_up, slot_gate, parts):
    pairs, held, rows, _ = row_in.shape
    units, depth, columns = parts[0].shape
    held_block = lambda width: pl.BlockSpec(
        (pairs, 1, rows, width), lambda j, m: (0, (j + m[0]) // 2, 0, 0)
    )
    unit_block = pl.BlockSpec((1, depth, columns), lambda j, m: (j, 0, 0))
    cut = units - LATE
    early_block = pl.BlockSpec((1, depth, columns), lambda j, m: (jnp.minimum(j, cut - 1), 0, 0))
    late_block = pl.BlockSpec((1, depth, columns), lambda j, m: (jnp.maximum(j - cut, 0), 0, 0))
    bf16 = jnp.bfloat16
    total = units * pairs * rows * D * columns * 6
    return pl.pallas_call(
        lambda *refs: expert_kernel(depth, *refs),
        grid_spec=pltpu.PrefetchScalarGridSpec(
            num_scalar_prefetch=1,
            grid=(units,),
            in_specs=[
                held_block(D),
                held_block(D),
                held_block(1),
            ]
            + [unit_block, unit_block, unit_block, early_block, late_block] * 2,
            out_specs=[held_block(D), held_block(D + 128)] + [unit_block] * 8,
            scratch_shapes=[
                pltpu.VMEM((D, columns), bf16),
                pltpu.VMEM((pairs * rows, HID), bf16),
                pltpu.VMEM((pairs * rows, HID // 2), bf16),
            ],
        ),
        out_shape=[
            jax.ShapeDtypeStruct((pairs, held, rows, D), bf16),
            jax.ShapeDtypeStruct((pairs, held, rows, D + 128), bf16),
        ]
        + [jax.ShapeDtypeStruct((units, depth, columns), bf16)] * 8,
        compiler_params=pltpu.CompilerParams(vmem_limit_bytes=56 * 2**20),
        cost_estimate=pl.CostEstimate(
            flops=total, bytes_accessed=60 * 2**20, transcendentals=units * pairs * rows * HID
        ),
        name="experts",
    )(meta, row_in, row_up, slot_gate, *parts)


def place_kernel(number, z_ref, *refs):
    in_ref, out_ref = refs[12:]
    half = refs[0].shape[-1] // 3
    for h in range(2):
        unit = 2 * pl.program_id(0) + h
        source = (unit // number) ^ z_ref[0]
        late = (source == 3) & (lax.rem(unit, number) >= number - LATE)
        source = jnp.where(late, 4, source)
        first, other, *rest = refs[6 * h : 6 * h + 6]
        for i, group in enumerate([(first, other)] + [(ref,) for ref in rest]):

            @pl.when(source == i)
            def _(h=h, group=group):
                total = group[0][0].astype(jnp.float32)
                for ref in group[1:]:
                    total = total + ref[0].astype(jnp.float32)
                in_ref[0, :, h * half : (h + 1) * half] = total[:, :half]
                in_ref[0, :, HID + h * half : HID + (h + 1) * half] = total[:, half : 2 * half]
                out_ref[0, :, h * half : (h + 1) * half] = total[:, 2 * half :]


def place_units(z_index, first, other, near, mid, far, late):
    number, depth, columns = first.shape

    def block(i, h):
        low, most = {3: (0, number - LATE - 1), 4: (number - LATE, LATE - 1)}.get(i, (0, number - 1))

        def index(e, z):
            unit = 2 * e + h
            at = jnp.clip(lax.rem(unit, number) - low, 0, most)
            return jnp.where((unit // number) ^ z[0] == min(i, 3), at, 0), 0, 0

        return pl.BlockSpec((1, depth, columns), index)

    return pl.pallas_call(
        lambda *refs: place_kernel(number, *refs),
        grid_spec=pltpu.PrefetchScalarGridSpec(
            num_scalar_prefetch=1,
            grid=(EXP_DEV,),
            in_specs=[block(i, h) for h in range(2) for i in (0, 0, 1, 2, 3, 4)],
            out_specs=[
                pl.BlockSpec((1, depth, 2 * HID), lambda e, z: (e, 0, 0)),
                pl.BlockSpec((1, depth, HID), lambda e, z: (e, 0, 0)),
            ],
        ),
        out_shape=[
            jax.ShapeDtypeStruct((EXP_DEV, depth, 2 * HID), jnp.float32),
            jax.ShapeDtypeStruct((EXP_DEV, depth, HID), jnp.float32),
        ],
        name="place_units",
    )(z_index.reshape(1), *[first, other, near, mid, far, late] * 2)


MESH = pl.DeviceIdType.MESH


def greet(peers):
    barrier = pltpu.get_barrier_semaphore()
    for peer in peers:
        pl.semaphore_signal(barrier, inc=1, device_id=peer, device_id_type=MESH)
    pl.semaphore_wait(barrier, len(peers))


def send(src, dst, sems, at, peer):
    copy = pltpu.make_async_remote_copy(
        src_ref=src,
        dst_ref=dst,
        send_sem=sems[0].at[at],
        recv_sem=sems[1].at[at],
        device_id=peer,
        device_id_type=MESH,
    )
    copy.start()
    return copy


def dma_pair(number):
    return [pltpu.SemaphoreType.DMA((number,)), pltpu.SemaphoreType.DMA((number,))]


def z_peers():
    z = lax.axis_index("z")
    return [{"z": z ^ s} for s in (3, 2, 1)]


def siblings(axes):
    return [{a: 1 - lax.axis_index(a)} for a in axes]


class Scatter:
    def __init__(self, part, axes, chunks, refs, direct=False):
        self.part, self.axes, self.chunks, self.direct = part, axes, chunks, direct
        depth = len(axes)
        self.own, self.came = refs[0], refs[1 : 1 + depth]
        self.sums = refs[1 + depth : 1 + 2 * depth]
        self.turn, self.line, self.result, self.load_sem = refs[1 + 2 * depth : 5 + 2 * depth]
        sems = refs[5 + 2 * depth :]
        self.sems = [sems[2 * i : 2 * i + 2] for i in range(depth + 1)]
        self.z = lax.axis_index("z")
        self.mine = [lax.axis_index(a) for a in axes]
        self.rows = part.shape[-2] // chunks
        self.flying = [[None] * chunks for _ in axes]

    @staticmethod
    def scratch(part, axes, chunks):
        n_z, rows, width, kind = part.shape[0], part.shape[-2], part.shape[-1], part.dtype
        depth = len(axes)

        def buffer(i):
            return pltpu.VMEM((chunks, n_z) + (2,) * i + (rows // chunks, width), kind)

        shapes = [buffer(depth - 1)] + [buffer(i) for i in range(depth)] * 2
        shapes += [buffer(0), pltpu.VMEM((chunks, n_z + 1, rows // chunks, width), kind)]
        shapes += [pltpu.VMEM((rows // chunks, width), jnp.float32)]
        shapes += [pltpu.SemaphoreType.DMA((chunks,))]
        for _ in range(depth):
            shapes += dma_pair(chunks)
        return shapes + dma_pair(chunks * (n_z + 1))

    def start(self):
        level = len(self.axes) - 1
        lead = (slice(None),) * len(self.axes)
        mine = self.mine[-1]
        self.loads = []
        for c in range(self.chunks):
            at = pl.ds(c * self.rows, self.rows)
            self.flying[level][c] = send(
                self.part.at[lead + (1 - mine, at)],
                self.came[level].at[c],
                self.sems[level],
                c,
                {self.axes[-1]: 1 - mine},
            )
            load = pltpu.make_async_copy(
                self.part.at[lead + (mine, at)], self.own.at[c], self.load_sem.at[c]
            )
            load.start()
            self.loads.append(load)

    def fold(self, level, c):
        self.flying[level][c].wait_recv()
        if level == len(self.axes) - 1:
            self.loads[c].wait()
            held = self.own[c]
        else:
            held = self.sums[level + 1][
                (c,) + (slice(None),) * (level + 1) + (self.mine[level],)
            ]
        total = held.astype(jnp.float32) + self.came[level][c].astype(jnp.float32)
        self.sums[level][c] = total.astype(held.dtype)
        if level > 0:
            mine = self.mine[level - 1]
            self.flying[level - 1][c] = send(
                self.sums[level].at[(c,) + (slice(None),) * level + (1 - mine,)],
                self.came[level - 1].at[c],
                self.sems[level - 1],
                c,
                {self.axes[level - 1]: 1 - mine},
            )

    def along(self, c, w, up):
        slot = w + 1 if up else w
        return pltpu.make_async_remote_copy(
            src_ref=self.turn.at[c, w],
            dst_ref=self.line.at[c, slot],
            send_sem=self.sems[-1][0].at[w * self.chunks + c],
            recv_sem=self.sems[-1][1].at[slot * self.chunks + c],
            device_id={"z": self.z + 1 if up else self.z - 1},
            device_id_type=MESH,
        )

    def steps(self):
        return [(3, True), (0, False), (2, True), (1, False), (1, True), (2, False)]

    def over_z(self, c, s):
        return pltpu.make_async_remote_copy(
            src_ref=self.sums[0].at[c, self.z ^ s],
            dst_ref=self.line.at[c, s],
            send_sem=self.sems[-1][0].at[s * self.chunks + c],
            recv_sem=self.sems[-1][1].at[s * self.chunks + c],
            device_id={"z": self.z ^ s},
            device_id_type=MESH,
        )

    def relay(self, c):
        z = self.z
        if self.direct:
            for s in (3, 2, 1):
                self.over_z(c, s).start()
            return
        for w, up in self.steps():
            slot = w + 1 if up else w

            @pl.when((z < w) if up else (z > w))
            def _(w=w, up=up, slot=slot):
                inner = (z > 0) if up else (z < 3)

                @pl.when(inner)
                def _():
                    self.along(c, w, up).wait_recv()
                    total = self.sums[0][c, w].astype(jnp.float32) + self.line[c, slot].astype(
                        jnp.float32
                    )
                    self.turn[c, w] = total.astype(self.turn.dtype)

                @pl.when(jnp.logical_not(inner))
                def _():
                    self.turn[c, w] = self.sums[0][c, w]

                self.along(c, w, up).start()

    def total(self, c):
        z = self.z
        if self.direct:
            total = self.sums[0][c, z].astype(jnp.float32)
            for s in (1, 2, 3):
                self.over_z(c, s).wait_recv()
                total = total + self.line[c, s].astype(jnp.float32)
            return total
        self.result[...] = self.sums[0][c, z].astype(jnp.float32)
        for up in (True, False):

            @pl.when((z > 0) if up else (z < 3))
            def _(up=up):
                self.along(c, z, up).wait_recv()
                self.result[...] += self.line[c, z + 1 if up else z].astype(jnp.float32)

        return self.result[...]

    lag = 1

    def length(self):
        return self.chunks + len(self.axes) + self.lag

    def advance(self, step, use):
        depth = len(self.axes)
        for level in range(depth - 1, -1, -1):
            c = step - (depth - 1 - level)
            if 0 <= c < self.chunks:
                self.fold(level, c)
        c = step - (depth - 1)
        if 0 <= c < self.chunks:
            self.relay(c)
        c = step - depth - self.lag + 1
        if 0 <= c < self.chunks:
            use(c, pl.ds(c * self.rows, self.rows), self.total(c))

    def run(self, use):
        for step in range(self.length()):
            self.advance(step, use)

    def finish(self):
        for copy in sum(self.flying, []):
            copy.wait_send()
        for c in range(self.chunks):
            if self.direct:
                for s in (1, 2, 3):
                    self.over_z(c, s).wait_send()
                continue
            for w, up in self.steps():

                @pl.when((self.z < w) if up else (self.z > w))
                def _(w=w, up=up, c=c):
                    self.along(c, w, up).wait_send()


class Gather:
    def __init__(self, own, out, axes, chunks, refs, direct=False):
        self.own, self.out, self.axes, self.chunks, self.direct = own, out, axes, chunks, direct
        self.keep_sem = refs[0]
        self.sems = [refs[1 + 2 * i : 3 + 2 * i] for i in range(len(axes) + 1)]
        self.z = lax.axis_index("z")
        self.mine = tuple(lax.axis_index(a) for a in axes)
        self.rows = own.shape[0] // chunks
        self.keeps = []

    @staticmethod
    def scratch(axes, chunks):
        shapes = [pltpu.SemaphoreType.DMA((chunks,)), *dma_pair(8 * chunks)]
        for i in range(len(axes)):
            shapes += dma_pair(4 * 2**i * chunks)
        return shapes

    def block(self, c, w, flips):
        places = tuple(
            1 - m if i < len(flips) and flips[i] else m for i, m in enumerate(self.mine)
        )
        return self.out.at[(w,) + places + (pl.ds(c * self.rows, self.rows),)]

    def along(self, c, w, up, own=False):
        where = self.block(c, w, ())
        return pltpu.make_async_remote_copy(
            src_ref=self.own.at[pl.ds(c * self.rows, self.rows)] if own else where,
            dst_ref=where,
            send_sem=self.sems[0][0].at[(w * 2 + int(up)) * self.chunks + c],
            recv_sem=self.sems[0][1].at[w * self.chunks + c],
            device_id={"z": self.z + 1 if up else self.z - 1},
            device_id_type=MESH,
        )

    def across(self, level, c, w, flips, own=False):
        where = self.block(c, w, flips)
        number = w
        for f in flips:
            number = number * 2 + f
        at = number * self.chunks + c
        return pltpu.make_async_remote_copy(
            src_ref=self.own.at[pl.ds(c * self.rows, self.rows)] if own else where,
            dst_ref=where,
            send_sem=self.sems[level + 1][0].at[at],
            recv_sem=self.sems[level + 1][1].at[at],
            device_id={self.axes[level]: 1 - self.mine[level]},
            device_id_type=MESH,
        )

    def over_z(self, c, s):
        where = self.block(c, self.z, ())
        return pltpu.make_async_remote_copy(
            src_ref=self.own.at[pl.ds(c * self.rows, self.rows)],
            dst_ref=where,
            send_sem=self.sems[0][0].at[s * self.chunks + c],
            recv_sem=self.sems[0][1].at[s * self.chunks + c],
            device_id={"z": self.z ^ s},
            device_id_type=MESH,
        )

    def start(self, c):
        z = self.z
        for s in (3, 2, 1) if self.direct else ():
            self.over_z(c, s).start()
        for up in () if self.direct else (True, False):

            @pl.when((z < 3) if up else (z > 0))
            def _(up=up):
                self.along(c, z, up, own=True).start()

        for level in range(len(self.axes)):
            self.across(level, c, z, (0,) * level, own=True).start()
        keep = pltpu.make_async_copy(
            self.own.at[pl.ds(c * self.rows, self.rows)], self.block(c, z, ()), self.keep_sem.at[c]
        )
        keep.start()
        self.keeps.append(keep)

    def forward(self, c, hops=(1, 2, 3)):
        z = self.z
        for s in hops if self.direct else ():
            self.over_z(c, s).wait_recv()
            for level in range(len(self.axes)):
                self.across(level, c, z ^ s, (0,) * level).start()
        for t in () if self.direct else hops:
            for up in (True, False):

                @pl.when((z >= t) if up else (z + t <= 3))
                def _(t=t, up=up):
                    w = z - t if up else z + t
                    self.along(c, w, up).wait_recv()

                    @pl.when((z < 3) if up else (z > 0))
                    def _():
                        self.along(c, w, up).start()

                    for level in range(len(self.axes)):
                        self.across(level, c, w, (0,) * level).start()

    def flips(self, level):
        return [tuple((i >> b) & 1 for b in range(level)) for i in range(2**level)]

    def spread(self, c):
        for level in range(len(self.axes) - 1):
            for s in range(4):
                for flips in self.flips(level):
                    w = self.z ^ s
                    turned = flips + (1,)
                    self.across(level, c, w, flips).wait_recv()
                    for later in range(level + 1, len(self.axes)):
                        self.across(later, c, w, turned + (0,) * (later - level - 1)).start()

    def finish(self):
        z, last = self.z, len(self.axes) - 1
        for keep in self.keeps:
            keep.wait()
        for c in range(self.chunks):
            for s in range(4):
                for flips in self.flips(last):
                    self.across(last, c, z ^ s, flips).wait_recv()
                for level in range(last + 1):
                    for flips in self.flips(level):
                        self.across(level, c, z ^ s, flips).wait_send()
            for s in (1, 2, 3) if self.direct else ():
                self.over_z(c, s).wait_send()
            for t in () if self.direct else (0, 1, 2, 3):
                for up in (True, False):
                    here = ((z >= t) & (z < 3)) if up else ((z + t <= 3) & (z > 0))

                    @pl.when(here)
                    def _(t=t, up=up, c=c):
                        self.along(c, z - t if up else z + t, up).wait_send()


VMEM_SPEC = pl.BlockSpec(memory_space=pltpu.VMEM)
ANY_SPEC = pl.BlockSpec(memory_space=pl.ANY)


def whole(shape):
    return pl.BlockSpec(tuple(shape), lambda i: (0,) * len(shape))


def exchange(kernel, name, number, inputs, specs, outs, out_specs, scratch):
    sizes = [len(inputs), len(outs)] + [len(s) for s in scratch]

    def run(*refs):
        groups, at = [], 0
        for size in sizes:
            groups.append(refs[at : at + size])
            at += size
        kernel(*groups)

    return pl.pallas_call(
        run,
        out_shape=outs,
        in_specs=specs,
        out_specs=out_specs,
        scratch_shapes=sum(scratch, []),
        compiler_params=pltpu.CompilerParams(
            collective_id=number, has_side_effects=True, vmem_limit_bytes=48 * 2**20
        ),
        name=name,
    )(*inputs)


def share_inputs(tokens, slices, wo, marked, win, wout):
    count, own = tokens.shape[0], wo.shape[0]
    columns, wide = slices.shape[-1], marked.shape[-1]
    depth, half = win.shape[1], HID // 2
    number = 2 * win.shape[0] // 4
    early = number - LATE
    chunks = 2
    bf16 = jnp.bfloat16

    def kernel(ins, outs, token_refs, wo_refs, marked_refs, other):
        tok, cut, wo_ref, marked_ref, win_ref, wout_ref = ins
        tok_out, cut_out, wo_out, marked_out = outs[:4]
        near, far, late = outs[4:8], (outs[8], None, *outs[9:11]), outs[11]
        keep, ctx_sems, exp_sems = other[0], other[1:3], other[3:5]
        near_sems, far_sems, win_in, wout_in, unit = other[5:7], other[7:9], *other[9:12]
        z, y, x, k = (lax.axis_index(a) for a in ("z", "y", "x", "k"))
        loads = [
            pltpu.make_async_copy(win_ref, win_in, keep.at[1]),
            pltpu.make_async_copy(wout_ref, wout_in, keep.at[2]),
        ]
        for copy in loads:
            copy.start()
        exp_peers = [((x ^ a, k ^ b), a * 2 + b) for a in (1, 0) for b in (1, 0) if a or b]
        greet(
            [{"z": p, "y": q} for p, q, _ in ctx_peers()]
            + [{"x": p, "k": q} for (p, q), _ in exp_peers]
        )
        gather = Gather(tok, tok_out, ("y",), chunks, token_refs)
        whole = Gather(wo_ref, wo_out, ("y", "x", "k"), 1, wo_refs)
        other_rows = Gather(marked_ref, marked_out, ("x", "k"), 1, marked_refs)
        over_ctx = [
            send(cut.at[p, q], cut_out.at[z, y, x, k], ctx_sems, i - 1, {"z": p, "y": q})
            for p, q, i in ctx_peers()
        ]
        whole.start(0)
        for c in range(chunks):
            gather.start(c)
        other_rows.start(0)
        copy_own = pltpu.make_async_copy(cut.at[z, y], cut_out.at[z, y, x, k], keep.at[0])
        copy_own.start()

        def over_z(i, j):
            return pltpu.make_async_remote_copy(
                src_ref=unit.at[i, j],
                dst_ref=near[i].at[j],
                send_sem=near_sems[0].at[i * number + j],
                recv_sem=near_sems[1].at[i * number + j],
                device_id={"z": z ^ i},
                device_id_type=MESH,
            )

        def over_y(i, j):
            return pltpu.make_async_remote_copy(
                src_ref=near[i].at[j] if i else unit.at[0, j],
                dst_ref=far[i].at[j],
                send_sem=far_sems[0].at[i * number + j],
                recv_sem=far_sems[1].at[i * number + j],
                device_id={"y": 1 - y},
                device_id_type=MESH,
            )

        def own_unit(j):
            return pltpu.make_async_copy(unit.at[0, j], near[0].at[j], keep.at[3 + j])

        def late_unit(j):
            return pltpu.make_async_copy(unit.at[3, j], late.at[j - early], keep.at[3 + number + j])

        def convert(j):
            for i in range(4):
                index = number * (z ^ i) + j
                e, h = index // 2, lax.rem(index, 2)
                first = pl.ds(pl.multiple_of(h * half, half), half)
                second = pl.ds(pl.multiple_of(HID + h * half, half), half)
                unit[i, j, :, :half] = win_in[e, :, first].astype(bf16)
                unit[i, j, :, half : 2 * half] = win_in[e, :, second].astype(bf16)
                unit[i, j, :, 2 * half :] = wout_in[e, :, first].astype(bf16)

        def send_units(j):
            for i in (3, 2, 1) if j < early else (2, 1):
                over_z(i, j).start()

        def pass_units(j):
            for i in (2, 3) if j < early else (2,):
                over_z(i, j).wait_recv()
                over_y(i, j).start()

        for copy in loads:
            copy.wait()
        convert(0)
        send_units(0)
        for j in range(number):
            if j:
                convert(j)
            own_unit(j).start()
            if j >= early:
                late_unit(j).start()
            over_y(0, j).start()
        for t in (1, 2, 3):
            whole.forward(0, (t,))
            for c in range(chunks):
                gather.forward(c, (t,))
            other_rows.forward(0, (t,))
            send_units(t)
            if t == 1:
                for copy in over_ctx:
                    copy.wait_recv()
                copy_own.wait()
                mine = cut_out.at[:, :, x, k]
                over_exp = [
                    send(mine, mine, exp_sems, i - 1, {"x": p, "k": q})
                    for (p, q), i in exp_peers
                ]
            pass_units(t - 1)
        for j in range(4, number):
            send_units(j)
        whole.spread(0)
        other_rows.spread(0)
        for j in range(3, number):
            pass_units(j)
        for copy in over_exp:
            copy.wait_recv()
        gather.finish()
        whole.finish()
        other_rows.finish()
        for copy in over_ctx + over_exp:
            copy.wait_send()
        for j in range(number):
            own_unit(j).wait()
            if j >= early:
                late_unit(j).wait()
            for i in range(4):
                if i == 3 and j >= early:
                    continue
                if i == 1:
                    over_z(i, j).wait_recv()
                else:
                    over_y(i, j).wait_recv()
                    over_y(i, j).wait_send()
                if i:
                    over_z(i, j).wait_send()

    units, most, few = (
        jax.ShapeDtypeStruct((n, depth, 3 * half), bf16) for n in (number, early, LATE)
    )
    outs = exchange(
        kernel,
        "share_inputs",
        1,
        (tokens, slices, wo, marked, win, wout),
        [ANY_SPEC] * 6,
        [
            jax.ShapeDtypeStruct((4, 2, count, D), bf16),
            jax.ShapeDtypeStruct((4, 2, 2, 2, own, columns), bf16),
            jax.ShapeDtypeStruct((4, 2, 2, 2, own, D), bf16),
            jax.ShapeDtypeStruct((4, 2, 2, count, wide), bf16),
        ]
        + [units] * 3
        + [most, units, units, most, few],
        [ANY_SPEC] * 12,
        [
            Gather.scratch(("y",), chunks),
            Gather.scratch(("y", "x", "k"), 1),
            Gather.scratch(("x", "k"), 1),
            [pltpu.SemaphoreType.DMA((3 + 2 * number,))]
            + dma_pair(7)
            + dma_pair(3)
            + dma_pair(4 * number)
            + dma_pair(4 * number)
            + [
                pltpu.VMEM(win.shape, jnp.float32),
                pltpu.VMEM(wout.shape, jnp.float32),
                pltpu.VMEM((4, number, depth, 3 * half), bf16),
            ],
        ],
    )
    return (*outs[:4], outs[4:8], outs[8:11], outs[11])


def ctx_peers():
    z, y = lax.axis_index("z"), lax.axis_index("y")
    return [(z ^ (i // 2), y ^ (i % 2), i) for i in range(7, 0, -1)]


def middle_step(heads, tokens, wo, gain, bulk):
    count, chunks = tokens.shape[0], 2
    width = heads.shape[-1]
    bf16, f32 = jnp.bfloat16, jnp.float32

    def kernel(ins, outs, hidden_refs, other):
        heads_ref, tok, wo_ref, gain_ref = ins[:4]
        attended_ref, middle_ref, hidden_out = outs[:3]
        own, sems, bulk_sems = other[0], other[1:3], other[3:5]
        z, y = lax.axis_index("z"), lax.axis_index("y")
        greet(
            [{"z": p, "y": q} for p, q, _ in ctx_peers()] + siblings(("x", "k"))
        )
        hidden = Gather(own, hidden_out, ("x", "k"), chunks, hidden_refs)
        copies = [
            send(heads_ref.at[p, q], attended_ref.at[z, y], sems, i - 1, {"z": p, "y": q})
            for p, q, i in ctx_peers()
        ]
        attended_ref[z, y] = heads_ref[z, y]
        bulk_copies = [
            send(a, b, bulk_sems, i, {"y": 1 - y}) for i, (a, b) in enumerate(zip(ins[4:], outs[3:]))
        ]
        for copy in copies:
            copy.wait_recv()
        step = count // chunks
        middle = tok[...].astype(f32)
        for i in range(8):
            middle = middle + jnp.dot(
                attended_ref[i // 2, i % 2],
                wo_ref[i * width : (i + 1) * width, :],
                preferred_element_type=f32,
            )
        middle_ref[...] = middle
        for c in range(chunks):
            at = pl.ds(c * step, step)
            middle = middle_ref[at, :]
            scale = lax.rsqrt(jnp.mean(middle * middle, axis=-1, keepdims=True) + EPSILON)
            own[at, :] = (middle * scale * gain_ref[...]).astype(bf16)
            hidden.start(c)
        for c in range(chunks):
            hidden.forward(c)
            hidden.spread(c)
        hidden.finish()
        for copy in bulk_copies:
            copy.wait_recv()
        for copy in copies + bulk_copies:
            copy.wait_send()

    return exchange(
        kernel,
        "middle_step",
        2,
        (heads, tokens, wo, gain, *bulk),
        [VMEM_SPEC] * 4 + [ANY_SPEC] * len(bulk),
        [
            jax.ShapeDtypeStruct((4, 2, count, width), bf16),
            jax.ShapeDtypeStruct((count, D), f32),
            jax.ShapeDtypeStruct((4, 2, 2, count, D), bf16),
        ]
        + [jax.ShapeDtypeStruct(a.shape, a.dtype) for a in bulk],
        [VMEM_SPEC, VMEM_SPEC, ANY_SPEC] + [ANY_SPEC] * len(bulk),
        [
            Gather.scratch(("x", "k"), chunks),
            [pltpu.VMEM((count, D), bf16)] + dma_pair(7) + dma_pair(len(bulk)),
        ],
    )


def router_step(part, mixed, middle, cotangent, gates, router, gain, wo, bulk, added):
    count, chunks = middle.shape[0], 4
    width, (number, depth, _) = wo.shape[0] // 8, added.shape
    early = number - LATE
    bf16, f32 = jnp.bfloat16, jnp.float32

    def kernel(ins, outs, scatter_refs, mixed_refs, other):
        part_ref, mixed_ref, middle_ref, up_ref, gates_ref, router_ref, gain_ref, wo_ref = ins[:8]
        logit_ref, gain_out, grad_ref, heads_out, out_ref = outs[:5]
        turned, sems, bulk_sems, first_sems, far_sems = other[0], *(
            other[i : i + 2] for i in (1, 3, 5, 7)
        )
        own_unit, came_unit, load_sem = other[9:12]
        bulk_in, bulk_out, added_ref = ins[8:-1], outs[6:], ins[-1]
        far_out = outs[5]
        z, y = lax.axis_index("z"), lax.axis_index("y")
        load = pltpu.make_async_copy(added_ref.at[pl.ds(0, early)], own_unit, load_sem.at[0])
        load.start()
        greet([{"z": p, "y": q} for p, q, _ in ctx_peers()] + siblings(("x", "k")))
        scatter = Scatter(part_ref, ("x", "k"), chunks, scatter_refs)
        mixture = Scatter(mixed_ref, ("x", "k"), chunks, mixed_refs)
        copies = []
        scatter.start()
        mixture.start()
        pieces = 2 * early
        piece = lambda ref, j: ref.at[j // 2, pl.ds(j % 2 * (depth // 2), depth // 2)]
        over_first = [
            send(piece(bulk_in[0], j), piece(came_unit, j), first_sems, j, {"y": 1 - y})
            for j in range(pieces)
        ]
        over_far = []
        bulk_copies = [
            send(
                bulk_in[0].at[pl.ds(early, number - early)], bulk_out[0], bulk_sems, 0, {"y": 1 - y}
            ),
            send(bulk_in[1], bulk_out[1], bulk_sems, 1, {"y": 1 - y}),
        ]
        load.wait()

        def send_far(j):
            over_first[j].wait_recv()
            mine = piece(own_unit, j)
            total = mine[...].astype(f32) + piece(came_unit, j)[...].astype(f32)
            mine[...] = total.astype(bf16)
            over_far.append(send(mine, piece(far_out, j), far_sems, j, {"z": z ^ 3}))

        gain_out[...] = jnp.zeros_like(gain_out)

        def use(c, at, total):
            gate, gate_grad = gates_ref[at, :], total[:, D:]
            inner = jnp.sum(gate * gate_grad, axis=-1, keepdims=True)
            logit_grad = (gate * (gate_grad - inner)).astype(bf16)
            logit_ref[at, :] = logit_grad
            grad = total[:, :D] + contract_cols(logit_grad, router_ref[...])
            middle = middle_ref[at, :]
            scale = lax.rsqrt(jnp.mean(middle * middle, axis=-1, keepdims=True) + EPSILON)
            normed = middle * scale
            gain_out[...] += jnp.sum(grad * normed, axis=0, keepdims=True)
            scaled = grad * gain_ref[...]
            result = up_ref[at, :].astype(f32) + scale * (
                scaled - normed * jnp.mean(scaled * normed, axis=-1, keepdims=True)
            )
            grad_ref[at, :] = result

        def to_heads():
            down = grad_ref[...].astype(bf16)
            for i in range(8):
                turned[i // 2, i % 2] = contract_cols(
                    down, wo_ref[i * width : (i + 1) * width, :]
                ).astype(bf16)
            for p, q, i in ctx_peers():
                copies.append(
                    send(
                        turned.at[p, q], heads_out.at[z, y], sems, i - 1, {"z": p, "y": q}
                    )
                )
            heads_out[z, y] = turned[z, y]
            bulk_copies.append(send(bulk_in[2], bulk_out[2], bulk_sems, 2, {"y": 1 - y}))

        def use_mixture(c, at, total):
            out_ref[at, :] = (middle_ref[at, :] + total).astype(bf16)

        behind = 3
        plan = [[0, 1], [2], [3], [4], [5]] + [[]] * 5
        for step in range(scatter.length() + behind):
            if step < scatter.length():
                scatter.advance(step, use)
            if step == scatter.length() - 1:
                to_heads()
            if step >= behind:
                mixture.advance(step - behind, use_mixture)
            for j in plan[step]:
                send_far(j)
        for copy in copies + bulk_copies + over_far:
            copy.wait_recv()
        for copy in copies + bulk_copies + over_first + over_far:
            copy.wait_send()
        scatter.finish()
        mixture.finish()

    return exchange(
        kernel,
        "router_step",
        3,
        (part, mixed, middle, cotangent, gates, router, gain, wo, *bulk, added),
        [ANY_SPEC] * 2 + [VMEM_SPEC] * 6 + [ANY_SPEC] * 4,
        [
            jax.ShapeDtypeStruct((count, 128), bf16),
            jax.ShapeDtypeStruct((1, D), f32),
            jax.ShapeDtypeStruct((count, D), f32),
            jax.ShapeDtypeStruct((4, 2, count, width), bf16),
            jax.ShapeDtypeStruct((count, D), bf16),
        ]
        + [
            jax.ShapeDtypeStruct((n, *added.shape[1:]), bf16)
            for n in (early, number - early, number, number)
        ],
        [VMEM_SPEC] * 5 + [ANY_SPEC] * 4,
        [
            Scatter.scratch(part, ("x", "k"), chunks),
            Scatter.scratch(mixed, ("x", "k"), chunks),
            [pltpu.VMEM((4, 2, count, width), bf16)] + dma_pair(7) + dma_pair(3) + dma_pair(2 * early) * 2
            + [pltpu.VMEM((early, *added.shape[1:]), bf16)] * 2 + [pltpu.SemaphoreType.DMA((1,))],
        ],
    )


def last_step(
    part, tokens, grad_middle, gain, qkv_part, wo_part, small_part
):
    count, chunks = tokens.shape[0], 4
    own, columns = qkv_part.shape[-2:]
    bf16, f32 = jnp.bfloat16, jnp.float32

    def kernel(ins, outs, part_refs, wo_refs, other):
        part_ref, tok, grad_ref, gain_ref, qkv, wo, small = ins
        tokens_ref, qkv_out, wo_out, small_out = outs
        qkv_came, qkv_sum, small_came = other[:3]
        sems = [other[3 + 2 * i : 5 + 2 * i] for i in range(3)]
        names = ("z", "y", "x", "k")
        z, y, x, k = (lax.axis_index(a) for a in names)
        everyone = [
            ((z ^ (i // 8), y ^ (i // 4 % 2), x ^ (i // 2 % 2), k ^ (i % 2)), i)
            for i in range(31, 0, -1)
        ]
        of_ctx = [(p, i // 4) for p, i in everyone if i % 4 == 0]
        of_exp = [(p, i) for p, i in everyone if i < 4]
        place = lambda p: dict(zip(names, p))
        greet([place(p) for p, _ in everyone])
        first = Scatter(part_ref, ("y",), chunks, part_refs)
        third = Scatter(wo, ("y", "x", "k"), 3, wo_refs, True)
        first.start()
        third.start()
        over_qkv = [
            send(qkv.at[p[2], p[3]], qkv_came.at[i - 1], sems[0], i - 1, place(p))
            for p, i in of_exp
        ]
        def use_first(c, at, total):
            resid = tok[at, :].astype(f32)
            scale = lax.rsqrt(jnp.mean(resid * resid, axis=-1, keepdims=True) + EPSILON)
            normed = resid * scale
            scaled = total * gain_ref[...]
            tokens_ref[at, :] = grad_ref[at, :] + scale * (
                scaled - normed * jnp.mean(scaled * normed, axis=-1, keepdims=True)
            )

        def use_third(c, at, total):
            wo_out[at, :] = total

        for step in range(third.length()):
            if step < first.length():
                first.advance(step, use_first)
            if step < third.length():
                third.advance(step, use_third)
            if step == 1:
                total = qkv[x, k].astype(f32)
                for copy, (_, i) in zip(over_qkv, of_exp):
                    copy.wait_recv()
                    total = total + qkv_came[i - 1].astype(f32)
                qkv_sum[...] = total.astype(bf16)
                qkv_out[z, y] = qkv_sum[z, y]
                over_ctx = [
                    send(qkv_sum.at[p[0], p[1]], qkv_out.at[z, y], sems[1], i - 1, place(p))
                    for p, i in of_ctx
                ]
                over_small = [
                    send(small.at[p], small_came.at[i - 1], sems[2], i - 1, place(p))
                    for p, i in everyone
                ]
        total = small[z, y, x, k].astype(f32)
        for copy, (_, i) in zip(over_small, everyone):
            copy.wait_recv()
            total = total + small_came[i - 1].astype(f32)
        small_out[...] = total
        for copy in over_ctx:
            copy.wait_recv()
        first.finish()
        third.finish()
        for copy in over_qkv + over_ctx + over_small:
            copy.wait_send()

    return exchange(
        kernel,
        "last_step",
        4,
        (part, tokens, grad_middle, gain, qkv_part, wo_part, small_part),
        [ANY_SPEC] + [VMEM_SPEC] * 4 + [ANY_SPEC, VMEM_SPEC],
        [
            jax.ShapeDtypeStruct((count, D), f32),
            jax.ShapeDtypeStruct((4, 2, own, columns), bf16),
            jax.ShapeDtypeStruct((own, D), f32),
            jax.ShapeDtypeStruct((own, 128), f32),
        ],
        [VMEM_SPEC] * 4,
        [
            Scatter.scratch(part, ("y",), chunks),
            Scatter.scratch(wo_part, ("y", "x", "k"), 3),
            [
                pltpu.VMEM((3, 4, 2, own, columns), bf16),
                pltpu.VMEM((4, 2, own, columns), bf16),
                pltpu.VMEM((31, own, 128), bf16),
            ]
            + dma_pair(3)
            + dma_pair(7)
            + dma_pair(31),
        ],
    )


def pick(rows, columns, kind, test):
    row = lax.broadcasted_iota(jnp.int32, (rows, columns), 0)
    column = lax.broadcasted_iota(jnp.int32, (rows, columns), 1)
    return jnp.where(test(row, column), 1.0, 0.0).astype(kind)


def half_swap():
    to_first = pick(256, 256, jnp.float32, lambda r, c: (c % HEAD < HEAD // 2) & (r == c + HEAD // 2))
    to_second = pick(
        256, 256, jnp.float32, lambda r, c: (c % HEAD >= HEAD // 2) & (r + HEAD // 2 == c)
    )
    return to_second - to_first


def twice(a):
    return jnp.concatenate([a, a], axis=-1)


def exact_dot(left, right):
    return jnp.dot(
        left, right, preferred_element_type=jnp.float32, precision=lax.Precision.HIGHEST
    )


def attention_forward_kernel(
    tok, weight, gain, cosine, sine, rows, starts, key_rows, hidden, qk, keys, values, out, lse
):
    bf16, f32 = jnp.bfloat16, jnp.float32
    swap = half_swap()
    width = out.shape[-1]
    to_keys = pick(256, 256, bf16, lambda r, c: (c < width) & (r - width == c % HEAD))
    to_values = pick(128, 256, bf16, lambda r, c: (c < width) & (r == c % HEAD))
    block = 256
    steps = tok.shape[0] // block

    def project(b, carry):
        at = pl.ds(pl.multiple_of(b * block, block), block)
        x = tok[at, :].astype(f32)
        normed = x * lax.rsqrt(jnp.mean(x * x, axis=-1, keepdims=True) + EPSILON)
        h = (normed * gain[...]).astype(bf16)
        hidden[at, :] = h
        t = jnp.dot(h, weight[...], preferred_element_type=f32)
        u = t[:, :256]
        turned = (u * twice(cosine[at, :]) + exact_dot(u, swap) * twice(sine[at, :])).astype(bf16)
        qk[at, :] = turned
        keys[at, :] = jnp.dot(turned, to_keys, preferred_element_type=f32).astype(bf16)
        values[at, :] = jnp.dot(
            t[:, 256:].astype(bf16), to_values, preferred_element_type=f32
        ).astype(bf16)
        return carry

    lax.fori_loop(0, steps, project, 0)
    head = lax.broadcasted_iota(jnp.int32, (block, 256), 1) // HEAD
    lane = lax.broadcasted_iota(jnp.int32, (block, 128), 1)

    def attend(b, carry):
        at = pl.ds(pl.multiple_of(b * block, block), block)
        mask = (key_rows[...] <= rows[at, :]) & (key_rows[...] >= starts[at, :])
        result = jnp.zeros((block, 256), f32)
        logs = jnp.zeros((block, 128), f32)
        for h in range(HEADS // KV_HEADS):
            query = jnp.where(head == h, qk[at, :], jnp.zeros((), bf16))
            scores = contract_cols(query, keys[...]) * HEAD ** (-0.5)
            scores = jnp.where(mask, scores, NEGATIVE)
            top = jnp.max(scores, axis=-1, keepdims=True)
            weights = jnp.exp(scores - top)
            total = jnp.sum(weights, axis=-1, keepdims=True)
            mixed = jnp.dot(weights.astype(bf16), values[...], preferred_element_type=f32)
            result = jnp.where(head == h, mixed / total, result)
            logs = jnp.where(lane == h, top + jnp.log(total), logs)
        out[at, :] = result[:, :width].astype(bf16)
        lse[at, :] = logs
        return carry

    lax.fori_loop(0, steps, attend, 0)


def attention_forward(tokens, weight, gain, cosine, sine, rows, starts):
    count, width = tokens.shape[0], HEADS // KV_HEADS * HEAD
    bf16, f32 = jnp.bfloat16, jnp.float32
    shape = jax.ShapeDtypeStruct
    inputs = (tokens, weight, gain, cosine, sine, rows[:, None], starts[:, None], rows[None, :])
    outs = (
        [shape((count, D), bf16)]
        + [shape((count, 256), bf16)] * 3
        + [shape((count, width), bf16), shape((count, 128), f32)]
    )
    return pl.pallas_call(
        attention_forward_kernel,
        grid=(1,),
        in_specs=[whole(a.shape) for a in inputs],
        out_specs=[whole(a.shape) for a in outs],
        out_shape=outs,
        compiler_params=pltpu.CompilerParams(vmem_limit_bytes=56 * 2**20),
        name="attention_forward",
    )(*inputs)


def attention_backward_kernel(
    hidden, qk, keys, values, lse, upstream, weight, cosine, sine, rows, starts, key_rows,
    weight_grad, hidden_grad, grads, query_grad, key_grad, value_grad, up
):
    bf16, f32 = jnp.bfloat16, jnp.float32
    width = upstream.shape[-1]
    scale = HEAD ** (-0.5)
    block = 256
    steps = hidden.shape[0] // block
    head = lax.broadcasted_iota(jnp.int32, (block, 256), 1) // HEAD
    lane = lax.broadcasted_iota(jnp.int32, (block, 128), 1)
    up[...] = jnp.zeros_like(up)
    up[:, :width] = upstream[...]
    key_grad[...] = jnp.zeros_like(key_grad)
    value_grad[...] = jnp.zeros_like(value_grad)

    def attend(b, carry):
        at = pl.ds(pl.multiple_of(b * block, block), block)
        mask = (key_rows[...] <= rows[at, :]) & (key_rows[...] >= starts[at, :])
        logs = lse[at, :]
        result = jnp.zeros((block, 256), f32)
        for h in range(HEADS // KV_HEADS):
            zero = jnp.zeros((), bf16)
            query = jnp.where(head == h, qk[at, :], zero)
            grad = jnp.where(head == h, up[at, :], zero)
            log = jnp.sum(jnp.where(lane == h, logs, 0.0), axis=-1, keepdims=True)
            scores = contract_cols(query, keys[...]) * scale
            weights = jnp.where(mask, jnp.exp(scores - log), 0.0)
            prob_grad = contract_cols(grad, values[...])
            drift = jnp.sum(weights * prob_grad, axis=-1, keepdims=True)
            score_grad = (weights * (prob_grad - drift)).astype(bf16)
            part = jnp.dot(score_grad, keys[...], preferred_element_type=f32)
            result = jnp.where(head == h, part, result)
            key_grad[...] += contract_rows(score_grad, query)
            value_grad[...] += contract_rows(weights.astype(bf16), grad)
        query_grad[at, :] = result
        return carry

    lax.fori_loop(0, steps, attend, 0)
    swap = half_swap()
    from_keys = pick(256, 256, f32, lambda r, c: (r < width) & (c - width == r % HEAD))
    from_values = pick(256, 128, f32, lambda r, c: (r < width) & (c == r % HEAD))

    def turn(b, carry):
        at = pl.ds(pl.multiple_of(b * block, block), block)
        t = jnp.where(head < HEADS // KV_HEADS, query_grad[at, :], 0.0)
        t = (t + exact_dot(key_grad[at, :], from_keys)) * scale
        grads[at, :256] = (
            t * twice(cosine[at, :]) - exact_dot(t, swap) * twice(sine[at, :])
        ).astype(bf16)
        grads[at, 256:] = exact_dot(value_grad[at, :], from_values).astype(bf16)
        hidden_grad[at, :] = contract_cols(grads[at, :], weight[...]).astype(bf16)
        return carry

    lax.fori_loop(0, steps, turn, 0)
    parts, places, own, columns = weight_grad.shape
    for i in range(places // 2):
        deep = 2 * parts * own
        part = contract_rows(hidden[:, i * deep : (i + 1) * deep], grads[...]).astype(bf16)
        for j in range(2 * parts):
            weight_grad[j % parts, 2 * i + j // parts] = part[j * own : (j + 1) * own, :columns]


def attention_backward(hidden, qk, keys, values, lse, upstream, weight, cosine, sine, rows, starts, own):
    count = hidden.shape[0]
    bf16, f32 = jnp.bfloat16, jnp.float32
    shape = jax.ShapeDtypeStruct
    inputs = (
        hidden, qk, keys, values, lse, upstream, weight, cosine, sine,
        rows[:, None], starts[:, None], rows[None, :],
    )
    outs = [
        shape((4, D // own // 4, own, upstream.shape[-1] + 2 * HEAD), bf16),
        shape((count, D), bf16),
    ]
    return pl.pallas_call(
        attention_backward_kernel,
        grid=(1,),
        in_specs=[whole(a.shape) for a in inputs],
        out_specs=[whole(a.shape) for a in outs],
        out_shape=outs,
        scratch_shapes=[
            pltpu.VMEM((count, 384), bf16),
            pltpu.VMEM((count, 256), f32),
            pltpu.VMEM((count, 256), f32),
            pltpu.VMEM((count, 256), f32),
            pltpu.VMEM((count, 256), bf16),
        ],
        compiler_params=pltpu.CompilerParams(vmem_limit_bytes=56 * 2**20),
        name="attention_backward",
    )(*inputs)


def body_heads(
    tokens,
    cotangent,
    lengths,
    span_perm,
    routes,
    norm_attn,
    attn_q,
    attn_k,
    attn_v,
    attn_o,
    router,
    norm_moe,
    expert_in,
    expert_out,
):
    bf16, f32 = jnp.bfloat16, jnp.float32
    n_z, n_y = (lax.axis_size(a) for a in ("z", "y"))
    n_exp = lax.axis_size("x") * lax.axis_size("k")
    n_ctx = n_z * n_y
    exp_index = lax.axis_index("x") * lax.axis_size("k") + lax.axis_index("k")
    count = tokens.shape[1]
    group = count * n_ctx
    repeat = HEADS // KV_HEADS
    width = repeat * HEAD
    experts = EXP_DEV * n_exp
    capacity = count * TOP * 3 // (2 * experts)
    slots = -(-capacity // 8) * 8
    own = attn_q.shape[0]
    softmax_scale = HEAD ** (-0.5)
    z_index = lax.axis_index("z")

    units = 2 * EXP_DEV // n_z
    y_index = lax.axis_index("y")
    win = expert_in.transpose(1, 0, 2)
    wout = expert_out.transpose(1, 0, 2)
    swap_z = [[(i, i ^ s) for i in range(n_z)] for s in range(n_z)]
    swap_y = [(i, i ^ 1) for i in range(n_y)]
    swap_z = [[(i, i ^ s) for i in range(n_z)] for s in range(n_z)]
    swap_y = [(i, i ^ 1) for i in range(n_y)]

    wq, wk, wv = (a.astype(bf16) for a in (attn_q, attn_k, attn_v))
    own_qkv = jnp.concatenate(
        [
            wq.reshape(own, n_ctx, width),
            wk.reshape(own, n_ctx, HEAD),
            wv.reshape(own, n_ctx, HEAD),
        ],
        axis=-1,
    )
    small = jnp.concatenate(
        [
            router.astype(bf16),
            norm_attn.astype(bf16)[:, None],
            norm_moe.astype(bf16)[:, None],
            jnp.zeros((own, 64 - experts - 2), bf16),
        ],
        axis=1,
    )
    slices = jnp.concatenate(
        [own_qkv.transpose(1, 0, 2), jnp.broadcast_to(small, (n_ctx, own, 64))], axis=-1
    )
    marked = jnp.concatenate(
        [cotangent[0], routes[0].astype(bf16), jnp.zeros((count, 128 - TOP), bf16)], axis=1
    )
    token_all, slices, wo, marked_blocks, near, far, late = share_inputs(
        tokens[0], slices.reshape(n_z, n_y, own, -1), attn_o.astype(bf16), marked, win, wout
    )
    late = lax.ppermute(late, "z", swap_z[3])
    token_all = token_all.reshape(group, D)
    slices = slices.reshape(D, -1)
    wo = wo.reshape(HEADS * HEAD, D)
    small = slices[:, width + 2 * HEAD :]
    weight_r = jnp.concatenate([small[:, :experts], jnp.zeros((D, 128 - experts), bf16)], axis=1)
    gain_one_f = small[:, experts].astype(f32)[None, :]
    gain_two_f = small[:, experts + 1].astype(f32)[None, :]

    perm_row = span_perm[0]
    first_len = lengths[0, 0]
    rows = global_rows(perm_row, jnp.arange(group, dtype=jnp.int32))
    starts = jnp.where(rows >= first_len, first_len, 0)
    freqs = jnp.exp(
        (jnp.arange(128) % (HEAD // 2)).astype(f32) * (-2.0 * math.log(10000.0) / HEAD)
    )
    angle = (rows - starts).astype(f32)[:, None] * freqs[None, :]
    cosine, sine = jnp.cos(angle), jnp.sin(angle)
    hidden_all, queries, keys, values, attended_b, log_total = attention_forward(
        token_all, slices, gain_one_f, cosine, sine, rows, starts
    )
    own_attended, middle, hidden_blocks, *passed = middle_step(
        attended_b.reshape(n_z, n_y, count, width), tokens[0], wo, gain_two_f, [near[1], late]
    )
    parts = [*near, late, far[0], passed[0], far[1], far[2], passed[1]]
    hidden_blocks = hidden_blocks.reshape(-1, count, D)
    marked_blocks = marked_blocks.reshape(-1, count, D + 128)

    blocks = hidden_blocks.shape[0]
    held = 3
    base = exp_index * EXP_DEV + (units * z_index) // 2
    shift = (units * z_index) % 2
    pairs = blocks // 2
    row_in, row_up, slot_gate, spread, gates_blocks = dispatch(
        base, hidden_blocks, marked_blocks, weight_r, held, slots
    )
    gates = lax.dynamic_index_in_dim(gates_blocks, z_index * n_exp + exp_index, 0, keepdims=False)

    meta = jnp.stack([shift, z_index, y_index, base]).astype(jnp.int32)
    made, back, *grads = run_experts(
        meta, row_in, row_up, slot_gate, parts
    )
    made, back = combine(spread, made, back)
    logit_grad, grad_gain_two, grad_middle, grad_heads, output, far_sum, *others = router_step(
        back.reshape(n_z, 2, 2, count, D + 128),
        made.reshape(n_z, 2, 2, count, D),
        middle,
        cotangent[0],
        gates,
        weight_r,
        gain_two_f,
        wo,
        [grads[7], grads[6], grads[5]],
        grads[3],
    )

    add = lambda a, b: (a.astype(f32) + b.astype(f32)).astype(bf16)
    late_sum, mid_sum = add(grads[3][-LATE:], others[0]), add(grads[2], others[1])
    late_sum, mid_sum, grads[4], grad_heads = lax.optimization_barrier(
        (late_sum, mid_sum, grads[4], grad_heads)
    )
    late_sum = lax.ppermute(late_sum, "z", swap_z[3])
    mid_sum = lax.ppermute(mid_sum, "z", swap_z[2])
    other = lax.ppermute(grads[4], "y", swap_y)
    near_sum = lax.ppermute(add(grads[1], others[2]), "z", swap_z[1])

    hidden_two = lax.dynamic_index_in_dim(
        hidden_blocks, z_index * n_exp + exp_index, 0, keepdims=False
    )
    small_grads = jnp.concatenate(
        [
            contract_rows(hidden_two, logit_grad)[:, : 128 - 1],
            grad_gain_two.reshape(D, 1),
        ],
        axis=1,
    )
    small_grads = small_grads.astype(bf16).reshape(n_z, n_y, 2, 2, own, 128)

    grad_wo = jnp.einsum(
        "cth,td->chd",
        own_attended.reshape(n_ctx, count, width),
        grad_middle.astype(bf16),
        preferred_element_type=f32,
    ).astype(bf16)
    grad_wqkv, grad_hidden = attention_backward(
        hidden_all,
        queries,
        keys,
        values,
        log_total,
        grad_heads.reshape(group, width),
        slices,
        cosine,
        sine,
        rows,
        starts,
        own,
    )
    grad_hidden = grad_hidden.reshape(n_z, n_y, count, D)
    grad_tokens, grad_wqkv, grad_wo, small_grads = last_step(
        grad_hidden,
        tokens[0],
        grad_middle,
        gain_one_f,
        grad_wqkv.reshape(2, 2, n_z, n_y, own, width + 2 * HEAD),
        grad_wo.reshape(n_z, n_y, 2, 2, own, D),
        small_grads,
    )
    grad_expert_in, grad_expert_out = place_units(
        z_index, grads[0], other, near_sum, mid_sum, far_sum, late_sum
    )
    grad_expert_in = grad_expert_in.transpose(1, 0, 2)
    grad_expert_out = grad_expert_out.transpose(1, 0, 2)
    grad_wqkv = grad_wqkv.reshape(n_ctx, own, width + 2 * HEAD).astype(f32)
    grad_q = grad_wqkv[:, :, :width].transpose(1, 0, 2).reshape(own, HEADS * HEAD)
    grad_k = grad_wqkv[:, :, width : width + HEAD].transpose(1, 0, 2).reshape(own, KV_HEADS * HEAD)
    grad_v = grad_wqkv[:, :, width + HEAD :].transpose(1, 0, 2).reshape(own, KV_HEADS * HEAD)
    grad_gain_one = jnp.sum(
        grad_wqkv.transpose(1, 0, 2) * own_qkv.astype(f32), axis=(1, 2)
    ) / norm_attn.astype(bf16).astype(f32)
    return (
        output[None],
        grad_tokens[None],
        grad_gain_one,
        grad_q,
        grad_k,
        grad_v,
        grad_wo,
        small_grads[:, :experts],
        small_grads[:, 127],
        grad_expert_in,
        grad_expert_out,
    )


def solution(mesh):
    ctx, exp = mesh.shape["ctx"], mesh.shape["exp"]
    if ctx == KV_HEADS and exp == 4:
        names = ("z", "y", "x", "k")
        inner = jax.sharding.Mesh(mesh.devices.reshape(4, 2, 2, 2), names)
        body, ctx_name, exp_name, both = body_heads, names[:2], names[2:], names
    else:
        inner, body, ctx_name, exp_name, both = mesh, body_general, "ctx", "exp", ("ctx", "exp")
    token = P(exp_name, ctx_name, None)
    group = P(exp_name, None)
    expert = P(ctx_name, exp_name, None)
    rows, gain = P(both, None), P(both)
    in_specs = (token, token, group, group, token, gain) + (rows,) * 5 + (gain, expert, expert)
    out_specs = (token, token, gain) + (rows,) * 5 + (gain, expert, expert)
    return jax.shard_map(
        body, mesh=inner, in_specs=in_specs, out_specs=out_specs, check_vma=False
    )
```

```python
import math

import jax
import jax.numpy as jnp
from jax import lax
from jax.experimental import pallas as pl
from jax.experimental.pallas import tpu as pltpu
from jax.sharding import PartitionSpec as P

D = 1536
HEADS = 24
KV_HEADS = 8
HEAD = 64
HID = 512
TOP = 8
EXP_DEV = 10
SPAN = 64


EPSILON = 1e-06
LATE = 2
NEGATIVE = -1e30


def global_rows(perm_row, rows):
    slots = rows // SPAN
    match = slots[:, None] == jnp.arange(perm_row.shape[0], dtype=jnp.int32)[None, :]
    spans = jnp.sum(jnp.where(match, perm_row[None, :], 0), axis=1)
    return spans * SPAN + rows % SPAN


def rotary(tensor, position, sign):
    half = HEAD // 2
    freqs = jnp.exp(jnp.arange(half, dtype=jnp.float32) * (-2.0 * math.log(10000.0) / HEAD))
    angle = position.astype(jnp.float32)[:, None] * freqs[None, :]
    cosine = jnp.cos(angle)[:, None, :]
    sine = sign * jnp.sin(angle)[:, None, :]
    first, second = (tensor[..., :half], tensor[..., half:])
    return jnp.concatenate(
        [first * cosine - second * sine, second * cosine + first * sine], axis=-1
    )


def allowed(query_rows, key_rows, first_len):
    later = key_rows[None, :] <= query_rows[:, None]
    same_seq = (key_rows[None, :] >= first_len) == (query_rows[:, None] >= first_len)
    return later & same_seq


def contract_rows(left, right):
    return lax.dot_general(
        left, right, (((0,), (0,)), ((), ())), preferred_element_type=jnp.float32
    )


def contract_cols(left, right):
    return lax.dot_general(
        left, right, (((1,), (1,)), ((), ())), preferred_element_type=jnp.float32
    )


def block_grads(
    query_block,
    grad_block,
    lse_block,
    drift_block,
    query_rows,
    key_block,
    value_block,
    key_rows,
    first_len,
):
    softmax_scale = HEAD ** (-0.5)
    scores = (
        jnp.einsum("qgrd,kgd->grqk", query_block, key_block, preferred_element_type=jnp.float32)
        * softmax_scale
    )
    mask = allowed(query_rows, key_rows, first_len)[None, None]
    weights = jnp.where(mask, jnp.exp(scores - lse_block.transpose(1, 2, 0)[..., None]), 0.0)
    prob_grad = jnp.einsum(
        "qgrd,kgd->grqk", grad_block, value_block, preferred_element_type=jnp.float32
    )
    score_grad = (weights * (prob_grad - drift_block.transpose(1, 2, 0)[..., None])).astype(
        jnp.bfloat16
    )
    query_grad = None
    key_grad = None
    value_grad = None
    query_grad = (
        jnp.einsum("grqk,kgd->qgrd", score_grad, key_block, preferred_element_type=jnp.float32)
        * softmax_scale
    )
    value_grad = jnp.einsum(
        "grqk,qgrd->kgd",
        weights.astype(jnp.bfloat16),
        grad_block,
        preferred_element_type=jnp.float32,
    )
    key_grad = (
        jnp.einsum("grqk,qgrd->kgd", score_grad, query_block, preferred_element_type=jnp.float32)
        * softmax_scale
    )
    return (query_grad, key_grad, value_grad)


def body_general(
    tokens,
    cotangent,
    lengths,
    span_perm,
    routes,
    norm_attn,
    attn_q,
    attn_k,
    attn_v,
    attn_o,
    router,
    norm_moe,
    expert_in,
    expert_out,
):
    count = tokens.shape[1]
    repeat = HEADS // KV_HEADS
    experts = EXP_DEV * lax.axis_size("exp")
    capacity = count * TOP * 3 // (2 * experts)
    softmax_scale = HEAD ** (-0.5)
    perm_row = span_perm[0]
    first_len = lengths[0, 0]
    query_rows = global_rows(
        perm_row, lax.axis_index("ctx") * count + jnp.arange(count, dtype=jnp.int32)
    )
    position = query_rows - jnp.where(query_rows >= first_len, first_len, 0)
    gathered = (
        lax.all_gather(norm_attn.astype(jnp.bfloat16), ("ctx", "exp"), axis=0, tiled=True),
        lax.all_gather(attn_q.astype(jnp.bfloat16), ("ctx", "exp"), axis=0, tiled=True),
        lax.all_gather(attn_k.astype(jnp.bfloat16), ("ctx", "exp"), axis=0, tiled=True),
        lax.all_gather(attn_v.astype(jnp.bfloat16), ("ctx", "exp"), axis=0, tiled=True),
        lax.all_gather(attn_o.astype(jnp.bfloat16), ("ctx", "exp"), axis=0, tiled=True),
        lax.all_gather(router.astype(jnp.bfloat16), ("ctx", "exp"), axis=0, tiled=True),
        lax.all_gather(norm_moe.astype(jnp.bfloat16), ("ctx", "exp"), axis=0, tiled=True),
    )
    gain_one, weight_q, weight_k, weight_v, weight_o, weight_r, gain_two = gathered
    weight_in, weight_out = (
        lax.all_gather(expert_in.astype(jnp.bfloat16), "ctx", axis=0, tiled=True),
        lax.all_gather(expert_out.astype(jnp.bfloat16), "ctx", axis=0, tiled=True),
    )
    gain_one_f = gain_one.astype(jnp.float32)
    gain_two_f = gain_two.astype(jnp.float32)
    resid = tokens[0].astype(jnp.float32)
    scale_one = lax.rsqrt(jnp.mean(resid * resid, axis=-1, keepdims=True) + EPSILON)
    normed_one = resid * scale_one
    hidden_one = (normed_one * gain_one_f).astype(jnp.bfloat16)
    query_pre = jnp.dot(hidden_one, weight_q, preferred_element_type=jnp.float32).reshape(
        count, HEADS, HEAD
    )
    queries = (
        rotary(query_pre, position, 1.0).astype(jnp.bfloat16).reshape(count, KV_HEADS, repeat, HEAD)
    )
    key_pre = jnp.dot(hidden_one, weight_k, preferred_element_type=jnp.float32).reshape(
        count, KV_HEADS, HEAD
    )
    keys = rotary(key_pre, position, 1.0).astype(jnp.bfloat16)
    values = (
        jnp.dot(hidden_one, weight_v, preferred_element_type=jnp.float32)
        .astype(jnp.bfloat16)
        .reshape(count, KV_HEADS, HEAD)
    )
    start_state = (
        jnp.full((KV_HEADS, repeat, count), NEGATIVE, jnp.float32),
        jnp.zeros((KV_HEADS, repeat, count), jnp.float32),
        jnp.zeros((KV_HEADS, repeat, count, HEAD), jnp.float32),
    )
    carry = start_state
    key_piece = lax.all_gather(keys, "ctx", axis=0, tiled=True)
    value_piece = lax.all_gather(values, "ctx", axis=0, tiled=True)
    size = key_piece.shape[0]
    block = math.gcd(size, 512)
    number = size // block
    key_blocks = key_piece.reshape(number, block, KV_HEADS, HEAD)
    value_blocks = value_piece.reshape(number, block, KV_HEADS, HEAD)
    offsets = jnp.arange(size, dtype=jnp.int32).reshape(number, block)

    def forward_step(state, inputs):
        highest, total, accum = state
        key_block, value_block, offset = inputs
        key_rows = global_rows(perm_row, offset)
        scores = (
            jnp.einsum("qgrd,kgd->grqk", queries, key_block, preferred_element_type=jnp.float32)
            * softmax_scale
        )
        mask = allowed(query_rows, key_rows, first_len)[None, None]
        scores = jnp.where(mask, scores, NEGATIVE)
        newmax = jnp.maximum(highest, jnp.max(scores, axis=-1))
        weights = jnp.where(mask, jnp.exp(scores - newmax[..., None]), 0.0)
        factor = jnp.exp(highest - newmax)
        total = total * factor + jnp.sum(weights, axis=-1)
        accum = accum * factor[..., None] + jnp.einsum(
            "grqk,kgd->grqd",
            weights.astype(jnp.bfloat16),
            value_block,
            preferred_element_type=jnp.float32,
        )
        return ((newmax, total, accum), None)

    carry, _ = lax.scan(forward_step, carry, (key_blocks, value_blocks, offsets))
    highest, total, accum = carry
    log_total = (highest + jnp.log(total)).transpose(2, 0, 1)
    attended = (accum / total[..., None]).transpose(2, 0, 1, 3)
    attended_b = attended.reshape(count, HEADS * HEAD).astype(jnp.bfloat16)
    middle = resid + jnp.dot(attended_b, weight_o, preferred_element_type=jnp.float32)
    scale_two = lax.rsqrt(jnp.mean(middle * middle, axis=-1, keepdims=True) + EPSILON)
    normed_two = middle * scale_two
    hidden_two = (normed_two * gain_two_f).astype(jnp.bfloat16)
    logits = jnp.dot(hidden_two, weight_r, preferred_element_type=jnp.float32)
    chosen = routes[0]
    picks = chosen[:, :, None] == jnp.arange(experts, dtype=jnp.int32)[None, None, :]
    selected = jnp.sum(jnp.where(picks, logits[:, None, :], 0.0), axis=-1)
    gates = jax.nn.softmax(selected, axis=-1)
    gates_b = gates.astype(jnp.bfloat16)
    flat_picks = picks.reshape(count * TOP, experts).astype(jnp.int32)
    placed = jnp.sum((jnp.cumsum(flat_picks, axis=0) - 1) * flat_picks, axis=-1)
    column = chosen.reshape(-1) * capacity + placed
    hits = (
        column.reshape(count, TOP)[:, :, None]
        == jnp.arange(experts * capacity, dtype=jnp.int32)[None, None, :]
    )
    spread = jnp.any(hits, axis=1).astype(jnp.bfloat16)
    weighted = jnp.sum(
        jnp.where(hits, gates_b.astype(jnp.float32)[:, :, None], 0.0), axis=1
    ).astype(jnp.bfloat16)
    outgoing = contract_rows(spread, hidden_two).astype(jnp.bfloat16).reshape(experts, capacity, D)
    incoming = lax.all_to_all(outgoing, "exp", split_axis=0, concat_axis=1, tiled=True)
    gate_up = jnp.einsum("erd,dec->erc", incoming, weight_in, preferred_element_type=jnp.float32)
    gate_part = gate_up[..., :HID]
    up_part = gate_up[..., HID:]
    sigmoid_gate = jax.nn.sigmoid(gate_part)
    silu_gate = gate_part * sigmoid_gate
    activated = (silu_gate * up_part).astype(jnp.bfloat16)
    produced = jnp.einsum(
        "erh,deh->erd", activated, weight_out, preferred_element_type=jnp.float32
    ).astype(jnp.bfloat16)
    returned = lax.all_to_all(produced, "exp", split_axis=1, concat_axis=0, tiled=True).reshape(
        experts * capacity, D
    )
    mixture = jnp.dot(weighted, returned, preferred_element_type=jnp.float32)
    output = (middle + mixture).astype(jnp.bfloat16)
    upstream = cotangent[0].astype(jnp.float32)
    upstream_b = upstream.astype(jnp.bfloat16)
    sent_grad = (
        contract_rows(weighted, upstream_b).astype(jnp.bfloat16).reshape(experts, capacity, D)
    )
    grad_in = lax.all_to_all(sent_grad, "exp", split_axis=0, concat_axis=1, tiled=True)
    picked = jnp.take(returned, column, axis=0).reshape(count, TOP, D)
    gate_grad = jnp.einsum("tkd,td->tk", picked, upstream_b, preferred_element_type=jnp.float32)
    grad_act = (
        jnp.einsum("erd,deh->erh", grad_in, weight_out, preferred_element_type=jnp.float32)
        .astype(jnp.bfloat16)
        .astype(jnp.float32)
    )
    grad_gate = grad_act * up_part * (sigmoid_gate * (1.0 + gate_part * (1.0 - sigmoid_gate)))
    grad_up = grad_act * silu_gate
    grad_gu = jnp.concatenate([grad_gate, grad_up], axis=-1).astype(jnp.bfloat16)
    grad_weight_out = jnp.einsum(
        "erd,erh->deh", grad_in, activated, preferred_element_type=jnp.float32
    )
    grad_weight_in = jnp.einsum(
        "erd,erc->dec", incoming, grad_gu, preferred_element_type=jnp.float32
    )
    grad_rows = jnp.einsum(
        "erc,dec->erd", grad_gu, weight_in, preferred_element_type=jnp.float32
    ).astype(jnp.bfloat16)
    back_rows = lax.all_to_all(grad_rows, "exp", split_axis=1, concat_axis=0, tiled=True).reshape(
        experts * capacity, D
    )
    expert_sums = (
        lax.psum_scatter(
            grad_weight_in.astype(jnp.bfloat16), "ctx", scatter_dimension=0, tiled=True
        ).astype(jnp.float32),
        lax.psum_scatter(
            grad_weight_out.astype(jnp.bfloat16), "ctx", scatter_dimension=0, tiled=True
        ).astype(jnp.float32),
    )
    centered = gate_grad - jnp.sum(gates * gate_grad, axis=-1, keepdims=True)
    select_grad = gates * centered
    logit_grad = jnp.sum(jnp.where(picks, select_grad[:, :, None], 0.0), axis=1).astype(
        jnp.bfloat16
    )
    grad_router = contract_rows(hidden_two, logit_grad)
    grad_norm_two = jnp.dot(spread, back_rows, preferred_element_type=jnp.float32) + contract_cols(
        logit_grad, weight_r
    )
    grad_gain_two = jnp.sum(grad_norm_two * normed_two, axis=0)
    scaled_two = grad_norm_two * gain_two_f
    grad_middle = upstream + scale_two * (
        scaled_two - normed_two * jnp.mean(scaled_two * normed_two, axis=-1, keepdims=True)
    )
    branch_grad = grad_middle.astype(jnp.bfloat16)
    grad_weight_o = contract_rows(attended_b, branch_grad)
    grad_heads = (
        contract_cols(branch_grad, weight_o)
        .astype(jnp.bfloat16)
        .reshape(count, KV_HEADS, repeat, HEAD)
    )
    drift = jnp.sum(grad_heads.astype(jnp.float32) * attended, axis=-1)
    query_acc = jnp.zeros((count, KV_HEADS, repeat, HEAD), jnp.float32)
    key_piece = lax.all_gather(keys, "ctx", axis=0, tiled=True)
    value_piece = lax.all_gather(values, "ctx", axis=0, tiled=True)
    size = key_piece.shape[0]
    block = math.gcd(size, 512)
    number = size // block
    key_blocks = key_piece.reshape(number, block, KV_HEADS, HEAD)
    value_blocks = value_piece.reshape(number, block, KV_HEADS, HEAD)
    offsets = jnp.arange(size, dtype=jnp.int32).reshape(number, block)

    def backward_step(acc, inputs):
        key_block, value_block, offset = inputs
        part_q, part_k, part_v = block_grads(
            queries,
            grad_heads,
            log_total,
            drift,
            query_rows,
            key_block,
            value_block,
            global_rows(perm_row, offset),
            first_len,
        )
        joined = jnp.concatenate(
            [part_k.reshape(block, KV_HEADS * HEAD), part_v.reshape(block, KV_HEADS * HEAD)],
            axis=-1,
        )
        return (acc + part_q, joined)

    query_acc, joined_parts = lax.scan(
        backward_step, query_acc, (key_blocks, value_blocks, offsets)
    )
    pair_acc = joined_parts.reshape(size, 2 * KV_HEADS * HEAD)
    query_grad, pair_acc = (query_acc, pair_acc)
    pair_own = lax.psum_scatter(
        pair_acc.astype(jnp.bfloat16), "ctx", scatter_dimension=0, tiled=True
    ).astype(jnp.float32)
    key_grad = pair_own[:, : KV_HEADS * HEAD].reshape(count, KV_HEADS, HEAD)
    value_grad = pair_own[:, KV_HEADS * HEAD :].reshape(count, KV_HEADS, HEAD)
    query_grad_b = (
        rotary(query_grad.reshape(count, HEADS, HEAD), position, -1.0)
        .astype(jnp.bfloat16)
        .reshape(count, HEADS * HEAD)
    )
    key_grad_b = (
        rotary(key_grad, position, -1.0).astype(jnp.bfloat16).reshape(count, KV_HEADS * HEAD)
    )
    value_grad_b = value_grad.astype(jnp.bfloat16).reshape(count, KV_HEADS * HEAD)
    grad_weight_q = contract_rows(hidden_one, query_grad_b)
    grad_weight_k = contract_rows(hidden_one, key_grad_b)
    grad_weight_v = contract_rows(hidden_one, value_grad_b)
    grad_hidden_one = (
        contract_cols(query_grad_b, weight_q)
        + contract_cols(key_grad_b, weight_k)
        + contract_cols(value_grad_b, weight_v)
    )
    grad_gain_one = jnp.sum(grad_hidden_one * normed_one, axis=0)
    scaled_one = grad_hidden_one * gain_one_f
    grad_tokens = grad_middle + scale_one * (
        scaled_one - normed_one * jnp.mean(scaled_one * normed_one, axis=-1, keepdims=True)
    )
    attn_sums = (
        lax.psum_scatter(grad_gain_one, ("ctx", "exp"), scatter_dimension=0, tiled=True),
        lax.psum_scatter(grad_weight_q, ("ctx", "exp"), scatter_dimension=0, tiled=True),
        lax.psum_scatter(grad_weight_k, ("ctx", "exp"), scatter_dimension=0, tiled=True),
        lax.psum_scatter(grad_weight_v, ("ctx", "exp"), scatter_dimension=0, tiled=True),
        lax.psum_scatter(grad_weight_o, ("ctx", "exp"), scatter_dimension=0, tiled=True),
        lax.psum_scatter(grad_router, ("ctx", "exp"), scatter_dimension=0, tiled=True),
        lax.psum_scatter(grad_gain_two, ("ctx", "exp"), scatter_dimension=0, tiled=True),
    )
    return (
        output[None],
        grad_tokens[None],
        attn_sums[0],
        attn_sums[1],
        attn_sums[2],
        attn_sums[3],
        attn_sums[4],
        attn_sums[5],
        attn_sums[6],
        expert_sums[0],
        expert_sums[1],
    )


def rotate(tensor, cosine, sine):
    half = HEAD // 2
    first, second = (tensor[..., :half], tensor[..., half:])
    return jnp.concatenate(
        [first * cosine - second * sine, second * cosine + first * sine], axis=-1
    )


def dispatch_kernel(base, hid_ref, mark_ref, router_ref, rows_ref, up_ref, gate_ref, spread_ref, gates_ref):
    bf16, f32 = jnp.bfloat16, jnp.float32
    count = hid_ref.shape[1]
    _, held, rows, _ = rows_ref.shape
    slots = rows // 2
    both = 2 * count
    x = hid_ref[...].reshape(both, D)
    logits = jnp.dot(x, router_ref[...], preferred_element_type=f32)
    routes = mark_ref[:, :, D:].reshape(both, 128).astype(f32)
    lane = lax.broadcasted_iota(jnp.int32, (both, 128), 1).astype(f32)
    picks = jnp.zeros((both, 128), f32)
    for i in range(TOP):
        picks = jnp.where(routes[:, i : i + 1] == lane, 1.0, picks)
    masked = jnp.where(picks > 0.0, logits, NEGATIVE)
    top = jnp.max(masked, axis=-1, keepdims=True)
    gates = jnp.where(picks > 0.0, jnp.exp(masked - top), 0.0)
    gates = gates / jnp.sum(gates, axis=-1, keepdims=True)
    gates_ref[...] = gates.reshape(2, count, 128)
    which = lax.broadcasted_iota(jnp.int32, (8, 128), 0)
    columns = lax.broadcasted_iota(jnp.int32, (8, 128), 1)
    chosen = jnp.where(columns == which + base[0], 1.0, 0.0).astype(bf16)
    hit = contract_cols(chosen, picks.astype(bf16))
    gate = contract_cols(chosen, gates.astype(bf16))
    earlier = lax.broadcasted_iota(jnp.int32, (both, both), 0)
    later = lax.broadcasted_iota(jnp.int32, (both, both), 1)
    upto = jnp.where((earlier <= later) & (earlier // count == later // count), 1.0, 0.0)
    rank = jnp.dot(hit.astype(bf16), upto.astype(bf16), preferred_element_type=f32)
    row = lax.broadcasted_iota(jnp.int32, (rows, both), 0)
    token = lax.broadcasted_iota(jnp.int32, (rows, both), 1)
    side = row // slots
    wanted = jnp.where(side == token // count, row - side * slots + 1, -1).astype(f32)
    for e in range(held):
        here = jnp.where((rank[e : e + 1] == wanted) & (hit[e : e + 1] > 0.0), 1.0, 0.0)
        gate_ref[0, e] = jnp.sum(here * gate[e : e + 1], axis=-1, keepdims=True)
        here = here.astype(bf16)
        spread_ref[0, e * rows : (e + 1) * rows, :] = here
        rows_ref[0, e] = jnp.dot(here, x, preferred_element_type=f32).astype(bf16)
        up_ref[0, e] = jnp.dot(
            here, mark_ref[:, :, :D].reshape(both, D), preferred_element_type=f32
        ).astype(bf16)


def dispatch(base, hidden, marked, router, held, slots):
    blocks, count, _ = hidden.shape
    pairs = blocks // 2
    bf16, f32 = jnp.bfloat16, jnp.float32
    pair = lambda *shape: pl.BlockSpec((1,) + shape, lambda p, b: (p,) + (0,) * len(shape))
    two = lambda width: pl.BlockSpec((2, count, width), lambda p, b: (p, 0, 0))
    return pl.pallas_call(
        dispatch_kernel,
        grid_spec=pltpu.PrefetchScalarGridSpec(
            num_scalar_prefetch=1,
            grid=(pairs,),
            in_specs=[two(D), two(D + 128), pl.BlockSpec((D, 128), lambda p, b: (0, 0))],
            out_specs=[
                pair(held, 2 * slots, D),
                pair(held, 2 * slots, D),
                pair(held, 2 * slots, 1),
                pair(held * 2 * slots, 2 * count),
                two(128),
            ],
        ),
        out_shape=[
            jax.ShapeDtypeStruct((pairs, held, 2 * slots, D), bf16),
            jax.ShapeDtypeStruct((pairs, held, 2 * slots, D), bf16),
            jax.ShapeDtypeStruct((pairs, held, 2 * slots, 1), f32),
            jax.ShapeDtypeStruct((pairs, held * 2 * slots, 2 * count), bf16),
            jax.ShapeDtypeStruct((blocks, count, 128), f32),
        ],
        compiler_params=pltpu.CompilerParams(vmem_limit_bytes=48 * 2**20),
        name="dispatch",
    )(base.reshape(1).astype(jnp.int32), hidden, marked, router)


def combine_kernel(spread, made, back, made_out, back_out):
    for rows, out in ((made, made_out), (back, back_out)):
        width = rows.shape[-1]
        total = contract_rows(spread[0], rows[0].reshape(-1, width))
        out[...] = total.astype(out.dtype).reshape(out.shape)


def combine(spread, made, back):
    pairs, slots, both = spread.shape
    count = both // 2
    rows = lambda a: pl.BlockSpec((1, *a.shape[1:]), lambda p: (p,) + (0,) * (a.ndim - 1))
    return pl.pallas_call(
        combine_kernel,
        grid=(pairs,),
        in_specs=[rows(spread), rows(made), rows(back)],
        out_specs=[
            pl.BlockSpec((2, count, a.shape[-1]), lambda p: (p, 0, 0)) for a in (made, back)
        ],
        out_shape=[
            jax.ShapeDtypeStruct((2 * pairs, count, a.shape[-1]), jnp.bfloat16)
            for a in (made, back)
        ],
        compiler_params=pltpu.CompilerParams(vmem_limit_bytes=48 * 2**20),
        name="combine",
    )(spread, made, back)


def expert_kernel(depth, meta, x_ref, g_ref, gate_ref, *refs):
    parts, (y_ref, d_ref), outs = refs[:10], refs[10:12], refs[12:20]
    weight, du_ref, act_ref = refs[20:]
    bf16, f32 = jnp.bfloat16, jnp.float32
    j = pl.program_id(0)
    shift, z, y, base = meta[0], meta[1], meta[2], meta[3]
    half = HID // 2
    offsets = [
        pl.multiple_of(((z ^ (i % 4)) * 2 + (y ^ (i // 4))) * depth, 64) for i in range(8)
    ]
    cut = pl.num_programs(0) - LATE
    for i, offset in enumerate(offsets):
        group = parts[i // 4 * 5 + i % 4 : i // 4 * 5 + i % 4 + (2 if i % 4 == 3 else 1)]
        for part, here in zip(group, (j < cut, j >= cut) if len(group) > 1 else (j >= 0,)):

            @pl.when(here)
            def _(part=part, offset=offset):
                weight[pl.ds(offset, depth), :] = part[0]

    expert = base + (j + shift) // 2
    first = jnp.logical_or(j == 0, lax.rem(j + shift, 2) == 0)
    keep = jnp.where(first, 0.0, 1.0)
    pairs, _, rows, _ = x_ref.shape
    step = 8

    def forward(i, carry):
        at = pl.ds(i * step, step)
        flat = pl.ds(pl.multiple_of(i * step * rows, 32), step * rows)
        x = x_ref[at, 0].reshape(step * rows, D)
        g = g_ref[at, 0].reshape(step * rows, D)
        gate = gate_ref[at, 0].reshape(step * rows, 1)
        u = jnp.dot(x, weight[:, : 2 * half], preferred_element_type=f32)
        raw = jnp.dot(g, weight[:, 2 * half :], preferred_element_type=f32)
        u1, u2 = u[:, :half], u[:, half:]
        sig = jax.nn.sigmoid(u1)
        silu = u1 * sig
        act = (silu * u2).astype(bf16).astype(f32)
        dgate = jnp.sum(raw * act, axis=-1, keepdims=True)
        dact = raw * gate
        du1 = dact * u2 * (sig * (1.0 + u1 * (1.0 - sig)))
        du = jnp.concatenate([du1, dact * silu], axis=-1).astype(bf16)
        act_gated = (act * gate).astype(bf16)
        du_ref[flat, :] = du
        act_ref[flat, :] = act_gated
        made = contract_cols(act_gated, weight[:, 2 * half :])
        back = contract_cols(du, weight[:, : 2 * half])
        lane = lax.broadcasted_iota(jnp.int32, (step * rows, 128), 1)
        tail = jnp.where(lane == expert, dgate, 0.0)

        @pl.when(first)
        def _():
            y_ref[at, 0] = made.astype(bf16).reshape(step, rows, D)
            d_ref[at, 0, :, :D] = back.astype(bf16).reshape(step, rows, D)
            d_ref[at, 0, :, D:] = tail.astype(bf16).reshape(step, rows, 128)

        @pl.when(jnp.logical_not(first))
        def _():
            old_y = y_ref[at, 0].reshape(step * rows, D).astype(f32)
            y_ref[at, 0] = (made + old_y).astype(bf16).reshape(step, rows, D)
            old_d = d_ref[at, 0].reshape(step * rows, D + 128).astype(f32)
            d_ref[at, 0, :, :D] = (back + old_d[:, :D]).astype(bf16).reshape(step, rows, D)
            d_ref[at, 0, :, D:] = (tail + old_d[:, D:]).astype(bf16).reshape(step, rows, 128)

        return carry

    lax.fori_loop(0, pairs // step, forward, 0)

    wide = D // 2

    def gradient(i, carry):
        at = pl.ds(pl.multiple_of(i * wide, wide), wide)
        x = x_ref[:, 0, :, at].reshape(pairs * rows, wide)
        g = g_ref[:, 0, :, at].reshape(pairs * rows, wide)
        weight[at, : 2 * half] = contract_rows(x, du_ref[...]).astype(bf16)
        weight[at, 2 * half :] = contract_rows(g, act_ref[...]).astype(bf16)
        return carry

    lax.fori_loop(0, D // wide, gradient, 0)
    for out, offset in zip(outs, offsets):
        out[0] = weight[pl.ds(offset, depth), :]


def run_experts(meta, row_in, row_up, slot_gate, parts):
    pairs, held, rows, _ = row_in.shape
    units, depth, columns = parts[0].shape
    held_block = lambda width: pl.BlockSpec(
        (pairs, 1, rows, width), lambda j, m: (0, (j + m[0]) // 2, 0, 0)
    )
    unit_block = pl.BlockSpec((1, depth, columns), lambda j, m: (j, 0, 0))
    cut = units - LATE
    early_block = pl.BlockSpec((1, depth, columns), lambda j, m: (jnp.minimum(j, cut - 1), 0, 0))
    late_block = pl.BlockSpec((1, depth, columns), lambda j, m: (jnp.maximum(j - cut, 0), 0, 0))
    bf16 = jnp.bfloat16
    total = units * pairs * rows * D * columns * 6
    return pl.pallas_call(
        lambda *refs: expert_kernel(depth, *refs),
        grid_spec=pltpu.PrefetchScalarGridSpec(
            num_scalar_prefetch=1,
            grid=(units,),
            in_specs=[
                held_block(D),
                held_block(D),
                held_block(1),
            ]
            + [unit_block, unit_block, unit_block, early_block, late_block] * 2,
            out_specs=[held_block(D), held_block(D + 128)] + [unit_block] * 8,
            scratch_shapes=[
                pltpu.VMEM((D, columns), bf16),
                pltpu.VMEM((pairs * rows, HID), bf16),
                pltpu.VMEM((pairs * rows, HID // 2), bf16),
            ],
        ),
        out_shape=[
            jax.ShapeDtypeStruct((pairs, held, rows, D), bf16),
            jax.ShapeDtypeStruct((pairs, held, rows, D + 128), bf16),
        ]
        + [jax.ShapeDtypeStruct((units, depth, columns), bf16)] * 8,
        compiler_params=pltpu.CompilerParams(vmem_limit_bytes=56 * 2**20),
        cost_estimate=pl.CostEstimate(
            flops=total, bytes_accessed=60 * 2**20, transcendentals=units * pairs * rows * HID
        ),
        name="experts",
    )(meta, row_in, row_up, slot_gate, *parts)


def place_kernel(number, z_ref, *refs):
    in_ref, out_ref = refs[12:]
    half = refs[0].shape[-1] // 3
    for h in range(2):
        unit = 2 * pl.program_id(0) + h
        source = (unit // number) ^ z_ref[0]
        late = (source == 3) & (lax.rem(unit, number) >= number - LATE)
        source = jnp.where(late, 4, source)
        first, other, *rest = refs[6 * h : 6 * h + 6]
        for i, group in enumerate([(first, other)] + [(ref,) for ref in rest]):

            @pl.when(source == i)
            def _(h=h, group=group):
                total = group[0][0].astype(jnp.float32)
                for ref in group[1:]:
                    total = total + ref[0].astype(jnp.float32)
                in_ref[0, :, h * half : (h + 1) * half] = total[:, :half]
                in_ref[0, :, HID + h * half : HID + (h + 1) * half] = total[:, half : 2 * half]
                out_ref[0, :, h * half : (h + 1) * half] = total[:, 2 * half :]


def place_units(z_index, first, other, near, mid, far, late):
    number, depth, columns = first.shape

    def block(i, h):
        low, most = {3: (0, number - LATE - 1), 4: (number - LATE, LATE - 1)}.get(i, (0, number - 1))

        def index(e, z):
            unit = 2 * e + h
            at = jnp.clip(lax.rem(unit, number) - low, 0, most)
            return jnp.where((unit // number) ^ z[0] == min(i, 3), at, 0), 0, 0

        return pl.BlockSpec((1, depth, columns), index)

    return pl.pallas_call(
        lambda *refs: place_kernel(number, *refs),
        grid_spec=pltpu.PrefetchScalarGridSpec(
            num_scalar_prefetch=1,
            grid=(EXP_DEV,),
            in_specs=[block(i, h) for h in range(2) for i in (0, 0, 1, 2, 3, 4)],
            out_specs=[
                pl.BlockSpec((1, depth, 2 * HID), lambda e, z: (e, 0, 0)),
                pl.BlockSpec((1, depth, HID), lambda e, z: (e, 0, 0)),
            ],
        ),
        out_shape=[
            jax.ShapeDtypeStruct((EXP_DEV, depth, 2 * HID), jnp.float32),
            jax.ShapeDtypeStruct((EXP_DEV, depth, HID), jnp.float32),
        ],
        name="place_units",
    )(z_index.reshape(1), *[first, other, near, mid, far, late] * 2)


MESH = pl.DeviceIdType.MESH


def greet(peers):
    barrier = pltpu.get_barrier_semaphore()
    for peer in peers:
        pl.semaphore_signal(barrier, inc=1, device_id=peer, device_id_type=MESH)
    pl.semaphore_wait(barrier, len(peers))


def send(src, dst, sems, at, peer):
    copy = pltpu.make_async_remote_copy(
        src_ref=src,
        dst_ref=dst,
        send_sem=sems[0].at[at],
        recv_sem=sems[1].at[at],
        device_id=peer,
        device_id_type=MESH,
    )
    copy.start()
    return copy


def dma_pair(number):
    return [pltpu.SemaphoreType.DMA((number,)), pltpu.SemaphoreType.DMA((number,))]


def z_peers():
    z = lax.axis_index("z")
    return [{"z": z ^ s} for s in (3, 2, 1)]


def siblings(axes):
    return [{a: 1 - lax.axis_index(a)} for a in axes]


class Scatter:
    def __init__(self, part, axes, chunks, refs, direct=False):
        self.part, self.axes, self.chunks, self.direct = part, axes, chunks, direct
        depth = len(axes)
        self.own, self.came = refs[0], refs[1 : 1 + depth]
        self.sums = refs[1 + depth : 1 + 2 * depth]
        self.turn, self.line, self.result, self.load_sem = refs[1 + 2 * depth : 5 + 2 * depth]
        sems = refs[5 + 2 * depth :]
        self.sems = [sems[2 * i : 2 * i + 2] for i in range(depth + 1)]
        self.z = lax.axis_index("z")
        self.mine = [lax.axis_index(a) for a in axes]
        self.rows = part.shape[-2] // chunks
        self.flying = [[None] * chunks for _ in axes]

    @staticmethod
    def scratch(part, axes, chunks):
        n_z, rows, width, kind = part.shape[0], part.shape[-2], part.shape[-1], part.dtype
        depth = len(axes)

        def buffer(i):
            return pltpu.VMEM((chunks, n_z) + (2,) * i + (rows // chunks, width), kind)

        shapes = [buffer(depth - 1)] + [buffer(i) for i in range(depth)] * 2
        shapes += [buffer(0), pltpu.VMEM((chunks, n_z + 1, rows // chunks, width), kind)]
        shapes += [pltpu.VMEM((rows // chunks, width), jnp.float32)]
        shapes += [pltpu.SemaphoreType.DMA((chunks,))]
        for _ in range(depth):
            shapes += dma_pair(chunks)
        return shapes + dma_pair(chunks * (n_z + 1))

    def start(self):
        level = len(self.axes) - 1
        lead = (slice(None),) * len(self.axes)
        mine = self.mine[-1]
        self.loads = []
        for c in range(self.chunks):
            at = pl.ds(c * self.rows, self.rows)
            self.flying[level][c] = send(
                self.part.at[lead + (1 - mine, at)],
                self.came[level].at[c],
                self.sems[level],
                c,
                {self.axes[-1]: 1 - mine},
            )
            load = pltpu.make_async_copy(
                self.part.at[lead + (mine, at)], self.own.at[c], self.load_sem.at[c]
            )
            load.start()
            self.loads.append(load)

    def fold(self, level, c):
        self.flying[level][c].wait_recv()
        if level == len(self.axes) - 1:
            self.loads[c].wait()
            held = self.own[c]
        else:
            held = self.sums[level + 1][
                (c,) + (slice(None),) * (level + 1) + (self.mine[level],)
            ]
        total = held.astype(jnp.float32) + self.came[level][c].astype(jnp.float32)
        self.sums[level][c] = total.astype(held.dtype)
        if level > 0:
            mine = self.mine[level - 1]
            self.flying[level - 1][c] = send(
                self.sums[level].at[(c,) + (slice(None),) * level + (1 - mine,)],
                self.came[level - 1].at[c],
                self.sems[level - 1],
                c,
                {self.axes[level - 1]: 1 - mine},
            )

    def along(self, c, w, up):
        slot = w + 1 if up else w
        return pltpu.make_async_remote_copy(
            src_ref=self.turn.at[c, w],
            dst_ref=self.line.at[c, slot],
            send_sem=self.sems[-1][0].at[w * self.chunks + c],
            recv_sem=self.sems[-1][1].at[slot * self.chunks + c],
            device_id={"z": self.z + 1 if up else self.z - 1},
            device_id_type=MESH,
        )

    def steps(self):
        return [(3, True), (0, False), (2, True), (1, False), (1, True), (2, False)]

    def over_z(self, c, s):
        return pltpu.make_async_remote_copy(
            src_ref=self.sums[0].at[c, self.z ^ s],
            dst_ref=self.line.at[c, s],
            send_sem=self.sems[-1][0].at[s * self.chunks + c],
            recv_sem=self.sems[-1][1].at[s * self.chunks + c],
            device_id={"z": self.z ^ s},
            device_id_type=MESH,
        )

    def relay(self, c):
        z = self.z
        if self.direct:
            for s in (3, 2, 1):
                self.over_z(c, s).start()
            return
        for w, up in self.steps():
            slot = w + 1 if up else w

            @pl.when((z < w) if up else (z > w))
            def _(w=w, up=up, slot=slot):
                inner = (z > 0) if up else (z < 3)

                @pl.when(inner)
                def _():
                    self.along(c, w, up).wait_recv()
                    total = self.sums[0][c, w].astype(jnp.float32) + self.line[c, slot].astype(
                        jnp.float32
                    )
                    self.turn[c, w] = total.astype(self.turn.dtype)

                @pl.when(jnp.logical_not(inner))
                def _():
                    self.turn[c, w] = self.sums[0][c, w]

                self.along(c, w, up).start()

    def total(self, c):
        z = self.z
        if self.direct:
            total = self.sums[0][c, z].astype(jnp.float32)
            for s in (1, 2, 3):
                self.over_z(c, s).wait_recv()
                total = total + self.line[c, s].astype(jnp.float32)
            return total
        self.result[...] = self.sums[0][c, z].astype(jnp.float32)
        for up in (True, False):

            @pl.when((z > 0) if up else (z < 3))
            def _(up=up):
                self.along(c, z, up).wait_recv()
                self.result[...] += self.line[c, z + 1 if up else z].astype(jnp.float32)

        return self.result[...]

    lag = 1

    def length(self):
        return self.chunks + len(self.axes) + self.lag

    def advance(self, step, use):
        depth = len(self.axes)
        for level in range(depth - 1, -1, -1):
            c = step - (depth - 1 - level)
            if 0 <= c < self.chunks:
                self.fold(level, c)
        c = step - (depth - 1)
        if 0 <= c < self.chunks:
            self.relay(c)
        c = step - depth - self.lag + 1
        if 0 <= c < self.chunks:
            use(c, pl.ds(c * self.rows, self.rows), self.total(c))

    def run(self, use):
        for step in range(self.length()):
            self.advance(step, use)

    def finish(self):
        for copy in sum(self.flying, []):
            copy.wait_send()
        for c in range(self.chunks):
            if self.direct:
                for s in (1, 2, 3):
                    self.over_z(c, s).wait_send()
                continue
            for w, up in self.steps():

                @pl.when((self.z < w) if up else (self.z > w))
                def _(w=w, up=up, c=c):
                    self.along(c, w, up).wait_send()


class Gather:
    def __init__(self, own, out, axes, chunks, refs, direct=False):
        self.own, self.out, self.axes, self.chunks, self.direct = own, out, axes, chunks, direct
        self.keep_sem = refs[0]
        self.sems = [refs[1 + 2 * i : 3 + 2 * i] for i in range(len(axes) + 1)]
        self.z = lax.axis_index("z")
        self.mine = tuple(lax.axis_index(a) for a in axes)
        self.rows = own.shape[0] // chunks
        self.keeps = []

    @staticmethod
    def scratch(axes, chunks):
        shapes = [pltpu.SemaphoreType.DMA((chunks,)), *dma_pair(8 * chunks)]
        for i in range(len(axes)):
            shapes += dma_pair(4 * 2**i * chunks)
        return shapes

    def block(self, c, w, flips):
        places = tuple(
            1 - m if i < len(flips) and flips[i] else m for i, m in enumerate(self.mine)
        )
        return self.out.at[(w,) + places + (pl.ds(c * self.rows, self.rows),)]

    def along(self, c, w, up, own=False):
        where = self.block(c, w, ())
        return pltpu.make_async_remote_copy(
            src_ref=self.own.at[pl.ds(c * self.rows, self.rows)] if own else where,
            dst_ref=where,
            send_sem=self.sems[0][0].at[(w * 2 + int(up)) * self.chunks + c],
            recv_sem=self.sems[0][1].at[w * self.chunks + c],
            device_id={"z": self.z + 1 if up else self.z - 1},
            device_id_type=MESH,
        )

    def across(self, level, c, w, flips, own=False):
        where = self.block(c, w, flips)
        number = w
        for f in flips:
            number = number * 2 + f
        at = number * self.chunks + c
        return pltpu.make_async_remote_copy(
            src_ref=self.own.at[pl.ds(c * self.rows, self.rows)] if own else where,
            dst_ref=where,
            send_sem=self.sems[level + 1][0].at[at],
            recv_sem=self.sems[level + 1][1].at[at],
            device_id={self.axes[level]: 1 - self.mine[level]},
            device_id_type=MESH,
        )

    def over_z(self, c, s):
        where = self.block(c, self.z, ())
        return pltpu.make_async_remote_copy(
            src_ref=self.own.at[pl.ds(c * self.rows, self.rows)],
            dst_ref=where,
            send_sem=self.sems[0][0].at[s * self.chunks + c],
            recv_sem=self.sems[0][1].at[s * self.chunks + c],
            device_id={"z": self.z ^ s},
            device_id_type=MESH,
        )

    def start(self, c):
        z = self.z
        for s in (3, 2, 1) if self.direct else ():
            self.over_z(c, s).start()
        for up in () if self.direct else (True, False):

            @pl.when((z < 3) if up else (z > 0))
            def _(up=up):
                self.along(c, z, up, own=True).start()

        for level in range(len(self.axes)):
            self.across(level, c, z, (0,) * level, own=True).start()
        keep = pltpu.make_async_copy(
            self.own.at[pl.ds(c * self.rows, self.rows)], self.block(c, z, ()), self.keep_sem.at[c]
        )
        keep.start()
        self.keeps.append(keep)

    def forward(self, c, hops=(1, 2, 3)):
        z = self.z
        for s in hops if self.direct else ():
            self.over_z(c, s).wait_recv()
            for level in range(len(self.axes)):
                self.across(level, c, z ^ s, (0,) * level).start()
        for t in () if self.direct else hops:
            for up in (True, False):

                @pl.when((z >= t) if up else (z + t <= 3))
                def _(t=t, up=up):
                    w = z - t if up else z + t
                    self.along(c, w, up).wait_recv()

                    @pl.when((z < 3) if up else (z > 0))
                    def _():
                        self.along(c, w, up).start()

                    for level in range(len(self.axes)):
                        self.across(level, c, w, (0,) * level).start()

    def flips(self, level):
        return [tuple((i >> b) & 1 for b in range(level)) for i in range(2**level)]

    def spread(self, c):
        for level in range(len(self.axes) - 1):
            for s in range(4):
                for flips in self.flips(level):
                    w = self.z ^ s
                    turned = flips + (1,)
                    self.across(level, c, w, flips).wait_recv()
                    for later in range(level + 1, len(self.axes)):
                        self.across(later, c, w, turned + (0,) * (later - level - 1)).start()

    def finish(self):
        z, last = self.z, len(self.axes) - 1
        for keep in self.keeps:
            keep.wait()
        for c in range(self.chunks):
            for s in range(4):
                for flips in self.flips(last):
                    self.across(last, c, z ^ s, flips).wait_recv()
                for level in range(last + 1):
                    for flips in self.flips(level):
                        self.across(level, c, z ^ s, flips).wait_send()
            for s in (1, 2, 3) if self.direct else ():
                self.over_z(c, s).wait_send()
            for t in () if self.direct else (0, 1, 2, 3):
                for up in (True, False):
                    here = ((z >= t) & (z < 3)) if up else ((z + t <= 3) & (z > 0))

                    @pl.when(here)
                    def _(t=t, up=up, c=c):
                        self.along(c, z - t if up else z + t, up).wait_send()


VMEM_SPEC = pl.BlockSpec(memory_space=pltpu.VMEM)
ANY_SPEC = pl.BlockSpec(memory_space=pl.ANY)


def whole(shape):
    return pl.BlockSpec(tuple(shape), lambda i: (0,) * len(shape))


def exchange(kernel, name, number, inputs, specs, outs, out_specs, scratch):
    sizes = [len(inputs), len(outs)] + [len(s) for s in scratch]

    def run(*refs):
        groups, at = [], 0
        for size in sizes:
            groups.append(refs[at : at + size])
            at += size
        kernel(*groups)

    return pl.pallas_call(
        run,
        out_shape=outs,
        in_specs=specs,
        out_specs=out_specs,
        scratch_shapes=sum(scratch, []),
        compiler_params=pltpu.CompilerParams(
            collective_id=number, has_side_effects=True, vmem_limit_bytes=50 * 2**20
        ),
        name=name,
    )(*inputs)


def share_inputs(tokens, slices, wo, marked, win, wout):
    count, own = tokens.shape[0], wo.shape[0]
    columns, wide = slices.shape[-1], marked.shape[-1]
    depth, half = win.shape[1], HID // 2
    number = 2 * win.shape[0] // 4
    early = number - LATE
    chunks = 2
    bf16 = jnp.bfloat16

    def kernel(ins, outs, token_refs, wo_refs, marked_refs, other):
        tok, cut, wo_ref, marked_ref, win_ref, wout_ref = ins
        tok_out, cut_out, wo_out, marked_out = outs[:4]
        near, far, late = outs[4:8], (outs[8], None, *outs[9:11]), outs[11]
        keep, ctx_sems, exp_sems = other[0], other[1:3], other[3:5]
        near_sems, far_sems, win_in, wout_in, unit = other[5:7], other[7:9], *other[9:12]
        z, y, x, k = (lax.axis_index(a) for a in ("z", "y", "x", "k"))
        loads = [
            pltpu.make_async_copy(win_ref, win_in, keep.at[1]),
            pltpu.make_async_copy(wout_ref, wout_in, keep.at[2]),
        ]
        for copy in loads:
            copy.start()
        exp_peers = [((x ^ a, k ^ b), a * 2 + b) for a in (1, 0) for b in (1, 0) if a or b]
        greet(
            [{"z": p, "y": q} for p, q, _ in ctx_peers()]
            + [{"x": p, "k": q} for (p, q), _ in exp_peers]
        )
        gather = Gather(tok, tok_out, ("y",), chunks, token_refs)
        whole = Gather(wo_ref, wo_out, ("y", "x", "k"), 1, wo_refs)
        other_rows = Gather(marked_ref, marked_out, ("x", "k"), 1, marked_refs)
        over_ctx = [
            send(cut.at[p, q], cut_out.at[z, y, x, k], ctx_sems, i - 1, {"z": p, "y": q})
            for p, q, i in ctx_peers()
        ]
        whole.start(0)
        for c in range(chunks):
            gather.start(c)
        other_rows.start(0)
        copy_own = pltpu.make_async_copy(cut.at[z, y], cut_out.at[z, y, x, k], keep.at[0])
        copy_own.start()

        def over_z(i, j):
            return pltpu.make_async_remote_copy(
                src_ref=unit.at[i, j],
                dst_ref=near[i].at[j],
                send_sem=near_sems[0].at[i * number + j],
                recv_sem=near_sems[1].at[i * number + j],
                device_id={"z": z ^ i},
                device_id_type=MESH,
            )

        def over_y(i, j):
            return pltpu.make_async_remote_copy(
                src_ref=near[i].at[j] if i else unit.at[0, j],
                dst_ref=far[i].at[j],
                send_sem=far_sems[0].at[i * number + j],
                recv_sem=far_sems[1].at[i * number + j],
                device_id={"y": 1 - y},
                device_id_type=MESH,
            )

        def own_unit(j):
            return pltpu.make_async_copy(unit.at[0, j], near[0].at[j], keep.at[3 + j])

        def late_unit(j):
            return pltpu.make_async_copy(unit.at[3, j], late.at[j - early], keep.at[3 + number + j])

        def convert(j):
            for i in range(4):
                index = number * (z ^ i) + j
                e, h = index // 2, lax.rem(index, 2)
                first = pl.ds(pl.multiple_of(h * half, half), half)
                second = pl.ds(pl.multiple_of(HID + h * half, half), half)
                unit[i, j, :, :half] = win_in[e, :, first].astype(bf16)
                unit[i, j, :, half : 2 * half] = win_in[e, :, second].astype(bf16)
                unit[i, j, :, 2 * half :] = wout_in[e, :, first].astype(bf16)

        def send_units(j):
            for i in (3, 2, 1) if j < early else (2, 1):
                over_z(i, j).start()

        def pass_units(j):
            for i in (2, 3) if j < early else (2,):
                over_z(i, j).wait_recv()
                over_y(i, j).start()

        for copy in loads:
            copy.wait()
        convert(0)
        send_units(0)
        for j in range(number):
            if j:
                convert(j)
            own_unit(j).start()
            if j >= early:
                late_unit(j).start()
            over_y(0, j).start()
        for t in (1, 2, 3):
            whole.forward(0, (t,))
            for c in range(chunks):
                gather.forward(c, (t,))
            other_rows.forward(0, (t,))
            send_units(t)
            if t == 1:
                for copy in over_ctx:
                    copy.wait_recv()
                copy_own.wait()
                mine = cut_out.at[:, :, x, k]
                over_exp = [
                    send(mine, mine, exp_sems, i - 1, {"x": p, "k": q})
                    for (p, q), i in exp_peers
                ]
            pass_units(t - 1)
        for j in range(4, number):
            send_units(j)
        whole.spread(0)
        other_rows.spread(0)
        for j in range(3, number):
            pass_units(j)
        for copy in over_exp:
            copy.wait_recv()
        gather.finish()
        whole.finish()
        other_rows.finish()
        for copy in over_ctx + over_exp:
            copy.wait_send()
        for j in range(number):
            own_unit(j).wait()
            if j >= early:
                late_unit(j).wait()
            for i in range(4):
                if i == 3 and j >= early:
                    continue
                if i == 1:
                    over_z(i, j).wait_recv()
                else:
                    over_y(i, j).wait_recv()
                    over_y(i, j).wait_send()
                if i:
                    over_z(i, j).wait_send()

    units, most, few = (
        jax.ShapeDtypeStruct((n, depth, 3 * half), bf16) for n in (number, early, LATE)
    )
    outs = exchange(
        kernel,
        "share_inputs",
        1,
        (tokens, slices, wo, marked, win, wout),
        [ANY_SPEC] * 6,
        [
            jax.ShapeDtypeStruct((4, 2, count, D), bf16),
            jax.ShapeDtypeStruct((4, 2, 2, 2, own, columns), bf16),
            jax.ShapeDtypeStruct((4, 2, 2, 2, own, D), bf16),
            jax.ShapeDtypeStruct((4, 2, 2, count, wide), bf16),
        ]
        + [units] * 3
        + [most, units, units, most, few],
        [ANY_SPEC] * 12,
        [
            Gather.scratch(("y",), chunks),
            Gather.scratch(("y", "x", "k"), 1),
            Gather.scratch(("x", "k"), 1),
            [pltpu.SemaphoreType.DMA((3 + 2 * number,))]
            + dma_pair(7)
            + dma_pair(3)
            + dma_pair(4 * number)
            + dma_pair(4 * number)
            + [
                pltpu.VMEM(win.shape, jnp.float32),
                pltpu.VMEM(wout.shape, jnp.float32),
                pltpu.VMEM((4, number, depth, 3 * half), bf16),
            ],
        ],
    )
    return (*outs[:4], outs[4:8], outs[8:11], outs[11])


def ctx_peers():
    z, y = lax.axis_index("z"), lax.axis_index("y")
    return [(z ^ (i // 2), y ^ (i % 2), i) for i in range(7, 0, -1)]


def middle_step(heads, tokens, wo, gain, bulk):
    count, chunks = tokens.shape[0], 2
    width = heads.shape[-1]
    bf16, f32 = jnp.bfloat16, jnp.float32

    def kernel(ins, outs, hidden_refs, other):
        heads_ref, tok, wo_ref, gain_ref = ins[:4]
        attended_ref, middle_ref, hidden_out = outs[:3]
        own, sems, bulk_sems = other[0], other[1:3], other[3:5]
        z, y = lax.axis_index("z"), lax.axis_index("y")
        greet(
            [{"z": p, "y": q} for p, q, _ in ctx_peers()] + siblings(("x", "k"))
        )
        hidden = Gather(own, hidden_out, ("x", "k"), chunks, hidden_refs)
        copies = [
            send(heads_ref.at[p, q], attended_ref.at[z, y], sems, i - 1, {"z": p, "y": q})
            for p, q, i in ctx_peers()
        ]
        attended_ref[z, y] = heads_ref[z, y]
        bulk_copies = [
            send(a, b, bulk_sems, i, {"y": 1 - y}) for i, (a, b) in enumerate(zip(ins[4:], outs[3:]))
        ]
        for copy in copies:
            copy.wait_recv()
        step = count // chunks
        middle = tok[...].astype(f32)
        for i in range(8):
            middle = middle + jnp.dot(
                attended_ref[i // 2, i % 2],
                wo_ref[i * width : (i + 1) * width, :],
                preferred_element_type=f32,
            )
        middle_ref[...] = middle
        for c in range(chunks):
            at = pl.ds(c * step, step)
            middle = middle_ref[at, :]
            scale = lax.rsqrt(jnp.mean(middle * middle, axis=-1, keepdims=True) + EPSILON)
            own[at, :] = (middle * scale * gain_ref[...]).astype(bf16)
            hidden.start(c)
        for c in range(chunks):
            hidden.forward(c)
            hidden.spread(c)
        hidden.finish()
        for copy in bulk_copies:
            copy.wait_recv()
        for copy in copies + bulk_copies:
            copy.wait_send()

    return exchange(
        kernel,
        "middle_step",
        2,
        (heads, tokens, wo, gain, *bulk),
        [VMEM_SPEC] * 4 + [ANY_SPEC] * len(bulk),
        [
            jax.ShapeDtypeStruct((4, 2, count, width), bf16),
            jax.ShapeDtypeStruct((count, D), f32),
            jax.ShapeDtypeStruct((4, 2, 2, count, D), bf16),
        ]
        + [jax.ShapeDtypeStruct(a.shape, a.dtype) for a in bulk],
        [VMEM_SPEC, VMEM_SPEC, ANY_SPEC] + [ANY_SPEC] * len(bulk),
        [
            Gather.scratch(("x", "k"), chunks),
            [pltpu.VMEM((count, D), bf16)] + dma_pair(7) + dma_pair(len(bulk)),
        ],
    )


def router_step(part, mixed, middle, cotangent, gates, router, gain, wo, bulk, added):
    count, chunks = middle.shape[0], 4
    width, (number, depth, _) = wo.shape[0] // 8, added.shape
    early = number - LATE
    bf16, f32 = jnp.bfloat16, jnp.float32

    def kernel(ins, outs, scatter_refs, mixed_refs, other):
        part_ref, mixed_ref, middle_ref, up_ref, gates_ref, router_ref, gain_ref, wo_ref = ins[:8]
        logit_ref, gain_out, grad_ref, heads_out, out_ref = outs[:5]
        turned, sems, bulk_sems, first_sems, far_sems = other[0], *(
            other[i : i + 2] for i in (1, 3, 5, 7)
        )
        own_unit, came_unit, load_sem = other[9:12]
        bulk_in, bulk_out, added_ref = ins[8:-1], outs[6:], ins[-1]
        far_out = outs[5]
        z, y = lax.axis_index("z"), lax.axis_index("y")
        load = pltpu.make_async_copy(added_ref.at[pl.ds(0, early)], own_unit, load_sem.at[0])
        load.start()
        greet([{"z": p, "y": q} for p, q, _ in ctx_peers()] + siblings(("x", "k")))
        scatter = Scatter(part_ref, ("x", "k"), chunks, scatter_refs)
        mixture = Scatter(mixed_ref, ("x", "k"), chunks, mixed_refs)
        copies = []
        scatter.start()
        mixture.start()
        pieces = 2 * early
        piece = lambda ref, j: ref.at[j // 2, pl.ds(j % 2 * (depth // 2), depth // 2)]
        over_first = [
            send(piece(bulk_in[0], j), piece(came_unit, j), first_sems, j, {"y": 1 - y})
            for j in range(pieces)
        ]
        over_far = []
        bulk_copies = [
            send(
                bulk_in[0].at[pl.ds(early, number - early)], bulk_out[0], bulk_sems, 0, {"y": 1 - y}
            ),
            send(bulk_in[1], bulk_out[1], bulk_sems, 1, {"y": 1 - y}),
        ]
        load.wait()

        def send_far(j):
            over_first[j].wait_recv()
            mine = piece(own_unit, j)
            total = mine[...].astype(f32) + piece(came_unit, j)[...].astype(f32)
            mine[...] = total.astype(bf16)
            over_far.append(send(mine, piece(far_out, j), far_sems, j, {"z": z ^ 3}))

        gain_out[...] = jnp.zeros_like(gain_out)

        def use(c, at, total):
            gate, gate_grad = gates_ref[at, :], total[:, D:]
            inner = jnp.sum(gate * gate_grad, axis=-1, keepdims=True)
            logit_grad = (gate * (gate_grad - inner)).astype(bf16)
            logit_ref[at, :] = logit_grad
            grad = total[:, :D] + contract_cols(logit_grad, router_ref[...])
            middle = middle_ref[at, :]
            scale = lax.rsqrt(jnp.mean(middle * middle, axis=-1, keepdims=True) + EPSILON)
            normed = middle * scale
            gain_out[...] += jnp.sum(grad * normed, axis=0, keepdims=True)
            scaled = grad * gain_ref[...]
            result = up_ref[at, :].astype(f32) + scale * (
                scaled - normed * jnp.mean(scaled * normed, axis=-1, keepdims=True)
            )
            grad_ref[at, :] = result

        def to_heads():
            down = grad_ref[...].astype(bf16)
            for i in range(8):
                turned[i // 2, i % 2] = contract_cols(
                    down, wo_ref[i * width : (i + 1) * width, :]
                ).astype(bf16)
            for p, q, i in ctx_peers():
                copies.append(
                    send(
                        turned.at[p, q], heads_out.at[z, y], sems, i - 1, {"z": p, "y": q}
                    )
                )
            heads_out[z, y] = turned[z, y]
            bulk_copies.append(send(bulk_in[2], bulk_out[2], bulk_sems, 2, {"y": 1 - y}))

        def use_mixture(c, at, total):
            out_ref[at, :] = (middle_ref[at, :] + total).astype(bf16)

        behind = 3
        plan = [[0, 1], [2], [3], [4], [5]] + [[]] * 5
        for step in range(scatter.length() + behind):
            if step < scatter.length():
                scatter.advance(step, use)
            if step == scatter.length() - 1:
                to_heads()
            if step >= behind:
                mixture.advance(step - behind, use_mixture)
            for j in plan[step]:
                send_far(j)
        for copy in copies + bulk_copies + over_far:
            copy.wait_recv()
        for copy in copies + bulk_copies + over_first + over_far:
            copy.wait_send()
        scatter.finish()
        mixture.finish()

    return exchange(
        kernel,
        "router_step",
        3,
        (part, mixed, middle, cotangent, gates, router, gain, wo, *bulk, added),
        [ANY_SPEC] * 2 + [VMEM_SPEC] * 6 + [ANY_SPEC] * 4,
        [
            jax.ShapeDtypeStruct((count, 128), bf16),
            jax.ShapeDtypeStruct((1, D), f32),
            jax.ShapeDtypeStruct((count, D), f32),
            jax.ShapeDtypeStruct((4, 2, count, width), bf16),
            jax.ShapeDtypeStruct((count, D), bf16),
        ]
        + [
            jax.ShapeDtypeStruct((n, *added.shape[1:]), bf16)
            for n in (early, number - early, number, number)
        ],
        [VMEM_SPEC] * 5 + [ANY_SPEC] * 4,
        [
            Scatter.scratch(part, ("x", "k"), chunks),
            Scatter.scratch(mixed, ("x", "k"), chunks),
            [pltpu.VMEM((4, 2, count, width), bf16)] + dma_pair(7) + dma_pair(3) + dma_pair(2 * early) * 2
            + [pltpu.VMEM((early, *added.shape[1:]), bf16)] * 2 + [pltpu.SemaphoreType.DMA((1,))],
        ],
    )


def last_step(
    part, tokens, grad_middle, gain, qkv_part, wo_part, small_part
):
    count, chunks = tokens.shape[0], 4
    own, columns = qkv_part.shape[-2:]
    bf16, f32 = jnp.bfloat16, jnp.float32

    def kernel(ins, outs, part_refs, wo_refs, other):
        part_ref, tok, grad_ref, gain_ref, qkv, wo, small = ins
        tokens_ref, qkv_out, wo_out, small_out = outs
        qkv_came, qkv_sum, small_came = other[:3]
        sems = [other[3 + 2 * i : 5 + 2 * i] for i in range(3)]
        names = ("z", "y", "x", "k")
        z, y, x, k = (lax.axis_index(a) for a in names)
        everyone = [
            ((z ^ (i // 8), y ^ (i // 4 % 2), x ^ (i // 2 % 2), k ^ (i % 2)), i)
            for i in range(31, 0, -1)
        ]
        of_ctx = [(p, i // 4) for p, i in everyone if i % 4 == 0]
        of_exp = [(p, i) for p, i in everyone if i < 4]
        place = lambda p: dict(zip(names, p))
        greet([place(p) for p, _ in everyone])
        first = Scatter(part_ref, ("y",), chunks, part_refs)
        third = Scatter(wo, ("y", "x", "k"), 3, wo_refs, True)
        first.start()
        third.start()
        over_qkv = [
            send(qkv.at[p[2], p[3]], qkv_came.at[i - 1], sems[0], i - 1, place(p))
            for p, i in of_exp
        ]
        def use_first(c, at, total):
            resid = tok[at, :].astype(f32)
            scale = lax.rsqrt(jnp.mean(resid * resid, axis=-1, keepdims=True) + EPSILON)
            normed = resid * scale
            scaled = total * gain_ref[...]
            tokens_ref[at, :] = grad_ref[at, :] + scale * (
                scaled - normed * jnp.mean(scaled * normed, axis=-1, keepdims=True)
            )

        def use_third(c, at, total):
            wo_out[at, :] = total

        for step in range(third.length()):
            if step < first.length():
                first.advance(step, use_first)
            if step < third.length():
                third.advance(step, use_third)
            if step == 1:
                total = qkv[x, k].astype(f32)
                for copy, (_, i) in zip(over_qkv, of_exp):
                    copy.wait_recv()
                    total = total + qkv_came[i - 1].astype(f32)
                qkv_sum[...] = total.astype(bf16)
                qkv_out[z, y] = qkv_sum[z, y]
                over_ctx = [
                    send(qkv_sum.at[p[0], p[1]], qkv_out.at[z, y], sems[1], i - 1, place(p))
                    for p, i in of_ctx
                ]
                over_small = [
                    send(small.at[p], small_came.at[i - 1], sems[2], i - 1, place(p))
                    for p, i in everyone
                ]
        total = small[z, y, x, k].astype(f32)
        for copy, (_, i) in zip(over_small, everyone):
            copy.wait_recv()
            total = total + small_came[i - 1].astype(f32)
        small_out[...] = total
        for copy in over_ctx:
            copy.wait_recv()
        first.finish()
        third.finish()
        for copy in over_qkv + over_ctx + over_small:
            copy.wait_send()

    return exchange(
        kernel,
        "last_step",
        4,
        (part, tokens, grad_middle, gain, qkv_part, wo_part, small_part),
        [ANY_SPEC] + [VMEM_SPEC] * 4 + [ANY_SPEC, VMEM_SPEC],
        [
            jax.ShapeDtypeStruct((count, D), f32),
            jax.ShapeDtypeStruct((4, 2, own, columns), bf16),
            jax.ShapeDtypeStruct((own, D), f32),
            jax.ShapeDtypeStruct((own, 128), f32),
        ],
        [VMEM_SPEC] * 4,
        [
            Scatter.scratch(part, ("y",), chunks),
            Scatter.scratch(wo_part, ("y", "x", "k"), 3),
            [
                pltpu.VMEM((3, 4, 2, own, columns), bf16),
                pltpu.VMEM((4, 2, own, columns), bf16),
                pltpu.VMEM((31, own, 128), bf16),
            ]
            + dma_pair(3)
            + dma_pair(7)
            + dma_pair(31),
        ],
    )


def pick(rows, columns, kind, test):
    row = lax.broadcasted_iota(jnp.int32, (rows, columns), 0)
    column = lax.broadcasted_iota(jnp.int32, (rows, columns), 1)
    return jnp.where(test(row, column), 1.0, 0.0).astype(kind)


def half_swap():
    to_first = pick(256, 256, jnp.float32, lambda r, c: (c % HEAD < HEAD // 2) & (r == c + HEAD // 2))
    to_second = pick(
        256, 256, jnp.float32, lambda r, c: (c % HEAD >= HEAD // 2) & (r + HEAD // 2 == c)
    )
    return to_second - to_first


def twice(a):
    return jnp.concatenate([a, a], axis=-1)


def exact_dot(left, right):
    return jnp.dot(
        left, right, preferred_element_type=jnp.float32, precision=lax.Precision.HIGHEST
    )


def attention_forward_kernel(
    experts, tok, weight, cosine, sine, rows, starts, key_rows,
    hidden, qk, keys, values, out, lse, gains, router
):
    bf16, f32 = jnp.bfloat16, jnp.float32
    swap = half_swap()
    width = out.shape[-1]
    to_keys = pick(256, 256, bf16, lambda r, c: (c < width) & (r - width == c % HEAD))
    to_values = pick(128, 256, bf16, lambda r, c: (c < width) & (r == c % HEAD))
    block = 256
    steps = tok.shape[0] // block
    first = width + 2 * HEAD
    chosen = pick(8, weight.shape[1], bf16, lambda r, c: (r < 2) & (c == first + experts + r))
    gains[...] = contract_cols(chosen, weight[...])
    to_router = pick(128, 128, bf16, lambda r, c: (c < experts) & (r + 256 == first + c))
    router[...] = jnp.dot(weight[:, 256:], to_router, preferred_element_type=f32).astype(bf16)

    def project(b, carry):
        at = pl.ds(pl.multiple_of(b * block, block), block)
        x = tok[at, :].astype(f32)
        normed = x * lax.rsqrt(jnp.mean(x * x, axis=-1, keepdims=True) + EPSILON)
        h = (normed * gains[0:1, :]).astype(bf16)
        hidden[at, :] = h
        t = jnp.dot(h, weight[...], preferred_element_type=f32)
        u = t[:, :256]
        turned = (u * twice(cosine[at, :]) + exact_dot(u, swap) * twice(sine[at, :])).astype(bf16)
        qk[at, :] = turned
        keys[at, :] = jnp.dot(turned, to_keys, preferred_element_type=f32).astype(bf16)
        values[at, :] = jnp.dot(
            t[:, 256:].astype(bf16), to_values, preferred_element_type=f32
        ).astype(bf16)
        return carry

    lax.fori_loop(0, steps, project, 0)
    head = lax.broadcasted_iota(jnp.int32, (block, 256), 1) // HEAD
    lane = lax.broadcasted_iota(jnp.int32, (block, 128), 1)

    def attend(b, carry):
        at = pl.ds(pl.multiple_of(b * block, block), block)
        mask = (key_rows[...] <= rows[at, :]) & (key_rows[...] >= starts[at, :])
        result = jnp.zeros((block, 256), f32)
        logs = jnp.zeros((block, 128), f32)
        for h in range(HEADS // KV_HEADS):
            query = jnp.where(head == h, qk[at, :], jnp.zeros((), bf16))
            scores = contract_cols(query, keys[...]) * HEAD ** (-0.5)
            scores = jnp.where(mask, scores, NEGATIVE)
            top = jnp.max(scores, axis=-1, keepdims=True)
            weights = jnp.exp(scores - top)
            total = jnp.sum(weights, axis=-1, keepdims=True)
            mixed = jnp.dot(weights.astype(bf16), values[...], preferred_element_type=f32)
            result = jnp.where(head == h, mixed / total, result)
            logs = jnp.where(lane == h, top + jnp.log(total), logs)
        out[at, :] = result[:, :width].astype(bf16)
        lse[at, :] = logs
        return carry

    lax.fori_loop(0, steps, attend, 0)


def attention_forward(experts, tokens, weight, cosine, sine, rows, starts):
    count, width = tokens.shape[0], HEADS // KV_HEADS * HEAD
    bf16, f32 = jnp.bfloat16, jnp.float32
    shape = jax.ShapeDtypeStruct
    inputs = (tokens, weight, cosine, sine, rows[:, None], starts[:, None], rows[None, :])
    outs = (
        [shape((count, D), bf16)]
        + [shape((count, 256), bf16)] * 3
        + [shape((count, width), bf16), shape((count, 128), f32)]
        + [shape((8, D), f32), shape((D, 128), bf16)]
    )
    return pl.pallas_call(
        lambda *refs: attention_forward_kernel(experts, *refs),
        grid=(1,),
        in_specs=[whole(a.shape) for a in inputs],
        out_specs=[whole(a.shape) for a in outs],
        out_shape=outs,
        compiler_params=pltpu.CompilerParams(vmem_limit_bytes=56 * 2**20),
        name="attention_forward",
    )(*inputs)


def attention_backward_kernel(
    hidden, qk, keys, values, lse, upstream, weight, cosine, sine, rows, starts, key_rows,
    weight_grad, hidden_grad, grads, query_grad, key_grad, value_grad, up
):
    bf16, f32 = jnp.bfloat16, jnp.float32
    width = upstream.shape[-1]
    scale = HEAD ** (-0.5)
    block = 256
    steps = hidden.shape[0] // block
    head = lax.broadcasted_iota(jnp.int32, (block, 256), 1) // HEAD
    lane = lax.broadcasted_iota(jnp.int32, (block, 128), 1)
    up[...] = jnp.zeros_like(up)
    up[:, :width] = upstream[...]
    key_grad[...] = jnp.zeros_like(key_grad)
    value_grad[...] = jnp.zeros_like(value_grad)

    def attend(b, carry):
        at = pl.ds(pl.multiple_of(b * block, block), block)
        mask = (key_rows[...] <= rows[at, :]) & (key_rows[...] >= starts[at, :])
        logs = lse[at, :]
        result = jnp.zeros((block, 256), f32)
        for h in range(HEADS // KV_HEADS):
            zero = jnp.zeros((), bf16)
            query = jnp.where(head == h, qk[at, :], zero)
            grad = jnp.where(head == h, up[at, :], zero)
            log = jnp.sum(jnp.where(lane == h, logs, 0.0), axis=-1, keepdims=True)
            scores = contract_cols(query, keys[...]) * scale
            weights = jnp.where(mask, jnp.exp(scores - log), 0.0)
            prob_grad = contract_cols(grad, values[...])
            drift = jnp.sum(weights * prob_grad, axis=-1, keepdims=True)
            score_grad = (weights * (prob_grad - drift)).astype(bf16)
            part = jnp.dot(score_grad, keys[...], preferred_element_type=f32)
            result = jnp.where(head == h, part, result)
            key_grad[...] += contract_rows(score_grad, query)
            value_grad[...] += contract_rows(weights.astype(bf16), grad)
        query_grad[at, :] = result
        return carry

    lax.fori_loop(0, steps, attend, 0)
    swap = half_swap()
    from_keys = pick(256, 256, f32, lambda r, c: (r < width) & (c - width == r % HEAD))
    from_values = pick(256, 128, f32, lambda r, c: (r < width) & (c == r % HEAD))

    def turn(b, carry):
        at = pl.ds(pl.multiple_of(b * block, block), block)
        t = jnp.where(head < HEADS // KV_HEADS, query_grad[at, :], 0.0)
        t = (t + exact_dot(key_grad[at, :], from_keys)) * scale
        grads[at, :256] = (
            t * twice(cosine[at, :]) - exact_dot(t, swap) * twice(sine[at, :])
        ).astype(bf16)
        grads[at, 256:] = exact_dot(value_grad[at, :], from_values).astype(bf16)
        hidden_grad[at, :] = contract_cols(grads[at, :], weight[...]).astype(bf16)
        return carry

    lax.fori_loop(0, steps, turn, 0)
    parts, places, own, columns = weight_grad.shape
    for i in range(places // 2):
        deep = 2 * parts * own
        part = contract_rows(hidden[:, i * deep : (i + 1) * deep], grads[...]).astype(bf16)
        for j in range(2 * parts):
            weight_grad[j % parts, 2 * i + j // parts] = part[j * own : (j + 1) * own, :columns]


def attention_backward(hidden, qk, keys, values, lse, upstream, weight, cosine, sine, rows, starts, own):
    count = hidden.shape[0]
    bf16, f32 = jnp.bfloat16, jnp.float32
    shape = jax.ShapeDtypeStruct
    inputs = (
        hidden, qk, keys, values, lse, upstream, weight, cosine, sine,
        rows[:, None], starts[:, None], rows[None, :],
    )
    outs = [
        shape((4, D // own // 4, own, upstream.shape[-1] + 2 * HEAD), bf16),
        shape((count, D), bf16),
    ]
    return pl.pallas_call(
        attention_backward_kernel,
        grid=(1,),
        in_specs=[whole(a.shape) for a in inputs],
        out_specs=[whole(a.shape) for a in outs],
        out_shape=outs,
        scratch_shapes=[
            pltpu.VMEM((count, 384), bf16),
            pltpu.VMEM((count, 256), f32),
            pltpu.VMEM((count, 256), f32),
            pltpu.VMEM((count, 256), f32),
            pltpu.VMEM((count, 256), bf16),
        ],
        compiler_params=pltpu.CompilerParams(vmem_limit_bytes=56 * 2**20),
        name="attention_backward",
    )(*inputs)


def body_heads(
    tokens,
    cotangent,
    lengths,
    span_perm,
    routes,
    norm_attn,
    attn_q,
    attn_k,
    attn_v,
    attn_o,
    router,
    norm_moe,
    expert_in,
    expert_out,
):
    bf16, f32 = jnp.bfloat16, jnp.float32
    n_z, n_y = (lax.axis_size(a) for a in ("z", "y"))
    n_exp = lax.axis_size("x") * lax.axis_size("k")
    n_ctx = n_z * n_y
    exp_index = lax.axis_index("x") * lax.axis_size("k") + lax.axis_index("k")
    count = tokens.shape[1]
    group = count * n_ctx
    repeat = HEADS // KV_HEADS
    width = repeat * HEAD
    experts = EXP_DEV * n_exp
    capacity = count * TOP * 3 // (2 * experts)
    slots = -(-capacity // 8) * 8
    own = attn_q.shape[0]
    softmax_scale = HEAD ** (-0.5)
    z_index = lax.axis_index("z")

    units = 2 * EXP_DEV // n_z
    y_index = lax.axis_index("y")
    win = expert_in.transpose(1, 0, 2)
    wout = expert_out.transpose(1, 0, 2)
    swap_z = [[(i, i ^ s) for i in range(n_z)] for s in range(n_z)]
    swap_y = [(i, i ^ 1) for i in range(n_y)]
    swap_z = [[(i, i ^ s) for i in range(n_z)] for s in range(n_z)]
    swap_y = [(i, i ^ 1) for i in range(n_y)]

    wq, wk, wv = (a.astype(bf16) for a in (attn_q, attn_k, attn_v))
    own_qkv = jnp.concatenate(
        [
            wq.reshape(own, n_ctx, width),
            wk.reshape(own, n_ctx, HEAD),
            wv.reshape(own, n_ctx, HEAD),
        ],
        axis=-1,
    )
    small = jnp.concatenate(
        [
            router.astype(bf16),
            norm_attn.astype(bf16)[:, None],
            norm_moe.astype(bf16)[:, None],
            jnp.zeros((own, 64 - experts - 2), bf16),
        ],
        axis=1,
    )
    slices = jnp.concatenate(
        [own_qkv.transpose(1, 0, 2), jnp.broadcast_to(small, (n_ctx, own, 64))], axis=-1
    )
    marked = jnp.concatenate(
        [cotangent[0], routes[0].astype(bf16), jnp.zeros((count, 128 - TOP), bf16)], axis=1
    )
    token_all, slices, wo, marked_blocks, near, far, late = share_inputs(
        tokens[0], slices.reshape(n_z, n_y, own, -1), attn_o.astype(bf16), marked, win, wout
    )
    late = lax.ppermute(late, "z", swap_z[3])
    token_all = token_all.reshape(group, D)
    slices = slices.reshape(D, -1)
    wo = wo.reshape(HEADS * HEAD, D)

    perm_row = span_perm[0]
    first_len = lengths[0, 0]
    rows = global_rows(perm_row, jnp.arange(group, dtype=jnp.int32))
    starts = jnp.where(rows >= first_len, first_len, 0)
    freqs = jnp.exp(
        (jnp.arange(128) % (HEAD // 2)).astype(f32) * (-2.0 * math.log(10000.0) / HEAD)
    )
    angle = (rows - starts).astype(f32)[:, None] * freqs[None, :]
    cosine, sine = jnp.cos(angle), jnp.sin(angle)
    hidden_all, queries, keys, values, attended_b, log_total, gains, weight_r = attention_forward(
        experts, token_all, slices, cosine, sine, rows, starts
    )
    gain_one_f, gain_two_f = gains[0:1], gains[1:2]
    own_attended, middle, hidden_blocks, *passed = middle_step(
        attended_b.reshape(n_z, n_y, count, width), tokens[0], wo, gain_two_f, [near[1], late]
    )
    parts = [*near, late, far[0], passed[0], far[1], far[2], passed[1]]
    hidden_blocks = hidden_blocks.reshape(-1, count, D)
    marked_blocks = marked_blocks.reshape(-1, count, D + 128)

    blocks = hidden_blocks.shape[0]
    held = 3
    base = exp_index * EXP_DEV + (units * z_index) // 2
    shift = (units * z_index) % 2
    pairs = blocks // 2
    row_in, row_up, slot_gate, spread, gates_blocks = dispatch(
        base, hidden_blocks, marked_blocks, weight_r, held, slots
    )
    gates = lax.dynamic_index_in_dim(gates_blocks, z_index * n_exp + exp_index, 0, keepdims=False)

    meta = jnp.stack([shift, z_index, y_index, base]).astype(jnp.int32)
    made, back, *grads = run_experts(
        meta, row_in, row_up, slot_gate, parts
    )
    made, back = combine(spread, made, back)
    logit_grad, grad_gain_two, grad_middle, grad_heads, output, far_sum, *others = router_step(
        back.reshape(n_z, 2, 2, count, D + 128),
        made.reshape(n_z, 2, 2, count, D),
        middle,
        cotangent[0],
        gates,
        weight_r,
        gain_two_f,
        wo,
        [grads[7], grads[6], grads[5]],
        grads[3],
    )

    add = lambda a, b: (a.astype(f32) + b.astype(f32)).astype(bf16)
    late_sum, mid_sum = add(grads[3][-LATE:], others[0]), add(grads[2], others[1])
    late_sum, mid_sum, grads[4], grad_heads = lax.optimization_barrier(
        (late_sum, mid_sum, grads[4], grad_heads)
    )
    late_sum = lax.ppermute(late_sum, "z", swap_z[3])
    mid_sum = lax.ppermute(mid_sum, "z", swap_z[2])
    other = lax.ppermute(grads[4], "y", swap_y)
    near_sum = lax.ppermute(add(grads[1], others[2]), "z", swap_z[1])

    hidden_two = lax.dynamic_index_in_dim(
        hidden_blocks, z_index * n_exp + exp_index, 0, keepdims=False
    )
    small_grads = jnp.concatenate(
        [
            contract_rows(hidden_two, logit_grad)[:, : 128 - 1],
            grad_gain_two.reshape(D, 1),
        ],
        axis=1,
    )
    small_grads = small_grads.astype(bf16).reshape(n_z, n_y, 2, 2, own, 128)

    grad_wo = jnp.einsum(
        "cth,td->chd",
        own_attended.reshape(n_ctx, count, width),
        grad_middle.astype(bf16),
        preferred_element_type=f32,
    ).astype(bf16)
    grad_wqkv, grad_hidden = attention_backward(
        hidden_all,
        queries,
        keys,
        values,
        log_total,
        grad_heads.reshape(group, width),
        slices,
        cosine,
        sine,
        rows,
        starts,
        own,
    )
    grad_hidden = grad_hidden.reshape(n_z, n_y, count, D)
    grad_tokens, grad_wqkv, grad_wo, small_grads = last_step(
        grad_hidden,
        tokens[0],
        grad_middle,
        gain_one_f,
        grad_wqkv.reshape(2, 2, n_z, n_y, own, width + 2 * HEAD),
        grad_wo.reshape(n_z, n_y, 2, 2, own, D),
        small_grads,
    )
    grad_expert_in, grad_expert_out = place_units(
        z_index, grads[0], other, near_sum, mid_sum, far_sum, late_sum
    )
    grad_expert_in = grad_expert_in.transpose(1, 0, 2)
    grad_expert_out = grad_expert_out.transpose(1, 0, 2)
    grad_wqkv = grad_wqkv.reshape(n_ctx, own, width + 2 * HEAD).astype(f32)
    grad_q = grad_wqkv[:, :, :width].transpose(1, 0, 2).reshape(own, HEADS * HEAD)
    grad_k = grad_wqkv[:, :, width : width + HEAD].transpose(1, 0, 2).reshape(own, KV_HEADS * HEAD)
    grad_v = grad_wqkv[:, :, width + HEAD :].transpose(1, 0, 2).reshape(own, KV_HEADS * HEAD)
    grad_gain_one = jnp.sum(
        grad_wqkv.transpose(1, 0, 2) * own_qkv.astype(f32), axis=(1, 2)
    ) / norm_attn.astype(bf16).astype(f32)
    return (
        output[None],
        grad_tokens[None],
        grad_gain_one,
        grad_q,
        grad_k,
        grad_v,
        grad_wo,
        small_grads[:, :experts],
        small_grads[:, 127],
        grad_expert_in,
        grad_expert_out,
    )


def solution(mesh):
    ctx, exp = mesh.shape["ctx"], mesh.shape["exp"]
    if ctx == KV_HEADS and exp == 4:
        names = ("z", "y", "x", "k")
        inner = jax.sharding.Mesh(mesh.devices.reshape(4, 2, 2, 2), names)
        body, ctx_name, exp_name, both = body_heads, names[:2], names[2:], names
    else:
        inner, body, ctx_name, exp_name, both = mesh, body_general, "ctx", "exp", ("ctx", "exp")
    token = P(exp_name, ctx_name, None)
    group = P(exp_name, None)
    expert = P(ctx_name, exp_name, None)
    rows, gain = P(both, None), P(both)
    in_specs = (token, token, group, group, token, gain) + (rows,) * 5 + (gain, expert, expert)
    out_specs = (token, token, gain) + (rows,) * 5 + (gain, expert, expert)
    return jax.shard_map(
        body, mesh=inner, in_specs=in_specs, out_specs=out_specs, check_vma=False
    )
```
